32 devices in a mesh: section: 4 (over y, core), rows: 8 (over z, x).
Axes of the slice: x: 2, y: 2, z: 4, core: 2. Of those that a mesh axis runs over, the one named last changes fastest.
Arguments:
- grad_in: bfloat16 [4, 2048, 256], P('section', 'rows'), may hold values from -6 to 6
- grad_last: bfloat16 [2048, 256], P('rows'), may hold values from -6 to 6
- support: bfloat16 [4, 2, 2, 2048, 256], P('section', None, None, 'rows'), may hold values from -6 to 6
- preact: bfloat16 [4, 2, 2, 2048, 256], P('section', None, None, 'rows'), may hold values from -6 to 6
- weights: bfloat16 [4, 2, 256, 256], P('section'), may hold values from -0.375 to 0.375
- tile_vals: bfloat16 [4, 2, 768, 128, 128], P('section', None, 'rows'), may hold values from -0.078125 to 0.078125
- tile_row: int32 [4, 2, 768], P('section', None, 'rows'), may hold values from 0 to 1
- tile_col: int32 [4, 2, 768], P('section', None, 'rows'), may hold values from 0 to 15, as said below
- tile_count: int32 [4, 2, 8], P('section', None, 'rows'), may hold values from 48 to 96, as said below
Outputs:
- handoff: bfloat16 [2, 4, 2048, 256], P(None, 'section', 'rows')
- init_grad: float32 [4, 2, 2048, 256], P('section', None, 'rows')
- weight_grad: float32 [4, 2, 256, 256], P('section')
The draws below stay inside these ranges and needn't reach their ends.
Inputs may be any that keep to these rules, and one draw needn't show every extreme that they name: tile_count[s, t, d] is the number of live entries in device d's list; in every section and micro-batch some device has all 96 live. `tile_col`: for every section, micro-batch and pair of devices d and o with o != d, all entries of device d's list (live or padding) whose column tile lies in device o's rows name one and the same of o's 2 row tiles.
All inputs are finite; a program needn't handle non-finite values.
Results may differ from the reference program's by a relative error of at most 0.0066.
Values may be sent and summed in bfloat16 or wider, within the bound.
No kernel may reach another device: no remote copies, remote signals or barrier semaphores. Data moves between devices by JAX's collectives and lax.ppermute only.
A program may use at most 128 MiB of HBM per device.

```python
import jax
import jax.numpy as jnp
from jax import lax

WIDTH = 256
TILE = 128
LAYERS = 2
TICKS = 2
TILES_DEV = 96
SECTIONS = 4
SHARDS = 8
NODES = 2048
BLOCKS = 16
ROW_TILES = 2
TILES = 768


def draw_tile_count(key, part):
    first, second = jax.random.split(jax.random.fold_in(key, 17))
    base = TILES_DEV - jax.random.randint(first, (SECTIONS, TICKS, SHARDS), 0, TILES_DEV // 2 + 1)
    picked = jax.random.randint(second, (SECTIONS, TICKS, 1), 0, SHARDS)
    full = jnp.arange(SHARDS)[None, None, :] == picked
    return jnp.where(full, TILES_DEV, base).astype(jnp.int32)


def draw_tile_col(key, part):
    keys = jax.random.split(jax.random.fold_in(key, 29), 5)
    allowed = jax.random.randint(keys[0], (SECTIONS, TICKS, SHARDS, SHARDS), 0, ROW_TILES)
    device = (jnp.arange(TILES) // TILES_DEV).astype(jnp.int32)
    kinds = jax.random.randint(keys[1], (SECTIONS, TICKS, TILES), 0, 4)
    sideways = 2 * jax.random.randint(keys[2], (SECTIONS, TICKS, TILES), 0, 2) - 1
    far_step = jax.random.randint(keys[3], (SECTIONS, TICKS, TILES), 1, SHARDS)
    own_block = jax.random.randint(keys[4], (SECTIONS, TICKS, TILES), 0, ROW_TILES)
    near_owner = (device[None, None, :] + sideways) % SHARDS
    far_owner = (device[None, None, :] + far_step) % SHARDS
    owners = jnp.where(kinds < 2, device[None, None, :], jnp.where(kinds == 2, near_owner, far_owner)).astype(jnp.int32)
    rows_of = allowed[:, :, device, :]
    remote_block = jnp.take_along_axis(rows_of, owners[..., None], axis=-1)[..., 0]
    block = jnp.where(kinds < 2, own_block, remote_block)
    return (owners * ROW_TILES + block).astype(jnp.int32)


def with_ends(result, stream_key, smallest, high):
    shape = result.shape
    index_at = [jax.random.randint(jax.random.fold_in(stream_key, axis), (), 0, shape[axis]) for axis in range(len(shape))]
    result = result.at[tuple(index_at)].set(smallest)
    longest = shape.index(max(shape))
    index_at[longest] = (index_at[longest] + 1) % shape[longest]
    return result.at[tuple(index_at)].set(high)


def shard_levels(stream_key, extent, pieces, smallest, largest):
    def one(dim, parts):
        steps = jax.random.uniform(jax.random.fold_in(jax.random.fold_in(stream_key, 6), dim), (parts,), jnp.float32, smallest / len(pieces), largest / len(pieces))
        return jnp.repeat(jnp.exp(steps), extent[dim] // parts).reshape((-1,) + (1,) * (len(extent) - dim - 1))

    loudness = one(*pieces[0])
    for cut in pieces[1:]:
        loudness = loudness * one(*cut)
    return loudness


def noise(stream_key, dims, scale, most, pieces=(), held_as=jnp.bfloat16):
    result = scale * jax.random.normal(stream_key, dims, jnp.float32)
    if pieces:
        result = result * shard_levels(stream_key, dims, pieces, -0.22, 0.18)
    return jnp.clip(result, -most, most).astype(held_as)


def setup_inputs(seed: int = 0) -> dict:
    arg_keys = jax.random.split(jax.random.key(seed), 10)
    grad_in = noise(arg_keys[0], (SECTIONS, NODES, WIDTH), 1.0, 6.0, ((0, 4), (1, 8)))
    grad_last = noise(arg_keys[1], (NODES, WIDTH), 1.0, 6.0, ((0, 8),))
    support = noise(arg_keys[2], (SECTIONS, TICKS, LAYERS, NODES, WIDTH), 1.0, 6.0, ((0, 4), (3, 8)))
    preact = noise(arg_keys[3], (SECTIONS, TICKS, LAYERS, NODES, WIDTH), 1.0, 6.0, ((0, 4), (3, 8)))
    weights = noise(arg_keys[4], (SECTIONS, LAYERS, WIDTH, WIDTH), WIDTH ** -0.5, 0.375, ((0, 4),))
    tile_vals = noise(arg_keys[5], (SECTIONS, TICKS, TILES, TILE, TILE), (TILE * TILES_DEV // ROW_TILES) ** -0.5, 0.078125, ((0, 4), (2, 8)))
    tile_row = with_ends(jax.random.randint(arg_keys[6], (SECTIONS, TICKS, TILES), 0, ROW_TILES), jax.random.fold_in(arg_keys[6], 1), 0, ROW_TILES - 1).astype(jnp.int32)
    tile_col = draw_tile_col(jax.random.fold_in(arg_keys[9], 71), 0)
    tile_count = draw_tile_count(jax.random.fold_in(arg_keys[9], 71), 0)
    return dict(grad_in=grad_in, grad_last=grad_last, support=support, preact=preact, weights=weights, tile_vals=tile_vals, tile_row=tile_row, tile_col=tile_col, tile_count=tile_count)


ALPHA = 0.1
BETA_SCALE = 0.5


def tile_product(dense, values, row_local, cols, counts):
    blocks = dense.astype(jnp.float32).reshape(BLOCKS, TILE, WIDTH)[cols]
    products = jnp.einsum("kab,kbf->kaf", values.astype(jnp.float32), blocks, precision=lax.Precision.HIGHEST)
    owner = (jnp.arange(TILES) // TILES_DEV).astype(jnp.int32)
    live = (jnp.arange(TILES) % TILES_DEV) < counts[owner]
    products = products * live.astype(jnp.float32)[:, None, None]
    row_global = (owner * ROW_TILES + row_local).astype(jnp.int32)
    summed = jax.ops.segment_sum(products, row_global, num_segments=BLOCKS)
    return summed.reshape(NODES, WIDTH)


def reference(grad_in, grad_last, support, preact, weights, tile_vals, tile_row, tile_col, tile_count):
    weight_acc = [[jnp.zeros((WIDTH, WIDTH), jnp.float32) for layer in range(LAYERS)] for section in range(SECTIONS)]
    handoff = []
    initial = []
    previous = None
    for tick in range(TICKS):
        outs_now = []
        init_now = []
        for section in range(SECTIONS):
            if tick == 0:
                grad = grad_in[section]
            elif section == SECTIONS - 1:
                grad = grad_last
            else:
                grad = previous[section + 1]
            toward = jnp.zeros((NODES, WIDTH), jnp.float32)
            for layer in reversed(range(LAYERS)):
                beta = jnp.log(BETA_SCALE / jnp.asarray(LAYERS * section + layer + 1, jnp.float32) + 1.0)
                weight = weights[section, layer]
                masked = jnp.where(preact[section, tick, layer] > 0, grad, jnp.zeros_like(grad))
                term = beta * jnp.dot(support[section, tick, layer].T, masked, preferred_element_type=jnp.float32)
                weight_acc[section][layer] = weight_acc[section][layer] + term
                image = ((1.0 - beta) * masked.astype(jnp.float32) + beta * jnp.dot(masked, weight.T, preferred_element_type=jnp.float32)).astype(jnp.bfloat16)
                toward = toward + ALPHA * image.astype(jnp.float32)
                spread = tile_product(image, tile_vals[section, tick], tile_row[section, tick], tile_col[section, tick], tile_count[section, tick])
                grad = ((1.0 - ALPHA) * spread).astype(jnp.bfloat16)
            outs_now.append(grad)
            init_now.append(toward)
        previous = outs_now
        handoff.append(jnp.stack(outs_now))
        initial.append(jnp.stack(init_now))
    weight_grad = jnp.stack([jnp.stack(weight_acc[section]) for section in range(SECTIONS)])
    return jnp.stack(handoff), jnp.stack(initial, axis=1), weight_grad
```

```python
import functools

import jax
import jax.numpy as jnp
import numpy as np
from jax import lax
from jax.experimental import pallas as pl
from jax.experimental.pallas import tpu as pltpu
from jax.sharding import PartitionSpec as P

ALPHA = 0.1
BETA_SCALE = 0.5
VMEM = pl.BlockSpec(memory_space=pltpu.VMEM)
SMEM = pl.BlockSpec(memory_space=pltpu.SMEM)


def cost(flops, nbytes):
    return pl.CostEstimate(flops=flops, bytes_accessed=nbytes, transcendentals=0)


def passed_along(block, axis, distance):
    devices = range(lax.axis_size(axis))
    route = [(i - distance, i) for i in devices if i - distance in devices]
    return lax.ppermute(block, axis, route)


def exchange(blocks):
    return lax.all_to_all(blocks, "rows", 0, 0, tiled=True)


def densify_kernel(row_tiles, n, tile, me_ref, rows_ref, cols_ref, count_ref, vals_ref, out_ref, acc):
    step = pl.program_id(0)
    chunk = vals_ref.shape[0]
    me = me_ref[0]

    @pl.when(step == 0)
    def _():
        acc[...] = jnp.zeros_like(acc)

    base = step * chunk

    def add(i, carry):
        entry = base + i
        row = rows_ref[entry]
        col = cols_ref[entry]
        owner = lax.div(col, row_tiles)
        block = lax.rem(col, row_tiles)
        slot = jnp.where((owner == me) & (block > 0), n - 1 + block, owner)
        rows = pl.ds(pl.multiple_of(row * tile, tile), tile)
        cols = pl.ds(pl.multiple_of(slot * tile, tile), tile)
        acc[rows, cols] += vals_ref[i].astype(jnp.float32)
        return carry

    lax.fori_loop(0, jnp.clip(count_ref[0] - base, 0, chunk), add, 0)

    @pl.when(step == pl.num_programs(0) - 1)
    def _():
        out_ref[...] = acc[...].astype(jnp.bfloat16)


def densify(me, rows, cols, count, vals, row_tiles, n):
    entries, tile, _ = vals.shape
    steps = 4 if entries % 4 == 0 else 1
    chunk = entries // steps
    wide = (n + row_tiles - 1) * tile
    return pl.pallas_call(
        functools.partial(densify_kernel, row_tiles, n, tile),
        grid=(steps,),
        out_shape=jax.ShapeDtypeStruct((row_tiles * tile, wide), jnp.bfloat16),
        in_specs=[SMEM, SMEM, SMEM, SMEM, pl.BlockSpec((chunk, tile, tile), lambda i: (i, 0, 0))],
        out_specs=pl.BlockSpec((row_tiles * tile, wide), lambda i: (0, 0)),
        scratch_shapes=[pltpu.VMEM((row_tiles * tile, wide), jnp.float32)],
        compiler_params=pltpu.CompilerParams(vmem_limit_bytes=24 * 2**20),
        cost_estimate=cost(entries * tile * tile * 20, vals.size * 2),
        name="densify",
    )(me, rows, cols, count, vals)


def spread_of(adj_ref, recv_ref, own_ref):
    n, tile, width = recv_ref.shape
    total = jnp.dot(
        adj_ref[:, : n * tile],
        recv_ref[...].reshape(n * tile, width),
        preferred_element_type=jnp.float32,
    )
    rest = own_ref.shape[0] - tile
    if rest:
        total = total + jnp.dot(
            adj_ref[:, n * tile :], own_ref[tile:, :], preferred_element_type=jnp.float32
        )
    return ((1.0 - ALPHA) * total).astype(jnp.bfloat16)


def emit_image(grad, beta, preact_ref, weight_ref, want_ref, image_ref, masked_ref, send_ref):
    tile = send_ref.shape[1]
    masked = jnp.where(preact_ref[...] > 0, grad, jnp.zeros_like(grad))
    masked_ref[...] = masked
    product = lax.dot_general(
        masked, weight_ref[...], (((1,), (1,)), ((), ())), preferred_element_type=jnp.float32
    )
    image = ((1.0 - beta) * masked.astype(jnp.float32) + beta * product).astype(jnp.bfloat16)
    image_ref[...] = image
    for d in range(send_ref.shape[0]):
        send_ref[d] = image_ref[pl.ds(pl.multiple_of(want_ref[d] * tile, tile), tile), :]
    return image


def entry_kernel(beta_ref, want_ref, grad_ref, preact_ref, weight_ref, image_ref, masked_ref, send_ref):
    emit_image(
        grad_ref[...], beta_ref[0], preact_ref, weight_ref, want_ref, image_ref, masked_ref, send_ref
    )


def middle_kernel(
    beta_ref, want_ref, adj_ref, recv_ref, own_ref, before_ref, preact_ref, weight_ref,
    image_ref, masked_ref, send_ref, toward_ref,
):
    grad = spread_of(adj_ref, recv_ref, own_ref)
    image = emit_image(
        grad, beta_ref[0], preact_ref, weight_ref, want_ref, image_ref, masked_ref, send_ref
    )
    toward_ref[...] = before_ref[...].astype(jnp.float32) + ALPHA * image.astype(jnp.float32)


def middle_first_kernel(
    beta_ref, want_ref, adj_ref, recv_ref, own_ref, preact_ref, weight_ref,
    image_ref, masked_ref, send_ref, toward_ref,
):
    grad = spread_of(adj_ref, recv_ref, own_ref)
    image = emit_image(
        grad, beta_ref[0], preact_ref, weight_ref, want_ref, image_ref, masked_ref, send_ref
    )
    toward_ref[...] = ALPHA * own_ref[...].astype(jnp.float32) + ALPHA * image.astype(jnp.float32)


def exit_kernel(adj_ref, recv_ref, own_ref, grad_ref):
    grad_ref[...] = spread_of(adj_ref, recv_ref, own_ref)


def shards(grad_in, grad_last, support, preact, weights, tile_vals, tile_row, tile_col, tile_count):
    section = lax.axis_index("section")
    me = lax.axis_index("rows")
    n = lax.axis_size("rows")
    sections = lax.axis_size("section")
    ticks = support.shape[1]
    layers = support.shape[2]
    rows_dev, width = grad_last.shape
    tile = tile_vals.shape[-1]
    row_tiles = rows_dev // tile
    me_arr = jnp.full((1,), me, jnp.int32)

    owner = tile_col[0] // row_tiles
    named = jnp.where(
        owner[:, :, None] == jnp.arange(n)[None, None, :], (tile_col[0] % row_tiles)[:, :, None], 0
    )
    pick = jnp.max(named, axis=1)
    pick = jnp.where(jnp.arange(n)[None, :] == me, 0, pick).astype(jnp.int32)
    want = exchange(pick.T)

    image_shapes = [
        jax.ShapeDtypeStruct((rows_dev, width), jnp.bfloat16),
        jax.ShapeDtypeStruct((rows_dev, width), jnp.bfloat16),
        jax.ShapeDtypeStruct((n, tile, width), jnp.bfloat16),
    ]
    toward_shape = jax.ShapeDtypeStruct((rows_dev, width), jnp.float32)
    small = cost(2 * rows_dev * width * width, (3 + n) * rows_dev * width)
    large = cost(
        2 * rows_dev * width * (width + (n + 1) * tile), (6 + 2 * n) * rows_dev * width
    )
    params = pltpu.CompilerParams(vmem_limit_bytes=24 * 2**20)
    weight_acc = [jnp.zeros((width, width), jnp.float32) for layer in range(layers)]
    handed = []
    initial = []
    for tick in range(ticks):
        if tick == 0:
            grad = grad_in[0]
        else:
            passed = passed_along(handed[-1], "section", -1)
            grad = jnp.where(section == sections - 1, grad_last, passed)
        adj = densify(
            me_arr, tile_row[0, tick], tile_col[0, tick], tile_count[0, tick], tile_vals[0, tick],
            row_tiles, n,
        )
        image = recv = toward = None
        for layer in reversed(range(layers)):
            beta = jnp.log(BETA_SCALE / (layers * section + layer + 1).astype(jnp.float32) + 1.0)
            beta_arr = jnp.full((1,), beta, jnp.float32)
            head = (beta_arr, want[:, tick])
            tail = (preact[0, tick, layer], weights[0, layer])
            if layer == layers - 1:
                image, masked, send = pl.pallas_call(
                    entry_kernel,
                    out_shape=image_shapes,
                    in_specs=[SMEM] * 2 + [VMEM] * 3,
                    out_specs=[VMEM] * 3,
                    compiler_params=params,
                    cost_estimate=small,
                    name="entry",
                )(*head, grad, *tail)
            else:
                first = layer == layers - 2
                before = () if first else (toward,)
                image, masked, send, toward = pl.pallas_call(
                    middle_first_kernel if first else middle_kernel,
                    out_shape=image_shapes + [toward_shape],
                    in_specs=[SMEM] * 2 + [VMEM] * (5 + len(before)),
                    out_specs=[VMEM] * 4,
                    compiler_params=params,
                    cost_estimate=large,
                    name="middle",
                )(*head, adj, recv, image, *before, *tail)
            term = beta * jnp.dot(
                support[0, tick, layer].T, masked, preferred_element_type=jnp.float32
            )
            weight_acc[layer] = weight_acc[layer] + term
            recv = exchange(send)
        handed.append(
            pl.pallas_call(
                exit_kernel,
                out_shape=image_shapes[0],
                in_specs=[VMEM] * 3,
                out_specs=VMEM,
                compiler_params=params,
                cost_estimate=large,
                name="exit",
            )(adj, recv, image)
        )
        initial.append(toward)
    parts = jnp.stack(weight_acc).reshape(layers, n, width // n, width).swapaxes(0, 1)
    summed = jnp.sum(exchange(parts.astype(jnp.bfloat16)).astype(jnp.float32), axis=0)
    whole = exchange(jnp.broadcast_to(summed[None].astype(jnp.bfloat16), parts.shape))
    weight_grad = whole.astype(jnp.float32).swapaxes(0, 1).reshape(layers, width, width)
    return (jnp.stack(handed)[:, None], jnp.stack(initial)[None], weight_grad[None])


def solution(mesh):
    return jax.shard_map(
        shards,
        mesh=mesh,
        in_specs=(
            P("section", "rows", None),
            P("rows", None),
            P("section", None, None, "rows", None),
            P("section", None, None, "rows", None),
            P("section", None, None, None),
            P("section", None, "rows", None, None),
            P("section", None, "rows"),
            P("section", None, "rows"),
            P("section", None, "rows"),
        ),
        out_specs=(
            P(None, "section", "rows", None),
            P("section", None, "rows", None),
            P("section", None, None, None),
        ),
        check_vma=False,
    )
```

```python
import functools

import jax
import jax.numpy as jnp
from jax import lax
from jax.experimental import pallas as pl
from jax.experimental.pallas import tpu as pltpu
from jax.sharding import PartitionSpec as P

ALPHA = 0.1
BETA_SCALE = 0.5
VMEM = pl.BlockSpec(memory_space=pltpu.VMEM)
SMEM = pl.BlockSpec(memory_space=pltpu.SMEM)
ANY = pl.BlockSpec(memory_space=pl.ANY)
PARAMS = pltpu.CompilerParams(vmem_limit_bytes=24 * 2**20)
F32 = jnp.float32
BF16 = jnp.bfloat16


def cost(flops, nbytes):
    return pl.CostEstimate(flops=flops, bytes_accessed=nbytes, transcendentals=0)


def passed_along(block, axis, distance):
    devices = range(lax.axis_size(axis))
    route = [(i - distance, i) for i in devices if i - distance in devices]
    return lax.ppermute(block, axis, route)


def power_of_two(n):
    return n & (n - 1) == 0


def target(me, k, n):
    return me ^ k if power_of_two(n) else (me + k) % n


def source(me, k, n):
    return me ^ k if power_of_two(n) else (me - k) % n


def dynamic_target(me, k, n):
    return jnp.bitwise_xor(me, k) if power_of_two(n) else lax.rem(me + k, n)


def dynamic_source(me, k, n):
    return jnp.bitwise_xor(me, k) if power_of_two(n) else lax.rem(me - k + n, n)


def exchange(messages):
    n = len(messages) + 1
    got = [None] * (n - 1)
    for k in reversed(range(1, n)):
        route = [(i, target(i, k, n)) for i in range(n)]
        got[k - 1] = lax.ppermute(messages[k - 1], "rows", route)
    return got


def densify_kernel(tick, row_tiles, n, me_ref, rows_ref, cols_ref, count_ref, vals_ref, out_ref, acc):
    step = pl.program_id(0)
    chunk, tile, _ = vals_ref.shape
    me = me_ref[0]

    @pl.when(step == 0)
    def _():
        acc[...] = jnp.zeros_like(acc)

    base = step * chunk

    def add(i, carry):
        row = rows_ref[0, tick, base + i]
        col = cols_ref[0, tick, base + i]
        owner = lax.div(col, row_tiles)
        block = lax.rem(col, row_tiles)
        if power_of_two(n):
            slot = jnp.bitwise_xor(owner, me)
        else:
            slot = lax.rem(me - owner + n, n)
        slot = jnp.where((owner == me) & (block > 0), n - 1 + block, slot)
        rows = pl.ds(pl.multiple_of(row * tile, tile), tile)
        cols = pl.ds(pl.multiple_of(slot * tile, tile), tile)
        acc[rows, cols] += vals_ref[i].astype(F32)
        return carry

    lax.fori_loop(0, jnp.clip(count_ref[0, tick, 0] - base, 0, chunk), add, 0)

    @pl.when(step == pl.num_programs(0) - 1)
    def _():
        out_ref[...] = acc[...].astype(BF16)


def densify(tick, me, rows, cols, count, vals, row_tiles, n):
    _, _, entries, tile, _ = vals.shape
    steps = 4 if entries % 4 == 0 else 1
    chunk = entries // steps
    shape = (row_tiles * tile, (n + row_tiles - 1) * tile)
    return pl.pallas_call(
        functools.partial(densify_kernel, tick, row_tiles, n),
        grid=(steps,),
        out_shape=jax.ShapeDtypeStruct(shape, BF16),
        in_specs=[SMEM] * 4
        + [pl.BlockSpec((None, None, chunk, tile, tile), lambda i: (0, tick, i, 0, 0))],
        out_specs=pl.BlockSpec(shape, lambda i: (0, 0)),
        scratch_shapes=[pltpu.VMEM(shape, F32)],
        compiler_params=PARAMS,
        cost_estimate=cost(entries * tile * tile * 20, entries * tile * tile * 2),
        name="densify",
    )(me, rows, cols, count, vals)


def spread_of(adj_ref, got, own_ref, tile):
    blocks = jnp.concatenate(
        [own_ref[:tile, :]] + [ref[:tile, :] for ref in got] + [own_ref[tile:, :]], axis=0
    )
    total = jnp.dot(adj_ref[...], blocks, preferred_element_type=F32)
    return ((1.0 - ALPHA) * total).astype(BF16)


def layer_kernel(c, *refs):
    refs = list(refs)

    def take(count):
        taken, refs[:count] = refs[:count], []
        return taken

    n, tile = c["n"], c["tile"]
    me_ref, section_ref, picks_ref, preact_all, weight_all = take(5)
    me = me_ref[0]
    section = section_ref[0]
    step = (c["layers"] * section + c["layer"] + 1).astype(F32)
    beta = jnp.log(BETA_SCALE / jnp.full((1, c["width"]), step, F32) + 1.0)
    got = []
    if c["entry"]:
        if c["tick"] == 0:
            (grad_all,) = take(1)
        else:
            last_ref, passed_ref = take(2)
    else:
        adj_ref, own_ref = take(2)
        got = take(n - 1)
        before_ref = take(1)[0] if c["before"] else None
        if c["toward"] and c["tick"] > 0:
            take(1)
    if c["final"]:
        support_all, acc_ref = take(2)
        if c["sum_above"]:
            (above_ref,) = take(1)
    image_ref, masked_ref = take(2)
    sends = take(n - 1)
    toward_ref = take(1)[0] if not c["entry"] else None
    own_sum_ref = take(1)[0] if c["sum_above"] else None
    term_ref = take(1)[0] if c["final"] else None
    if c["toward"]:
        hold_ref, sem = take(2)
    preact_ref, weight_ref, load_sems = take(3)
    loads = [
        (preact_all.at[0, c["tick"], c["layer"]], preact_ref),
        (weight_all.at[0, c["layer"]], weight_ref),
    ]
    if c["entry"] and c["tick"] == 0:
        (grad_ref,) = take(1)
        loads.append((grad_all.at[0], grad_ref))
    if c["final"]:
        (support_ref,) = take(1)
        loads.append((support_all.at[0, c["tick"], c["layer"]], support_ref))
    loads = [pltpu.make_async_copy(a, b, load_sems.at[i]) for i, (a, b) in enumerate(loads)]
    for load in loads:
        load.start()
    if not c["entry"]:
        grad = spread_of(adj_ref, got, own_ref, tile)
    for load in loads:
        load.wait()
    if c["entry"]:
        if c["tick"] == 0:
            grad = grad_ref[...]
        else:
            is_last = section == c["sections"] - 1
            grad = jnp.where(is_last, last_ref[...], passed_ref[...])

    masked = jnp.where(preact_ref[...] > 0, grad, jnp.zeros_like(grad))
    masked_ref[...] = masked
    product = lax.dot_general(
        masked, weight_ref[...], (((1,), (1,)), ((), ())), preferred_element_type=F32
    )
    image = ((1.0 - beta) * masked.astype(F32) + beta * product).astype(BF16)
    image_ref[...] = image
    for k in range(1, n):
        want = picks_ref[dynamic_target(me, k, n), c["tick"] * n + me]
        sends[k - 1][:tile, :] = image_ref[pl.ds(pl.multiple_of(want * tile, tile), tile), :]
    copy = None
    if not c["entry"]:
        before = before_ref[...] if c["before"] else ALPHA * own_ref[...].astype(F32)
        total = before + ALPHA * image.astype(F32)
        if c["toward"]:
            hold_ref[...] = total
            copy = pltpu.make_async_copy(hold_ref, toward_ref.at[0, c["tick"]], sem)
            copy.start()
        else:
            toward_ref[...] = total
    if c["final"]:
        part, room = c["part"], c["room"]
        term = lax.dot_general(
            support_ref[...], masked, (((0,), (0,)), ((), ())), preferred_element_type=F32
        )
        term_ref[...] = acc_ref[...] + beta * term
        at = tile
        if c["sum_above"]:
            total = above_ref[pl.ds(pl.multiple_of(me * part, 8), part), :]
            for ref in got:
                total = total + ref[tile + c["above_at"] : tile + c["above_at"] + part, :].astype(F32)
            own_sum_ref[...] = total.astype(BF16)
            for send in sends:
                send[at : at + part, :] = own_sum_ref[...]
            at += room
        for k in range(1, n):
            start = pl.multiple_of(dynamic_target(me, k, n) * part, 8)
            sends[k - 1][at : at + part, :] = term_ref[pl.ds(start, part), :].astype(BF16)
    if copy is not None:
        copy.wait()


def exit_kernel(c, *refs):
    refs = list(refs)

    def take(count):
        taken, refs[:count] = refs[:count], []
        return taken

    n, tile, part, room = c["n"], c["tile"], c["part"], c["room"]
    me_ref, adj_ref, own_ref = take(3)
    me = me_ref[0]
    got = take(n - 1)
    if c["tick"] > 0:
        take(1)
    if c["final"]:
        (acc_ref,) = take(1)
        own_sum_ref = take(1)[0] if c["above"] else None
    (out_ref,) = take(1)
    grad_ref = None if c["final"] else take(1)[0]
    if c["final"]:
        last_sum_ref, weight_ref = take(2)
    hold_ref, sem = take(2)
    if c["final"] and c["above"]:
        hold_weight_ref, weight_sem = take(2)
    grad = spread_of(adj_ref, got, own_ref, tile)
    hold_ref[...] = grad
    copy = pltpu.make_async_copy(hold_ref, out_ref.at[c["tick"], 0], sem)
    copy.start()
    if c["final"]:
        at = tile + (room if c["above"] else 0)
        total = acc_ref[pl.ds(pl.multiple_of(me * part, 8), part), :]
        for ref in got:
            total = total + ref[at : at + part, :].astype(F32)
        last_sum_ref[...] = total.astype(BF16)
        if c["above"]:
            place(hold_weight_ref, me, n, part, own_sum_ref, [ref.at[tile : tile + part, :] for ref in got])
            weight_copy = pltpu.make_async_copy(hold_weight_ref, weight_ref.at[0, 1], weight_sem)
            weight_copy.start()
            weight_copy.wait()
    else:
        grad_ref[...] = grad
    copy.wait()


def place(whole_ref, me, n, part, own_ref, others):
    whole_ref[pl.ds(pl.multiple_of(me * part, 8), part), :] = own_ref[...].astype(F32)
    for k in range(1, n):
        start = pl.multiple_of(dynamic_source(me, k, n) * part, 8)
        whole_ref[pl.ds(start, part), :] = others[k - 1][...].astype(F32)


def finish_kernel(n, part, *refs):
    me_ref, own_ref = refs[:2]
    others = refs[2 : n + 1]
    weight_ref, hold_ref, sem = refs[n + 2 :]
    place(hold_ref, me_ref[0], n, part, own_ref, others)
    copy = pltpu.make_async_copy(hold_ref, weight_ref.at[0, 0], sem)
    copy.start()
    copy.wait()


def shards(grad_in, grad_last, support, preact, weights, tile_vals, tile_row, tile_col, tile_count):
    section = lax.axis_index("section")
    me = lax.axis_index("rows")
    n = lax.axis_size("rows")
    sections = lax.axis_size("section")
    ticks = support.shape[1]
    layers = support.shape[2]
    rows_dev, width = grad_last.shape
    tile = tile_vals.shape[-1]
    row_tiles = rows_dev // tile
    part = width // n
    room = max(part, 16)
    me_arr = me.astype(jnp.int32).reshape(1)
    section_arr = section.astype(jnp.int32).reshape(1)

    owner = tile_col[0] // row_tiles
    named = jnp.where(
        owner[:, :, None] == jnp.arange(n)[None, None, :], (tile_col[0] % row_tiles)[:, :, None], 0
    )
    pick = jnp.max(named, axis=1).reshape(1, ticks * n).astype(jnp.int32)
    picks = jnp.where(jnp.arange(n)[:, None] == me, pick, 0)
    if power_of_two(n):
        k = 1
        while k < n:
            picks = picks + lax.ppermute(picks, "rows", [(i, i ^ k) for i in range(n)])
            k *= 2
    else:
        picks = lax.psum(picks, "rows")

    def shape(rows, dtype):
        return jax.ShapeDtypeStruct((rows, width), dtype)

    handoff = initial = passed = None
    above_sum = None
    weight_acc = [None] * layers
    for tick in range(ticks):
        final = tick == ticks - 1
        if tick > 0:
            passed = passed_along(passed, "section", -1)
        adj = densify(
            tick, me_arr, tile_row, tile_col, tile_count, tile_vals, row_tiles, n
        )
        image = got = toward = None
        for layer in reversed(range(layers)):
            entry = layer == layers - 1
            c = dict(
                n=n, tile=tile, width=width, layers=layers, layer=layer, tick=tick, sections=sections,
                entry=entry, final=final, part=part, room=room,
                before=not entry and layer < layers - 2,
                toward=layer == 0 and not entry,
                sum_above=final and not entry,
                above_at=0 if layer >= layers - 2 else room,
            )
            message = tile + (room * (1 if entry else 2) if final else 0)
            operands = [me_arr, section_arr, picks, preact, weights]
            specs = [SMEM, SMEM, SMEM, ANY, ANY]
            aliases = {}
            if entry:
                if tick == 0:
                    operands.append(grad_in)
                    specs.append(ANY)
                else:
                    operands += [grad_last, passed]
                    specs += [VMEM, VMEM]
            else:
                operands += [adj, image] + got
                specs += [VMEM] * (n + 1)
                if c["before"]:
                    operands.append(toward)
                    specs.append(VMEM)
                if c["toward"] and tick > 0:
                    aliases[len(operands)] = n + 1
                    operands.append(initial)
                    specs.append(ANY)
            if final:
                operands += [support, weight_acc[layer]]
                specs += [ANY, VMEM]
                if c["sum_above"]:
                    operands.append(above_sum)
                    specs.append(VMEM)
            outs = [shape(rows_dev, BF16)] * 2 + [shape(message, BF16)] * (n - 1)
            out_specs = [VMEM] * (n + 1)
            scratch = []
            if not entry:
                if c["toward"]:
                    outs.append(jax.ShapeDtypeStruct((1, ticks, rows_dev, width), F32))
                    out_specs.append(ANY)
                    scratch = [pltpu.VMEM((rows_dev, width), F32), pltpu.SemaphoreType.DMA]
                else:
                    outs.append(shape(rows_dev, F32))
                    out_specs.append(VMEM)
            if c["sum_above"]:
                outs.append(shape(part, BF16))
                out_specs.append(VMEM)
            if final:
                outs.append(shape(width, F32))
                out_specs.append(VMEM)
            scratch += [
                pltpu.VMEM((rows_dev, width), BF16),
                pltpu.VMEM((width, width), BF16),
                pltpu.SemaphoreType.DMA((4,)),
            ]
            if entry and tick == 0:
                scratch.append(pltpu.VMEM((rows_dev, width), BF16))
            if final:
                scratch.append(pltpu.VMEM((rows_dev, width), BF16))
            results = pl.pallas_call(
                functools.partial(layer_kernel, c),
                out_shape=outs,
                in_specs=specs,
                out_specs=out_specs,
                scratch_shapes=scratch,
                input_output_aliases=aliases,
                compiler_params=PARAMS,
                cost_estimate=cost(
                    2 * rows_dev * width * (width + (n + 1) * tile), (6 + 2 * n) * rows_dev * width
                ),
                name="entry" if entry else "middle",
            )(*operands)
            results = list(results)
            image, masked = results[:2]
            sends = results[2 : n + 1]
            rest = results[n + 1 :]
            if not entry:
                toward = rest.pop(0)
                if c["toward"]:
                    initial = toward
            if c["sum_above"]:
                own_sum = rest.pop(0)
            if final:
                above_sum = rest.pop(0)
            else:
                beta = jnp.log(
                    BETA_SCALE / (layers * section + layer + 1).astype(F32) + 1.0
                )
                term = beta * jnp.dot(
                    support[0, tick, layer].T, masked, preferred_element_type=F32
                )
                old = weight_acc[layer]
                weight_acc[layer] = term if old is None else old + term
            got = exchange(sends)
        c = dict(n=n, tile=tile, tick=tick, final=final, part=part, room=room, above=layers > 1)
        operands = [me_arr, adj, image] + got
        specs = [SMEM] + [VMEM] * (n + 1)
        aliases = {}
        if tick > 0:
            aliases[len(operands)] = 0
            operands.append(handoff)
            specs.append(ANY)
        outs = [jax.ShapeDtypeStruct((ticks, 1, rows_dev, width), BF16)]
        out_specs = [ANY]
        scratch = [pltpu.VMEM((rows_dev, width), BF16), pltpu.SemaphoreType.DMA]
        if final:
            operands += [above_sum, own_sum]
            specs += [VMEM, VMEM]
            outs += [shape(part, BF16), jax.ShapeDtypeStruct((1, layers, width, width), F32)]
            out_specs += [VMEM, ANY]
            scratch += [pltpu.VMEM((width, width), F32), pltpu.SemaphoreType.DMA]
        else:
            outs.append(shape(rows_dev, BF16))
            out_specs.append(VMEM)
        results = pl.pallas_call(
            functools.partial(exit_kernel, c),
            out_shape=outs,
            in_specs=specs,
            out_specs=out_specs,
            scratch_shapes=scratch,
            input_output_aliases=aliases,
            compiler_params=PARAMS,
            cost_estimate=cost(
                2 * rows_dev * width * (n + 1) * tile, (6 + 2 * n) * rows_dev * width
            ),
            name="exit",
        )(*operands)
        handoff = results[0]
        if final:
            last_sum, weight_grad = results[1:]
        else:
            passed = results[1]
    others = exchange([last_sum] * (n - 1))
    weight_grad = pl.pallas_call(
        functools.partial(finish_kernel, n, part),
        out_shape=jax.ShapeDtypeStruct((1, layers, width, width), F32),
        in_specs=[SMEM] + [VMEM] * n + [ANY],
        out_specs=ANY,
        scratch_shapes=[pltpu.VMEM((width, width), F32), pltpu.SemaphoreType.DMA],
        input_output_aliases={n + 1: 0},
        compiler_params=PARAMS,
        name="finish",
    )(me_arr, last_sum, *others, weight_grad)
    return handoff, initial, weight_grad


def solution(mesh):
    return jax.shard_map(
        shards,
        mesh=mesh,
        in_specs=(
            P("section", "rows", None),
            P("rows", None),
            P("section", None, None, "rows", None),
            P("section", None, None, "rows", None),
            P("section", None, None, None),
            P("section", None, "rows", None, None),
            P("section", None, "rows"),
            P("section", None, "rows"),
            P("section", None, "rows"),
        ),
        out_specs=(
            P(None, "section", "rows", None),
            P("section", None, "rows", None),
            P("section", None, None, None),
        ),
        check_vma=False,
    )
```

```python
import functools

import jax
import jax.numpy as jnp
from jax import lax
from jax.experimental import pallas as pl
from jax.experimental.pallas import tpu as pltpu
from jax.sharding import PartitionSpec as P

ALPHA = 0.1
BETA_SCALE = 0.5
VMEM = pl.BlockSpec(memory_space=pltpu.VMEM)
SMEM = pl.BlockSpec(memory_space=pltpu.SMEM)
ANY = pl.BlockSpec(memory_space=pl.ANY)
PARAMS = pltpu.CompilerParams(vmem_limit_bytes=24 * 2**20)
F32 = jnp.float32
BF16 = jnp.bfloat16


def cost(flops, nbytes):
    return pl.CostEstimate(flops=flops, bytes_accessed=nbytes, transcendentals=0)


def passed_along(block, axis, distance):
    devices = range(lax.axis_size(axis))
    route = [(i - distance, i) for i in devices if i - distance in devices]
    return lax.ppermute(block, axis, route)


def power_of_two(n):
    return n & (n - 1) == 0


def target(me, k, n):
    return me ^ k if power_of_two(n) else (me + k) % n


def source(me, k, n):
    return me ^ k if power_of_two(n) else (me - k) % n


def dynamic_target(me, k, n):
    return jnp.bitwise_xor(me, k) if power_of_two(n) else lax.rem(me + k, n)


def dynamic_source(me, k, n):
    return jnp.bitwise_xor(me, k) if power_of_two(n) else lax.rem(me - k + n, n)


def exchange(messages):
    n = len(messages) + 1
    got = [None] * (n - 1)
    for k in reversed(range(1, n)):
        route = [(i, target(i, k, n)) for i in range(n)]
        got[k - 1] = lax.ppermute(messages[k - 1], "rows", route)
    return got


def densify_kernel(tick, row_tiles, n, me_ref, rows_ref, cols_ref, count_ref, vals_ref, out_ref, acc):
    step = pl.program_id(0)
    chunk, tile, _ = vals_ref.shape
    me = me_ref[0]

    @pl.when(step == 0)
    def _():
        acc[...] = jnp.zeros_like(acc)

    base = step * chunk

    def add(i, carry):
        row = rows_ref[0, tick, base + i]
        col = cols_ref[0, tick, base + i]
        owner = lax.div(col, row_tiles)
        block = lax.rem(col, row_tiles)
        if power_of_two(n):
            slot = jnp.bitwise_xor(owner, me)
        else:
            slot = lax.rem(me - owner + n, n)
        slot = jnp.where((owner == me) & (block > 0), n - 1 + block, slot)
        rows = pl.ds(pl.multiple_of(row * tile, tile), tile)
        cols = pl.ds(pl.multiple_of(slot * tile, tile), tile)
        acc[rows, cols] += vals_ref[i].astype(F32)
        return carry

    lax.fori_loop(0, jnp.clip(count_ref[0, tick, 0] - base, 0, chunk), add, 0)

    @pl.when(step == pl.num_programs(0) - 1)
    def _():
        out_ref[...] = acc[...].astype(BF16)


def densify(tick, me, rows, cols, count, vals, row_tiles, n):
    _, _, entries, tile, _ = vals.shape
    steps = 4 if entries % 4 == 0 else 1
    chunk = entries // steps
    shape = (row_tiles * tile, (n + row_tiles - 1) * tile)
    return pl.pallas_call(
        functools.partial(densify_kernel, tick, row_tiles, n),
        grid=(steps,),
        out_shape=jax.ShapeDtypeStruct(shape, BF16),
        in_specs=[SMEM] * 4
        + [pl.BlockSpec((None, None, chunk, tile, tile), lambda i: (0, tick, i, 0, 0))],
        out_specs=pl.BlockSpec(shape, lambda i: (0, 0)),
        scratch_shapes=[pltpu.VMEM(shape, F32)],
        compiler_params=PARAMS,
        cost_estimate=cost(entries * tile * tile * 20, entries * tile * tile * 2),
        name="densify",
    )(me, rows, cols, count, vals)


def spread_of(adj_ref, got, own_ref, tile):
    blocks = jnp.concatenate(
        [own_ref[:tile, :]] + [ref[:tile, :] for ref in got] + [own_ref[tile:, :]], axis=0
    )
    total = jnp.dot(adj_ref[...], blocks, preferred_element_type=F32)
    return ((1.0 - ALPHA) * total).astype(BF16)


def layer_kernel(c, *refs):
    refs = list(refs)

    def take(count):
        taken, refs[:count] = refs[:count], []
        return taken

    n, tile = c["n"], c["tile"]
    me_ref, section_ref, picks_ref, preact_all, weight_all = take(5)
    me = me_ref[0]
    section = section_ref[0]
    step = (c["layers"] * section + c["layer"] + 1).astype(F32)
    beta = jnp.log(BETA_SCALE / jnp.full((1, c["width"]), step, F32) + 1.0)
    got = []
    if c["entry"]:
        if c["tick"] == 0:
            (grad_all,) = take(1)
        else:
            last_ref, passed_ref = take(2)
    else:
        adj_ref, own_ref = take(2)
        got = take(n - 1)
        before_ref = take(1)[0] if c["before"] else None
        if c["toward"] and c["tick"] > 0:
            take(1)
    if c["final"]:
        support_all, acc_ref = take(2)
    image_ref, masked_ref = take(2)
    sends = take(n - 1)
    toward_ref = take(1)[0] if not c["entry"] else None
    term_ref = take(1)[0] if c["final"] else None
    if c["toward"]:
        hold_ref, sem = take(2)
    preact_ref, weight_ref, load_sems = take(3)
    loads = [
        (preact_all.at[0, c["tick"], c["layer"]], preact_ref),
        (weight_all.at[0, c["layer"]], weight_ref),
    ]
    if c["entry"] and c["tick"] == 0:
        (grad_ref,) = take(1)
        loads.append((grad_all.at[0], grad_ref))
    if c["final"]:
        (support_ref,) = take(1)
        loads.append((support_all.at[0, c["tick"], c["layer"]], support_ref))
    loads = [pltpu.make_async_copy(a, b, load_sems.at[i]) for i, (a, b) in enumerate(loads)]
    for load in loads:
        load.start()
    if not c["entry"]:
        grad = spread_of(adj_ref, got, own_ref, tile)
    for load in loads:
        load.wait()
    if c["entry"]:
        if c["tick"] == 0:
            grad = grad_ref[...]
        else:
            is_last = section == c["sections"] - 1
            grad = jnp.where(is_last, last_ref[...], passed_ref[...])

    masked = jnp.where(preact_ref[...] > 0, grad, jnp.zeros_like(grad))
    masked_ref[...] = masked
    product = lax.dot_general(
        masked, weight_ref[...], (((1,), (1,)), ((), ())), preferred_element_type=F32
    )
    image = ((1.0 - beta) * masked.astype(F32) + beta * product).astype(BF16)
    image_ref[...] = image
    for k in range(1, n):
        want = picks_ref[dynamic_target(me, k, n), c["tick"] * n + me]
        sends[k - 1][:tile, :] = image_ref[pl.ds(pl.multiple_of(want * tile, tile), tile), :]
    copy = None
    if not c["entry"]:
        before = before_ref[...] if c["before"] else ALPHA * own_ref[...].astype(F32)
        total = before + ALPHA * image.astype(F32)
        if c["toward"]:
            hold_ref[...] = total
            copy = pltpu.make_async_copy(hold_ref, toward_ref.at[0, c["tick"]], sem)
            copy.start()
        else:
            toward_ref[...] = total
    if c["final"]:
        term = lax.dot_general(
            support_ref[...], masked, (((0,), (0,)), ((), ())), preferred_element_type=F32
        )
        term_ref[...] = (acc_ref[...] + beta * term).astype(BF16)
    if copy is not None:
        copy.wait()


def exit_kernel(c, *refs):
    refs = list(refs)

    def take(count):
        taken, refs[:count] = refs[:count], []
        return taken

    adj_ref, own_ref = take(2)
    got = take(c["n"] - 1)
    if c["tick"] > 0:
        take(1)
    (out_ref,) = take(1)
    grad_ref = None if c["final"] else take(1)[0]
    hold_ref, sem = take(2)
    grad = spread_of(adj_ref, got, own_ref, c["tile"])
    hold_ref[...] = grad
    copy = pltpu.make_async_copy(hold_ref, out_ref.at[c["tick"], 0], sem)
    copy.start()
    if grad_ref is not None:
        grad_ref[...] = grad
    copy.wait()


def shards(grad_in, grad_last, support, preact, weights, tile_vals, tile_row, tile_col, tile_count):
    section = lax.axis_index("section")
    me = lax.axis_index("rows")
    n = lax.axis_size("rows")
    sections = lax.axis_size("section")
    ticks = support.shape[1]
    layers = support.shape[2]
    rows_dev, width = grad_last.shape
    tile = tile_vals.shape[-1]
    row_tiles = rows_dev // tile
    me_arr = me.astype(jnp.int32).reshape(1)
    section_arr = section.astype(jnp.int32).reshape(1)

    owner = tile_col[0] // row_tiles
    named = jnp.where(
        owner[:, :, None] == jnp.arange(n)[None, None, :], (tile_col[0] % row_tiles)[:, :, None], 0
    )
    pick = jnp.max(named, axis=1).reshape(1, ticks * n).astype(jnp.int32)
    picks = jnp.where(jnp.arange(n)[:, None] == me, pick, 0)
    if power_of_two(n):
        k = 1
        while k < n:
            picks = picks + lax.ppermute(picks, "rows", [(i, i ^ k) for i in range(n)])
            k *= 2
    else:
        picks = lax.psum(picks, "rows")

    def shape(rows, dtype):
        return jax.ShapeDtypeStruct((rows, width), dtype)

    handoff = initial = passed = None
    weight_sums = [None] * layers
    weight_acc = [None] * layers
    for tick in range(ticks):
        final = tick == ticks - 1
        if tick > 0:
            passed = passed_along(passed, "section", -1)
        adj = densify(
            tick, me_arr, tile_row, tile_col, tile_count, tile_vals, row_tiles, n
        )
        image = got = toward = None
        for layer in reversed(range(layers)):
            entry = layer == layers - 1
            c = dict(
                n=n, tile=tile, width=width, layers=layers, layer=layer, tick=tick, sections=sections,
                entry=entry, final=final,
                before=not entry and layer < layers - 2,
                toward=layer == 0 and not entry,
            )
            operands = [me_arr, section_arr, picks, preact, weights]
            specs = [SMEM, SMEM, SMEM, ANY, ANY]
            aliases = {}
            if entry:
                if tick == 0:
                    operands.append(grad_in)
                    specs.append(ANY)
                else:
                    operands += [grad_last, passed]
                    specs += [VMEM, VMEM]
            else:
                operands += [adj, image] + got
                specs += [VMEM] * (n + 1)
                if c["before"]:
                    operands.append(toward)
                    specs.append(VMEM)
                if c["toward"] and tick > 0:
                    aliases[len(operands)] = n + 1
                    operands.append(initial)
                    specs.append(ANY)
            if final:
                operands += [support, weight_acc[layer]]
                specs += [ANY, VMEM]
            outs = [shape(rows_dev, BF16)] * 2 + [shape(tile, BF16)] * (n - 1)
            out_specs = [VMEM] * (n + 1)
            scratch = []
            if not entry:
                if c["toward"]:
                    outs.append(jax.ShapeDtypeStruct((1, ticks, rows_dev, width), F32))
                    out_specs.append(ANY)
                    scratch = [pltpu.VMEM((rows_dev, width), F32), pltpu.SemaphoreType.DMA]
                else:
                    outs.append(shape(rows_dev, F32))
                    out_specs.append(VMEM)
            if final:
                outs.append(shape(width, BF16))
                out_specs.append(VMEM)
            scratch += [
                pltpu.VMEM((rows_dev, width), BF16),
                pltpu.VMEM((width, width), BF16),
                pltpu.SemaphoreType.DMA((4,)),
            ]
            if entry and tick == 0:
                scratch.append(pltpu.VMEM((rows_dev, width), BF16))
            if final:
                scratch.append(pltpu.VMEM((rows_dev, width), BF16))
            results = pl.pallas_call(
                functools.partial(layer_kernel, c),
                out_shape=outs,
                in_specs=specs,
                out_specs=out_specs,
                scratch_shapes=scratch,
                input_output_aliases=aliases,
                compiler_params=PARAMS,
                cost_estimate=cost(
                    2 * rows_dev * width * (width + (n + 1) * tile), (6 + 2 * n) * rows_dev * width
                ),
                name="entry" if entry else "middle",
            )(*operands)
            results = list(results)
            image, masked = results[:2]
            sends = results[2 : n + 1]
            rest = results[n + 1 :]
            if not entry:
                toward = rest.pop(0)
                if c["toward"]:
                    initial = toward
            if final:
                term = rest.pop(0)
                if not entry:
                    term, weight_sums[layer + 1] = lax.optimization_barrier(
                        (term, weight_sums[layer + 1])
                    )
                weight_sums[layer] = lax.psum(term, "rows")
            else:
                beta = jnp.log(
                    BETA_SCALE / (layers * section + layer + 1).astype(F32) + 1.0
                )
                term = beta * jnp.dot(
                    support[0, tick, layer].T, masked, preferred_element_type=F32
                )
                old = weight_acc[layer]
                weight_acc[layer] = term if old is None else old + term
            got = exchange(sends)
        c = dict(n=n, tile=tile, tick=tick, final=final)
        operands = [adj, image] + got
        specs = [VMEM] * (n + 1)
        aliases = {}
        if tick > 0:
            aliases[len(operands)] = 0
            operands.append(handoff)
            specs.append(ANY)
        outs = [jax.ShapeDtypeStruct((ticks, 1, rows_dev, width), BF16)]
        out_specs = [ANY]
        scratch = [pltpu.VMEM((rows_dev, width), BF16), pltpu.SemaphoreType.DMA]
        if not final:
            outs.append(shape(rows_dev, BF16))
            out_specs.append(VMEM)
        results = pl.pallas_call(
            functools.partial(exit_kernel, c),
            out_shape=outs,
            in_specs=specs,
            out_specs=out_specs,
            scratch_shapes=scratch,
            input_output_aliases=aliases,
            compiler_params=PARAMS,
            cost_estimate=cost(
                2 * rows_dev * width * (n + 1) * tile, (6 + 2 * n) * rows_dev * width
            ),
            name="exit",
        )(*operands)
        handoff = results[0]
        if not final:
            passed = results[1]
    return handoff, initial, jnp.stack(weight_sums).astype(F32)[None]


def solution(mesh):
    return jax.shard_map(
        shards,
        mesh=mesh,
        in_specs=(
            P("section", "rows", None),
            P("rows", None),
            P("section", None, None, "rows", None),
            P("section", None, None, "rows", None),
            P("section", None, None, None),
            P("section", None, "rows", None, None),
            P("section", None, "rows"),
            P("section", None, "rows"),
            P("section", None, "rows"),
        ),
        out_specs=(
            P(None, "section", "rows", None),
            P("section", None, "rows", None),
            P("section", None, None, None),
        ),
        check_vma=False,
    )
```

```python
import functools

import jax
import jax.numpy as jnp
from jax import lax
from jax.experimental import pallas as pl
from jax.experimental.pallas import tpu as pltpu
from jax.sharding import PartitionSpec as P

ALPHA = 0.1
BETA_SCALE = 0.5
VMEM = pl.BlockSpec(memory_space=pltpu.VMEM)
SMEM = pl.BlockSpec(memory_space=pltpu.SMEM)
HBM = pl.BlockSpec(memory_space=pltpu.HBM)
PARAMS = pltpu.CompilerParams(vmem_limit_bytes=24 * 2**20)
F32 = jnp.float32
BF16 = jnp.bfloat16


def cost(flops, nbytes):
    return pl.CostEstimate(flops=flops, bytes_accessed=nbytes, transcendentals=0)


def swapped(block, k):
    n = lax.axis_size("rows")
    return lax.ppermute(block, "rows", [(i, i ^ k) for i in range(n)])


def passed_along(block, axis, distance):
    devices = range(lax.axis_size(axis))
    route = [(i - distance, i) for i in devices if i - distance in devices]
    return lax.ppermute(block, axis, route)


class Refs:
    def __init__(self, refs):
        self.refs = list(refs)

    def take(self, count=None):
        many = 1 if count is None else count
        taken, self.refs = self.refs[:many], self.refs[many:]
        return taken[0] if count is None else taken


class Call:
    def __init__(self):
        self.operands, self.specs, self.outs, self.out_specs, self.scratch = [], [], [], [], []
        self.aliases = {}

    def give(self, spec, *arrays):
        self.operands += arrays
        self.specs += [spec] * len(arrays)

    def want(self, spec, shape, dtype, count=1):
        self.outs += [jax.ShapeDtypeStruct(shape, dtype)] * count
        self.out_specs += [spec] * count

    def run(self, kernel, name, estimate, params=PARAMS):
        return pl.pallas_call(
            kernel,
            out_shape=self.outs,
            in_specs=self.specs,
            out_specs=self.out_specs,
            scratch_shapes=self.scratch,
            input_output_aliases=self.aliases,
            compiler_params=params,
            cost_estimate=estimate,
            name=name,
        )(*self.operands)


def densify_kernel(row_tiles, n, chunks, *refs):
    refs = Refs(refs)
    me_ref, rows_ref, cols_ref, count_ref, vals_ref = refs.take(5)
    ticks = vals_ref.shape[1]
    outs = refs.take(ticks)
    vals, acc, sems = refs.take(3)
    entries, tile = vals.shape[1:3]
    chunk = entries // chunks
    me = me_ref[0]
    copies = {}
    for t in range(ticks):
        for c in range(chunks):
            part = pl.ds(c * chunk, chunk)
            copies[t, c] = pltpu.make_async_copy(
                vals_ref.at[0, t, part], vals.at[t, part], sems.at[t, c]
            )
            copies[t, c].start()
    for t in range(ticks):
        acc[...] = jnp.zeros_like(acc)

        def add(e, carry):
            owner = lax.div(cols_ref[0, t, e], row_tiles)
            block = lax.rem(cols_ref[0, t, e], row_tiles)
            slot = jnp.bitwise_xor(owner, me)
            slot = jnp.where((owner == me) & (block > 0), n - 1 + block, slot)
            rows = pl.ds(pl.multiple_of(rows_ref[0, t, e] * tile, tile), tile)
            cols = pl.ds(pl.multiple_of(slot * tile, tile), tile)
            acc[rows, cols] += vals[t, e].astype(F32)
            return carry

        for c in range(chunks):
            copies[t, c].wait()
            stop = jnp.clip(count_ref[0, t, 0], c * chunk, (c + 1) * chunk)
            lax.fori_loop(c * chunk, stop, add, 0)
        outs[t][...] = acc[...].astype(BF16)


def densify(me, rows, cols, count, vals, row_tiles, n):
    _, ticks, entries, tile, _ = vals.shape
    chunks = 4 if entries % 4 == 0 else 1
    shape = (row_tiles * tile, (n + row_tiles - 1) * tile)
    call = Call()
    call.give(SMEM, me, rows, cols, count)
    call.give(HBM, vals)
    call.want(VMEM, shape, BF16, ticks)
    call.scratch = [
        pltpu.VMEM(vals.shape[1:], BF16),
        pltpu.VMEM(shape, F32),
        pltpu.SemaphoreType.DMA((ticks, chunks)),
    ]
    return call.run(
        functools.partial(densify_kernel, row_tiles, n, chunks),
        "densify",
        cost(ticks * entries * tile * tile * 20, ticks * entries * tile * tile * 2),
        pltpu.CompilerParams(vmem_limit_bytes=58 * 2**20),
    )


def tile_at(ref, index, tile):
    return ref[pl.ds(pl.multiple_of(index * tile, tile), tile), :]


def give_got(call, got):
    call.give(VMEM, got["far"], *got["near"], *got["relayed"])


def take_got(refs, c):
    h, tile = c["n"] // 2, c["tile"]
    far = refs.take()
    near = refs.take(h - 1) if c["own_sent"] else None
    relayed = refs.take(h - 1)
    if near is None:
        near = [ref.at[tile:, :] for ref in relayed]
    return far, near, relayed


def spread_of(adj_ref, own_ref, got, pick_ref, me, c):
    n, tile = c["n"], c["tile"]
    far, near, relayed = got
    far_index = pick_ref[0, c["from_tick"] * n + jnp.bitwise_xor(me, n // 2)]
    blocks = jnp.concatenate(
        [own_ref[:tile, :]]
        + [ref[:tile, :] for ref in near]
        + [tile_at(far, far_index, tile)]
        + [ref[:tile, :] for ref in relayed]
        + [own_ref[tile : c["rows"], :]],
        axis=0,
    )
    total = jnp.dot(adj_ref[...], blocks, preferred_element_type=F32)
    return ((1.0 - ALPHA) * total).astype(BF16)


def chunk_total(kept_ref, relayed, c):
    total = kept_ref[...]
    for ref in relayed:
        total = total + ref[c["tile"] : c["tile"] + c["part"], :].astype(F32)
    return total.astype(BF16)


def layer_kernel(c, *refs):
    refs = Refs(refs)
    n, tile, rows, width = c["n"], c["tile"], c["rows"], c["width"]
    h = n // 2
    me_ref, section_ref, preact_all, weight_all = refs.take(4)
    picks = refs.take(h)
    if c["entry"]:
        last_ref, passed_ref = refs.take(2)
    else:
        adj_ref, own_ref = refs.take(2)
        got = take_got(refs, c)
    if c["final"]:
        support_all, acc_ref = refs.take(2)
    if c["sum_before"]:
        kept_before = refs.take()
    payload_ref = refs.take()
    sends = refs.take(h - 1)
    if c["final"]:
        kept_ref = refs.take()
    else:
        masked_ref = refs.take()
    if c["sum_before"]:
        chunk_ref = refs.take()
    preact_ref, weight_ref, load_sems = refs.take(3)

    me = me_ref[0]
    section = section_ref[0]
    loads = [
        (preact_all.at[0, c["tick"], c["layer"]], preact_ref),
        (weight_all.at[0, c["layer"]], weight_ref),
    ]
    if c["final"]:
        support_ref, term_ref = refs.take(2)
        loads.append((support_all.at[0, c["tick"], c["layer"]], support_ref))
    loads = [pltpu.make_async_copy(a, b, load_sems.at[i]) for i, (a, b) in enumerate(loads)]
    for load in loads:
        load.start()
    step = (c["layers"] * section + c["layer"] + 1).astype(F32)
    beta = jnp.log(BETA_SCALE / jnp.full((1, width), step, F32) + 1.0)
    if not c["entry"]:
        grad = spread_of(adj_ref, own_ref, got, picks[0], me, c)
    for load in loads:
        load.wait()
    if c["entry"]:
        grad = jnp.where(section == c["sections"] - 1, last_ref[...], passed_ref[...])

    masked = jnp.where(preact_ref[...] > 0, grad, jnp.zeros_like(grad))
    product = lax.dot_general(
        masked, weight_ref[...], (((1,), (1,)), ((), ())), preferred_element_type=F32
    )
    image = ((1.0 - beta) * masked.astype(F32) + beta * product).astype(BF16)
    payload_ref[:rows, :] = image
    for k in range(1, h):
        sends[k - 1][...] = tile_at(payload_ref, picks[k][0, c["tick"] * n + me], tile)
    if c["final"]:
        term = lax.dot_general(
            support_ref[...], masked, (((0,), (0,)), ((), ())), preferred_element_type=F32
        )
        term_ref[...] = acc_ref[...] + beta * term
        half = width // 2
        mine = lax.div(me, h)
        payload_ref[rows:, :] = tile_at(term_ref, 1 - mine, half).astype(BF16)
        kept_ref[...] = tile_at(term_ref, mine, half)
    else:
        masked_ref[...] = masked
    if c["sum_before"]:
        chunk_ref[...] = chunk_total(kept_before, got[2], c)


def relay_kernel(c, *refs):
    refs = Refs(refs)
    n, tile, part = c["n"], c["tile"], c["part"]
    h = n // 2
    me_ref, far_ref = refs.take(2)
    picks = refs.take(h - 1)
    if not c["own_sends"]:
        own_ref = refs.take()
    if c["final"]:
        kept_ref = refs.take()
    sends = refs.take(h - 1)
    if c["final"]:
        kept_chunk, sum_ref = refs.take(2)
    me = me_ref[0]
    base = c["tick"] * n
    for k in range(1, h):
        index = picks[k - 1][0, base + jnp.bitwise_xor(me, h)]
        sends[k - 1][:tile, :] = tile_at(far_ref, index, tile)
        if not c["own_sends"]:
            sends[k - 1][tile:, :] = tile_at(own_ref, picks[k - 1][0, base + me], tile)
    if c["final"]:
        sum_ref[...] = kept_ref[...] + far_ref[c["rows"] :, :].astype(F32)
        place = lax.rem(me, h)
        for k in range(1, h):
            sends[k - 1][tile : tile + part, :] = tile_at(
                sum_ref, jnp.bitwise_xor(place, k), part
            ).astype(BF16)
        kept_chunk[...] = tile_at(sum_ref, place, part)


def exit_kernel(c, *refs):
    refs = Refs(refs)
    me_ref, pick_ref, adj_ref, own_ref = refs.take(4)
    got = take_got(refs, c)
    if c["tick"] > 0:
        refs.take()
    if c["final"]:
        kept_ref, above = refs.take(), refs.take(c["layers"] - 1)
    out_ref, extra_ref, hold_ref, sem = refs.take(4)
    grad = spread_of(adj_ref, own_ref, got, pick_ref, me_ref[0], c)
    hold_ref[...] = grad
    copy = pltpu.make_async_copy(hold_ref, out_ref.at[c["tick"], 0], sem)
    copy.start()
    if c["final"]:
        extra_ref[0] = chunk_total(kept_ref, got[2], c)
        for i, ref in enumerate(above):
            extra_ref[i + 1] = ref[...]
    else:
        extra_ref[...] = grad
    copy.wait()


def finish_kernel(n, part, *refs):
    refs = Refs(refs)
    me_ref = refs.take()
    sums = refs.take(n)
    out_ref, hold_ref, sems = refs.take(3)
    layers = hold_ref.shape[0]
    copies = []
    for layer in range(layers):
        for k in range(n):
            start = pl.multiple_of(jnp.bitwise_xor(me_ref[0], k) * part, 8)
            hold_ref[layer, pl.ds(start, part), :] = sums[k][layer].astype(F32)
        copy = pltpu.make_async_copy(hold_ref.at[layer], out_ref.at[0, layer], sems.at[layer])
        copy.start()
        copies.append(copy)
    for copy in copies:
        copy.wait()


def shards(grad_in, grad_last, support, preact, weights, tile_vals, tile_row, tile_col, tile_count):
    section = lax.axis_index("section")
    me = lax.axis_index("rows")
    n = lax.axis_size("rows")
    h = n // 2
    sections = lax.axis_size("section")
    ticks = support.shape[1]
    layers = support.shape[2]
    rows, width = grad_last.shape
    tile = tile_vals.shape[-1]
    row_tiles = rows // tile
    part = width // n
    room = max(part, 16)
    me_arr = me.astype(jnp.int32).reshape(1)
    section_arr = section.astype(jnp.int32).reshape(1)

    owner = tile_col[0] // row_tiles
    named = jnp.where(
        owner[:, :, None] == jnp.arange(n)[None, None, :], (tile_col[0] % row_tiles)[:, :, None], 0
    )
    pick = jnp.max(named, axis=1).reshape(1, ticks * n).astype(jnp.int32)
    picks = [pick] + [swapped(pick, k) for k in range(1, h)]

    adjs = densify(me_arr, tile_row, tile_col, tile_count, tile_vals, row_tiles, n)
    handoff = passed = kept = None
    weight_acc = [None] * layers
    chunks = []
    initial = []
    base = dict(
        n=n, tile=tile, rows=rows, width=width, layers=layers, sections=sections, part=part
    )
    layer_cost = cost(2 * rows * width * (width + (n + 1) * tile), (6 + 2 * n) * rows * width)
    small_cost = cost(rows * width, 2 * n * rows * width)
    for tick in range(ticks):
        final = tick == ticks - 1
        if tick > 0:
            passed = passed_along(passed, "section", -1)
        adj = adjs[tick]
        payload = got = None
        toward = 0.0
        own_sent = None
        for layer in reversed(range(layers)):
            entry = layer == layers - 1
            own_sends = not (tick == 0 and entry)
            c = dict(
                base, layer=layer, tick=tick, from_tick=tick, entry=entry, final=final,
                own_sends=own_sends, own_sent=own_sent, sum_before=final and not entry,
            )
            if own_sends:
                call = Call()
                call.give(SMEM, me_arr, section_arr)
                call.give(HBM, preact, weights)
                call.give(SMEM, *picks)
                if entry:
                    call.give(VMEM, grad_last, passed)
                else:
                    call.give(VMEM, adj, payload)
                    give_got(call, got)
                if final:
                    call.give(HBM, support)
                    call.give(VMEM, weight_acc[layer])
                if c["sum_before"]:
                    call.give(VMEM, kept)
                call.want(VMEM, (rows + (width // 2 if final else 0), width), BF16)
                call.want(VMEM, (tile, width), BF16, h - 1)
                if final:
                    call.want(VMEM, (width // 2, width), F32)
                else:
                    call.want(VMEM, (rows, width), BF16)
                if c["sum_before"]:
                    call.want(VMEM, (part, width), BF16)
                call.scratch = [
                    pltpu.VMEM((rows, width), BF16),
                    pltpu.VMEM((width, width), BF16),
                    pltpu.SemaphoreType.DMA((4,)),
                ]
                if final:
                    call.scratch.append(pltpu.VMEM((rows, width), BF16))
                    call.scratch.append(pltpu.VMEM((width, width), F32))
                results = Refs(
                    call.run(
                        functools.partial(layer_kernel, c), "entry" if entry else "middle", layer_cost
                    )
                )
            else:
                beta = jnp.log(BETA_SCALE / (layers * section + layer + 1).astype(F32) + 1.0)
                masked = jnp.where(preact[0, tick, layer] > 0, grad_in[0], jnp.zeros_like(grad_in[0]))
                product = jnp.dot(masked, weights[0, layer].T, preferred_element_type=F32)
                image = ((1.0 - beta) * masked.astype(F32) + beta * product).astype(BF16)
                results = Refs([image, masked])
            payload = results.take()
            sends = results.take(h - 1) if own_sends else []
            if final:
                kept_half = results.take()
            else:
                beta = jnp.log(BETA_SCALE / (layers * section + layer + 1).astype(F32) + 1.0)
                term = beta * jnp.dot(
                    support[0, tick, layer].T, results.take(), preferred_element_type=F32
                )
                old = weight_acc[layer]
                weight_acc[layer] = term if old is None else old + term
            if c["sum_before"]:
                chunks.insert(0, results.take())
            toward = toward + ALPHA * payload[:rows].astype(F32)

            far = swapped(payload, h)
            near = [swapped(send, k + 1) for k, send in enumerate(sends)]
            call = Call()
            call.give(SMEM, me_arr)
            call.give(VMEM, far)
            call.give(SMEM, *picks[1:])
            if not own_sends:
                call.give(VMEM, payload)
            if final:
                call.give(VMEM, kept_half)
            message = tile * (1 if own_sends else 2) + (room if final else 0)
            call.want(VMEM, (message, width), BF16, h - 1)
            if final:
                call.want(VMEM, (part, width), F32)
                call.scratch = [pltpu.VMEM((width // 2, width), F32)]
            results = Refs(call.run(functools.partial(relay_kernel, c), "relay", small_cost))
            relays = results.take(h - 1)
            if final:
                kept = results.take()
            relayed = [swapped(relay, k + 1) for k, relay in enumerate(relays)]
            got = dict(far=far, near=near, relayed=relayed)
            own_sent = own_sends
        initial.append(toward)
        c = dict(base, tick=tick, from_tick=tick, final=final, own_sent=own_sent)
        call = Call()
        call.give(SMEM, me_arr, pick)
        call.give(VMEM, adj, payload)
        give_got(call, got)
        if tick > 0:
            call.aliases[len(call.operands)] = 0
            call.give(HBM, handoff)
        if final:
            call.give(VMEM, kept, *chunks)
        call.want(HBM, (ticks, 1, rows, width), BF16)
        if final:
            call.want(VMEM, (layers, part, width), BF16)
        else:
            call.want(VMEM, (rows, width), BF16)
        call.scratch = [pltpu.VMEM((rows, width), BF16), pltpu.SemaphoreType.DMA]
        handoff, passed = call.run(functools.partial(exit_kernel, c), "exit", layer_cost)
    far = swapped(passed, h)
    near = [passed] + [swapped(passed, k) for k in range(1, h)]
    forwarded = [far] + [swapped(far, k) for k in range(1, h)]
    call = Call()
    call.give(SMEM, me_arr)
    call.give(VMEM, *near, *forwarded)
    call.want(HBM, (1, layers, width, width), F32)
    call.scratch = [pltpu.VMEM((layers, width, width), F32), pltpu.SemaphoreType.DMA((layers,))]
    (weight_grad,) = call.run(functools.partial(finish_kernel, n, part), "finish", small_cost)
    return handoff, jnp.stack(initial)[None], weight_grad


def solution(mesh):
    return jax.shard_map(
        shards,
        mesh=mesh,
        in_specs=(
            P("section", "rows", None),
            P("rows", None),
            P("section", None, None, "rows", None),
            P("section", None, None, "rows", None),
            P("section", None, None, None),
            P("section", None, "rows", None, None),
            P("section", None, "rows"),
            P("section", None, "rows"),
            P("section", None, "rows"),
        ),
        out_specs=(
            P(None, "section", "rows", None),
            P("section", None, "rows", None),
            P("section", None, None, None),
        ),
        check_vma=False,
    )
```

```python
import functools

import jax
import jax.numpy as jnp
from jax import lax
from jax.experimental import pallas as pl
from jax.experimental.pallas import tpu as pltpu
from jax.sharding import PartitionSpec as P

ALPHA = 0.1
BETA_SCALE = 0.5
VMEM = pl.BlockSpec(memory_space=pltpu.VMEM)
SMEM = pl.BlockSpec(memory_space=pltpu.SMEM)
HBM = pl.BlockSpec(memory_space=pltpu.HBM)
PARAMS = pltpu.CompilerParams(vmem_limit_bytes=24 * 2**20)
F32 = jnp.float32
BF16 = jnp.bfloat16


def cost(flops, nbytes):
    return pl.CostEstimate(flops=flops, bytes_accessed=nbytes, transcendentals=0)


def swapped(block, k):
    n = lax.axis_size("rows")
    return lax.ppermute(block, "rows", [(i, i ^ k) for i in range(n)])


def passed_along(block, axis, distance):
    devices = range(lax.axis_size(axis))
    route = [(i - distance, i) for i in devices if i - distance in devices]
    return lax.ppermute(block, axis, route)


class Refs:
    def __init__(self, refs):
        self.refs = list(refs)

    def take(self, count=None):
        many = 1 if count is None else count
        taken, self.refs = self.refs[:many], self.refs[many:]
        return taken[0] if count is None else taken


class Call:
    def __init__(self):
        self.operands, self.specs, self.outs, self.out_specs, self.scratch = [], [], [], [], []
        self.aliases = {}

    def give(self, spec, *arrays):
        self.operands += arrays
        self.specs += [spec] * len(arrays)

    def want(self, spec, shape, dtype, count=1):
        self.outs += [jax.ShapeDtypeStruct(shape, dtype)] * count
        self.out_specs += [spec] * count

    def run(self, kernel, name, estimate, params=PARAMS):
        return pl.pallas_call(
            kernel,
            out_shape=self.outs,
            in_specs=self.specs,
            out_specs=self.out_specs,
            scratch_shapes=self.scratch,
            input_output_aliases=self.aliases,
            compiler_params=params,
            cost_estimate=estimate,
            name=name,
        )(*self.operands)


def densify_kernel(tick, row_tiles, n, chunks, *refs):
    me_ref, rows_ref, cols_ref, count_ref, vals_ref, out_ref, vals, acc, sems = refs
    entries, tile = vals.shape[:2]
    chunk = entries // chunks
    me = me_ref[0]
    copies = []
    for c in range(chunks):
        part = pl.ds(c * chunk, chunk)
        copies.append(
            pltpu.make_async_copy(vals_ref.at[0, tick, part], vals.at[part], sems.at[c])
        )
        copies[c].start()
    acc[...] = jnp.zeros_like(acc)

    def add(e, carry):
        owner = lax.div(cols_ref[0, tick, e], row_tiles)
        block = lax.rem(cols_ref[0, tick, e], row_tiles)
        slot = jnp.bitwise_xor(owner, me)
        slot = jnp.where((owner == me) & (block > 0), n - 1 + block, slot)
        rows = pl.ds(pl.multiple_of(rows_ref[0, tick, e] * tile, tile), tile)
        cols = pl.ds(pl.multiple_of(slot * tile, tile), tile)
        acc[rows, cols] += vals[e].astype(F32)
        return carry

    for c in range(chunks):
        copies[c].wait()
        stop = jnp.clip(count_ref[0, tick], c * chunk, (c + 1) * chunk)
        lax.fori_loop(c * chunk, stop, add, 0)
    out_ref[...] = acc[...].astype(BF16)


def densify(tick, me, rows, cols, count, vals, row_tiles, n):
    entries, tile = vals.shape[2:4]
    chunks = 4 if entries % 4 == 0 else 1
    shape = (row_tiles * tile, (n + row_tiles - 1) * tile)
    call = Call()
    call.give(SMEM, me, rows, cols, count)
    call.give(HBM, vals)
    call.want(VMEM, shape, BF16)
    call.scratch = [
        pltpu.VMEM(vals.shape[2:], BF16),
        pltpu.VMEM(shape, F32),
        pltpu.SemaphoreType.DMA((chunks,)),
    ]
    (adj,) = call.run(
        functools.partial(densify_kernel, tick, row_tiles, n, chunks),
        "densify",
        cost(entries * tile * tile * 20, entries * tile * tile * 2),
        pltpu.CompilerParams(vmem_limit_bytes=50 * 2**20),
    )
    return adj


def tile_at(ref, index, tile):
    return ref[pl.ds(pl.multiple_of(index * tile, tile), tile), :]


def take_got(refs, n):
    far, near, relayed = refs.take(), refs.take(n // 2 - 1), refs.take(n // 2 - 1)
    return far, near, relayed


def spread_of(adj_ref, own_ref, got, pick_ref, me, c):
    n, tile = c["n"], c["tile"]
    far, near, relayed = got

    def named(ref, k):
        index = pick_ref[0, c["tick"] * n + jnp.bitwise_xor(me, k)]
        return tile_at(ref, index, tile)

    if c["whole"]:
        near = [named(ref, k) for k, ref in enumerate(near, 1)]
        relayed = [named(ref, n // 2 + k) for k, ref in enumerate(relayed, 1)]
    else:
        near = [ref[:tile, :] for ref in near]
        relayed = [ref[...] for ref in relayed]
    blocks = jnp.concatenate(
        [own_ref[:tile, :]] + near + [named(far, n // 2)] + relayed + [own_ref[tile:, :]], axis=0
    )
    total = jnp.dot(adj_ref[...], blocks, preferred_element_type=F32)
    return ((1.0 - ALPHA) * total).astype(BF16)


def chunk_total(mine_ref, far_ref):
    return (mine_ref[...].astype(F32) + far_ref[...].astype(F32)).astype(BF16)


def layer_kernel(c, *refs):
    refs = Refs(refs)
    n, tile, width, chunk = c["n"], c["tile"], c["width"], c["chunk"]
    h = n // 2
    me_ref, section_ref, preact_all, weight_all = refs.take(4)
    picks = refs.take(h)
    if c["entry"]:
        last_ref, passed_ref = refs.take(2)
    else:
        adj_ref, own_ref = refs.take(2)
        got = take_got(refs, n)
    if c["final"]:
        support_all, acc_ref = refs.take(2)
    if c["sum_above"]:
        above_mine, above_far = refs.take(2)
    image_ref = refs.take()
    sends = refs.take(h - 1)
    out_ref = refs.take()
    if c["sum_above"]:
        above_ref = refs.take()
    preact_ref, weight_ref, load_sems = refs.take(3)

    me = me_ref[0]
    section = section_ref[0]
    loads = [
        (preact_all.at[0, c["tick"], c["layer"]], preact_ref),
        (weight_all.at[0, c["layer"]], weight_ref),
    ]
    if c["final"]:
        support_ref, term_ref = refs.take(2)
        loads.append((support_all.at[0, c["tick"], c["layer"]], support_ref))
    loads = [pltpu.make_async_copy(a, b, load_sems.at[i]) for i, (a, b) in enumerate(loads)]
    for load in loads:
        load.start()
    step = (c["layers"] * section + c["layer"] + 1).astype(F32)
    beta = jnp.log(BETA_SCALE / jnp.full((1, width), step, F32) + 1.0)
    if not c["entry"]:
        grad = spread_of(adj_ref, own_ref, got, picks[0], me, c)
    for load in loads:
        load.wait()
    if c["entry"]:
        grad = jnp.where(section == c["sections"] - 1, last_ref[...], passed_ref[...])

    masked = jnp.where(preact_ref[...] > 0, grad, jnp.zeros_like(grad))
    product = lax.dot_general(
        masked, weight_ref[...], (((1,), (1,)), ((), ())), preferred_element_type=F32
    )
    image = ((1.0 - beta) * masked.astype(F32) + beta * product).astype(BF16)
    image_ref[...] = image
    for k in range(1, h):
        sends[k - 1][:tile, :] = tile_at(image_ref, picks[k][0, c["tick"] * n + me], tile)
    if c["final"]:
        term = lax.dot_general(
            support_ref[...], masked, (((0,), (0,)), ((), ())), preferred_element_type=F32
        )
        term_ref[...] = acc_ref[...] + beta * term
        place = lax.rem(me, h)
        for k in range(1, h):
            sends[k - 1][tile : tile + chunk, :] = tile_at(
                term_ref, jnp.bitwise_xor(place, k), chunk
            ).astype(BF16)
        out_ref[...] = tile_at(term_ref, place, chunk)
    else:
        out_ref[...] = masked
    if c["sum_above"]:
        above_ref[...] = chunk_total(above_mine, above_far)
        for send in sends:
            send[tile + chunk :, :] = above_ref[...]


def relay_kernel(c, *refs):
    refs = Refs(refs)
    n, tile, chunk = c["n"], c["tile"], c["chunk"]
    h = n // 2
    me_ref, far_ref = refs.take(2)
    picks = refs.take(h - 1)
    if c["final"]:
        kept_ref, near = refs.take(), refs.take(h - 1)
    sends = refs.take(h - 1)
    me = me_ref[0]
    for k in range(1, h):
        index = picks[k - 1][0, c["tick"] * n + jnp.bitwise_xor(me, h)]
        sends[k - 1][...] = tile_at(far_ref, index, tile)
    if c["final"]:
        total = kept_ref[...]
        for ref in near:
            total = total + ref[tile : tile + chunk, :].astype(F32)
        refs.take()[...] = total.astype(BF16)


def exit_kernel(c, *refs):
    refs = Refs(refs)
    me_ref, pick_ref, adj_ref, own_ref = refs.take(4)
    got = take_got(refs, c["n"])
    if not c["final"]:
        refs.take()[...] = spread_of(adj_ref, own_ref, got, pick_ref, me_ref[0], c)
        return
    handed = refs.take(c["tick"])
    mine_ref, far_ref = refs.take(2)
    out_ref, sum_ref, hold_ref, sems = refs.take(4)
    copies = [
        pltpu.make_async_copy(ref, out_ref.at[t, 0], sems.at[t])
        for t, ref in enumerate(handed + [hold_ref])
    ]
    for copy in copies[:-1]:
        copy.start()
    sum_ref[...] = chunk_total(mine_ref, far_ref)
    hold_ref[...] = spread_of(adj_ref, own_ref, got, pick_ref, me_ref[0], c)
    copies[-1].start()
    for copy in copies:
        copy.wait()


def finish_kernel(h, layers, chunk, tile, *refs):
    refs = Refs(refs)
    me_ref = refs.take()
    sums = [refs.take(h) for layer in range(layers)]
    out_ref, hold_ref, sems = refs.take(3)
    place = lax.rem(me_ref[0], h)
    copies = []
    for layer in range(layers):
        for k in range(h):
            skip = tile + chunk if layer > 0 and k > 0 else 0
            start = pl.multiple_of(jnp.bitwise_xor(place, k) * chunk, chunk)
            hold_ref[layer, pl.ds(start, chunk), :] = sums[layer][k][skip:, :].astype(F32)
        copy = pltpu.make_async_copy(hold_ref.at[layer], out_ref.at[0, layer], sems.at[layer])
        copy.start()
        copies.append(copy)
    for copy in copies:
        copy.wait()


def shards(grad_in, grad_last, support, preact, weights, tile_vals, tile_row, tile_col, tile_count):
    section = lax.axis_index("section")
    me = lax.axis_index("rows")
    n = lax.axis_size("rows")
    h = n // 2
    sections = lax.axis_size("section")
    ticks = support.shape[1]
    layers = support.shape[2]
    rows, width = grad_last.shape
    tile = tile_vals.shape[-1]
    row_tiles = rows // tile
    chunk = width // h
    me_arr = me.astype(jnp.int32).reshape(1)
    section_arr = section.astype(jnp.int32).reshape(1)
    counts = tile_count.reshape(1, ticks)

    owner = tile_col[0] // row_tiles
    named = jnp.where(
        owner[:, :, None] == jnp.arange(n)[None, None, :], (tile_col[0] % row_tiles)[:, :, None], 0
    )
    pick = jnp.max(named, axis=1).reshape(1, ticks * n).astype(jnp.int32)
    picks = [pick] + [swapped(pick, k) for k in range(1, h)]

    handed = []
    passed = None
    weight_acc = [None] * layers
    weight_sums = [None] * layers
    initial = []
    base = dict(n=n, tile=tile, width=width, layers=layers, sections=sections, chunk=chunk)
    layer_cost = cost(2 * rows * width * (width + (n + 1) * tile), (6 + 2 * n) * rows * width)
    small_cost = cost(rows * width, 2 * n * rows * width)
    for tick in range(ticks):
        final = tick == ticks - 1
        if tick > 0:
            passed = passed_along(handed[-1], "section", -1)
        adj = densify(tick, me_arr, tile_row, tile_col, counts, tile_vals, row_tiles, n)
        image = got = whole = mine = None
        toward = 0.0
        for layer in reversed(range(layers)):
            entry = layer == layers - 1
            beta = jnp.log(BETA_SCALE / (layers * section + layer + 1).astype(F32) + 1.0)
            c = dict(
                base, layer=layer, tick=tick, entry=entry, final=final,
                sum_above=final and not entry, whole=whole,
            )
            if tick == 0 and entry:
                masked = jnp.where(
                    preact[0, tick, layer] > 0, grad_in[0], jnp.zeros_like(grad_in[0])
                )
                product = jnp.dot(masked, weights[0, layer].T, preferred_element_type=F32)
                image = ((1.0 - beta) * masked.astype(F32) + beta * product).astype(BF16)
                far = swapped(image, h)
                near = [swapped(image, k) for k in range(1, h)]
                got = [far, *near, *(swapped(far, k) for k in range(1, h))]
            else:
                call = Call()
                call.give(SMEM, me_arr, section_arr)
                call.give(HBM, preact, weights)
                call.give(SMEM, *picks)
                if entry:
                    call.give(VMEM, grad_last, passed)
                else:
                    call.give(VMEM, adj, image, *got)
                if final:
                    call.give(HBM, support)
                    call.give(VMEM, weight_acc[layer])
                if c["sum_above"]:
                    call.give(VMEM, mine, swapped(mine, h))
                message = tile + chunk * (final + c["sum_above"])
                call.want(VMEM, (rows, width), BF16)
                call.want(VMEM, (message, width), BF16, h - 1)
                if final:
                    call.want(VMEM, (chunk, width), F32)
                else:
                    call.want(VMEM, (rows, width), BF16)
                if c["sum_above"]:
                    call.want(VMEM, (chunk, width), BF16)
                call.scratch = [
                    pltpu.VMEM((rows, width), BF16),
                    pltpu.VMEM((width, width), BF16),
                    pltpu.SemaphoreType.DMA((3,)),
                ]
                if final:
                    call.scratch.append(pltpu.VMEM((rows, width), BF16))
                    call.scratch.append(pltpu.VMEM((width, width), F32))
                results = Refs(
                    call.run(
                        functools.partial(layer_kernel, c), "entry" if entry else "middle", layer_cost
                    )
                )
                image = results.take()
                sends = results.take(h - 1)
                kept = masked = results.take()
                far = swapped(image, h)
                near = [swapped(send, k) for k, send in enumerate(sends, 1)]
                if c["sum_above"]:
                    weight_sums[layer + 1] = [results.take(), *near]
                call = Call()
                call.give(SMEM, me_arr)
                call.give(VMEM, far)
                call.give(SMEM, *picks[1:])
                if final:
                    call.give(VMEM, kept, *near)
                call.want(VMEM, (tile, width), BF16, h - 1)
                if final:
                    call.want(VMEM, (chunk, width), BF16)
                results = Refs(call.run(functools.partial(relay_kernel, c), "relay", small_cost))
                relayed = [swapped(relay, k) for k, relay in enumerate(results.take(h - 1), 1)]
                if final:
                    mine = results.take()
                got = [far, *near, *relayed]
            whole = tick == 0 and entry
            toward = toward + ALPHA * image.astype(F32)
            if not final:
                term = beta * jnp.dot(
                    support[0, tick, layer].T, masked, preferred_element_type=F32
                )
                old = weight_acc[layer]
                weight_acc[layer] = term if old is None else old + term
        initial.append(toward)
        c = dict(base, tick=tick, final=final, whole=whole)
        call = Call()
        call.give(SMEM, me_arr, pick)
        call.give(VMEM, adj, image, *got)
        if final:
            call.give(VMEM, *handed, mine, swapped(mine, h))
            call.want(HBM, (ticks, 1, rows, width), BF16)
            call.want(VMEM, (chunk, width), BF16)
            call.scratch = [pltpu.VMEM((rows, width), BF16), pltpu.SemaphoreType.DMA((ticks,))]
        else:
            call.want(VMEM, (rows, width), BF16)
        results = call.run(functools.partial(exit_kernel, c), "exit", layer_cost)
        if final:
            handoff, last = results
        else:
            handed.append(results[0])
    weight_sums[0] = [last] + [swapped(last, k) for k in range(1, h)]
    call = Call()
    call.give(SMEM, me_arr)
    for sums in weight_sums:
        call.give(VMEM, *sums)
    call.want(HBM, (1, layers, width, width), F32)
    call.scratch = [pltpu.VMEM((layers, width, width), F32), pltpu.SemaphoreType.DMA((layers,))]
    (weight_grad,) = call.run(
        functools.partial(finish_kernel, h, layers, chunk, tile), "finish", small_cost
    )
    return handoff, jnp.stack(initial)[None], weight_grad


def solution(mesh):
    return jax.shard_map(
        shards,
        mesh=mesh,
        in_specs=(
            P("section", "rows", None),
            P("rows", None),
            P("section", None, None, "rows", None),
            P("section", None, None, "rows", None),
            P("section", None, None, None),
            P("section", None, "rows", None, None),
            P("section", None, "rows"),
            P("section", None, "rows"),
            P("section", None, "rows"),
        ),
        out_specs=(
            P(None, "section", "rows", None),
            P("section", None, "rows", None),
            P("section", None, None, None),
        ),
        check_vma=False,
    )
```

```python
import functools

import jax
import jax.numpy as jnp
from jax import lax
from jax.experimental import pallas as pl
from jax.experimental.pallas import tpu as pltpu
from jax.sharding import PartitionSpec as P

ALPHA = 0.1
BETA_SCALE = 0.5
VMEM = pl.BlockSpec(memory_space=pltpu.VMEM)
SMEM = pl.BlockSpec(memory_space=pltpu.SMEM)
HBM = pl.BlockSpec(memory_space=pltpu.HBM)
PARAMS = pltpu.CompilerParams(vmem_limit_bytes=24 * 2**20)
F32 = jnp.float32
BF16 = jnp.bfloat16


def cost(flops, nbytes):
    return pl.CostEstimate(flops=flops, bytes_accessed=nbytes, transcendentals=0)


def swapped(block, k):
    n = lax.axis_size("rows")
    return lax.ppermute(block, "rows", [(i, i ^ k) for i in range(n)])


def passed_along(block, axis, distance):
    devices = range(lax.axis_size(axis))
    route = [(i - distance, i) for i in devices if i - distance in devices]
    return lax.ppermute(block, axis, route)


class Refs:
    def __init__(self, refs):
        self.refs = list(refs)

    def take(self, count=None):
        many = 1 if count is None else count
        taken, self.refs = self.refs[:many], self.refs[many:]
        return taken[0] if count is None else taken


class Call:
    def __init__(self):
        self.operands, self.specs, self.outs, self.out_specs, self.scratch = [], [], [], [], []
        self.aliases = {}

    def give(self, spec, *arrays):
        self.operands += arrays
        self.specs += [spec] * len(arrays)

    def want(self, spec, shape, dtype, count=1):
        self.outs += [jax.ShapeDtypeStruct(shape, dtype)] * count
        self.out_specs += [spec] * count

    def run(self, kernel, name, estimate, params=PARAMS):
        return pl.pallas_call(
            kernel,
            out_shape=self.outs,
            in_specs=self.specs,
            out_specs=self.out_specs,
            scratch_shapes=self.scratch,
            input_output_aliases=self.aliases,
            compiler_params=params,
            cost_estimate=estimate,
            name=name,
        )(*self.operands)


def densify_kernel(tick, row_tiles, n, chunks, *refs):
    me_ref, rows_ref, cols_ref, count_ref, vals_ref, out_ref, vals, acc, sems = refs
    entries, tile = vals.shape[:2]
    chunk = entries // chunks
    me = me_ref[0]
    copies = []
    for c in range(chunks):
        part = pl.ds(c * chunk, chunk)
        copies.append(
            pltpu.make_async_copy(vals_ref.at[0, tick, part], vals.at[part], sems.at[c])
        )
        copies[c].start()
    acc[...] = jnp.zeros_like(acc)

    def add(e, carry):
        owner = lax.div(cols_ref[0, tick, e], row_tiles)
        block = lax.rem(cols_ref[0, tick, e], row_tiles)
        slot = jnp.bitwise_xor(owner, me)
        slot = jnp.where((owner == me) & (block > 0), n - 1 + block, slot)
        rows = pl.ds(pl.multiple_of(rows_ref[0, tick, e] * tile, tile), tile)
        cols = pl.ds(pl.multiple_of(slot * tile, tile), tile)
        acc[rows, cols] += vals[e].astype(F32)
        return carry

    for c in range(chunks):
        copies[c].wait()
        stop = jnp.clip(count_ref[0, tick], c * chunk, (c + 1) * chunk)
        lax.fori_loop(c * chunk, stop, add, 0)
    out_ref[...] = acc[...].astype(BF16)


def densify(tick, me, rows, cols, count, vals, row_tiles, n):
    entries, tile = vals.shape[2:4]
    chunks = 4 if entries % 4 == 0 else 1
    shape = (row_tiles * tile, (n + row_tiles - 1) * tile)
    call = Call()
    call.give(SMEM, me, rows, cols, count)
    call.give(HBM, vals)
    call.want(VMEM, shape, BF16)
    call.scratch = [
        pltpu.VMEM(vals.shape[2:], BF16),
        pltpu.VMEM(shape, F32),
        pltpu.SemaphoreType.DMA((chunks,)),
    ]
    (adj,) = call.run(
        functools.partial(densify_kernel, tick, row_tiles, n, chunks),
        "densify",
        cost(entries * tile * tile * 20, entries * tile * tile * 2),
        pltpu.CompilerParams(vmem_limit_bytes=50 * 2**20),
    )
    return adj


def tile_at(ref, index, tile):
    return ref[pl.ds(pl.multiple_of(index * tile, tile), tile), :]


def take_got(refs, n):
    far, near, relayed = refs.take(), refs.take(n // 2 - 1), refs.take(n // 2 - 1)
    return far, near, relayed


def spread_of(adj_ref, own_ref, got, pick_ref, me, c):
    n, tile = c["n"], c["tile"]
    far, near, relayed = got

    def named(ref, k):
        index = pick_ref[0, c["tick"] * n + jnp.bitwise_xor(me, k)]
        return tile_at(ref, index, tile)

    if c["whole"]:
        near = [named(ref, k) for k, ref in enumerate(near, 1)]
        relayed = [named(ref, n // 2 + k) for k, ref in enumerate(relayed, 1)]
    else:
        near = [ref[:tile, :] for ref in near]
        relayed = [ref[...] for ref in relayed]
    blocks = jnp.concatenate(
        [own_ref[:tile, :]] + near + [named(far, n // 2)] + relayed + [own_ref[tile:, :]], axis=0
    )
    total = jnp.dot(adj_ref[...], blocks, preferred_element_type=F32)
    return ((1.0 - ALPHA) * total).astype(BF16)


def layer_kernel(c, *refs):
    refs = Refs(refs)
    n, tile, width, chunk = c["n"], c["tile"], c["width"], c["chunk"]
    h = n // 2
    me_ref, section_ref, preact_all, weight_all = refs.take(4)
    picks = refs.take(h)
    if c["entry"]:
        last_ref, passed_ref = refs.take(2)
    else:
        adj_ref, own_ref = refs.take(2)
        got = take_got(refs, n)
    if c["final"]:
        support_all, acc_ref = refs.take(2)
    image_ref = refs.take()
    sends = refs.take(h - 1)
    out_ref = refs.take()
    preact_ref, weight_ref, load_sems = refs.take(3)

    me = me_ref[0]
    section = section_ref[0]
    loads = [
        (preact_all.at[0, c["tick"], c["layer"]], preact_ref),
        (weight_all.at[0, c["layer"]], weight_ref),
    ]
    if c["final"]:
        support_ref, term_ref = refs.take(2)
        loads.append((support_all.at[0, c["tick"], c["layer"]], support_ref))
    loads = [pltpu.make_async_copy(a, b, load_sems.at[i]) for i, (a, b) in enumerate(loads)]
    for load in loads:
        load.start()
    step = (c["layers"] * section + c["layer"] + 1).astype(F32)
    beta = jnp.log(BETA_SCALE / jnp.full((1, width), step, F32) + 1.0)
    if not c["entry"]:
        grad = spread_of(adj_ref, own_ref, got, picks[0], me, c)
    for load in loads:
        load.wait()
    if c["entry"]:
        grad = jnp.where(section == c["sections"] - 1, last_ref[...], passed_ref[...])

    masked = jnp.where(preact_ref[...] > 0, grad, jnp.zeros_like(grad))
    product = lax.dot_general(
        masked, weight_ref[...], (((1,), (1,)), ((), ())), preferred_element_type=F32
    )
    image = ((1.0 - beta) * masked.astype(F32) + beta * product).astype(BF16)
    image_ref[...] = image
    for k in range(1, h):
        sends[k - 1][:tile, :] = tile_at(image_ref, picks[k][0, c["tick"] * n + me], tile)
    if c["final"]:
        term = lax.dot_general(
            support_ref[...], masked, (((0,), (0,)), ((), ())), preferred_element_type=F32
        )
        term_ref[...] = acc_ref[...] + beta * term
        place = lax.rem(me, h)
        for k in range(1, h):
            sends[k - 1][tile : tile + chunk, :] = tile_at(
                term_ref, jnp.bitwise_xor(place, k), chunk
            ).astype(BF16)
        out_ref[...] = tile_at(term_ref, place, chunk)
    else:
        out_ref[...] = masked


def relay_kernel(c, *refs):
    refs = Refs(refs)
    n, tile = c["n"], c["tile"]
    h = n // 2
    me_ref, far_ref = refs.take(2)
    picks = refs.take(h - 1)
    sends = refs.take(h - 1)
    me = me_ref[0]
    for k in range(1, h):
        index = picks[k - 1][0, c["tick"] * n + jnp.bitwise_xor(me, h)]
        sends[k - 1][...] = tile_at(far_ref, index, tile)


def half_sum_kernel(tile, kept_ref, *refs):
    total = kept_ref[...]
    for ref in refs[:-1]:
        total = total + ref[tile:, :].astype(F32)
    refs[-1][...] = total.astype(BF16)


def total_kernel(layers, *refs):
    for layer in range(layers):
        mine_ref, far_ref = refs[2 * layer : 2 * layer + 2]
        total = mine_ref[...].astype(F32) + far_ref[...].astype(F32)
        refs[-1][layer] = total.astype(BF16)


def exit_kernel(c, *refs):
    refs = Refs(refs)
    me_ref, pick_ref, adj_ref, own_ref = refs.take(4)
    got = take_got(refs, c["n"])
    if not c["final"]:
        refs.take()[...] = spread_of(adj_ref, own_ref, got, pick_ref, me_ref[0], c)
        return
    handed = refs.take(c["tick"])
    out_ref, hold_ref, sems = refs.take(3)
    copies = [
        pltpu.make_async_copy(ref, out_ref.at[t, 0], sems.at[t])
        for t, ref in enumerate(handed + [hold_ref])
    ]
    for copy in copies[:-1]:
        copy.start()
    hold_ref[...] = spread_of(adj_ref, own_ref, got, pick_ref, me_ref[0], c)
    copies[-1].start()
    for copy in copies:
        copy.wait()


def finish_kernel(h, me_ref, *refs):
    sums, (out_ref, hold_ref, sems) = refs[:h], refs[h:]
    layers, chunk, _ = sums[0].shape
    place = lax.rem(me_ref[0], h)
    copies = []
    for layer in range(layers):
        for k in range(h):
            start = pl.multiple_of(jnp.bitwise_xor(place, k) * chunk, chunk)
            hold_ref[layer, pl.ds(start, chunk), :] = sums[k][layer].astype(F32)
        copy = pltpu.make_async_copy(hold_ref.at[layer], out_ref.at[0, layer], sems.at[layer])
        copy.start()
        copies.append(copy)
    for copy in copies:
        copy.wait()


def shards(grad_in, grad_last, support, preact, weights, tile_vals, tile_row, tile_col, tile_count):
    section = lax.axis_index("section")
    me = lax.axis_index("rows")
    n = lax.axis_size("rows")
    h = n // 2
    sections = lax.axis_size("section")
    ticks = support.shape[1]
    layers = support.shape[2]
    rows, width = grad_last.shape
    tile = tile_vals.shape[-1]
    row_tiles = rows // tile
    chunk = width // h
    me_arr = me.astype(jnp.int32).reshape(1)
    section_arr = section.astype(jnp.int32).reshape(1)
    counts = tile_count.reshape(1, ticks)

    owner = tile_col[0] // row_tiles
    named = jnp.where(
        owner[:, :, None] == jnp.arange(n)[None, None, :], (tile_col[0] % row_tiles)[:, :, None], 0
    )
    pick = jnp.max(named, axis=1).reshape(1, ticks * n).astype(jnp.int32)
    picks = None

    handed = []
    passed = None
    weight_acc = [None] * layers
    weight_sums = []
    initial = []
    base = dict(n=n, tile=tile, width=width, layers=layers, sections=sections, chunk=chunk)
    layer_cost = cost(2 * rows * width * (width + (n + 1) * tile), (6 + 2 * n) * rows * width)
    small_cost = cost(rows * width, 2 * n * rows * width)
    relay_cost = cost(rows * width, 8 * n * rows * width)
    densify_tick = functools.partial(
        densify, me=me_arr, rows=tile_row, cols=tile_col, count=counts, vals=tile_vals,
        row_tiles=row_tiles, n=n,
    )
    adj_next = densify_tick(0)
    for tick in range(ticks):
        final = tick == ticks - 1
        if tick > 0:
            passed = passed_along(handed[-1], "section", -1)
        adj = adj_next
        image = got = whole = None
        toward = 0.0
        for layer in reversed(range(layers)):
            entry = layer == layers - 1
            beta = jnp.log(BETA_SCALE / (layers * section + layer + 1).astype(F32) + 1.0)
            c = dict(
                base, layer=layer, tick=tick, entry=entry, final=final, whole=whole
            )
            if tick == 0 and entry:
                masked = jnp.where(
                    preact[0, tick, layer] > 0, grad_in[0], jnp.zeros_like(grad_in[0])
                )
                product = jnp.dot(masked, weights[0, layer].T, preferred_element_type=F32)
                image = ((1.0 - beta) * masked.astype(F32) + beta * product).astype(BF16)
                far = swapped(image, h)
                near = [swapped(image, k) for k in range(1, h)]
                got = [far, *near, *(swapped(far, k) for k in range(1, h))]
                pick, _ = lax.optimization_barrier((pick, far))
                picks = [pick] + [swapped(pick, k) for k in range(1, h)]
            else:
                call = Call()
                call.give(SMEM, me_arr, section_arr)
                call.give(HBM, preact, weights)
                call.give(SMEM, *picks)
                if entry:
                    call.give(VMEM, grad_last, passed)
                else:
                    call.give(VMEM, adj, image, *got)
                if final:
                    call.give(HBM, support)
                    call.give(VMEM, weight_acc[layer])
                message = tile + (chunk if final else 0)
                call.want(VMEM, (rows, width), BF16)
                call.want(VMEM, (message, width), BF16, h - 1)
                if final:
                    call.want(VMEM, (chunk, width), F32)
                else:
                    call.want(VMEM, (rows, width), BF16)
                call.scratch = [
                    pltpu.VMEM((rows, width), BF16),
                    pltpu.VMEM((width, width), BF16),
                    pltpu.SemaphoreType.DMA((3,)),
                ]
                if final:
                    call.scratch.append(pltpu.VMEM((rows, width), BF16))
                    call.scratch.append(pltpu.VMEM((width, width), F32))
                results = Refs(
                    call.run(
                        functools.partial(layer_kernel, c), "entry" if entry else "middle", layer_cost
                    )
                )
                image = results.take()
                sends = results.take(h - 1)
                kept = masked = results.take()
                far = swapped(image, h)
                near = [swapped(send, k) for k, send in enumerate(sends, 1)]
                if layer == 0 and not final:
                    adj_next = densify_tick(tick + 1)
                    far, adj_next = lax.optimization_barrier((far, adj_next))
                call = Call()
                call.give(SMEM, me_arr)
                call.give(VMEM, far)
                call.give(SMEM, *picks[1:])
                call.want(VMEM, (tile, width), BF16, h - 1)
                relays = call.run(functools.partial(relay_kernel, c), "relay", relay_cost)
                relayed = [swapped(relay, k) for k, relay in enumerate(relays, 1)]
                if final:
                    kept, *_ = lax.optimization_barrier((kept, *relays))
                    call = Call()
                    call.give(VMEM, kept, *near)
                    call.want(VMEM, (chunk, width), BF16)
                    (mine,) = call.run(
                        functools.partial(half_sum_kernel, tile), "half_sum", small_cost
                    )
                    relayed, mine = lax.optimization_barrier((relayed, mine))
                    weight_sums = [mine, swapped(mine, h), *weight_sums]
                got = [far, *near, *relayed]
            whole = tick == 0 and entry
            toward = toward + ALPHA * image.astype(F32)
            if not final:
                term = beta * jnp.dot(
                    support[0, tick, layer].T, masked, preferred_element_type=F32
                )
                old = weight_acc[layer]
                weight_acc[layer] = term if old is None else old + term
        initial.append(toward)
        c = dict(base, tick=tick, final=final, whole=whole)
        call = Call()
        call.give(SMEM, me_arr, pick)
        call.give(VMEM, adj, image, *got)
        if final:
            call.give(VMEM, *handed)
            call.want(HBM, (ticks, 1, rows, width), BF16)
            call.scratch = [pltpu.VMEM((rows, width), BF16), pltpu.SemaphoreType.DMA((ticks,))]
        else:
            call.want(VMEM, (rows, width), BF16)
        results = call.run(functools.partial(exit_kernel, c), "exit", layer_cost)
        handed.append(results[0])
    weight_sums, got = lax.optimization_barrier((weight_sums, got))
    call = Call()
    call.give(VMEM, *weight_sums)
    call.want(VMEM, (layers, chunk, width), BF16)
    (total,) = call.run(functools.partial(total_kernel, layers), "total", small_cost)
    call = Call()
    call.give(SMEM, me_arr)
    call.give(VMEM, total, *(swapped(total, k) for k in range(1, h)))
    call.want(HBM, (1, layers, width, width), F32)
    call.scratch = [pltpu.VMEM((layers, width, width), F32), pltpu.SemaphoreType.DMA((layers,))]
    (weight_grad,) = call.run(functools.partial(finish_kernel, h), "finish", small_cost)
    return handed[-1], jnp.stack(initial)[None], weight_grad


def solution(mesh):
    return jax.shard_map(
        shards,
        mesh=mesh,
        in_specs=(
            P("section", "rows", None),
            P("rows", None),
            P("section", None, None, "rows", None),
            P("section", None, None, "rows", None),
            P("section", None, None, None),
            P("section", None, "rows", None, None),
            P("section", None, "rows"),
            P("section", None, "rows"),
            P("section", None, "rows"),
        ),
        out_specs=(
            P(None, "section", "rows", None),
            P("section", None, "rows", None),
            P("section", None, None, None),
        ),
        check_vma=False,
    )
```

```python
import functools

import jax
import jax.numpy as jnp
from jax import lax
from jax.experimental import pallas as pl
from jax.experimental.pallas import tpu as pltpu
from jax.sharding import PartitionSpec as P

ALPHA = 0.1
BETA_SCALE = 0.5
VMEM = pl.BlockSpec(memory_space=pltpu.VMEM)
SMEM = pl.BlockSpec(memory_space=pltpu.SMEM)
HBM = pl.BlockSpec(memory_space=pltpu.HBM)
PARAMS = pltpu.CompilerParams(vmem_limit_bytes=24 * 2**20)
F32 = jnp.float32
BF16 = jnp.bfloat16


def cost(flops, nbytes):
    return pl.CostEstimate(flops=flops, bytes_accessed=nbytes, transcendentals=0)


def swapped(block, k):
    n = lax.axis_size("rows")
    return lax.ppermute(block, "rows", [(i, i ^ k) for i in range(n)])


def shared(blocks):
    moved = {k: swapped(block, k) for k, block in reversed(list(enumerate(blocks, 1)))}
    return [moved[k] for k in sorted(moved)]


def passed_along(block, axis, distance):
    devices = range(lax.axis_size(axis))
    route = [(i - distance, i) for i in devices if i - distance in devices]
    return lax.ppermute(block, axis, route)


class Refs:
    def __init__(self, refs):
        self.refs = list(refs)

    def take(self, count=None):
        many = 1 if count is None else count
        taken, self.refs = self.refs[:many], self.refs[many:]
        return taken[0] if count is None else taken


class Call:
    def __init__(self):
        self.operands, self.specs, self.outs, self.out_specs, self.scratch = [], [], [], [], []
        self.aliases = {}

    def give(self, spec, *arrays):
        self.operands += arrays
        self.specs += [spec] * len(arrays)

    def want(self, spec, shape, dtype, count=1):
        self.outs += [jax.ShapeDtypeStruct(shape, dtype)] * count
        self.out_specs += [spec] * count

    def run(self, kernel, name, estimate, params=PARAMS):
        return pl.pallas_call(
            kernel,
            out_shape=self.outs,
            in_specs=self.specs,
            out_specs=self.out_specs,
            scratch_shapes=self.scratch,
            input_output_aliases=self.aliases,
            compiler_params=params,
            cost_estimate=estimate,
            name=name,
        )(*self.operands)


def densify_kernel(tick, row_tiles, n, chunks, *refs):
    me_ref, rows_ref, cols_ref, count_ref, vals_ref, out_ref, vals, acc, sems = refs
    entries, tile = vals.shape[:2]
    chunk = entries // chunks
    me = me_ref[0]
    copies = []
    for c in range(chunks):
        part = pl.ds(c * chunk, chunk)
        copies.append(
            pltpu.make_async_copy(vals_ref.at[0, tick, part], vals.at[part], sems.at[c])
        )
        copies[c].start()
    acc[...] = jnp.zeros_like(acc)

    def add(e, carry):
        owner = lax.div(cols_ref[0, tick, e], row_tiles)
        block = lax.rem(cols_ref[0, tick, e], row_tiles)
        slot = jnp.bitwise_xor(owner, me)
        slot = jnp.where((owner == me) & (block > 0), n - 1 + block, slot)
        rows = pl.ds(pl.multiple_of(rows_ref[0, tick, e] * tile, tile), tile)
        cols = pl.ds(pl.multiple_of(slot * tile, tile), tile)
        acc[rows, cols] += vals[e].astype(F32)
        return carry

    for c in range(chunks):
        copies[c].wait()
        stop = jnp.clip(count_ref[0, tick], c * chunk, (c + 1) * chunk)
        lax.fori_loop(c * chunk, stop, add, 0)
    out_ref[...] = acc[...].astype(BF16)


def densify(tick, me, rows, cols, count, vals, row_tiles, n):
    entries, tile = vals.shape[2:4]
    chunks = 4 if entries % 4 == 0 else 1
    shape = (row_tiles * tile, (n + row_tiles - 1) * tile)
    call = Call()
    call.give(SMEM, me, rows, cols, count)
    call.give(HBM, vals)
    call.want(VMEM, shape, BF16)
    call.scratch = [
        pltpu.VMEM(vals.shape[2:], BF16),
        pltpu.VMEM(shape, F32),
        pltpu.SemaphoreType.DMA((chunks,)),
    ]
    (adj,) = call.run(
        functools.partial(densify_kernel, tick, row_tiles, n, chunks),
        "densify",
        cost(entries * tile * tile * 20, entries * tile * tile * 2),
        pltpu.CompilerParams(vmem_limit_bytes=50 * 2**20),
    )
    return adj


def tile_at(ref, index, tile):
    return ref[pl.ds(pl.multiple_of(index * tile, tile), tile), :]


def take_got(refs, n):
    far, near, relayed = refs.take(), refs.take(n // 2 - 1), refs.take(n // 2 - 1)
    return far, near, relayed


def spread_of(adj_ref, own_ref, got, pick_ref, me, c):
    n, tile = c["n"], c["tile"]
    far, near, relayed = got

    def named(ref, k):
        index = pick_ref[0, c["tick"] * n + jnp.bitwise_xor(me, k)]
        return tile_at(ref, index, tile)

    if c["whole"]:
        near = [named(ref, k) for k, ref in enumerate(near, 1)]
        relayed = [named(ref, n // 2 + k) for k, ref in enumerate(relayed, 1)]
    else:
        near = [ref[:tile, :] for ref in near]
        relayed = [ref[...] for ref in relayed]
    blocks = jnp.concatenate(
        [own_ref[:tile, :]] + near + [named(far, n // 2)] + relayed + [own_ref[tile:, :]], axis=0
    )
    total = jnp.dot(adj_ref[...], blocks, preferred_element_type=F32)
    return ((1.0 - ALPHA) * total).astype(BF16)


def layer_kernel(c, *refs):
    refs = Refs(refs)
    n, tile, width, chunk = c["n"], c["tile"], c["width"], c["chunk"]
    h = n // 2
    me_ref, section_ref, preact_all, weight_all = refs.take(4)
    picks = refs.take(h)
    if c["entry"]:
        last_ref, passed_ref = refs.take(2)
    else:
        adj_ref, own_ref = refs.take(2)
        got = take_got(refs, n)
    if c["final"]:
        support_all, acc_ref = refs.take(2)
    image_ref = refs.take()
    sends = refs.take(h - 1)
    out_ref = refs.take()
    preact_ref, weight_ref, load_sems = refs.take(3)

    me = me_ref[0]
    section = section_ref[0]
    loads = [
        (preact_all.at[0, c["tick"], c["layer"]], preact_ref),
        (weight_all.at[0, c["layer"]], weight_ref),
    ]
    if c["final"]:
        support_ref, term_ref = refs.take(2)
        loads.append((support_all.at[0, c["tick"], c["layer"]], support_ref))
    loads = [pltpu.make_async_copy(a, b, load_sems.at[i]) for i, (a, b) in enumerate(loads)]
    for load in loads:
        load.start()
    step = (c["layers"] * section + c["layer"] + 1).astype(F32)
    beta = jnp.log(BETA_SCALE / jnp.full((1, width), step, F32) + 1.0)
    if not c["entry"]:
        grad = spread_of(adj_ref, own_ref, got, picks[0], me, c)
    for load in loads:
        load.wait()
    if c["entry"]:
        grad = jnp.where(section == c["sections"] - 1, last_ref[...], passed_ref[...])

    masked = jnp.where(preact_ref[...] > 0, grad, jnp.zeros_like(grad))
    product = lax.dot_general(
        masked, weight_ref[...], (((1,), (1,)), ((), ())), preferred_element_type=F32
    )
    image = ((1.0 - beta) * masked.astype(F32) + beta * product).astype(BF16)
    image_ref[...] = image
    for k in range(1, h):
        sends[k - 1][:tile, :] = tile_at(image_ref, picks[k][0, c["tick"] * n + me], tile)
    if c["final"]:
        term = lax.dot_general(
            support_ref[...], masked, (((0,), (0,)), ((), ())), preferred_element_type=F32
        )
        term_ref[...] = acc_ref[...] + beta * term
        place = lax.rem(me, h)
        for k in range(1, h):
            sends[k - 1][tile : tile + chunk, :] = tile_at(
                term_ref, jnp.bitwise_xor(place, k), chunk
            ).astype(BF16)
        out_ref[...] = tile_at(term_ref, place, chunk)
    else:
        out_ref[...] = masked


def relay_kernel(c, *refs):
    refs = Refs(refs)
    n, tile = c["n"], c["tile"]
    h = n // 2
    me_ref, far_ref = refs.take(2)
    picks = refs.take(h - 1)
    sends = refs.take(h - 1)
    me = me_ref[0]
    for k in range(1, h):
        index = picks[k - 1][0, c["tick"] * n + jnp.bitwise_xor(me, h)]
        sends[k - 1][...] = tile_at(far_ref, index, tile)


def half_sum_kernel(tile, kept_ref, *refs):
    total = kept_ref[...]
    for ref in refs[:-1]:
        total = total + ref[tile:, :].astype(F32)
    refs[-1][...] = total.astype(BF16)


def total_kernel(layers, *refs):
    for layer in range(layers):
        mine_ref, far_ref = refs[2 * layer : 2 * layer + 2]
        total = mine_ref[...].astype(F32) + far_ref[...].astype(F32)
        refs[-1][layer] = total.astype(BF16)


def exit_kernel(c, *refs):
    refs = Refs(refs)
    me_ref, pick_ref, adj_ref, own_ref = refs.take(4)
    got = take_got(refs, c["n"])
    if not c["final"]:
        refs.take()[...] = spread_of(adj_ref, own_ref, got, pick_ref, me_ref[0], c)
        return
    handed = refs.take(c["tick"])
    out_ref, hold_ref, sems = refs.take(3)
    copies = [
        pltpu.make_async_copy(ref, out_ref.at[t, 0], sems.at[t])
        for t, ref in enumerate(handed + [hold_ref])
    ]
    for copy in copies[:-1]:
        copy.start()
    hold_ref[...] = spread_of(adj_ref, own_ref, got, pick_ref, me_ref[0], c)
    copies[-1].start()
    for copy in copies:
        copy.wait()


def finish_kernel(h, me_ref, *refs):
    sums, (out_ref, hold_ref, sems) = refs[:h], refs[h:]
    layers, chunk, _ = sums[0].shape
    place = lax.rem(me_ref[0], h)
    copies = []
    for layer in range(layers):
        for k in range(h):
            start = pl.multiple_of(jnp.bitwise_xor(place, k) * chunk, chunk)
            hold_ref[layer, pl.ds(start, chunk), :] = sums[k][layer].astype(F32)
        copy = pltpu.make_async_copy(hold_ref.at[layer], out_ref.at[0, layer], sems.at[layer])
        copy.start()
        copies.append(copy)
    for copy in copies:
        copy.wait()


def shards(grad_in, grad_last, support, preact, weights, tile_vals, tile_row, tile_col, tile_count):
    section = lax.axis_index("section")
    me = lax.axis_index("rows")
    n = lax.axis_size("rows")
    h = n // 2
    sections = lax.axis_size("section")
    ticks = support.shape[1]
    layers = support.shape[2]
    rows, width = grad_last.shape
    tile = tile_vals.shape[-1]
    row_tiles = rows // tile
    chunk = width // h
    me_arr = me.astype(jnp.int32).reshape(1)
    section_arr = section.astype(jnp.int32).reshape(1)
    counts = tile_count.reshape(1, ticks)

    handed = []
    passed = None
    weight_acc = [None] * layers
    weight_sums = []
    initial = []
    base = dict(n=n, tile=tile, width=width, layers=layers, sections=sections, chunk=chunk)
    layer_cost = cost(2 * rows * width * (width + (n + 1) * tile), (6 + 2 * n) * rows * width)
    small_cost = cost(rows * width, 2 * n * rows * width)
    relay_cost = cost(rows * width, 8 * n * rows * width)
    for tick in range(ticks):
        final = tick == ticks - 1
        if tick > 0:
            passed = passed_along(handed[-1], "section", -1)
        image = got = whole = None
        toward = 0.0
        for layer in reversed(range(layers)):
            entry = layer == layers - 1
            beta = jnp.log(BETA_SCALE / (layers * section + layer + 1).astype(F32) + 1.0)
            c = dict(
                base, layer=layer, tick=tick, entry=entry, final=final, whole=whole
            )
            if tick == 0 and entry:
                masked = jnp.where(
                    preact[0, tick, layer] > 0, grad_in[0], jnp.zeros_like(grad_in[0])
                )
                product = jnp.dot(masked, weights[0, layer].T, preferred_element_type=F32)
                image = ((1.0 - beta) * masked.astype(F32) + beta * product).astype(BF16)
                far = swapped(image, h)
                near = shared([image] * (h - 1))
                cols, _ = lax.optimization_barrier((tile_col[0], image))
                owner = (cols // row_tiles)[:, :, None] == jnp.arange(n)[None, None, :]
                pick = jnp.max(jnp.where(owner, (cols % row_tiles)[:, :, None], 0), axis=1)
                pick = pick.reshape(1, ticks * n).astype(jnp.int32)
                told = jnp.pad(pick.astype(BF16), ((0, 15), (0, width - ticks * n)))
                build = functools.partial(
                    densify, rows=tile_row, cols=tile_col, count=counts, vals=tile_vals,
                    row_tiles=row_tiles, n=n,
                )
                far, adj = lax.optimization_barrier((far, build(0, me_arr)))
                later, *_ = lax.optimization_barrier((me_arr, *near))
                adjs = [adj] + [build(t, later) for t in range(1, ticks)]
                adjs = lax.optimization_barrier(adjs)
                relayed = shared([jnp.concatenate([far, told], axis=0)] * (h - 1))
                picks = [pick] + [
                    block[rows : rows + 1, : ticks * n].astype(jnp.int32) for block in relayed
                ]
                got = [far, *near, *relayed]
            else:
                call = Call()
                call.give(SMEM, me_arr, section_arr)
                call.give(HBM, preact, weights)
                call.give(SMEM, *picks)
                if entry:
                    call.give(VMEM, grad_last, passed)
                else:
                    call.give(VMEM, adjs[tick], image, *got)
                if final:
                    call.give(HBM, support)
                    call.give(VMEM, weight_acc[layer])
                message = tile + (chunk if final else 0)
                call.want(VMEM, (rows, width), BF16)
                call.want(VMEM, (message, width), BF16, h - 1)
                if final:
                    call.want(VMEM, (chunk, width), F32)
                else:
                    call.want(VMEM, (rows, width), BF16)
                call.scratch = [
                    pltpu.VMEM((rows, width), BF16),
                    pltpu.VMEM((width, width), BF16),
                    pltpu.SemaphoreType.DMA((3,)),
                ]
                if final:
                    call.scratch.append(pltpu.VMEM((rows, width), BF16))
                    call.scratch.append(pltpu.VMEM((width, width), F32))
                results = Refs(
                    call.run(
                        functools.partial(layer_kernel, c), "entry" if entry else "middle", layer_cost
                    )
                )
                image = results.take()
                sends = results.take(h - 1)
                kept = masked = results.take()
                far = swapped(image, h)
                near = shared(sends)
                call = Call()
                call.give(SMEM, me_arr)
                call.give(VMEM, far)
                call.give(SMEM, *picks[1:])
                call.want(VMEM, (tile, width), BF16, h - 1)
                relays = call.run(functools.partial(relay_kernel, c), "relay", relay_cost)
                relayed = shared(relays)
                if final:
                    kept, *_ = lax.optimization_barrier((kept, *relays))
                    call = Call()
                    call.give(VMEM, kept, *near)
                    call.want(VMEM, (chunk, width), BF16)
                    (mine,) = call.run(
                        functools.partial(half_sum_kernel, tile), "half_sum", small_cost
                    )
                    if layer == 0:
                        weight_sums = [mine, swapped(mine, h), *weight_sums]
                        relayed, weight_sums = lax.optimization_barrier((relayed, weight_sums))
                    else:
                        relayed, mine = lax.optimization_barrier((relayed, mine))
                        weight_sums = [mine, swapped(mine, h), *weight_sums]
                got = [far, *near, *relayed]
            whole = tick == 0 and entry
            toward = toward + ALPHA * image.astype(F32)
            if not final:
                term = beta * jnp.dot(
                    support[0, tick, layer].T, masked, preferred_element_type=F32
                )
                old = weight_acc[layer]
                weight_acc[layer] = term if old is None else old + term
        initial.append(toward)
        c = dict(base, tick=tick, final=final, whole=whole)
        call = Call()
        call.give(SMEM, me_arr, pick)
        call.give(VMEM, adjs[tick], image, *got)
        if final:
            call.give(VMEM, *handed)
            call.want(HBM, (ticks, 1, rows, width), BF16)
            call.scratch = [pltpu.VMEM((rows, width), BF16), pltpu.SemaphoreType.DMA((ticks,))]
        else:
            call.want(VMEM, (rows, width), BF16)
        results = call.run(functools.partial(exit_kernel, c), "exit", layer_cost)
        handed.append(results[0])
    call = Call()
    call.give(VMEM, *weight_sums)
    call.want(VMEM, (layers, chunk, width), BF16)
    (total,) = call.run(functools.partial(total_kernel, layers), "total", small_cost)
    call = Call()
    call.give(SMEM, me_arr)
    call.give(VMEM, total, *shared([total] * (h - 1)))
    call.want(HBM, (1, layers, width, width), F32)
    call.scratch = [pltpu.VMEM((layers, width, width), F32), pltpu.SemaphoreType.DMA((layers,))]
    (weight_grad,) = call.run(functools.partial(finish_kernel, h), "finish", small_cost)
    return handed[-1], jnp.stack(initial)[None], weight_grad


def solution(mesh):
    return jax.shard_map(
        shards,
        mesh=mesh,
        in_specs=(
            P("section", "rows", None),
            P("rows", None),
            P("section", None, None, "rows", None),
            P("section", None, None, "rows", None),
            P("section", None, None, None),
            P("section", None, "rows", None, None),
            P("section", None, "rows"),
            P("section", None, "rows"),
            P("section", None, "rows"),
        ),
        out_specs=(
            P(None, "section", "rows", None),
            P("section", None, "rows", None),
            P("section", None, None, None),
        ),
        check_vma=False,
    )
```

```python
import functools

import jax
import jax.numpy as jnp
from jax import lax
from jax.experimental import pallas as pl
from jax.experimental.pallas import tpu as pltpu
from jax.sharding import PartitionSpec as P

ALPHA = 0.1
BETA_SCALE = 0.5
VMEM = pl.BlockSpec(memory_space=pltpu.VMEM)
SMEM = pl.BlockSpec(memory_space=pltpu.SMEM)
HBM = pl.BlockSpec(memory_space=pltpu.HBM)
PARAMS = pltpu.CompilerParams(vmem_limit_bytes=24 * 2**20)
F32 = jnp.float32
BF16 = jnp.bfloat16


def cost(flops, nbytes):
    return pl.CostEstimate(flops=flops, bytes_accessed=nbytes, transcendentals=0)


def swapped(block, k):
    n = lax.axis_size("rows")
    return lax.ppermute(block, "rows", [(i, i ^ k) for i in range(n)])


def shared(blocks):
    moved = {k: swapped(block, k) for k, block in reversed(list(enumerate(blocks, 1)))}
    return [moved[k] for k in sorted(moved)]


def passed_along(block, axis, distance):
    devices = range(lax.axis_size(axis))
    route = [(i - distance, i) for i in devices if i - distance in devices]
    return lax.ppermute(block, axis, route)


class Refs:
    def __init__(self, refs):
        self.refs = list(refs)

    def take(self, count=None):
        many = 1 if count is None else count
        taken, self.refs = self.refs[:many], self.refs[many:]
        return taken[0] if count is None else taken


class Call:
    def __init__(self):
        self.operands, self.specs, self.outs, self.out_specs, self.scratch = [], [], [], [], []
        self.aliases = {}

    def give(self, spec, *arrays):
        self.operands += arrays
        self.specs += [spec] * len(arrays)

    def want(self, spec, shape, dtype, count=1):
        self.outs += [jax.ShapeDtypeStruct(shape, dtype)] * count
        self.out_specs += [spec] * count

    def run(self, kernel, name, estimate, params=PARAMS):
        return pl.pallas_call(
            kernel,
            out_shape=self.outs,
            in_specs=self.specs,
            out_specs=self.out_specs,
            scratch_shapes=self.scratch,
            input_output_aliases=self.aliases,
            compiler_params=params,
            cost_estimate=estimate,
            name=name,
        )(*self.operands)


def densify_kernel(tick, row_tiles, n, chunks, *refs):
    rows_ref, cols_ref, count_ref, vals_ref, out_ref, vals, acc, sems = refs
    entries, tile = vals.shape[:2]
    chunk = entries // chunks
    me = lax.axis_index("rows")
    copies = []
    for c in range(chunks):
        part = pl.ds(c * chunk, chunk)
        copies.append(
            pltpu.make_async_copy(vals_ref.at[0, tick, part], vals.at[part], sems.at[c])
        )
        copies[c].start()
    acc[...] = jnp.zeros_like(acc)

    def add(e, carry):
        owner = lax.div(cols_ref[0, tick, e], row_tiles)
        block = lax.rem(cols_ref[0, tick, e], row_tiles)
        slot = jnp.bitwise_xor(owner, me)
        slot = jnp.where((owner == me) & (block > 0), n - 1 + block, slot)
        rows = pl.ds(pl.multiple_of(rows_ref[0, tick, e] * tile, tile), tile)
        cols = pl.ds(pl.multiple_of(slot * tile, tile), tile)
        acc[rows, cols] += vals[e].astype(F32)
        return carry

    for c in range(chunks):
        copies[c].wait()
        stop = jnp.clip(count_ref[0, tick], c * chunk, (c + 1) * chunk)
        lax.fori_loop(c * chunk, stop, add, 0)
    out_ref[...] = acc[...].astype(BF16)


def densify(tick, rows, cols, count, vals, row_tiles, n):
    entries, tile = vals.shape[2:4]
    chunks = 4 if entries % 4 == 0 else 1
    shape = (row_tiles * tile, (n + row_tiles - 1) * tile)
    call = Call()
    call.give(SMEM, rows, cols, count)
    call.give(HBM, vals)
    call.want(VMEM, shape, BF16)
    call.scratch = [
        pltpu.VMEM(vals.shape[2:], BF16),
        pltpu.VMEM(shape, F32),
        pltpu.SemaphoreType.DMA((chunks,)),
    ]
    (adj,) = call.run(
        functools.partial(densify_kernel, tick, row_tiles, n, chunks),
        "densify",
        cost(entries * tile * tile * 20, entries * tile * tile * 2),
        pltpu.CompilerParams(vmem_limit_bytes=50 * 2**20),
    )
    return adj


def tile_at(ref, index, tile):
    return ref[pl.ds(pl.multiple_of(index * tile, tile), tile), :]


def name_kernel(n, row_tiles, cols_ref, *out_refs):
    me = lax.axis_index("rows")
    ticks = cols_ref.shape[1]
    width = out_refs[0].shape[1]
    for t in range(ticks):
        cols = cols_ref[0, t : t + 1, :]

        def named(k):
            index = cols - jnp.bitwise_xor(me, k) * row_tiles
            index = jnp.where((index >= 0) & (index < row_tiles), index, 0)
            most = jnp.max(index.astype(F32), axis=1, keepdims=True)
            return jnp.broadcast_to(most, (1, width))

        for k in range(1, n // 2):
            out_refs[k][2 * t : 2 * t + 1, :] = named(k)
            out_refs[k][2 * t + 1 : 2 * t + 2, :] = named(n // 2 + k)
        out_refs[0][t : t + 1, :] = named(n // 2)


def chosen(image_ref, row, rows, tile):
    index = jnp.broadcast_to(row.astype(BF16), (tile, row.shape[1]))
    result = image_ref[:tile, :]
    for i in range(1, rows // tile):
        result = jnp.where(index > i - 0.5, image_ref[i * tile : (i + 1) * tile, :], result)
    return result


def take_got(refs, n):
    return refs.take(), refs.take(n // 2 - 1), refs.take(n // 2 - 1)


def spread_of(adj_ref, own_ref, got, names_ref, c):
    tile, rows = c["tile"], c["rows"]
    far, near, relayed = got
    far = chosen(far, names_ref[c["tick"] : c["tick"] + 1, :], rows, tile)
    near = [ref[:tile, :] for ref in near]
    relayed = [ref[...] for ref in relayed]
    blocks = jnp.concatenate(
        [own_ref[:tile, :]] + near + [far] + relayed + [own_ref[tile:, :]], axis=0
    )
    total = jnp.dot(adj_ref[...], blocks, preferred_element_type=F32)
    return ((1.0 - ALPHA) * total).astype(BF16)


def layer_kernel(c, *refs):
    refs = Refs(refs)
    n, tile, width, chunk = c["n"], c["tile"], c["width"], c["chunk"]
    h = n // 2
    preact_all, weight_all, names_ref = refs.take(3)
    asked = refs.take(h - 1)
    if c["entry"]:
        last_ref, passed_ref = refs.take(2)
    else:
        adj_ref, own_ref = refs.take(2)
        got = take_got(refs, n)
    if c["final"]:
        support_all, acc_ref = refs.take(2)
    image_ref = refs.take()
    sends = refs.take(h - 1)
    out_ref = refs.take()
    preact_ref, weight_ref, load_sems = refs.take(3)

    section = lax.axis_index("section")
    loads = [
        (preact_all.at[0, c["tick"], c["layer"]], preact_ref),
        (weight_all.at[0, c["layer"]], weight_ref),
    ]
    if c["final"]:
        support_ref, term_ref = refs.take(2)
        loads.append((support_all.at[0, c["tick"], c["layer"]], support_ref))
    loads = [pltpu.make_async_copy(a, b, load_sems.at[i]) for i, (a, b) in enumerate(loads)]
    for load in loads:
        load.start()
    step = (c["layers"] * section + c["layer"] + 1).astype(F32)
    beta = jnp.log(BETA_SCALE / jnp.full((1, width), step, F32) + 1.0)
    if not c["entry"]:
        grad = spread_of(adj_ref, own_ref, got, names_ref, c)
    for load in loads:
        load.wait()
    if c["entry"]:
        grad = jnp.where(section == c["sections"] - 1, last_ref[...], passed_ref[...])

    masked = jnp.where(preact_ref[...] > 0, grad, jnp.zeros_like(grad))
    product = lax.dot_general(
        masked, weight_ref[...], (((1,), (1,)), ((), ())), preferred_element_type=F32
    )
    image = ((1.0 - beta) * masked.astype(F32) + beta * product).astype(BF16)
    image_ref[...] = image
    for send, asked_ref in zip(sends, asked):
        row = asked_ref[2 * c["tick"] : 2 * c["tick"] + 1, :]
        send[:tile, :] = chosen(image_ref, row, c["rows"], tile)
    if c["final"]:
        term = lax.dot_general(
            support_ref[...], masked, (((0,), (0,)), ((), ())), preferred_element_type=F32
        )
        term_ref[...] = acc_ref[...] + beta * term
        place = lax.rem(lax.axis_index("rows"), h)
        for k in range(1, h):
            sends[k - 1][tile : tile + chunk, :] = tile_at(
                term_ref, jnp.bitwise_xor(place, k), chunk
            ).astype(BF16)
        out_ref[...] = tile_at(term_ref, place, chunk)
    else:
        out_ref[...] = masked


def select_kernel(c, first, image_ref, *refs):
    count = c["n"] // 2 - 1
    for asked_ref, send in zip(refs[:count], refs[count:]):
        row = 2 * c["tick"] + first
        send[...] = chosen(image_ref, asked_ref[row : row + 1, :], c["rows"], c["tile"])


def half_sum_kernel(tile, kept_ref, *refs):
    total = kept_ref[...]
    for ref in refs[:-1]:
        total = total + ref[tile:, :].astype(F32)
    refs[-1][...] = total.astype(BF16)


def total_kernel(layers, *refs):
    for layer in range(layers):
        mine_ref, far_ref = refs[2 * layer : 2 * layer + 2]
        total = mine_ref[...].astype(F32) + far_ref[...].astype(F32)
        refs[-1][layer] = total.astype(BF16)


def exit_kernel(c, *refs):
    refs = Refs(refs)
    names_ref, adj_ref, own_ref = refs.take(3)
    got = take_got(refs, c["n"])
    if not c["final"]:
        refs.take()[...] = spread_of(adj_ref, own_ref, got, names_ref, c)
        return
    handed = refs.take(c["tick"])
    out_ref, hold_ref, sems = refs.take(3)
    copies = [
        pltpu.make_async_copy(ref, out_ref.at[t, 0], sems.at[t])
        for t, ref in enumerate(handed + [hold_ref])
    ]
    for copy in copies[:-1]:
        copy.start()
    hold_ref[...] = spread_of(adj_ref, own_ref, got, names_ref, c)
    copies[-1].start()
    for copy in copies:
        copy.wait()


def finish_kernel(h, *refs):
    sums, (out_ref, hold_ref, sems) = refs[:h], refs[h:]
    layers, chunk, _ = sums[0].shape
    place = lax.rem(lax.axis_index("rows"), h)
    copies = []
    for layer in range(layers):
        for k in range(h):
            start = pl.multiple_of(jnp.bitwise_xor(place, k) * chunk, chunk)
            hold_ref[layer, pl.ds(start, chunk), :] = sums[k][layer].astype(F32)
        copy = pltpu.make_async_copy(hold_ref.at[layer], out_ref.at[0, layer], sems.at[layer])
        copy.start()
        copies.append(copy)
    for copy in copies:
        copy.wait()


def shards(grad_in, grad_last, support, preact, weights, tile_vals, tile_row, tile_col, tile_count):
    section = lax.axis_index("section")
    n = lax.axis_size("rows")
    h = n // 2
    sections = lax.axis_size("section")
    ticks = support.shape[1]
    layers = support.shape[2]
    rows, width = grad_last.shape
    tile = tile_vals.shape[-1]
    row_tiles = rows // tile
    chunk = width // h
    counts = tile_count.reshape(1, ticks)

    handed = []
    passed = None
    weight_acc = [None] * layers
    weight_sums = []
    initial = []
    base = dict(n=n, tile=tile, rows=rows, width=width, layers=layers, sections=sections, chunk=chunk)
    layer_cost = cost(2 * rows * width * (width + (n + 1) * tile), (6 + 2 * n) * rows * width)
    small_cost = cost(rows * width, 2 * n * rows * width)
    relay_cost = cost(rows * width, 8 * n * rows * width)
    call = Call()
    call.give(VMEM, tile_col)
    call.want(VMEM, (ticks, width), F32)
    call.want(VMEM, (2 * ticks, width), F32, h - 1)
    names, *asking = call.run(functools.partial(name_kernel, n, row_tiles), "name", small_cost)
    asked = shared(asking)

    def select(c, first, block):
        call = Call()
        call.give(VMEM, block, *asked)
        call.want(VMEM, (tile, width), BF16, h - 1)
        return call.run(functools.partial(select_kernel, c, first), "select", small_cost)

    adjs = [None] * ticks
    for tick in range(ticks):
        final = tick == ticks - 1
        if tick > 0:
            passed = passed_along(handed[-1], "section", -1)
        image = got = None
        toward = 0.0
        for layer in reversed(range(layers)):
            entry = layer == layers - 1
            beta = jnp.log(BETA_SCALE / (layers * section + layer + 1).astype(F32) + 1.0)
            c = dict(
                base, layer=layer, tick=tick, entry=entry, final=final
            )
            first = tick == 0 and entry
            if first:
                grad, *_ = lax.optimization_barrier((grad_in[0], *asking))
                masked = jnp.where(preact[0, tick, layer] > 0, grad, jnp.zeros_like(grad))
                product = jnp.dot(masked, weights[0, layer].T, preferred_element_type=F32)
                image = ((1.0 - beta) * masked.astype(F32) + beta * product).astype(BF16)
                sends = select(c, 0, image)
            else:
                call = Call()
                call.give(HBM, preact, weights)
                call.give(VMEM, names, *asked)
                if entry:
                    call.give(VMEM, grad_last, passed)
                else:
                    call.give(VMEM, adjs[tick], image, *got)
                if final:
                    call.give(HBM, support)
                    call.give(VMEM, weight_acc[layer])
                message = tile + (chunk if final else 0)
                call.want(VMEM, (rows, width), BF16)
                call.want(VMEM, (message, width), BF16, h - 1)
                if final:
                    call.want(VMEM, (chunk, width), F32)
                else:
                    call.want(VMEM, (rows, width), BF16)
                call.scratch = [
                    pltpu.VMEM((rows, width), BF16),
                    pltpu.VMEM((width, width), BF16),
                    pltpu.SemaphoreType.DMA((3,)),
                ]
                if final:
                    call.scratch.append(pltpu.VMEM((rows, width), BF16))
                    call.scratch.append(pltpu.VMEM((width, width), F32))
                results = Refs(
                    call.run(
                        functools.partial(layer_kernel, c), "entry" if entry else "middle", layer_cost
                    )
                )
                image = results.take()
                sends = results.take(h - 1)
                kept = masked = results.take()
            far = swapped(image, h)
            near = shared(sends)
            if first:
                far, adjs[0] = lax.optimization_barrier((far, densify(0, tile_row, tile_col, counts, tile_vals, row_tiles, n)))
            relays = select(c, 1, far)
            relayed = shared(relays)
            if first:
                cols, *_ = lax.optimization_barrier((tile_col, *near))
                adjs[1:] = [
                    densify(t, tile_row, cols, counts, tile_vals, row_tiles, n)
                    for t in range(1, ticks)
                ]
                adjs = list(lax.optimization_barrier(adjs))
            if final:
                kept, *_ = lax.optimization_barrier((kept, *relays))
                call = Call()
                call.give(VMEM, kept, *near)
                call.want(VMEM, (chunk, width), BF16)
                (mine,) = call.run(
                    functools.partial(half_sum_kernel, tile), "half_sum", small_cost
                )
                if layer == 0:
                    weight_sums = [mine, swapped(mine, h), *weight_sums]
                    relayed, weight_sums = lax.optimization_barrier((relayed, weight_sums))
                else:
                    relayed, mine = lax.optimization_barrier((relayed, mine))
                    weight_sums = [mine, swapped(mine, h), *weight_sums]
            got = [far, *near, *relayed]
            toward = toward + ALPHA * image.astype(F32)
            if not final:
                term = beta * jnp.dot(
                    support[0, tick, layer].T, masked, preferred_element_type=F32
                )
                old = weight_acc[layer]
                weight_acc[layer] = term if old is None else old + term
        initial.append(toward)
        c = dict(base, tick=tick, final=final)
        call = Call()
        call.give(VMEM, names, adjs[tick], image, *got)
        if final:
            call.give(VMEM, *handed)
            call.want(HBM, (ticks, 1, rows, width), BF16)
            call.scratch = [pltpu.VMEM((rows, width), BF16), pltpu.SemaphoreType.DMA((ticks,))]
        else:
            call.want(VMEM, (rows, width), BF16)
        results = call.run(functools.partial(exit_kernel, c), "exit", layer_cost)
        handed.append(results[0])
    call = Call()
    call.give(VMEM, *weight_sums)
    call.want(VMEM, (layers, chunk, width), BF16)
    (total,) = call.run(functools.partial(total_kernel, layers), "total", small_cost)
    call = Call()
    call.give(VMEM, total, *shared([total] * (h - 1)))
    call.want(HBM, (1, layers, width, width), F32)
    call.scratch = [pltpu.VMEM((layers, width, width), F32), pltpu.SemaphoreType.DMA((layers,))]
    (weight_grad,) = call.run(functools.partial(finish_kernel, h), "finish", small_cost)
    return handed[-1], jnp.stack(initial)[None], weight_grad


def solution(mesh):
    return jax.shard_map(
        shards,
        mesh=mesh,
        in_specs=(
            P("section", "rows", None),
            P("rows", None),
            P("section", None, None, "rows", None),
            P("section", None, None, "rows", None),
            P("section", None, None, None),
            P("section", None, "rows", None, None),
            P("section", None, "rows"),
            P("section", None, "rows"),
            P("section", None, "rows"),
        ),
        out_specs=(
            P(None, "section", "rows", None),
            P("section", None, "rows", None),
            P("section", None, None, None),
        ),
        check_vma=False,
    )
```

```python
import functools

import jax
import jax.numpy as jnp
from jax import lax
from jax.experimental import pallas as pl
from jax.experimental.pallas import tpu as pltpu
from jax.sharding import PartitionSpec as P

ALPHA = 0.1
BETA_SCALE = 0.5
VMEM = pl.BlockSpec(memory_space=pltpu.VMEM)
SMEM = pl.BlockSpec(memory_space=pltpu.SMEM)
HBM = pl.BlockSpec(memory_space=pltpu.HBM)
PARAMS = pltpu.CompilerParams(vmem_limit_bytes=24 * 2**20)
F32 = jnp.float32
BF16 = jnp.bfloat16


def cost(flops, nbytes):
    return pl.CostEstimate(flops=flops, bytes_accessed=nbytes, transcendentals=0)


def swapped(block, k):
    n = lax.axis_size("rows")
    return lax.ppermute(block, "rows", [(i, i ^ k) for i in range(n)])


def shared(blocks):
    moved = {k: swapped(block, k) for k, block in reversed(list(enumerate(blocks, 1)))}
    return [moved[k] for k in sorted(moved)]


def passed_along(block, axis, distance):
    devices = range(lax.axis_size(axis))
    route = [(i - distance, i) for i in devices if i - distance in devices]
    return lax.ppermute(block, axis, route)


class Refs:
    def __init__(self, refs):
        self.refs = list(refs)

    def take(self, count=None):
        many = 1 if count is None else count
        taken, self.refs = self.refs[:many], self.refs[many:]
        return taken[0] if count is None else taken


class Call:
    def __init__(self):
        self.operands, self.specs, self.outs, self.out_specs, self.scratch = [], [], [], [], []
        self.aliases = {}

    def give(self, spec, *arrays):
        self.operands += arrays
        self.specs += [spec] * len(arrays)

    def want(self, spec, shape, dtype, count=1):
        self.outs += [jax.ShapeDtypeStruct(shape, dtype)] * count
        self.out_specs += [spec] * count

    def run(self, kernel, name, estimate, params=PARAMS):
        return pl.pallas_call(
            kernel,
            out_shape=self.outs,
            in_specs=self.specs,
            out_specs=self.out_specs,
            scratch_shapes=self.scratch,
            input_output_aliases=self.aliases,
            compiler_params=params,
            cost_estimate=estimate,
            name=name,
        )(*self.operands)


def densify_kernel(tick, row_tiles, n, chunks, *refs):
    rows_ref, cols_ref, count_ref, vals_ref, out_ref, vals, acc, sems = refs
    entries, tile = vals.shape[:2]
    chunk = entries // chunks
    me = lax.axis_index("rows")
    copies = []
    for c in range(chunks):
        part = pl.ds(c * chunk, chunk)
        copies.append(
            pltpu.make_async_copy(vals_ref.at[0, tick, part], vals.at[part], sems.at[c])
        )
        copies[c].start()
    acc[...] = jnp.zeros_like(acc)

    def add(e, carry):
        owner = lax.div(cols_ref[0, tick, e], row_tiles)
        block = lax.rem(cols_ref[0, tick, e], row_tiles)
        slot = jnp.bitwise_xor(owner, me)
        slot = jnp.where((owner == me) & (block > 0), n - 1 + block, slot)
        rows = pl.ds(pl.multiple_of(rows_ref[0, tick, e] * tile, tile), tile)
        cols = pl.ds(pl.multiple_of(slot * tile, tile), tile)
        acc[rows, cols] += vals[e].astype(F32)
        return carry

    for c in range(chunks):
        copies[c].wait()
        stop = jnp.clip(count_ref[0, tick], c * chunk, (c + 1) * chunk)
        lax.fori_loop(c * chunk, stop, add, 0)
    out_ref[...] = acc[...].astype(BF16)


def densify(tick, rows, cols, count, vals, row_tiles, n):
    entries, tile = vals.shape[2:4]
    chunks = 4 if entries % 4 == 0 else 1
    shape = (row_tiles * tile, (n + row_tiles - 1) * tile)
    call = Call()
    call.give(SMEM, rows, cols, count)
    call.give(HBM, vals)
    call.want(VMEM, shape, BF16)
    call.scratch = [
        pltpu.VMEM(vals.shape[2:], BF16),
        pltpu.VMEM(shape, F32),
        pltpu.SemaphoreType.DMA((chunks,)),
    ]
    (adj,) = call.run(
        functools.partial(densify_kernel, tick, row_tiles, n, chunks),
        "densify",
        cost(entries * tile * tile * 20, entries * tile * tile * 2),
        pltpu.CompilerParams(vmem_limit_bytes=50 * 2**20),
    )
    return adj


def tile_at(ref, index, tile):
    return ref[pl.ds(pl.multiple_of(index * tile, tile), tile), :]


def name_kernel(n, row_tiles, cols_ref, *out_refs):
    me = lax.axis_index("rows")
    ticks = cols_ref.shape[1]
    width = out_refs[0].shape[1]
    for t in range(ticks):
        cols = cols_ref[0, t : t + 1, :]

        def named(k):
            index = cols - jnp.bitwise_xor(me, k) * row_tiles
            index = jnp.where((index >= 0) & (index < row_tiles), index, 0)
            most = jnp.max(index.astype(F32), axis=1, keepdims=True)
            return jnp.broadcast_to(most, (1, width))

        for k in range(1, n // 2):
            out_refs[k][2 * t : 2 * t + 1, :] = named(k)
            out_refs[k][2 * t + 1 : 2 * t + 2, :] = named(n // 2 + k)
        out_refs[0][t : t + 1, :] = named(n // 2)


def chosen(image_ref, row, rows, tile):
    index = jnp.broadcast_to(row.astype(BF16), (tile, row.shape[1]))
    result = image_ref[:tile, :]
    for i in range(1, rows // tile):
        result = jnp.where(index > i - 0.5, image_ref[i * tile : (i + 1) * tile, :], result)
    return result


def take_got(refs, n):
    return refs.take(), refs.take(n // 2 - 1), refs.take(n // 2 - 1)


def spread_of(adj_ref, own_ref, got, names_ref, c):
    tile, rows = c["tile"], c["rows"]
    far, near, relayed = got
    far = chosen(far, names_ref[c["tick"] : c["tick"] + 1, :], rows, tile)
    near = [ref[:tile, :] for ref in near]
    relayed = [ref[...] for ref in relayed]
    blocks = jnp.concatenate(
        [own_ref[:tile, :]] + near + [far] + relayed + [own_ref[tile:, :]], axis=0
    )
    total = jnp.dot(adj_ref[...], blocks, preferred_element_type=F32)
    return ((1.0 - ALPHA) * total).astype(BF16)


def layer_kernel(c, *refs):
    refs = Refs(refs)
    n, tile, width, chunk = c["n"], c["tile"], c["width"], c["chunk"]
    h = n // 2
    preact_all, weight_all, names_ref = refs.take(3)
    asked = refs.take(h - 1)
    if c["entry"]:
        last_ref, passed_ref = refs.take(2)
    else:
        adj_ref, own_ref = refs.take(2)
        got = take_got(refs, n)
    if c["final"]:
        support_all, acc_ref = refs.take(2)
    image_ref = refs.take()
    sends = refs.take(h - 1)
    out_ref = refs.take()
    preact_ref, weight_ref, load_sems = refs.take(3)

    section = lax.axis_index("section")
    loads = [
        (preact_all.at[0, c["tick"], c["layer"]], preact_ref),
        (weight_all.at[0, c["layer"]], weight_ref),
    ]
    if c["final"]:
        support_ref, term_ref = refs.take(2)
        loads.append((support_all.at[0, c["tick"], c["layer"]], support_ref))
    loads = [pltpu.make_async_copy(a, b, load_sems.at[i]) for i, (a, b) in enumerate(loads)]
    for load in loads:
        load.start()
    step = (c["layers"] * section + c["layer"] + 1).astype(F32)
    beta = jnp.log(BETA_SCALE / jnp.full((1, width), step, F32) + 1.0)
    if not c["entry"]:
        grad = spread_of(adj_ref, own_ref, got, names_ref, c)
    for load in loads:
        load.wait()
    if c["entry"]:
        grad = jnp.where(section == c["sections"] - 1, last_ref[...], passed_ref[...])

    masked = jnp.where(preact_ref[...] > 0, grad, jnp.zeros_like(grad))
    product = lax.dot_general(
        masked, weight_ref[...], (((1,), (1,)), ((), ())), preferred_element_type=F32
    )
    image = ((1.0 - beta) * masked.astype(F32) + beta * product).astype(BF16)
    image_ref[...] = image
    for send, asked_ref in zip(sends, asked):
        row = asked_ref[2 * c["tick"] : 2 * c["tick"] + 1, :]
        send[:tile, :] = chosen(image_ref, row, c["rows"], tile)
    if c["final"]:
        term = lax.dot_general(
            support_ref[...], masked, (((0,), (0,)), ((), ())), preferred_element_type=F32
        )
        term_ref[...] = acc_ref[...] + beta * term
        place = lax.rem(lax.axis_index("rows"), h)
        for k in range(1, h):
            sends[k - 1][tile : tile + chunk, :] = tile_at(
                term_ref, jnp.bitwise_xor(place, k), chunk
            ).astype(BF16)
        out_ref[...] = tile_at(term_ref, place, chunk)
    else:
        out_ref[...] = masked


def select_kernel(c, first, image_ref, *refs):
    count = c["n"] // 2 - 1
    for asked_ref, send in zip(refs[:count], refs[count:]):
        row = 2 * c["tick"] + first
        send[...] = chosen(image_ref, asked_ref[row : row + 1, :], c["rows"], c["tile"])


def half_sum_kernel(tile, kept_ref, *refs):
    total = kept_ref[...]
    for ref in refs[:-1]:
        total = total + ref[tile:, :].astype(F32)
    refs[-1][...] = total.astype(BF16)


def total_kernel(layers, *refs):
    for layer in range(layers):
        mine_ref, far_ref = refs[2 * layer : 2 * layer + 2]
        total = mine_ref[...].astype(F32) + far_ref[...].astype(F32)
        refs[-1][layer] = total.astype(BF16)


def exit_kernel(c, *refs):
    refs = Refs(refs)
    names_ref, adj_ref, own_ref = refs.take(3)
    got = take_got(refs, c["n"])
    if not c["final"]:
        refs.take()[...] = spread_of(adj_ref, own_ref, got, names_ref, c)
        return
    handed = refs.take(c["tick"])
    out_ref, hold_ref, sems = refs.take(3)
    copies = [
        pltpu.make_async_copy(ref, out_ref.at[t, 0], sems.at[t])
        for t, ref in enumerate(handed + [hold_ref])
    ]
    for copy in copies[:-1]:
        copy.start()
    hold_ref[...] = spread_of(adj_ref, own_ref, got, names_ref, c)
    copies[-1].start()
    for copy in copies:
        copy.wait()


def finish_kernel(h, *refs):
    sums, (out_ref, hold_ref, sems) = refs[:h], refs[h:]
    layers, chunk, _ = sums[0].shape
    place = lax.rem(lax.axis_index("rows"), h)
    copies = []
    for layer in range(layers):
        for k in range(h):
            start = pl.multiple_of(jnp.bitwise_xor(place, k) * chunk, chunk)
            hold_ref[layer, pl.ds(start, chunk), :] = sums[k][layer].astype(F32)
        copy = pltpu.make_async_copy(hold_ref.at[layer], out_ref.at[0, layer], sems.at[layer])
        copy.start()
        copies.append(copy)
    for copy in copies:
        copy.wait()


def shards(grad_in, grad_last, support, preact, weights, tile_vals, tile_row, tile_col, tile_count):
    section = lax.axis_index("section")
    n = lax.axis_size("rows")
    h = n // 2
    sections = lax.axis_size("section")
    ticks = support.shape[1]
    layers = support.shape[2]
    rows, width = grad_last.shape
    tile = tile_vals.shape[-1]
    row_tiles = rows // tile
    chunk = width // h
    counts = tile_count.reshape(1, ticks)

    handed = []
    passed = None
    weight_acc = [None] * layers
    weight_sums = []
    initial = []
    base = dict(n=n, tile=tile, rows=rows, width=width, layers=layers, sections=sections, chunk=chunk)
    layer_cost = cost(2 * rows * width * (width + (n + 1) * tile), (6 + 2 * n) * rows * width)
    small_cost = cost(rows * width, 2 * n * rows * width)
    relay_cost = cost(rows * width, 8 * n * rows * width)
    call = Call()
    call.give(VMEM, tile_col)
    call.want(VMEM, (ticks, width), F32)
    call.want(VMEM, (2 * ticks, width), F32, h - 1)
    names, *asking = call.run(functools.partial(name_kernel, n, row_tiles), "name", small_cost)
    asked = shared(asking)

    def select(c, first, block):
        call = Call()
        call.give(VMEM, block, *asked)
        call.want(VMEM, (tile, width), BF16, h - 1)
        return call.run(functools.partial(select_kernel, c, first), "select", small_cost)

    adjs = [None] * ticks
    for tick in range(ticks):
        final = tick == ticks - 1
        if tick > 0:
            passed = passed_along(handed[-1], "section", -1)
        image = got = None
        toward = 0.0
        for layer in reversed(range(layers)):
            entry = layer == layers - 1
            beta = jnp.log(BETA_SCALE / (layers * section + layer + 1).astype(F32) + 1.0)
            c = dict(
                base, layer=layer, tick=tick, entry=entry, final=final
            )
            first = tick == 0 and entry
            if first:
                masked = jnp.where(
                    preact[0, tick, layer] > 0, grad_in[0], jnp.zeros_like(grad_in[0])
                )
                product = jnp.dot(masked, weights[0, layer].T, preferred_element_type=F32)
                image = ((1.0 - beta) * masked.astype(F32) + beta * product).astype(BF16)
                adjs[0] = densify(0, tile_row, tile_col, counts, tile_vals, row_tiles, n)
                ready, adjs[0] = lax.optimization_barrier((image, adjs[0]))
                sends = select(c, 0, ready)
            else:
                call = Call()
                call.give(HBM, preact, weights)
                call.give(VMEM, names, *asked)
                if entry:
                    call.give(VMEM, grad_last, passed)
                else:
                    call.give(VMEM, adjs[tick], image, *got)
                if final:
                    call.give(HBM, support)
                    call.give(VMEM, weight_acc[layer])
                message = tile + (chunk if final else 0)
                call.want(VMEM, (rows, width), BF16)
                call.want(VMEM, (message, width), BF16, h - 1)
                if final:
                    call.want(VMEM, (chunk, width), F32)
                else:
                    call.want(VMEM, (rows, width), BF16)
                call.scratch = [
                    pltpu.VMEM((rows, width), BF16),
                    pltpu.VMEM((width, width), BF16),
                    pltpu.SemaphoreType.DMA((3,)),
                ]
                if final:
                    call.scratch.append(pltpu.VMEM((rows, width), BF16))
                    call.scratch.append(pltpu.VMEM((width, width), F32))
                results = Refs(
                    call.run(
                        functools.partial(layer_kernel, c), "entry" if entry else "middle", layer_cost
                    )
                )
                image = results.take()
                sends = results.take(h - 1)
                kept = masked = results.take()
            far = swapped(image, h)
            near = shared(sends)
            relays = select(c, 1, far)
            relayed = shared(relays)
            if first:
                cols, *_ = lax.optimization_barrier((tile_col, *near))
                adjs[1:] = [
                    densify(t, tile_row, cols, counts, tile_vals, row_tiles, n)
                    for t in range(1, ticks)
                ]
                adjs = list(lax.optimization_barrier(adjs))
            if final:
                kept, *_ = lax.optimization_barrier((kept, *relays))
                call = Call()
                call.give(VMEM, kept, *near)
                call.want(VMEM, (chunk, width), BF16)
                (mine,) = call.run(
                    functools.partial(half_sum_kernel, tile), "half_sum", small_cost
                )
                if layer == 0:
                    weight_sums = [mine, swapped(mine, h), *weight_sums]
                    relayed, weight_sums = lax.optimization_barrier((relayed, weight_sums))
                else:
                    relayed, mine = lax.optimization_barrier((relayed, mine))
                    weight_sums = [mine, swapped(mine, h), *weight_sums]
            got = [far, *near, *relayed]
            toward = toward + ALPHA * image.astype(F32)
            if not final:
                term = beta * jnp.dot(
                    support[0, tick, layer].T, masked, preferred_element_type=F32
                )
                old = weight_acc[layer]
                weight_acc[layer] = term if old is None else old + term
        initial.append(toward)
        c = dict(base, tick=tick, final=final)
        call = Call()
        call.give(VMEM, names, adjs[tick], image, *got)
        if final:
            call.give(VMEM, *handed)
            call.want(HBM, (ticks, 1, rows, width), BF16)
            call.scratch = [pltpu.VMEM((rows, width), BF16), pltpu.SemaphoreType.DMA((ticks,))]
        else:
            call.want(VMEM, (rows, width), BF16)
        results = call.run(functools.partial(exit_kernel, c), "exit", layer_cost)
        handed.append(results[0])
    call = Call()
    call.give(VMEM, *weight_sums)
    call.want(VMEM, (layers, chunk, width), BF16)
    (total,) = call.run(functools.partial(total_kernel, layers), "total", small_cost)
    call = Call()
    call.give(VMEM, total, *shared([total] * (h - 1)))
    call.want(HBM, (1, layers, width, width), F32)
    call.scratch = [pltpu.VMEM((layers, width, width), F32), pltpu.SemaphoreType.DMA((layers,))]
    (weight_grad,) = call.run(functools.partial(finish_kernel, h), "finish", small_cost)
    return handed[-1], jnp.stack(initial)[None], weight_grad


def solution(mesh):
    return jax.shard_map(
        shards,
        mesh=mesh,
        in_specs=(
            P("section", "rows", None),
            P("rows", None),
            P("section", None, None, "rows", None),
            P("section", None, None, "rows", None),
            P("section", None, None, None),
            P("section", None, "rows", None, None),
            P("section", None, "rows"),
            P("section", None, "rows"),
            P("section", None, "rows"),
        ),
        out_specs=(
            P(None, "section", "rows", None),
            P("section", None, "rows", None),
            P("section", None, None, None),
        ),
        check_vma=False,
    )
```

```python
import functools

import jax
import jax.numpy as jnp
from jax import lax
from jax.experimental import pallas as pl
from jax.experimental.pallas import tpu as pltpu
from jax.sharding import PartitionSpec as P

ALPHA = 0.1
BETA_SCALE = 0.5
VMEM = pl.BlockSpec(memory_space=pltpu.VMEM)
SMEM = pl.BlockSpec(memory_space=pltpu.SMEM)
HBM = pl.BlockSpec(memory_space=pltpu.HBM)
PARAMS = pltpu.CompilerParams(vmem_limit_bytes=24 * 2**20)
F32 = jnp.float32
BF16 = jnp.bfloat16


def cost(flops, nbytes):
    return pl.CostEstimate(flops=flops, bytes_accessed=nbytes, transcendentals=0)


def swapped(block, k):
    n = lax.axis_size("rows")
    return lax.ppermute(block, "rows", [(i, i ^ k) for i in range(n)])


def shared(blocks):
    moved = {k: swapped(block, k) for k, block in reversed(list(enumerate(blocks, 1)))}
    return [moved[k] for k in sorted(moved)]


def passed_along(block, axis, distance):
    devices = range(lax.axis_size(axis))
    route = [(i - distance, i) for i in devices if i - distance in devices]
    return lax.ppermute(block, axis, route)


class Refs:
    def __init__(self, refs):
        self.refs = list(refs)

    def take(self, count=None):
        many = 1 if count is None else count
        taken, self.refs = self.refs[:many], self.refs[many:]
        return taken[0] if count is None else taken


class Call:
    def __init__(self):
        self.operands, self.specs, self.outs, self.out_specs, self.scratch = [], [], [], [], []
        self.aliases = {}

    def give(self, spec, *arrays):
        self.operands += arrays
        self.specs += [spec] * len(arrays)

    def want(self, spec, shape, dtype, count=1):
        self.outs += [jax.ShapeDtypeStruct(shape, dtype)] * count
        self.out_specs += [spec] * count

    def run(self, kernel, name, estimate, params=PARAMS):
        return pl.pallas_call(
            kernel,
            out_shape=self.outs,
            in_specs=self.specs,
            out_specs=self.out_specs,
            scratch_shapes=self.scratch,
            input_output_aliases=self.aliases,
            compiler_params=params,
            cost_estimate=estimate,
            name=name,
        )(*self.operands)


def packed(tile_row, tile_col, tile_count, row_tiles):
    owner = jnp.bitwise_xor(tile_col // row_tiles, lax.axis_index("rows"))
    words = (owner * row_tiles + tile_col % row_tiles) * row_tiles + tile_row
    counts = tile_count.reshape(1, -1)
    counts = jnp.pad(counts, ((0, 0), (0, words.shape[2] - counts.shape[1])))
    return jnp.concatenate([words[0], counts], axis=0)


def densify_kernel(tick, row_tiles, n, chunks, words_ref, vals_ref, out_ref, vals, acc, sems):
    entries, tile = vals.shape[:2]
    chunk = entries // chunks
    copies = []
    for c in range(chunks):
        part = pl.ds(c * chunk, chunk)
        copies.append(
            pltpu.make_async_copy(vals_ref.at[0, tick, part], vals.at[part], sems.at[c])
        )
        copies[c].start()
    acc[...] = jnp.zeros_like(acc)

    def add(e, carry):
        word = words_ref[tick, e]
        row = lax.rem(word, row_tiles)
        block = lax.rem(lax.div(word, row_tiles), row_tiles)
        slot = lax.div(word, row_tiles * row_tiles)
        slot = jnp.where((slot == 0) & (block > 0), n - 1 + block, slot)
        rows = pl.ds(pl.multiple_of(row * tile, tile), tile)
        cols = pl.ds(pl.multiple_of(slot * tile, tile), tile)
        acc[rows, cols] += vals[e].astype(F32)
        return carry

    count = words_ref[words_ref.shape[0] - 1, tick]
    for c in range(chunks):
        copies[c].wait()
        stop = jnp.clip(count, c * chunk, (c + 1) * chunk)
        lax.fori_loop(c * chunk, stop, add, 0)
    out_ref[...] = acc[...].astype(BF16)


def densify(tick, words, vals, row_tiles, n):
    entries, tile = vals.shape[2:4]
    chunks = 4 if entries % 4 == 0 else 1
    shape = (row_tiles * tile, (n + row_tiles - 1) * tile)
    call = Call()
    call.give(SMEM, words)
    call.give(HBM, vals)
    call.want(VMEM, shape, BF16)
    call.scratch = [
        pltpu.VMEM(vals.shape[2:], BF16),
        pltpu.VMEM(shape, F32),
        pltpu.SemaphoreType.DMA((chunks,)),
    ]
    (adj,) = call.run(
        functools.partial(densify_kernel, tick, row_tiles, n, chunks),
        "densify",
        cost(entries * tile * tile * 20, entries * tile * tile * 2),
        pltpu.CompilerParams(vmem_limit_bytes=50 * 2**20),
    )
    return adj


def tile_at(ref, index, tile):
    return ref[pl.ds(pl.multiple_of(index * tile, tile), tile), :]


def name_kernel(n, row_tiles, words_ref, *out_refs):
    ticks, width = out_refs[0].shape
    for t in range(ticks):
        index = words_ref[t : t + 1, :] // row_tiles

        def named(k):
            block = index - k * row_tiles
            block = jnp.where((block >= 0) & (block < row_tiles), block, 0)
            most = jnp.max(block.astype(F32), axis=1, keepdims=True)
            return jnp.broadcast_to(most, (1, width))

        for k in range(1, n // 2):
            out_refs[k][2 * t : 2 * t + 1, :] = named(k)
            out_refs[k][2 * t + 1 : 2 * t + 2, :] = named(n // 2 + k)
        out_refs[0][t : t + 1, :] = named(n // 2)


def chosen(image_ref, row, rows, tile):
    index = jnp.broadcast_to(row.astype(BF16), (tile, row.shape[1]))
    result = image_ref[:tile, :]
    for i in range(1, rows // tile):
        result = jnp.where(index > i - 0.5, image_ref[i * tile : (i + 1) * tile, :], result)
    return result


def take_got(refs, c):
    far, near = refs.take(), refs.take(c["n"] // 2 - 1)
    if c["joined"]:
        return far, near, [ref.at[c["tile"] :, :] for ref in near]
    return far, near, refs.take(c["n"] // 2 - 1)


def spread_of(adj_ref, own_ref, got, names_ref, c):
    tile, rows = c["tile"], c["rows"]
    far, near, relayed = got
    far = chosen(far, names_ref[c["tick"] : c["tick"] + 1, :], rows, tile)
    near = [ref[:tile, :] for ref in near]
    relayed = [ref[...] for ref in relayed]
    blocks = jnp.concatenate(
        [own_ref[:tile, :]] + near + [far] + relayed + [own_ref[tile:, :]], axis=0
    )
    total = jnp.dot(adj_ref[...], blocks, preferred_element_type=F32)
    return ((1.0 - ALPHA) * total).astype(BF16)


def layer_kernel(c, *refs):
    refs = Refs(refs)
    n, tile, width, chunk = c["n"], c["tile"], c["width"], c["chunk"]
    h = n // 2
    preact_all, weight_all, names_ref = refs.take(3)
    asked = refs.take(h - 1)
    if c["entry"]:
        last_ref, passed_ref = refs.take(2)
    else:
        adj_ref, own_ref = refs.take(2)
        got = take_got(refs, c)
    if c["final"]:
        support_all, acc_ref = refs.take(2)
    image_ref = refs.take()
    sends = refs.take(h - 1)
    out_ref = refs.take()
    preact_ref, weight_ref, load_sems = refs.take(3)

    section = lax.axis_index("section")
    loads = [
        (preact_all.at[0, c["tick"], c["layer"]], preact_ref),
        (weight_all.at[0, c["layer"]], weight_ref),
    ]
    if c["final"]:
        support_ref, term_ref = refs.take(2)
        loads.append((support_all.at[0, c["tick"], c["layer"]], support_ref))
    loads = [pltpu.make_async_copy(a, b, load_sems.at[i]) for i, (a, b) in enumerate(loads)]
    for load in loads:
        load.start()
    step = (c["layers"] * section + c["layer"] + 1).astype(F32)
    beta = jnp.log(BETA_SCALE / jnp.full((1, width), step, F32) + 1.0)
    if not c["entry"]:
        grad = spread_of(adj_ref, own_ref, got, names_ref, c)
    for load in loads:
        load.wait()
    if c["entry"]:
        grad = jnp.where(section == c["sections"] - 1, last_ref[...], passed_ref[...])

    masked = jnp.where(preact_ref[...] > 0, grad, jnp.zeros_like(grad))
    product = lax.dot_general(
        masked, weight_ref[...], (((1,), (1,)), ((), ())), preferred_element_type=F32
    )
    image = ((1.0 - beta) * masked.astype(F32) + beta * product).astype(BF16)
    image_ref[...] = image
    for send, asked_ref in zip(sends, asked):
        row = asked_ref[2 * c["tick"] : 2 * c["tick"] + 1, :]
        send[:tile, :] = chosen(image_ref, row, c["rows"], tile)
    if c["final"]:
        term = lax.dot_general(
            support_ref[...], masked, (((0,), (0,)), ((), ())), preferred_element_type=F32
        )
        term_ref[...] = acc_ref[...] + beta * term
        place = lax.rem(lax.axis_index("rows"), h)
        for k in range(1, h):
            sends[k - 1][tile : tile + chunk, :] = tile_at(
                term_ref, jnp.bitwise_xor(place, k), chunk
            ).astype(BF16)
        out_ref[...] = tile_at(term_ref, place, chunk)
    else:
        out_ref[...] = masked


def forward_kernel(c, *refs):
    refs = Refs(refs)
    count, tile, rows = c["n"] // 2 - 1, c["tile"], c["rows"]
    far_ref = refs.take()
    own_ref = refs.take() if c["first"] else None
    for asked_ref, send in zip(refs.take(count), refs.take(count)):
        row = 2 * c["tick"]
        if c["first"]:
            send[:tile, :] = chosen(own_ref, asked_ref[row : row + 1, :], rows, tile)
            send[tile:, :] = chosen(far_ref, asked_ref[row + 1 : row + 2, :], rows, tile)
        else:
            send[...] = chosen(far_ref, asked_ref[row + 1 : row + 2, :], rows, tile)


def half_sum_kernel(tile, kept_ref, *refs):
    total = kept_ref[...]
    for ref in refs[:-1]:
        total = total + ref[tile:, :].astype(F32)
    refs[-1][...] = total.astype(BF16)


def total_kernel(layers, *refs):
    for layer in range(layers):
        mine_ref, far_ref = refs[2 * layer : 2 * layer + 2]
        total = mine_ref[...].astype(F32) + far_ref[...].astype(F32)
        refs[-1][layer] = total.astype(BF16)


def exit_kernel(c, *refs):
    refs = Refs(refs)
    names_ref, adj_ref, own_ref = refs.take(3)
    got = take_got(refs, c)
    if not c["final"]:
        refs.take()[...] = spread_of(adj_ref, own_ref, got, names_ref, c)
        return
    handed = refs.take(c["tick"])
    out_ref, hold_ref, sems = refs.take(3)
    copies = [
        pltpu.make_async_copy(ref, out_ref.at[t, 0], sems.at[t])
        for t, ref in enumerate(handed + [hold_ref])
    ]
    for copy in copies[:-1]:
        copy.start()
    hold_ref[...] = spread_of(adj_ref, own_ref, got, names_ref, c)
    copies[-1].start()
    for copy in copies:
        copy.wait()


def finish_kernel(h, *refs):
    sums, (out_ref, hold_ref, sems) = refs[:h], refs[h:]
    layers, chunk, _ = sums[0].shape
    place = lax.rem(lax.axis_index("rows"), h)
    copies = []
    for layer in range(layers):
        for k in range(h):
            start = pl.multiple_of(jnp.bitwise_xor(place, k) * chunk, chunk)
            hold_ref[layer, pl.ds(start, chunk), :] = sums[k][layer].astype(F32)
        copy = pltpu.make_async_copy(hold_ref.at[layer], out_ref.at[0, layer], sems.at[layer])
        copy.start()
        copies.append(copy)
    for copy in copies:
        copy.wait()


def shards(grad_in, grad_last, support, preact, weights, tile_vals, tile_row, tile_col, tile_count):
    section = lax.axis_index("section")
    n = lax.axis_size("rows")
    h = n // 2
    sections = lax.axis_size("section")
    ticks = support.shape[1]
    layers = support.shape[2]
    rows, width = grad_last.shape
    tile = tile_vals.shape[-1]
    row_tiles = rows // tile
    chunk = width // h
    words = packed(tile_row, tile_col, tile_count, row_tiles)

    handed = []
    passed = None
    weight_acc = [None] * layers
    weight_sums = []
    initial = []
    base = dict(n=n, tile=tile, rows=rows, width=width, layers=layers, sections=sections, chunk=chunk)
    layer_cost = cost(2 * rows * width * (width + (n + 1) * tile), (6 + 2 * n) * rows * width)
    small_cost = cost(rows * width, 2 * n * rows * width)
    relay_cost = cost(rows * width, 8 * n * rows * width)
    call = Call()
    call.give(VMEM, words)
    call.want(VMEM, (ticks, width), F32)
    call.want(VMEM, (2 * ticks, width), F32, h - 1)
    names, *asking = call.run(functools.partial(name_kernel, n, row_tiles), "name", small_cost)
    asked = shared(asking)

    adjs = [None] * ticks
    for tick in range(ticks):
        final = tick == ticks - 1
        if tick > 0:
            passed = passed_along(handed[-1], "section", -1)
        image = got = joined = None
        toward = 0.0
        for layer in reversed(range(layers)):
            entry = layer == layers - 1
            beta = jnp.log(BETA_SCALE / (layers * section + layer + 1).astype(F32) + 1.0)
            c = dict(
                base, layer=layer, tick=tick, entry=entry, final=final, joined=joined,
                first=tick == 0 and entry,
            )
            if c["first"]:
                masked = jnp.where(
                    preact[0, tick, layer] > 0, grad_in[0], jnp.zeros_like(grad_in[0])
                )
                product = jnp.dot(masked, weights[0, layer].T, preferred_element_type=F32)
                image = ((1.0 - beta) * masked.astype(F32) + beta * product).astype(BF16)
            else:
                call = Call()
                call.give(HBM, preact, weights)
                call.give(VMEM, names, *asked)
                if entry:
                    call.give(VMEM, grad_last, passed)
                else:
                    call.give(VMEM, adjs[tick], image, *got)
                if final:
                    call.give(HBM, support)
                    call.give(VMEM, weight_acc[layer])
                message = tile + (chunk if final else 0)
                call.want(VMEM, (rows, width), BF16)
                call.want(VMEM, (message, width), BF16, h - 1)
                if final:
                    call.want(VMEM, (chunk, width), F32)
                else:
                    call.want(VMEM, (rows, width), BF16)
                call.scratch = [
                    pltpu.VMEM((rows, width), BF16),
                    pltpu.VMEM((width, width), BF16),
                    pltpu.SemaphoreType.DMA((3,)),
                ]
                if final:
                    call.scratch.append(pltpu.VMEM((rows, width), BF16))
                    call.scratch.append(pltpu.VMEM((width, width), F32))
                results = Refs(
                    call.run(
                        functools.partial(layer_kernel, c), "entry" if entry else "middle", layer_cost
                    )
                )
                image = results.take()
                sends = results.take(h - 1)
                kept = masked = results.take()
            far = swapped(image, h)
            near = [] if c["first"] else shared(sends)
            call = Call()
            call.give(VMEM, far)
            if c["first"]:
                adjs[0] = densify(0, words, tile_vals, row_tiles, n)
                ready, adjs[0] = lax.optimization_barrier((image, adjs[0]))
                call.give(VMEM, ready)
            call.give(VMEM, *asked)
            call.want(VMEM, (tile * (1 + c["first"]), width), BF16, h - 1)
            relays = call.run(functools.partial(forward_kernel, c), "forward", small_cost)
            relayed = shared(relays)
            if layer == 0 and not final:
                later, *_ = lax.optimization_barrier((words, *near))
                adjs[tick + 1] = densify(tick + 1, later, tile_vals, row_tiles, n)
                relayed, adjs[tick + 1] = lax.optimization_barrier((relayed, adjs[tick + 1]))
            if final:
                kept, *_ = lax.optimization_barrier((kept, *relays))
                call = Call()
                call.give(VMEM, kept, *near)
                call.want(VMEM, (chunk, width), BF16)
                (mine,) = call.run(
                    functools.partial(half_sum_kernel, tile), "half_sum", small_cost
                )
                if layer > 0:
                    relayed, mine = lax.optimization_barrier((relayed, mine))
                weight_sums = [mine, swapped(mine, h), *weight_sums]
            got = [far, *near, *relayed]
            joined = c["first"]
            toward = toward + ALPHA * image.astype(F32)
            if not final:
                term = beta * jnp.dot(
                    support[0, tick, layer].T, masked, preferred_element_type=F32
                )
                old = weight_acc[layer]
                weight_acc[layer] = term if old is None else old + term
        initial.append(toward)
        c = dict(base, tick=tick, final=final, joined=joined)
        call = Call()
        call.give(VMEM, names, adjs[tick], image, *got)
        if final:
            call.give(VMEM, *handed)
            call.want(HBM, (ticks, 1, rows, width), BF16)
            call.scratch = [pltpu.VMEM((rows, width), BF16), pltpu.SemaphoreType.DMA((ticks,))]
        else:
            call.want(VMEM, (rows, width), BF16)
        results = call.run(functools.partial(exit_kernel, c), "exit", layer_cost)
        handed.append(results[0])
    call = Call()
    call.give(VMEM, *weight_sums)
    call.want(VMEM, (layers, chunk, width), BF16)
    (total,) = call.run(functools.partial(total_kernel, layers), "total", small_cost)
    call = Call()
    call.give(VMEM, total, *shared([total] * (h - 1)))
    call.want(HBM, (1, layers, width, width), F32)
    call.scratch = [pltpu.VMEM((layers, width, width), F32), pltpu.SemaphoreType.DMA((layers,))]
    (weight_grad,) = call.run(functools.partial(finish_kernel, h), "finish", small_cost)
    return handed[-1], jnp.stack(initial)[None], weight_grad


def solution(mesh):
    return jax.shard_map(
        shards,
        mesh=mesh,
        in_specs=(
            P("section", "rows", None),
            P("rows", None),
            P("section", None, None, "rows", None),
            P("section", None, None, "rows", None),
            P("section", None, None, None),
            P("section", None, "rows", None, None),
            P("section", None, "rows"),
            P("section", None, "rows"),
            P("section", None, "rows"),
        ),
        out_specs=(
            P(None, "section", "rows", None),
            P("section", None, "rows", None),
            P("section", None, None, None),
        ),
        check_vma=False,
    )
```

```python
import functools

import jax
import jax.numpy as jnp
from jax import lax
from jax.experimental import pallas as pl
from jax.experimental.pallas import tpu as pltpu
from jax.sharding import PartitionSpec as P

ALPHA = 0.1
BETA_SCALE = 0.5
VMEM = pl.BlockSpec(memory_space=pltpu.VMEM)
SMEM = pl.BlockSpec(memory_space=pltpu.SMEM)
HBM = pl.BlockSpec(memory_space=pltpu.HBM)
PARAMS = pltpu.CompilerParams(vmem_limit_bytes=24 * 2**20)
F32 = jnp.float32
BF16 = jnp.bfloat16


def cost(flops, nbytes):
    return pl.CostEstimate(flops=flops, bytes_accessed=nbytes, transcendentals=0)


def swapped(block, k):
    n = lax.axis_size("rows")
    return lax.ppermute(block, "rows", [(i, i ^ k) for i in range(n)])


def shared(blocks):
    moved = {k: swapped(block, k) for k, block in reversed(list(enumerate(blocks, 1)))}
    return [moved[k] for k in sorted(moved)]


def passed_along(block, axis, distance):
    devices = range(lax.axis_size(axis))
    route = [(i - distance, i) for i in devices if i - distance in devices]
    return lax.ppermute(block, axis, route)


class Refs:
    def __init__(self, refs):
        self.refs = list(refs)

    def take(self, count=None):
        many = 1 if count is None else count
        taken, self.refs = self.refs[:many], self.refs[many:]
        return taken[0] if count is None else taken


class Call:
    def __init__(self):
        self.operands, self.specs, self.outs, self.out_specs, self.scratch = [], [], [], [], []
        self.aliases = {}

    def give(self, spec, *arrays):
        self.operands += arrays
        self.specs += [spec] * len(arrays)

    def want(self, spec, shape, dtype, count=1):
        self.outs += [jax.ShapeDtypeStruct(shape, dtype)] * count
        self.out_specs += [spec] * count

    def run(self, kernel, name, estimate, params=PARAMS):
        return pl.pallas_call(
            kernel,
            out_shape=self.outs,
            in_specs=self.specs,
            out_specs=self.out_specs,
            scratch_shapes=self.scratch,
            input_output_aliases=self.aliases,
            compiler_params=params,
            cost_estimate=estimate,
            name=name,
        )(*self.operands)


def packed(tile_row, tile_col, tile_count, row_tiles):
    owner = jnp.bitwise_xor(tile_col // row_tiles, lax.axis_index("rows"))
    words = (owner * row_tiles + tile_col % row_tiles) * row_tiles + tile_row
    counts = tile_count.reshape(1, -1)
    counts = jnp.pad(counts, ((0, 0), (0, words.shape[2] - counts.shape[1])))
    return jnp.concatenate([words[0], counts], axis=0)


def densify_kernel(tick, row_tiles, n, chunks, words_ref, vals_ref, out_ref, vals, acc, sems):
    entries, tile = vals.shape[:2]
    chunk = entries // chunks
    copies = []
    for c in range(chunks):
        part = pl.ds(c * chunk, chunk)
        copies.append(
            pltpu.make_async_copy(vals_ref.at[0, tick, part], vals.at[part], sems.at[c])
        )
        copies[c].start()
    acc[...] = jnp.zeros_like(acc)

    def add(e, carry):
        word = words_ref[tick, e]
        row = lax.rem(word, row_tiles)
        block = lax.rem(lax.div(word, row_tiles), row_tiles)
        slot = lax.div(word, row_tiles * row_tiles)
        slot = jnp.where((slot == 0) & (block > 0), n - 1 + block, slot)
        rows = pl.ds(pl.multiple_of(row * tile, tile), tile)
        cols = pl.ds(pl.multiple_of(slot * tile, tile), tile)
        acc[rows, cols] += vals[e].astype(F32)
        return carry

    count = words_ref[words_ref.shape[0] - 1, tick]
    for c in range(chunks):
        copies[c].wait()
        stop = jnp.clip(count, c * chunk, (c + 1) * chunk)
        lax.fori_loop(c * chunk, stop, add, 0)
    out_ref[...] = acc[...].astype(BF16)


def densify(tick, words, vals, row_tiles, n):
    entries, tile = vals.shape[2:4]
    chunks = 4 if entries % 4 == 0 else 1
    shape = (row_tiles * tile, (n + row_tiles - 1) * tile)
    call = Call()
    call.give(SMEM, words)
    call.give(HBM, vals)
    call.want(VMEM, shape, BF16)
    call.scratch = [
        pltpu.VMEM(vals.shape[2:], BF16),
        pltpu.VMEM(shape, F32),
        pltpu.SemaphoreType.DMA((chunks,)),
    ]
    (adj,) = call.run(
        functools.partial(densify_kernel, tick, row_tiles, n, chunks),
        "densify",
        cost(entries * tile * tile * 20, entries * tile * tile * 2),
        pltpu.CompilerParams(vmem_limit_bytes=50 * 2**20),
    )
    return adj


def tile_at(ref, index, tile):
    return ref[pl.ds(pl.multiple_of(index * tile, tile), tile), :]


def name_kernel(n, row_tiles, words_ref, *out_refs):
    ticks, width = out_refs[0].shape
    for t in range(ticks):
        index = words_ref[t : t + 1, :] // row_tiles

        def named(k):
            block = index - k * row_tiles
            block = jnp.where((block >= 0) & (block < row_tiles), block, 0)
            most = jnp.max(block.astype(F32), axis=1, keepdims=True)
            return jnp.broadcast_to(most, (1, width))

        for k in range(1, n // 2):
            out_refs[k][2 * t : 2 * t + 1, :] = named(k)
            out_refs[k][2 * t + 1 : 2 * t + 2, :] = named(n // 2 + k)
        out_refs[0][t : t + 1, :] = named(n // 2)


def chosen(image_ref, row, rows, tile):
    index = jnp.broadcast_to(row.astype(BF16), (tile, row.shape[1]))
    result = image_ref[:tile, :]
    for i in range(1, rows // tile):
        result = jnp.where(index > i - 0.5, image_ref[i * tile : (i + 1) * tile, :], result)
    return result


def take_got(refs, c):
    far, near = refs.take(), refs.take(c["n"] // 2 - 1)
    if c["joined"]:
        return far, near, [ref.at[c["tile"] :, :] for ref in near]
    return far, near, refs.take(c["n"] // 2 - 1)


def spread_of(adj_ref, own_ref, got, names_ref, c):
    tile, rows = c["tile"], c["rows"]
    far, near, relayed = got
    far = chosen(far, names_ref[c["tick"] : c["tick"] + 1, :], rows, tile)
    near = [ref[:tile, :] for ref in near]
    relayed = [ref[...] for ref in relayed]
    blocks = jnp.concatenate(
        [own_ref[:tile, :]] + near + [far] + relayed + [own_ref[tile:, :]], axis=0
    )
    total = jnp.dot(adj_ref[...], blocks, preferred_element_type=F32)
    return ((1.0 - ALPHA) * total).astype(BF16)


def layer_kernel(c, *refs):
    refs = Refs(refs)
    n, tile, width, chunk = c["n"], c["tile"], c["width"], c["chunk"]
    h = n // 2
    preact_all, weight_all, names_ref = refs.take(3)
    asked = refs.take(h - 1)
    if c["entry"]:
        last_ref, passed_ref = refs.take(2)
    else:
        adj_ref, own_ref = refs.take(2)
        got = take_got(refs, c)
    if c["final"]:
        support_all, acc_ref = refs.take(2)
    image_ref = refs.take()
    sends = refs.take(h - 1)
    out_ref = refs.take()
    preact_ref, weight_ref, load_sems = refs.take(3)

    section = lax.axis_index("section")
    loads = [
        (preact_all.at[0, c["tick"], c["layer"]], preact_ref),
        (weight_all.at[0, c["layer"]], weight_ref),
    ]
    if c["final"]:
        support_ref, term_ref = refs.take(2)
        loads.append((support_all.at[0, c["tick"], c["layer"]], support_ref))
    loads = [pltpu.make_async_copy(a, b, load_sems.at[i]) for i, (a, b) in enumerate(loads)]
    for load in loads:
        load.start()
    step = (c["layers"] * section + c["layer"] + 1).astype(F32)
    beta = jnp.log(BETA_SCALE / jnp.full((1, width), step, F32) + 1.0)
    if not c["entry"]:
        grad = spread_of(adj_ref, own_ref, got, names_ref, c)
    for load in loads:
        load.wait()
    if c["entry"]:
        grad = jnp.where(section == c["sections"] - 1, last_ref[...], passed_ref[...])

    masked = jnp.where(preact_ref[...] > 0, grad, jnp.zeros_like(grad))
    product = lax.dot_general(
        masked, weight_ref[...], (((1,), (1,)), ((), ())), preferred_element_type=F32
    )
    image = ((1.0 - beta) * masked.astype(F32) + beta * product).astype(BF16)
    image_ref[...] = image
    if not c["join"]:
        for send, asked_ref in zip(sends, asked):
            row = asked_ref[2 * c["tick"] : 2 * c["tick"] + 1, :]
            send[:tile, :] = chosen(image_ref, row, c["rows"], tile)
    if c["final"]:
        term = lax.dot_general(
            support_ref[...], masked, (((0,), (0,)), ((), ())), preferred_element_type=F32
        )
        term_ref[...] = acc_ref[...] + beta * term
        place = lax.rem(lax.axis_index("rows"), h)
        for k in range(1, h):
            part = tile_at(term_ref, jnp.bitwise_xor(place, k), chunk).astype(BF16)
            if c["join"]:
                sends[k - 1][...] = part
            else:
                sends[k - 1][tile : tile + chunk, :] = part
        out_ref[...] = tile_at(term_ref, place, chunk)
    else:
        out_ref[...] = masked


def forward_kernel(c, *refs):
    refs = Refs(refs)
    count, tile, rows = c["n"] // 2 - 1, c["tile"], c["rows"]
    far_ref = refs.take()
    own_ref = refs.take() if c["join"] else None
    for asked_ref, send in zip(refs.take(count), refs.take(count)):
        row = 2 * c["tick"]
        if c["join"]:
            send[:tile, :] = chosen(own_ref, asked_ref[row : row + 1, :], rows, tile)
            send[tile:, :] = chosen(far_ref, asked_ref[row + 1 : row + 2, :], rows, tile)
        else:
            send[...] = chosen(far_ref, asked_ref[row + 1 : row + 2, :], rows, tile)


def half_sum_kernel(kept_ref, *refs):
    total = kept_ref[...]
    for ref in refs[:-1]:
        total = total + ref[ref.shape[0] - total.shape[0] :, :].astype(F32)
    refs[-1][...] = total.astype(BF16)


def total_kernel(layers, *refs):
    for layer in range(layers):
        mine_ref, far_ref = refs[2 * layer : 2 * layer + 2]
        total = mine_ref[...].astype(F32) + far_ref[...].astype(F32)
        refs[-1][layer] = total.astype(BF16)


def exit_kernel(c, *refs):
    refs = Refs(refs)
    names_ref, adj_ref, own_ref = refs.take(3)
    got = take_got(refs, c)
    if not c["final"]:
        refs.take()[...] = spread_of(adj_ref, own_ref, got, names_ref, c)
        return
    handed = refs.take(c["tick"])
    out_ref, hold_ref, sems = refs.take(3)
    copies = [
        pltpu.make_async_copy(ref, out_ref.at[t, 0], sems.at[t])
        for t, ref in enumerate(handed + [hold_ref])
    ]
    for copy in copies[:-1]:
        copy.start()
    hold_ref[...] = spread_of(adj_ref, own_ref, got, names_ref, c)
    copies[-1].start()
    for copy in copies:
        copy.wait()


def finish_kernel(h, *refs):
    sums, (out_ref, hold_ref, sems) = refs[:h], refs[h:]
    layers, chunk, _ = sums[0].shape
    place = lax.rem(lax.axis_index("rows"), h)
    copies = []
    for layer in range(layers):
        for k in range(h):
            start = pl.multiple_of(jnp.bitwise_xor(place, k) * chunk, chunk)
            hold_ref[layer, pl.ds(start, chunk), :] = sums[k][layer].astype(F32)
        copy = pltpu.make_async_copy(hold_ref.at[layer], out_ref.at[0, layer], sems.at[layer])
        copy.start()
        copies.append(copy)
    for copy in copies:
        copy.wait()


def shards(grad_in, grad_last, support, preact, weights, tile_vals, tile_row, tile_col, tile_count):
    section = lax.axis_index("section")
    n = lax.axis_size("rows")
    h = n // 2
    sections = lax.axis_size("section")
    ticks = support.shape[1]
    layers = support.shape[2]
    rows, width = grad_last.shape
    tile = tile_vals.shape[-1]
    row_tiles = rows // tile
    chunk = width // h
    words = packed(tile_row, tile_col, tile_count, row_tiles)

    handed = []
    passed = None
    weight_acc = [None] * layers
    weight_sums = []
    initial = []
    base = dict(n=n, tile=tile, rows=rows, width=width, layers=layers, sections=sections, chunk=chunk)
    layer_cost = cost(2 * rows * width * (width + (n + 1) * tile), (6 + 2 * n) * rows * width)
    small_cost = cost(rows * width, 2 * n * rows * width)
    relay_cost = cost(rows * width, 8 * n * rows * width)
    call = Call()
    call.give(VMEM, words)
    call.want(VMEM, (ticks, width), F32)
    call.want(VMEM, (2 * ticks, width), F32, h - 1)
    names, *asking = call.run(functools.partial(name_kernel, n, row_tiles), "name", small_cost)
    asked = shared(asking)

    adjs = [None] * ticks
    for tick in range(ticks):
        final = tick == ticks - 1
        if tick > 0:
            passed = passed_along(handed[-1], "section", -1)
        image = got = joined = None
        toward = 0.0
        for layer in reversed(range(layers)):
            entry = layer == layers - 1
            beta = jnp.log(BETA_SCALE / (layers * section + layer + 1).astype(F32) + 1.0)
            c = dict(
                base, layer=layer, tick=tick, entry=entry, final=final, joined=joined,
                first=tick == 0 and entry,
            )
            c["join"] = c["first"] or (final and layer == 0)
            if c["first"]:
                masked = jnp.where(
                    preact[0, tick, layer] > 0, grad_in[0], jnp.zeros_like(grad_in[0])
                )
                product = jnp.dot(masked, weights[0, layer].T, preferred_element_type=F32)
                image = ((1.0 - beta) * masked.astype(F32) + beta * product).astype(BF16)
            else:
                call = Call()
                call.give(HBM, preact, weights)
                call.give(VMEM, names, *asked)
                if entry:
                    call.give(VMEM, grad_last, passed)
                else:
                    call.give(VMEM, adjs[tick], image, *got)
                if final:
                    call.give(HBM, support)
                    call.give(VMEM, weight_acc[layer])
                message = (0 if c["join"] else tile) + (chunk if final else 0)
                call.want(VMEM, (rows, width), BF16)
                call.want(VMEM, (message, width), BF16, h - 1)
                if final:
                    call.want(VMEM, (chunk, width), F32)
                else:
                    call.want(VMEM, (rows, width), BF16)
                call.scratch = [
                    pltpu.VMEM((rows, width), BF16),
                    pltpu.VMEM((width, width), BF16),
                    pltpu.SemaphoreType.DMA((3,)),
                ]
                if final:
                    call.scratch.append(pltpu.VMEM((rows, width), BF16))
                    call.scratch.append(pltpu.VMEM((width, width), F32))
                results = Refs(
                    call.run(
                        functools.partial(layer_kernel, c), "entry" if entry else "middle", layer_cost
                    )
                )
                image = results.take()
                sends = results.take(h - 1)
                kept = masked = results.take()
            far = swapped(image, h)
            near = [] if c["first"] else shared(sends)
            ready = image
            if c["first"]:
                adjs[0] = densify(0, words, tile_vals, row_tiles, n)
                ready, adjs[0] = lax.optimization_barrier((image, adjs[0]))
            call = Call()
            call.give(VMEM, far)
            if c["join"]:
                call.give(VMEM, ready)
            call.give(VMEM, *asked)
            call.want(VMEM, (tile * (1 + c["join"]), width), BF16, h - 1)
            relays = call.run(functools.partial(forward_kernel, c), "forward", small_cost)
            relayed = shared(relays)
            if layer == 0 and not final:
                later, *_ = lax.optimization_barrier((words, *near))
                adjs[tick + 1] = densify(tick + 1, later, tile_vals, row_tiles, n)
                relayed, adjs[tick + 1] = lax.optimization_barrier((relayed, adjs[tick + 1]))
            if final:
                if layer > 0:
                    kept, *_ = lax.optimization_barrier((kept, *relays))
                call = Call()
                call.give(VMEM, kept, *near)
                call.want(VMEM, (chunk, width), BF16)
                (mine,) = call.run(
                    half_sum_kernel, "half_sum", small_cost
                )
                if layer > 0:
                    relayed, mine = lax.optimization_barrier((relayed, mine))
                else:
                    mine, _ = lax.optimization_barrier((mine, far))
                weight_sums = [mine, swapped(mine, h), *weight_sums]
            got = [far, *relayed] if c["join"] else [far, *near, *relayed]
            joined = c["join"]
            toward = toward + ALPHA * image.astype(F32)
            if not final:
                term = beta * jnp.dot(
                    support[0, tick, layer].T, masked, preferred_element_type=F32
                )
                old = weight_acc[layer]
                weight_acc[layer] = term if old is None else old + term
        initial.append(toward)
        c = dict(base, tick=tick, final=final, joined=joined)
        call = Call()
        call.give(VMEM, names, adjs[tick], image, *got)
        if final:
            call.give(VMEM, *handed)
            call.want(HBM, (ticks, 1, rows, width), BF16)
            call.scratch = [pltpu.VMEM((rows, width), BF16), pltpu.SemaphoreType.DMA((ticks,))]
        else:
            call.want(VMEM, (rows, width), BF16)
        results = call.run(functools.partial(exit_kernel, c), "exit", layer_cost)
        handed.append(results[0])
    call = Call()
    call.give(VMEM, *weight_sums)
    call.want(VMEM, (layers, chunk, width), BF16)
    (total,) = call.run(functools.partial(total_kernel, layers), "total", small_cost)
    call = Call()
    call.give(VMEM, total, *shared([total] * (h - 1)))
    call.want(HBM, (1, layers, width, width), F32)
    call.scratch = [pltpu.VMEM((layers, width, width), F32), pltpu.SemaphoreType.DMA((layers,))]
    (weight_grad,) = call.run(functools.partial(finish_kernel, h), "finish", small_cost)
    return handed[-1], jnp.stack(initial)[None], weight_grad


def solution(mesh):
    return jax.shard_map(
        shards,
        mesh=mesh,
        in_specs=(
            P("section", "rows", None),
            P("rows", None),
            P("section", None, None, "rows", None),
            P("section", None, None, "rows", None),
            P("section", None, None, None),
            P("section", None, "rows", None, None),
            P("section", None, "rows"),
            P("section", None, "rows"),
            P("section", None, "rows"),
        ),
        out_specs=(
            P(None, "section", "rows", None),
            P("section", None, "rows", None),
            P("section", None, None, None),
        ),
        check_vma=False,
    )
```

```python
import functools

import jax
import jax.numpy as jnp
from jax import lax
from jax.experimental import pallas as pl
from jax.experimental.pallas import tpu as pltpu
from jax.sharding import PartitionSpec as P

ALPHA = 0.1
BETA_SCALE = 0.5
VMEM = pl.BlockSpec(memory_space=pltpu.VMEM)
SMEM = pl.BlockSpec(memory_space=pltpu.SMEM)
HBM = pl.BlockSpec(memory_space=pltpu.HBM)
PARAMS = pltpu.CompilerParams(vmem_limit_bytes=24 * 2**20)
F32 = jnp.float32
BF16 = jnp.bfloat16


def cost(flops, nbytes):
    return pl.CostEstimate(flops=flops, bytes_accessed=nbytes, transcendentals=0)


def swapped(block, k):
    n = lax.axis_size("rows")
    return lax.ppermute(block, "rows", [(i, i ^ k) for i in range(n)])


def lowered(block, k):
    n, sections = lax.axis_size("rows"), lax.axis_size("section")
    route = [
        (s * n + i, (s - 1) % sections * n + (i ^ k)) for s in range(sections) for i in range(n)
    ]
    return lax.ppermute(block, ("section", "rows"), route)


def raised(block):
    sections = lax.axis_size("section")
    return lax.ppermute(block, "section", [(s, (s + 1) % sections) for s in range(sections)])


def shared(blocks, move=swapped):
    moved = {k: move(block, k) for k, block in reversed(list(enumerate(blocks, 1)))}
    return [moved[k] for k in sorted(moved)]


class Refs:
    def __init__(self, refs):
        self.refs = list(refs)

    def take(self, count=None):
        many = 1 if count is None else count
        taken, self.refs = self.refs[:many], self.refs[many:]
        return taken[0] if count is None else taken


class Call:
    def __init__(self):
        self.operands, self.specs, self.outs, self.out_specs, self.scratch = [], [], [], [], []
        self.aliases = {}

    def give(self, spec, *arrays):
        self.operands += arrays
        self.specs += [spec] * len(arrays)

    def want(self, spec, shape, dtype, count=1):
        self.outs += [jax.ShapeDtypeStruct(shape, dtype)] * count
        self.out_specs += [spec] * count

    def run(self, kernel, name, estimate, params=PARAMS):
        return pl.pallas_call(
            kernel,
            out_shape=self.outs,
            in_specs=self.specs,
            out_specs=self.out_specs,
            scratch_shapes=self.scratch,
            input_output_aliases=self.aliases,
            compiler_params=params,
            cost_estimate=estimate,
            name=name,
        )(*self.operands)


def packed(tile_row, tile_col, tile_count, row_tiles):
    owner = jnp.bitwise_xor(tile_col // row_tiles, lax.axis_index("rows"))
    words = (owner * row_tiles + tile_col % row_tiles) * row_tiles + tile_row
    counts = tile_count.reshape(1, -1)
    counts = jnp.pad(counts, ((0, 0), (0, words.shape[2] - counts.shape[1])))
    return jnp.concatenate([words[0], counts], axis=0)


def densify_kernel(tick, row_tiles, n, chunks, words_ref, vals_ref, out_ref, vals, acc, sems):
    entries, tile = vals.shape[:2]
    chunk = entries // chunks
    copies = []
    for c in range(chunks):
        part = pl.ds(c * chunk, chunk)
        copies.append(
            pltpu.make_async_copy(vals_ref.at[0, tick, part], vals.at[part], sems.at[c])
        )
        copies[c].start()
    acc[...] = jnp.zeros_like(acc)

    def add(e, carry):
        word = words_ref[tick, e]
        row = lax.rem(word, row_tiles)
        block = lax.rem(lax.div(word, row_tiles), row_tiles)
        slot = lax.div(word, row_tiles * row_tiles)
        slot = jnp.where((slot == 0) & (block > 0), n - 1 + block, slot)
        rows = pl.ds(pl.multiple_of(row * tile, tile), tile)
        cols = pl.ds(pl.multiple_of(slot * tile, tile), tile)
        acc[rows, cols] += vals[e].astype(F32)
        return carry

    count = words_ref[words_ref.shape[0] - 1, tick]
    for c in range(chunks):
        copies[c].wait()
        stop = jnp.clip(count, c * chunk, (c + 1) * chunk)
        lax.fori_loop(c * chunk, stop, add, 0)
    out_ref[...] = acc[...].astype(BF16)


def densify(tick, words, vals, row_tiles, n):
    entries, tile = vals.shape[2:4]
    chunks = 4 if entries % 4 == 0 else 1
    shape = (row_tiles * tile, (n + row_tiles - 1) * tile)
    call = Call()
    call.give(SMEM, words)
    call.give(HBM, vals)
    call.want(VMEM, shape, BF16)
    call.scratch = [
        pltpu.VMEM(vals.shape[2:], BF16),
        pltpu.VMEM(shape, F32),
        pltpu.SemaphoreType.DMA((chunks,)),
    ]
    (adj,) = call.run(
        functools.partial(densify_kernel, tick, row_tiles, n, chunks),
        "densify",
        cost(entries * tile * tile * 20, entries * tile * tile * 2),
        pltpu.CompilerParams(vmem_limit_bytes=50 * 2**20),
    )
    return adj


def tile_at(ref, index, tile):
    return ref[pl.ds(pl.multiple_of(index * tile, tile), tile), :]


def name_kernel(n, row_tiles, words_ref, *out_refs):
    ticks, width = out_refs[0].shape
    for t in range(ticks):
        index = words_ref[t : t + 1, :] // row_tiles

        def named(k):
            block = index - k * row_tiles
            block = jnp.where((block >= 0) & (block < row_tiles), block, 0)
            most = jnp.max(block.astype(F32), axis=1, keepdims=True)
            return jnp.broadcast_to(most, (1, width))

        for k in range(1, n // 2):
            out_refs[k][2 * t : 2 * t + 1, :] = named(k)
            out_refs[k][2 * t + 1 : 2 * t + 2, :] = named(n // 2 + k)
        out_refs[0][t : t + 1, :] = named(n // 2)


def pack_kernel(tick, layer, preact_all, weight_all, *refs):
    asked, (out_ref, sems) = refs[:-2], refs[-2:]
    rows, width = preact_all.shape[-2:]
    loads = [
        pltpu.make_async_copy(preact_all.at[0, tick, layer], out_ref.at[:rows], sems.at[0]),
        pltpu.make_async_copy(
            weight_all.at[0, layer], out_ref.at[rows : rows + width], sems.at[1]
        ),
    ]
    for load in loads:
        load.start()
    used = sum(ref.shape[0] for ref in asked)
    rest = out_ref.shape[0] - rows - width - used
    parts = [ref[...] for ref in asked] + ([jnp.zeros((rest, width), F32)] if rest else [])
    out_ref[rows + width :, :] = jnp.concatenate(parts, axis=0).astype(BF16)
    for load in loads:
        load.wait()


def chosen(image_ref, row, rows, tile):
    index = jnp.broadcast_to(row.astype(BF16), (tile, row.shape[1]))
    result = image_ref[:tile, :]
    for i in range(1, rows // tile):
        result = jnp.where(index > i - 0.5, image_ref[i * tile : (i + 1) * tile, :], result)
    return result


def take_got(refs, c):
    far, near = refs.take(), refs.take(c["n"] // 2 - 1)
    if c["joined"]:
        return far, near, [ref.at[c["tile"] :, :] for ref in near]
    return far, near, refs.take(c["n"] // 2 - 1)


def spread_of(adj_ref, own_ref, got, names_ref, c):
    tile, rows = c["tile"], c["rows"]
    far, near, relayed = got
    far = chosen(far, names_ref[c["tick"] : c["tick"] + 1, :], rows, tile)
    near = [ref[:tile, :] for ref in near]
    relayed = [ref[:tile, :] for ref in relayed]
    blocks = jnp.concatenate(
        [own_ref[:tile, :]] + near + [far] + relayed + [own_ref[tile:, :]], axis=0
    )
    total = jnp.dot(adj_ref[...], blocks, preferred_element_type=F32)
    return ((1.0 - ALPHA) * total).astype(BF16)


def image_of(c, section, layer, grad, preact, weight):
    step = (c["layers"] * section + layer + 1).astype(F32)
    beta = jnp.log(BETA_SCALE / jnp.full((1, c["width"]), step, F32) + 1.0)
    masked = jnp.where(preact > 0, grad, jnp.zeros_like(grad))
    product = lax.dot_general(
        masked, weight, (((1,), (1,)), ((), ())), preferred_element_type=F32
    )
    image = ((1.0 - beta) * masked.astype(F32) + beta * product).astype(BF16)
    return beta, masked, image


def layer_kernel(c, *refs):
    refs = Refs(refs)
    n, tile, width, chunk = c["n"], c["tile"], c["width"], c["chunk"]
    h = n // 2
    preact_all, weight_all, names_ref = refs.take(3)
    asked = refs.take(h - 1)
    if c["entry"]:
        last_ref, passed_ref = refs.take(2)
    else:
        adj_ref, own_ref = refs.take(2)
        got = take_got(refs, c)
    if c["final"]:
        support_all, acc_ref = refs.take(2)
    image_ref = refs.take()
    sends = refs.take(h - 1) if c["final"] or not c["entry"] else []
    out_ref = refs.take()
    preact_ref, weight_ref, load_sems = refs.take(3)

    section = lax.axis_index("section")
    loads = [
        (preact_all.at[0, c["tick"], c["layer"]], preact_ref),
        (weight_all.at[0, c["layer"]], weight_ref),
    ]
    if c["final"]:
        support_ref, term_ref = refs.take(2)
        loads.append((support_all.at[0, c["tick"], c["layer"]], support_ref))
    loads = [pltpu.make_async_copy(a, b, load_sems.at[i]) for i, (a, b) in enumerate(loads)]
    for load in loads:
        load.start()
    if not c["entry"]:
        grad = spread_of(adj_ref, own_ref, got, names_ref, c)
    for load in loads:
        load.wait()
    if c["entry"]:
        grad = jnp.where(section == c["sections"] - 1, last_ref[...], passed_ref[...])

    beta, masked, image = image_of(
        c, section, c["layer"], grad, preact_ref[...], weight_ref[...]
    )
    image_ref[...] = image
    if not c["entry"]:
        for send, asked_ref in zip(sends, asked):
            row = asked_ref[2 * c["tick"] : 2 * c["tick"] + 1, :]
            send[:tile, :] = chosen(image_ref, row, c["rows"], tile)
    if c["final"]:
        term = lax.dot_general(
            support_ref[...], masked, (((0,), (0,)), ((), ())), preferred_element_type=F32
        )
        term_ref[...] = acc_ref[...] + beta * term
        place = lax.rem(lax.axis_index("rows"), h)
        for k in range(1, h):
            part = tile_at(term_ref, jnp.bitwise_xor(place, k), chunk).astype(BF16)
            if c["entry"]:
                sends[k - 1][...] = part
            else:
                sends[k - 1][tile : tile + chunk, :] = part
        out_ref[...] = tile_at(term_ref, place, chunk)
    else:
        out_ref[...] = masked


def forward_kernel(c, *refs):
    refs = Refs(refs)
    count, tile, rows = c["n"] // 2 - 1, c["tile"], c["rows"]
    far_ref = refs.take()
    own_ref = refs.take() if c["first"] else None
    asked = refs.take(count)
    for asked_ref, send in zip(asked, refs.take(count)):
        row = 2 * c["tick"]
        if c["first"]:
            send[:tile, :] = chosen(own_ref, asked_ref[row : row + 1, :], rows, tile)
            send[tile:, :] = chosen(far_ref, asked_ref[row + 1 : row + 2, :], rows, tile)
        else:
            send[...] = chosen(far_ref, asked_ref[row + 1 : row + 2, :], rows, tile)


def half_sum_kernel(kept_ref, *refs):
    total = kept_ref[...]
    for ref in refs[:-1]:
        total = total + ref[ref.shape[0] - total.shape[0] :, :].astype(F32)
    refs[-1][...] = total.astype(BF16)


def total_kernel(layers, *refs):
    for layer in range(layers):
        mine_ref, far_ref = refs[2 * layer : 2 * layer + 2]
        total = mine_ref[...].astype(F32) + far_ref[...].astype(F32)
        refs[-1][layer] = total.astype(BF16)


def turn_kernel(c, *refs):
    refs = Refs(refs)
    names_ref, adj_ref, own_ref = refs.take(3)
    got = take_got(refs, c)
    below_ref, last_ref = refs.take(2)
    grad_ref, image_ref = refs.take(2)
    sends = refs.take(c["n"] // 2 - 1)
    tile, rows, width = c["tile"], c["rows"], c["width"]
    grad = spread_of(adj_ref, own_ref, got, names_ref, c)
    grad_ref[...] = grad
    section = lax.axis_index("section")
    grad = jnp.where(section == 0, last_ref[...], grad)
    below = jnp.where(section == 0, c["sections"], section) - 1
    _, _, image = image_of(
        c, below, c["layers"] - 1, grad, below_ref[:rows, :], below_ref[rows : rows + width, :]
    )
    image_ref[...] = image
    asked = below_ref[rows + width :, :].astype(F32)
    for k, send in enumerate(sends):
        row = 2 * (k * c["ticks"] + c["tick"] + 1)
        send[...] = chosen(image_ref, asked[row : row + 1, :], rows, tile)


def exit_kernel(c, *refs):
    refs = Refs(refs)
    names_ref, adj_ref, own_ref = refs.take(3)
    got = take_got(refs, c)
    handed = refs.take(c["tick"])
    out_ref, hold_ref, sems = refs.take(3)
    copies = [
        pltpu.make_async_copy(ref, out_ref.at[t, 0], sems.at[t])
        for t, ref in enumerate(handed + [hold_ref])
    ]
    for copy in copies[:-1]:
        copy.start()
    hold_ref[...] = spread_of(adj_ref, own_ref, got, names_ref, c)
    copies[-1].start()
    for copy in copies:
        copy.wait()


def finish_kernel(h, *refs):
    sums, (out_ref, hold_ref, sems) = refs[:h], refs[h:]
    layers, chunk, _ = sums[0].shape
    place = lax.rem(lax.axis_index("rows"), h)
    copies = []
    for layer in range(layers):
        for k in range(h):
            start = pl.multiple_of(jnp.bitwise_xor(place, k) * chunk, chunk)
            hold_ref[layer, pl.ds(start, chunk), :] = sums[k][layer].astype(F32)
        copy = pltpu.make_async_copy(hold_ref.at[layer], out_ref.at[0, layer], sems.at[layer])
        copy.start()
        copies.append(copy)
    for copy in copies:
        copy.wait()


def shards(grad_in, grad_last, support, preact, weights, tile_vals, tile_row, tile_col, tile_count):
    section = lax.axis_index("section")
    n = lax.axis_size("rows")
    h = n // 2
    sections = lax.axis_size("section")
    ticks = support.shape[1]
    layers = support.shape[2]
    rows, width = grad_last.shape
    tile = tile_vals.shape[-1]
    row_tiles = rows // tile
    chunk = width // h
    words = packed(tile_row, tile_col, tile_count, row_tiles)

    handed = []
    turned = None
    weight_acc = [None] * layers
    weight_sums = []
    initial = []
    base = dict(
        n=n, tile=tile, rows=rows, width=width, layers=layers, sections=sections, chunk=chunk,
        ticks=ticks,
    )
    layer_cost = cost(2 * rows * width * (width + (n + 1) * tile), (6 + 2 * n) * rows * width)
    small_cost = cost(rows * width, 2 * n * rows * width)
    relay_cost = cost(rows * width, 8 * n * rows * width)
    call = Call()
    call.give(VMEM, words)
    call.want(VMEM, (ticks, width), F32)
    call.want(VMEM, (2 * ticks, width), F32, h - 1)
    names, *asking = call.run(functools.partial(name_kernel, n, row_tiles), "name", small_cost)
    asked = shared(asking)

    adjs = [None] * ticks
    for tick in range(ticks):
        final = tick == ticks - 1
        if tick > 0:
            passed = lowered(handed[-1], 0)
        image = got = joined = None
        toward = 0.0
        for layer in reversed(range(layers)):
            entry = layer == layers - 1
            beta = jnp.log(BETA_SCALE / (layers * section + layer + 1).astype(F32) + 1.0)
            c = dict(
                base, layer=layer, tick=tick, entry=entry, final=final, joined=joined,
                first=tick == 0 and entry,
            )
            if c["first"]:
                masked = jnp.where(
                    preact[0, tick, layer] > 0, grad_in[0], jnp.zeros_like(grad_in[0])
                )
                product = jnp.dot(masked, weights[0, layer].T, preferred_element_type=F32)
                image = ((1.0 - beta) * masked.astype(F32) + beta * product).astype(BF16)
            else:
                call = Call()
                call.give(HBM, preact, weights)
                call.give(VMEM, names, *asked)
                if entry:
                    call.give(VMEM, grad_last, passed)
                else:
                    call.give(VMEM, adjs[tick], image, *got)
                if final:
                    call.give(HBM, support)
                    call.give(VMEM, weight_acc[layer])
                message = (0 if entry else tile) + (chunk if final else 0)
                call.want(VMEM, (rows, width), BF16)
                if message:
                    call.want(VMEM, (message, width), BF16, h - 1)
                if final:
                    call.want(VMEM, (chunk, width), F32)
                else:
                    call.want(VMEM, (rows, width), BF16)
                call.scratch = [
                    pltpu.VMEM((rows, width), BF16),
                    pltpu.VMEM((width, width), BF16),
                    pltpu.SemaphoreType.DMA((3,)),
                ]
                if final:
                    call.scratch.append(pltpu.VMEM((rows, width), BF16))
                    call.scratch.append(pltpu.VMEM((width, width), F32))
                results = Refs(
                    call.run(
                        functools.partial(layer_kernel, c),
                        "home" if entry else "middle",
                        layer_cost,
                    )
                )
                image = results.take()
                sends = results.take(h - 1) if message else []
                kept = masked = results.take()
            parts = near = []
            if turned is not None:
                far = lowered(turned[0], h)
                near = shared(turned[1:], lowered)
                far, *near = lax.optimization_barrier((far, *near))
                turned = None
                if final:
                    parts = shared(sends)
            else:
                far = swapped(image, h)
                near = parts = [] if c["first"] else shared(sends)
            ready = image
            if c["first"]:
                adjs[0] = densify(0, words, tile_vals, row_tiles, n)
                ready, adjs[0] = lax.optimization_barrier((image, adjs[0]))
            call = Call()
            call.give(VMEM, far)
            if c["first"]:
                call.give(VMEM, ready)
            call.give(VMEM, *asked)
            call.want(VMEM, (tile * (1 + c["first"]), width), BF16, h - 1)
            relays = call.run(functools.partial(forward_kernel, c), "forward", small_cost)
            relayed = shared(relays)
            if layer == 0 and not final:
                later, *_ = lax.optimization_barrier((words, *near))
                adjs[tick + 1] = densify(tick + 1, later, tile_vals, row_tiles, n)
                relayed, adjs[tick + 1] = lax.optimization_barrier((relayed, adjs[tick + 1]))
            if final:
                if not entry:
                    kept, *_ = lax.optimization_barrier((kept, *relays))
                call = Call()
                call.give(VMEM, kept, *parts)
                call.want(VMEM, (chunk, width), BF16)
                (mine,) = call.run(
                    half_sum_kernel, "half_sum", small_cost
                )
                if layer > 0:
                    relayed, mine = lax.optimization_barrier((relayed, mine))
                weight_sums = [mine, swapped(mine, h), *weight_sums]
            got = [far, *near, *relayed]
            joined = c["first"]
            toward = toward + ALPHA * image.astype(F32)
            if not final:
                term = beta * jnp.dot(
                    support[0, tick, layer].T, masked, preferred_element_type=F32
                )
                old = weight_acc[layer]
                weight_acc[layer] = term if old is None else old + term
        initial.append(toward)
        c = dict(base, tick=tick, final=final, joined=joined)
        call = Call()
        call.give(VMEM, names, adjs[tick], image, *got)
        if not final:
            up = Call()
            up.give(HBM, preact, weights)
            up.give(VMEM, *asked)
            length = rows + width + -(-2 * ticks * (h - 1) // 16) * 16
            up.want(VMEM, (length, width), BF16)
            up.scratch = [pltpu.SemaphoreType.DMA((2,))]
            (pack,) = up.run(
                functools.partial(pack_kernel, tick + 1, layers - 1), "pack", small_cost
            )
            call.give(VMEM, raised(pack), grad_last)
            call.want(VMEM, (rows, width), BF16, 2)
            call.want(VMEM, (tile, width), BF16, h - 1)
            grad, *turned = call.run(functools.partial(turn_kernel, c), "turn", layer_cost)
            handed.append(grad)
            continue
        call.give(VMEM, *handed)
        call.want(HBM, (ticks, 1, rows, width), BF16)
        call.scratch = [pltpu.VMEM((rows, width), BF16), pltpu.SemaphoreType.DMA((ticks,))]
        (handoff,) = call.run(functools.partial(exit_kernel, c), "exit", layer_cost)
    call = Call()
    call.give(VMEM, *weight_sums)
    call.want(VMEM, (layers, chunk, width), BF16)
    (total,) = call.run(functools.partial(total_kernel, layers), "total", small_cost)
    call = Call()
    call.give(VMEM, total, *shared([total] * (h - 1)))
    call.want(HBM, (1, layers, width, width), F32)
    call.scratch = [pltpu.VMEM((layers, width, width), F32), pltpu.SemaphoreType.DMA((layers,))]
    (weight_grad,) = call.run(functools.partial(finish_kernel, h), "finish", small_cost)
    return handoff, jnp.stack(initial)[None], weight_grad


def solution(mesh):
    return jax.shard_map(
        shards,
        mesh=mesh,
        in_specs=(
            P("section", "rows", None),
            P("rows", None),
            P("section", None, None, "rows", None),
            P("section", None, None, "rows", None),
            P("section", None, None, None),
            P("section", None, "rows", None, None),
            P("section", None, "rows"),
            P("section", None, "rows"),
            P("section", None, "rows"),
        ),
        out_specs=(
            P(None, "section", "rows", None),
            P("section", None, "rows", None),
            P("section", None, None, None),
        ),
        check_vma=False,
    )
```

```python
import functools

import jax
import jax.numpy as jnp
from jax import lax
from jax.experimental import pallas as pl
from jax.experimental.pallas import tpu as pltpu
from jax.sharding import PartitionSpec as P

ALPHA = 0.1
BETA_SCALE = 0.5
VMEM = pl.BlockSpec(memory_space=pltpu.VMEM)
SMEM = pl.BlockSpec(memory_space=pltpu.SMEM)
HBM = pl.BlockSpec(memory_space=pltpu.HBM)
PARAMS = pltpu.CompilerParams(vmem_limit_bytes=24 * 2**20)
F32 = jnp.float32
BF16 = jnp.bfloat16


def cost(flops, nbytes):
    return pl.CostEstimate(flops=flops, bytes_accessed=nbytes, transcendentals=0)


def swapped(block, k):
    n = lax.axis_size("rows")
    return lax.ppermute(block, "rows", [(i, i ^ k) for i in range(n)])


def lowered(block, k):
    n, sections = lax.axis_size("rows"), lax.axis_size("section")
    route = [
        (s * n + i, (s - 1) % sections * n + (i ^ k)) for s in range(sections) for i in range(n)
    ]
    return lax.ppermute(block, ("section", "rows"), route)


def raised(block):
    sections = lax.axis_size("section")
    return lax.ppermute(block, "section", [(s, (s + 1) % sections) for s in range(sections)])


def shared(blocks, move=swapped):
    moved = {k: move(block, k) for k, block in reversed(list(enumerate(blocks, 1)))}
    return [moved[k] for k in sorted(moved)]


class Refs:
    def __init__(self, refs):
        self.refs = list(refs)

    def take(self, count=None):
        many = 1 if count is None else count
        taken, self.refs = self.refs[:many], self.refs[many:]
        return taken[0] if count is None else taken


class Call:
    def __init__(self):
        self.operands, self.specs, self.outs, self.out_specs, self.scratch = [], [], [], [], []
        self.aliases = {}

    def give(self, spec, *arrays):
        self.operands += arrays
        self.specs += [spec] * len(arrays)

    def want(self, spec, shape, dtype, count=1):
        self.outs += [jax.ShapeDtypeStruct(shape, dtype)] * count
        self.out_specs += [spec] * count

    def run(self, kernel, name, estimate, params=PARAMS):
        return pl.pallas_call(
            kernel,
            out_shape=self.outs,
            in_specs=self.specs,
            out_specs=self.out_specs,
            scratch_shapes=self.scratch,
            input_output_aliases=self.aliases,
            compiler_params=params,
            cost_estimate=estimate,
            name=name,
        )(*self.operands)


def packed(tile_row, tile_col, tile_count, row_tiles):
    owner = jnp.bitwise_xor(tile_col // row_tiles, lax.axis_index("rows"))
    words = (owner * row_tiles + tile_col % row_tiles) * row_tiles + tile_row
    counts = tile_count.reshape(1, -1)
    counts = jnp.pad(counts, ((0, 0), (0, words.shape[2] - counts.shape[1])))
    return jnp.concatenate([words[0], counts], axis=0)


def densify_kernel(tick, row_tiles, n, chunks, words_ref, vals_ref, out_ref, vals, acc, sems):
    entries, tile = vals.shape[:2]
    chunk = entries // chunks
    copies = []
    for c in range(chunks):
        part = pl.ds(c * chunk, chunk)
        copies.append(
            pltpu.make_async_copy(vals_ref.at[0, tick, part], vals.at[part], sems.at[c])
        )
        copies[c].start()
    acc[...] = jnp.zeros_like(acc)

    def add(e, carry):
        word = words_ref[tick, e]
        row = lax.rem(word, row_tiles)
        block = lax.rem(lax.div(word, row_tiles), row_tiles)
        slot = lax.div(word, row_tiles * row_tiles)
        slot = jnp.where((slot == 0) & (block > 0), n - 1 + block, slot)
        rows = pl.ds(pl.multiple_of(row * tile, tile), tile)
        cols = pl.ds(pl.multiple_of(slot * tile, tile), tile)
        acc[rows, cols] += vals[e].astype(F32)
        return carry

    count = words_ref[words_ref.shape[0] - 1, tick]
    for c in range(chunks):
        copies[c].wait()
        stop = jnp.clip(count, c * chunk, (c + 1) * chunk)
        lax.fori_loop(c * chunk, stop, add, 0)
    out_ref[...] = acc[...].astype(BF16)


def densify(tick, words, vals, row_tiles, n):
    entries, tile = vals.shape[2:4]
    chunks = 4 if entries % 4 == 0 else 1
    shape = (row_tiles * tile, (n + row_tiles - 1) * tile)
    call = Call()
    call.give(SMEM, words)
    call.give(HBM, vals)
    call.want(VMEM, shape, BF16)
    call.scratch = [
        pltpu.VMEM(vals.shape[2:], BF16),
        pltpu.VMEM(shape, F32),
        pltpu.SemaphoreType.DMA((chunks,)),
    ]
    (adj,) = call.run(
        functools.partial(densify_kernel, tick, row_tiles, n, chunks),
        "densify",
        cost(entries * tile * tile * 20, entries * tile * tile * 2),
        pltpu.CompilerParams(vmem_limit_bytes=50 * 2**20),
    )
    return adj


def tile_at(ref, index, tile):
    return ref[pl.ds(pl.multiple_of(index * tile, tile), tile), :]


def name_kernel(n, row_tiles, words_ref, *out_refs):
    ticks, width = out_refs[0].shape
    for t in range(ticks):
        index = words_ref[t : t + 1, :] // row_tiles

        def named(k):
            block = index - k * row_tiles
            block = jnp.where((block >= 0) & (block < row_tiles), block, 0)
            most = jnp.max(block.astype(F32), axis=1, keepdims=True)
            return jnp.broadcast_to(most, (1, width))

        for k in range(1, n // 2):
            out_refs[k][2 * t : 2 * t + 1, :] = named(k)
            out_refs[k][2 * t + 1 : 2 * t + 2, :] = named(n // 2 + k)
        out_refs[0][t : t + 1, :] = named(n // 2)


def pack_kernel(tick, layer, preact_all, weight_all, *refs):
    asked, (out_ref, sems) = refs[:-2], refs[-2:]
    rows, width = preact_all.shape[-2:]
    loads = [
        pltpu.make_async_copy(preact_all.at[0, tick, layer], out_ref.at[:rows], sems.at[0]),
        pltpu.make_async_copy(
            weight_all.at[0, layer], out_ref.at[rows : rows + width], sems.at[1]
        ),
    ]
    for load in loads:
        load.start()
    used = sum(ref.shape[0] for ref in asked)
    rest = out_ref.shape[0] - rows - width - used
    parts = [ref[...] for ref in asked] + ([jnp.zeros((rest, width), F32)] if rest else [])
    out_ref[rows + width :, :] = jnp.concatenate(parts, axis=0).astype(BF16)
    for load in loads:
        load.wait()


def chosen(image_ref, row, rows, tile):
    index = jnp.broadcast_to(row.astype(BF16), (tile, row.shape[1]))
    result = image_ref[:tile, :]
    for i in range(1, rows // tile):
        result = jnp.where(index > i - 0.5, image_ref[i * tile : (i + 1) * tile, :], result)
    return result


def take_got(refs, c):
    far, near = refs.take(), refs.take(c["n"] // 2 - 1)
    if c["joined"]:
        return far, near, [ref.at[c["tile"] :, :] for ref in near]
    return far, near, refs.take(c["n"] // 2 - 1)


def spread_of(adj_ref, own_ref, got, names_ref, c):
    tile, rows = c["tile"], c["rows"]
    far, near, relayed = got
    far = chosen(far, names_ref[c["tick"] : c["tick"] + 1, :], rows, tile)
    near = [ref[:tile, :] for ref in near]
    relayed = [ref[:tile, :] for ref in relayed]
    blocks = jnp.concatenate(
        [own_ref[:tile, :]] + near + [far] + relayed + [own_ref[tile:, :]], axis=0
    )
    total = jnp.dot(adj_ref[...], blocks, preferred_element_type=F32)
    return ((1.0 - ALPHA) * total).astype(BF16)


def image_of(c, section, layer, grad, preact, weight):
    step = (c["layers"] * section + layer + 1).astype(F32)
    beta = jnp.log(BETA_SCALE / jnp.full((1, c["width"]), step, F32) + 1.0)
    masked = jnp.where(preact > 0, grad, jnp.zeros_like(grad))
    product = lax.dot_general(
        masked, weight, (((1,), (1,)), ((), ())), preferred_element_type=F32
    )
    image = ((1.0 - beta) * masked.astype(F32) + beta * product).astype(BF16)
    return beta, masked, image


def layer_kernel(c, *refs):
    refs = Refs(refs)
    n, tile, width, chunk = c["n"], c["tile"], c["width"], c["chunk"]
    h = n // 2
    preact_all, weight_all, names_ref = refs.take(3)
    asked = refs.take(h - 1)
    if c["entry"]:
        last_ref, passed_ref = refs.take(2)
    else:
        adj_ref, own_ref = refs.take(2)
        got = take_got(refs, c)
    if c["final"]:
        support_all, acc_ref = refs.take(2)
        pending = refs.take(c["pending"])
    image_ref = refs.take()
    sends = [] if c["entry"] else refs.take(h - 1)
    parts = refs.take(h - 1) if c["final"] and c["layer"] else []
    out_ref = refs.take()
    preact_ref, weight_ref, load_sems = refs.take(3)

    section = lax.axis_index("section")
    loads = [
        (preact_all.at[0, c["tick"], c["layer"]], preact_ref),
        (weight_all.at[0, c["layer"]], weight_ref),
    ]
    if c["final"]:
        support_ref, term_ref = refs.take(2)
        loads.append((support_all.at[0, c["tick"], c["layer"]], support_ref))
    loads = [pltpu.make_async_copy(a, b, load_sems.at[i]) for i, (a, b) in enumerate(loads)]
    for load in loads:
        load.start()
    if not c["entry"]:
        grad = spread_of(adj_ref, own_ref, got, names_ref, c)
    for load in loads:
        load.wait()
    if c["entry"]:
        grad = jnp.where(section == c["sections"] - 1, last_ref[...], passed_ref[...])

    beta, masked, image = image_of(
        c, section, c["layer"], grad, preact_ref[...], weight_ref[...]
    )
    image_ref[...] = image
    if not c["entry"]:
        for send, asked_ref in zip(sends, asked):
            row = asked_ref[2 * c["tick"] : 2 * c["tick"] + 1, :]
            send[:tile, :] = chosen(image_ref, row, c["rows"], tile)
    if c["final"]:
        term = lax.dot_general(
            support_ref[...], masked, (((0,), (0,)), ((), ())), preferred_element_type=F32
        )
        term_ref[...] = acc_ref[...] + beta * term
        place = lax.rem(lax.axis_index("rows"), h)
        for k in range(1, h):
            part = tile_at(term_ref, jnp.bitwise_xor(place, k), chunk).astype(BF16)
            if c["layer"]:
                parts[k - 1][...] = part
            else:
                sends[k - 1][tile : tile + chunk, :] = part
                for i, ref in enumerate(pending[k - 1 :: h - 1], 1):
                    sends[k - 1][tile + i * chunk : tile + (i + 1) * chunk, :] = ref[...]
        out_ref[...] = tile_at(term_ref, place, chunk)
    else:
        out_ref[...] = masked


def forward_kernel(c, *refs):
    refs = Refs(refs)
    count, tile, rows = c["n"] // 2 - 1, c["tile"], c["rows"]
    far_ref = refs.take()
    own_ref = refs.take() if c["first"] else None
    asked = refs.take(count)
    for asked_ref, send in zip(asked, refs.take(count)):
        row = 2 * c["tick"]
        if c["first"]:
            send[:tile, :] = chosen(own_ref, asked_ref[row : row + 1, :], rows, tile)
            send[tile:, :] = chosen(far_ref, asked_ref[row + 1 : row + 2, :], rows, tile)
        else:
            send[...] = chosen(far_ref, asked_ref[row + 1 : row + 2, :], rows, tile)


def half_sum_kernel(layers, tile, *refs):
    out_ref = refs[-1]
    chunk = out_ref.shape[1]
    for layer in range(layers):
        total = refs[layer][...]
        at = tile + layer * chunk
        for ref in refs[layers:-1]:
            total = total + ref[at : at + chunk, :].astype(F32)
        out_ref[layer] = total.astype(BF16)


def total_kernel(mine_ref, far_ref, out_ref):
    out_ref[...] = (mine_ref[...].astype(F32) + far_ref[...].astype(F32)).astype(BF16)


def turn_kernel(c, *refs):
    refs = Refs(refs)
    names_ref, adj_ref, own_ref = refs.take(3)
    got = take_got(refs, c)
    below_ref, last_ref = refs.take(2)
    grad_ref, image_ref = refs.take(2)
    sends = refs.take(c["n"] // 2 - 1)
    tile, rows, width = c["tile"], c["rows"], c["width"]
    grad = spread_of(adj_ref, own_ref, got, names_ref, c)
    grad_ref[...] = grad
    section = lax.axis_index("section")
    grad = jnp.where(section == 0, last_ref[...], grad)
    below = jnp.where(section == 0, c["sections"], section) - 1
    _, _, image = image_of(
        c, below, c["layers"] - 1, grad, below_ref[:rows, :], below_ref[rows : rows + width, :]
    )
    image_ref[...] = image
    asked = below_ref[rows + width :, :].astype(F32)
    for k, send in enumerate(sends):
        row = 2 * (k * c["ticks"] + c["tick"] + 1)
        send[...] = chosen(image_ref, asked[row : row + 1, :], rows, tile)


def exit_kernel(c, *refs):
    refs = Refs(refs)
    names_ref, adj_ref, own_ref = refs.take(3)
    got = take_got(refs, c)
    handed = refs.take(c["tick"])
    out_ref, hold_ref, sems = refs.take(3)
    copies = [
        pltpu.make_async_copy(ref, out_ref.at[t, 0], sems.at[t])
        for t, ref in enumerate(handed + [hold_ref])
    ]
    for copy in copies[:-1]:
        copy.start()
    hold_ref[...] = spread_of(adj_ref, own_ref, got, names_ref, c)
    copies[-1].start()
    for copy in copies:
        copy.wait()


def finish_kernel(h, *refs):
    sums, (out_ref, hold_ref, sems) = refs[:h], refs[h:]
    layers, chunk, _ = sums[0].shape
    place = lax.rem(lax.axis_index("rows"), h)
    copies = []
    for layer in range(layers):
        for k in range(h):
            start = pl.multiple_of(jnp.bitwise_xor(place, k) * chunk, chunk)
            hold_ref[layer, pl.ds(start, chunk), :] = sums[k][layer].astype(F32)
        copy = pltpu.make_async_copy(hold_ref.at[layer], out_ref.at[0, layer], sems.at[layer])
        copy.start()
        copies.append(copy)
    for copy in copies:
        copy.wait()


def shards(grad_in, grad_last, support, preact, weights, tile_vals, tile_row, tile_col, tile_count):
    section = lax.axis_index("section")
    n = lax.axis_size("rows")
    h = n // 2
    sections = lax.axis_size("section")
    ticks = support.shape[1]
    layers = support.shape[2]
    rows, width = grad_last.shape
    tile = tile_vals.shape[-1]
    row_tiles = rows // tile
    chunk = width // h
    words = packed(tile_row, tile_col, tile_count, row_tiles)

    handed = []
    turned = None
    weight_acc = [None] * layers
    kept_chunks, pending = [], []
    initial = []
    base = dict(
        n=n, tile=tile, rows=rows, width=width, layers=layers, sections=sections, chunk=chunk,
        ticks=ticks,
    )
    layer_cost = cost(2 * rows * width * (width + (n + 1) * tile), (6 + 2 * n) * rows * width)
    small_cost = cost(rows * width, 2 * n * rows * width)
    relay_cost = cost(rows * width, 8 * n * rows * width)
    call = Call()
    call.give(VMEM, words)
    call.want(VMEM, (ticks, width), F32)
    call.want(VMEM, (2 * ticks, width), F32, h - 1)
    names, *asking = call.run(functools.partial(name_kernel, n, row_tiles), "name", small_cost)
    asked = shared(asking)

    adjs = [None] * ticks
    for tick in range(ticks):
        final = tick == ticks - 1
        if tick > 0:
            passed = lowered(handed[-1], 0)
        image = got = joined = None
        toward = 0.0
        for layer in reversed(range(layers)):
            entry = layer == layers - 1
            beta = jnp.log(BETA_SCALE / (layers * section + layer + 1).astype(F32) + 1.0)
            c = dict(
                base, layer=layer, tick=tick, entry=entry, final=final, joined=joined,
                first=tick == 0 and entry, pending=0 if layer else len(pending),
            )
            if c["first"]:
                masked = jnp.where(
                    preact[0, tick, layer] > 0, grad_in[0], jnp.zeros_like(grad_in[0])
                )
                product = jnp.dot(masked, weights[0, layer].T, preferred_element_type=F32)
                image = ((1.0 - beta) * masked.astype(F32) + beta * product).astype(BF16)
            else:
                call = Call()
                call.give(HBM, preact, weights)
                call.give(VMEM, names, *asked)
                if entry:
                    call.give(VMEM, grad_last, passed)
                else:
                    call.give(VMEM, adjs[tick], image, *got)
                if final:
                    call.give(HBM, support)
                    call.give(VMEM, weight_acc[layer])
                    if layer == 0:
                        call.give(VMEM, *pending)
                call.want(VMEM, (rows, width), BF16)
                if not entry:
                    message = tile + (layers * chunk if final and layer == 0 else 0)
                    call.want(VMEM, (message, width), BF16, h - 1)
                if final and layer:
                    call.want(VMEM, (chunk, width), BF16, h - 1)
                if final:
                    call.want(VMEM, (chunk, width), F32)
                else:
                    call.want(VMEM, (rows, width), BF16)
                call.scratch = [
                    pltpu.VMEM((rows, width), BF16),
                    pltpu.VMEM((width, width), BF16),
                    pltpu.SemaphoreType.DMA((3,)),
                ]
                if final:
                    call.scratch.append(pltpu.VMEM((rows, width), BF16))
                    call.scratch.append(pltpu.VMEM((width, width), F32))
                results = Refs(
                    call.run(
                        functools.partial(layer_kernel, c),
                        "home" if entry else "middle",
                        layer_cost,
                    )
                )
                image = results.take()
                sends = [] if entry else results.take(h - 1)
                if final and layer:
                    pending = results.take(h - 1) + pending
                kept = masked = results.take()
            if turned is not None:
                far = lowered(turned[0], h)
                near = shared(turned[1:], lowered)
                far, *near = lax.optimization_barrier((far, *near))
                turned = None
                if final:
                    parts = shared(sends)
            else:
                far = swapped(image, h)
                near = [] if c["first"] else shared(sends)
            ready = image
            if c["first"]:
                adjs[0] = densify(0, words, tile_vals, row_tiles, n)
                ready, adjs[0] = lax.optimization_barrier((image, adjs[0]))
            call = Call()
            call.give(VMEM, far)
            if c["first"]:
                call.give(VMEM, ready)
            call.give(VMEM, *asked)
            call.want(VMEM, (tile * (1 + c["first"]), width), BF16, h - 1)
            relays = call.run(functools.partial(forward_kernel, c), "forward", small_cost)
            relayed = shared(relays)
            if layer == 0 and not final:
                later, *_ = lax.optimization_barrier((words, *near))
                adjs[tick + 1] = densify(tick + 1, later, tile_vals, row_tiles, n)
                relayed, adjs[tick + 1] = lax.optimization_barrier((relayed, adjs[tick + 1]))
            if final:
                kept_chunks.insert(0, kept)
            if final and layer == 0:
                kept, _ = lax.optimization_barrier((kept_chunks, relays))
                call = Call()
                call.give(VMEM, *kept, *near)
                call.want(VMEM, (layers, chunk, width), BF16)
                (mine,) = call.run(
                    functools.partial(half_sum_kernel, layers, tile), "half_sum", small_cost
                )
            got = [far, *near, *relayed]
            joined = c["first"]
            toward = toward + ALPHA * image.astype(F32)
            if not final:
                term = beta * jnp.dot(
                    support[0, tick, layer].T, masked, preferred_element_type=F32
                )
                old = weight_acc[layer]
                weight_acc[layer] = term if old is None else old + term
        initial.append(toward)
        c = dict(base, tick=tick, final=final, joined=joined)
        call = Call()
        call.give(VMEM, names, adjs[tick], image, *got)
        if not final:
            up = Call()
            up.give(HBM, preact, weights)
            up.give(VMEM, *asked)
            length = rows + width + -(-2 * ticks * (h - 1) // 16) * 16
            up.want(VMEM, (length, width), BF16)
            up.scratch = [pltpu.SemaphoreType.DMA((2,))]
            (pack,) = up.run(
                functools.partial(pack_kernel, tick + 1, layers - 1), "pack", small_cost
            )
            call.give(VMEM, raised(pack), grad_last)
            call.want(VMEM, (rows, width), BF16, 2)
            call.want(VMEM, (tile, width), BF16, h - 1)
            grad, *turned = call.run(functools.partial(turn_kernel, c), "turn", layer_cost)
            handed.append(grad)
            continue
        call.give(VMEM, *handed)
        call.want(HBM, (ticks, 1, rows, width), BF16)
        call.scratch = [pltpu.VMEM((rows, width), BF16), pltpu.SemaphoreType.DMA((ticks,))]
        (handoff,) = call.run(functools.partial(exit_kernel, c), "exit", layer_cost)
    call = Call()
    call.give(VMEM, mine, swapped(mine, h))
    call.want(VMEM, (layers, chunk, width), BF16)
    (total,) = call.run(total_kernel, "total", small_cost)
    call = Call()
    call.give(VMEM, total, *shared([total] * (h - 1)))
    call.want(HBM, (1, layers, width, width), F32)
    call.scratch = [pltpu.VMEM((layers, width, width), F32), pltpu.SemaphoreType.DMA((layers,))]
    (weight_grad,) = call.run(functools.partial(finish_kernel, h), "finish", small_cost)
    return handoff, jnp.stack(initial)[None], weight_grad


def solution(mesh):
    return jax.shard_map(
        shards,
        mesh=mesh,
        in_specs=(
            P("section", "rows", None),
            P("rows", None),
            P("section", None, None, "rows", None),
            P("section", None, None, "rows", None),
            P("section", None, None, None),
            P("section", None, "rows", None, None),
            P("section", None, "rows"),
            P("section", None, "rows"),
            P("section", None, "rows"),
        ),
        out_specs=(
            P(None, "section", "rows", None),
            P("section", None, "rows", None),
            P("section", None, None, None),
        ),
        check_vma=False,
    )
```

```python
import functools

import jax
import jax.numpy as jnp
from jax import lax
from jax.experimental import pallas as pl
from jax.experimental.pallas import tpu as pltpu
from jax.sharding import PartitionSpec as P

ALPHA = 0.1
BETA_SCALE = 0.5
VMEM = pl.BlockSpec(memory_space=pltpu.VMEM)
SMEM = pl.BlockSpec(memory_space=pltpu.SMEM)
HBM = pl.BlockSpec(memory_space=pltpu.HBM)
PARAMS = pltpu.CompilerParams(vmem_limit_bytes=24 * 2**20)
F32 = jnp.float32
BF16 = jnp.bfloat16


def cost(flops, nbytes):
    return pl.CostEstimate(flops=flops, bytes_accessed=nbytes, transcendentals=0)


def swapped(block, k):
    n = lax.axis_size("rows")
    return lax.ppermute(block, "rows", [(i, i ^ k) for i in range(n)])


def lowered(block, k):
    n, sections = lax.axis_size("rows"), lax.axis_size("section")
    route = [
        (s * n + i, (s - 1) % sections * n + (i ^ k)) for s in range(sections) for i in range(n)
    ]
    return lax.ppermute(block, ("section", "rows"), route)


def raised(block):
    sections = lax.axis_size("section")
    return lax.ppermute(block, "section", [(s, (s + 1) % sections) for s in range(sections)])


def shared(blocks, move=swapped):
    moved = {k: move(block, k) for k, block in reversed(list(enumerate(blocks, 1)))}
    return [moved[k] for k in sorted(moved)]


class Refs:
    def __init__(self, refs):
        self.refs = list(refs)

    def take(self, count=None):
        many = 1 if count is None else count
        taken, self.refs = self.refs[:many], self.refs[many:]
        return taken[0] if count is None else taken


class Call:
    def __init__(self):
        self.operands, self.specs, self.outs, self.out_specs, self.scratch = [], [], [], [], []
        self.aliases = {}

    def give(self, spec, *arrays):
        self.operands += arrays
        self.specs += [spec] * len(arrays)

    def want(self, spec, shape, dtype, count=1):
        self.outs += [jax.ShapeDtypeStruct(shape, dtype)] * count
        self.out_specs += [spec] * count

    def run(self, kernel, name, estimate, params=PARAMS):
        return pl.pallas_call(
            kernel,
            out_shape=self.outs,
            in_specs=self.specs,
            out_specs=self.out_specs,
            scratch_shapes=self.scratch,
            input_output_aliases=self.aliases,
            compiler_params=params,
            cost_estimate=estimate,
            name=name,
        )(*self.operands)


def packed(tile_row, tile_col, tile_count, row_tiles):
    owner = jnp.bitwise_xor(tile_col // row_tiles, lax.axis_index("rows"))
    words = (owner * row_tiles + tile_col % row_tiles) * row_tiles + tile_row
    live = lax.broadcasted_iota(jnp.int32, words.shape, 2) < tile_count
    return jnp.where(live, words, -1)[0]


def densify_kernel(tick, row_tiles, n, chunks, words_ref, vals_ref, out_ref, vals, acc, sems):
    entries, tile = vals.shape[:2]
    chunk = entries // chunks
    copies = []
    for c in range(chunks):
        part = pl.ds(c * chunk, chunk)
        copies.append(
            pltpu.make_async_copy(vals_ref.at[0, tick, part], vals.at[part], sems.at[c])
        )
        copies[c].start()
    acc[...] = jnp.zeros_like(acc)

    def add(e):
        word = words_ref[tick, e]
        row = lax.rem(word, row_tiles)
        block = lax.rem(lax.div(word, row_tiles), row_tiles)
        slot = lax.div(word, row_tiles * row_tiles)
        slot = jnp.where((slot == 0) & (block > 0), n - 1 + block, slot)
        rows = pl.ds(pl.multiple_of(row * tile, tile), tile)
        cols = pl.ds(pl.multiple_of(slot * tile, tile), tile)
        acc[rows, cols] += vals[e].astype(F32)

    for c in range(chunks):
        copies[c].wait()

        @pl.loop(c * chunk, (c + 1) * chunk)
        def _(e):
            @pl.when(words_ref[tick, e] >= 0)
            def _():
                add(e)

    out_ref[...] = acc[...].astype(BF16)


def densify(tick, words, vals, row_tiles, n):
    entries, tile = vals.shape[2:4]
    chunks = 4 if entries % 4 == 0 else 1
    shape = (row_tiles * tile, (n + row_tiles - 1) * tile)
    call = Call()
    call.give(SMEM, words)
    call.give(HBM, vals)
    call.want(VMEM, shape, BF16)
    call.scratch = [
        pltpu.VMEM(vals.shape[2:], BF16),
        pltpu.VMEM(shape, F32),
        pltpu.SemaphoreType.DMA((chunks,)),
    ]
    (adj,) = call.run(
        functools.partial(densify_kernel, tick, row_tiles, n, chunks),
        "densify",
        cost(entries * tile * tile * 20, entries * tile * tile * 2),
        pltpu.CompilerParams(vmem_limit_bytes=50 * 2**20),
    )
    return adj


def tile_at(ref, index, tile):
    return ref[pl.ds(pl.multiple_of(index * tile, tile), tile), :]


def name_kernel(n, row_tiles, words_ref, *out_refs):
    ticks, width = out_refs[0].shape
    for t in range(ticks):
        words = words_ref[t : t + 1, :]
        index = jnp.where(words < 0, -1, words // row_tiles)

        def named(k):
            block = index - k * row_tiles
            block = jnp.where((block >= 0) & (block < row_tiles), block, 0)
            most = jnp.max(block.astype(F32), axis=1, keepdims=True)
            return jnp.broadcast_to(most, (1, width))

        for k in range(1, n // 2):
            out_refs[k][2 * t : 2 * t + 1, :] = named(k)
            out_refs[k][2 * t + 1 : 2 * t + 2, :] = named(n // 2 + k)
        out_refs[0][t : t + 1, :] = named(n // 2)


def pack_kernel(tick, layer, preact_all, weight_all, *refs):
    asked, (out_ref, sems) = refs[:-2], refs[-2:]
    rows, width = preact_all.shape[-2:]
    loads = [
        pltpu.make_async_copy(preact_all.at[0, tick, layer], out_ref.at[:rows], sems.at[0]),
        pltpu.make_async_copy(
            weight_all.at[0, layer], out_ref.at[rows : rows + width], sems.at[1]
        ),
    ]
    for load in loads:
        load.start()
    used = sum(ref.shape[0] for ref in asked)
    rest = out_ref.shape[0] - rows - width - used
    parts = [ref[...] for ref in asked] + ([jnp.zeros((rest, width), F32)] if rest else [])
    out_ref[rows + width :, :] = jnp.concatenate(parts, axis=0).astype(BF16)
    for load in loads:
        load.wait()


def chosen(image_ref, row, rows, tile):
    index = jnp.broadcast_to(row.astype(BF16), (tile, row.shape[1]))
    result = image_ref[:tile, :]
    for i in range(1, rows // tile):
        result = jnp.where(index > i - 0.5, image_ref[i * tile : (i + 1) * tile, :], result)
    return result


def take_got(refs, c):
    far, near = refs.take(), refs.take(c["n"] // 2 - 1)
    if c["joined"]:
        return far, near, [ref.at[c["tile"] :, :] for ref in near]
    return far, near, refs.take(c["n"] // 2 - 1)


def spread_of(adj_ref, own_ref, got, names_ref, c):
    tile, rows = c["tile"], c["rows"]
    far, near, relayed = got
    far = chosen(far, names_ref[c["tick"] : c["tick"] + 1, :], rows, tile)
    near = [ref[:tile, :] for ref in near]
    relayed = [ref[:tile, :] for ref in relayed]
    blocks = jnp.concatenate(
        [own_ref[:tile, :]] + near + [far] + relayed + [own_ref[tile:, :]], axis=0
    )
    total = jnp.dot(adj_ref[...], blocks, preferred_element_type=F32)
    return ((1.0 - ALPHA) * total).astype(BF16)


def image_of(c, section, layer, grad, preact, weight):
    step = (c["layers"] * section + layer + 1).astype(F32)
    beta = jnp.log(BETA_SCALE / jnp.full((1, c["width"]), step, F32) + 1.0)
    masked = jnp.where(preact > 0, grad, jnp.zeros_like(grad))
    product = lax.dot_general(
        masked, weight, (((1,), (1,)), ((), ())), preferred_element_type=F32
    )
    image = ((1.0 - beta) * masked.astype(F32) + beta * product).astype(BF16)
    return beta, masked, image


def layer_kernel(c, *refs):
    refs = Refs(refs)
    n, tile, width, chunk = c["n"], c["tile"], c["width"], c["chunk"]
    h = n // 2
    preact_all, weight_all, names_ref = refs.take(3)
    asked = refs.take(h - 1)
    if c["entry"]:
        last_ref, passed_ref = refs.take(2)
    else:
        adj_ref, own_ref = refs.take(2)
        got = take_got(refs, c)
    if c["final"]:
        support_all, acc_ref = refs.take(2)
        pending = refs.take(c["pending"])
    image_ref = refs.take()
    sends = [] if c["entry"] else refs.take(h - 1)
    parts = refs.take(h - 1) if c["final"] and c["layer"] else []
    out_ref = refs.take()
    if c["final"]:
        term_ref = refs.take()
    preact_ref = preact_all.at[0, c["tick"], c["layer"]]
    weight_ref = weight_all.at[0, c["layer"]]
    section = lax.axis_index("section")
    if not c["entry"]:
        grad = spread_of(adj_ref, own_ref, got, names_ref, c)
    if c["entry"]:
        grad = jnp.where(section == c["sections"] - 1, last_ref[...], passed_ref[...])

    beta, masked, image = image_of(
        c, section, c["layer"], grad, preact_ref[...], weight_ref[...]
    )
    image_ref[...] = image
    if not c["entry"]:
        for send, asked_ref in zip(sends, asked):
            row = asked_ref[2 * c["tick"] : 2 * c["tick"] + 1, :]
            send[:tile, :] = chosen(image_ref, row, c["rows"], tile)
    if c["final"]:
        term = lax.dot_general(
            support_all[0, c["tick"], c["layer"]],
            masked,
            (((0,), (0,)), ((), ())),
            preferred_element_type=F32,
        )
        term_ref[...] = acc_ref[...] + beta * term
        place = lax.rem(lax.axis_index("rows"), h)
        for k in range(1, h):
            part = tile_at(term_ref, jnp.bitwise_xor(place, k), chunk).astype(BF16)
            if c["layer"]:
                parts[k - 1][...] = part
            else:
                sends[k - 1][tile : tile + chunk, :] = part
                for i, ref in enumerate(pending[k - 1 :: h - 1], 1):
                    sends[k - 1][tile + i * chunk : tile + (i + 1) * chunk, :] = ref[...]
        out_ref[...] = tile_at(term_ref, place, chunk)
    else:
        out_ref[...] = masked


def forward_kernel(c, *refs):
    refs = Refs(refs)
    count, tile, rows = c["n"] // 2 - 1, c["tile"], c["rows"]
    far_ref = refs.take()
    own_ref = refs.take() if c["first"] else None
    asked = refs.take(count)
    for asked_ref, send in zip(asked, refs.take(count)):
        row = 2 * c["tick"]
        if c["first"]:
            send[:tile, :] = chosen(own_ref, asked_ref[row : row + 1, :], rows, tile)
            send[tile:, :] = chosen(far_ref, asked_ref[row + 1 : row + 2, :], rows, tile)
        else:
            send[...] = chosen(far_ref, asked_ref[row + 1 : row + 2, :], rows, tile)


def half_sum_kernel(layers, tile, *refs):
    out_ref = refs[-1]
    chunk = out_ref.shape[1]
    for layer in range(layers):
        total = refs[layer][...]
        at = tile + layer * chunk
        for ref in refs[layers:-1]:
            total = total + ref[at : at + chunk, :].astype(F32)
        out_ref[layer] = total.astype(BF16)


def total_kernel(mine_ref, far_ref, out_ref):
    out_ref[...] = (mine_ref[...].astype(F32) + far_ref[...].astype(F32)).astype(BF16)


def turn_kernel(c, *refs):
    refs = Refs(refs)
    names_ref, adj_ref, own_ref = refs.take(3)
    got = take_got(refs, c)
    below_ref, last_ref = refs.take(2)
    grad_ref, image_ref = refs.take(2)
    sends = refs.take(c["n"] // 2 - 1)
    tile, rows, width = c["tile"], c["rows"], c["width"]
    grad = spread_of(adj_ref, own_ref, got, names_ref, c)
    grad_ref[...] = grad
    section = lax.axis_index("section")
    grad = jnp.where(section == 0, last_ref[...], grad)
    below = jnp.where(section == 0, c["sections"], section) - 1
    _, _, image = image_of(
        c, below, c["layers"] - 1, grad, below_ref[:rows, :], below_ref[rows : rows + width, :]
    )
    image_ref[...] = image
    asked = below_ref[rows + width :, :].astype(F32)
    for k, send in enumerate(sends):
        row = 2 * (k * c["ticks"] + c["tick"] + 1)
        send[...] = chosen(image_ref, asked[row : row + 1, :], rows, tile)


def exit_kernel(c, *refs):
    refs = Refs(refs)
    names_ref, adj_ref, own_ref = refs.take(3)
    got = take_got(refs, c)
    handed = refs.take(c["tick"])
    out_ref, hold_ref, sems = refs.take(3)
    copies = [
        pltpu.make_async_copy(ref, out_ref.at[t, 0], sems.at[t])
        for t, ref in enumerate(handed + [hold_ref])
    ]
    for copy in copies[:-1]:
        copy.start()
    hold_ref[...] = spread_of(adj_ref, own_ref, got, names_ref, c)
    copies[-1].start()
    for copy in copies:
        copy.wait()


def finish_kernel(h, *refs):
    sums, (out_ref, hold_ref, sems) = refs[:h], refs[h:]
    layers, chunk, _ = sums[0].shape
    place = lax.rem(lax.axis_index("rows"), h)
    copies = []
    for layer in range(layers):
        for k in range(h):
            start = pl.multiple_of(jnp.bitwise_xor(place, k) * chunk, chunk)
            hold_ref[layer, pl.ds(start, chunk), :] = sums[k][layer].astype(F32)
        copy = pltpu.make_async_copy(hold_ref.at[layer], out_ref.at[0, layer], sems.at[layer])
        copy.start()
        copies.append(copy)
    for copy in copies:
        copy.wait()


def shards(grad_in, grad_last, support, preact, weights, tile_vals, tile_row, tile_col, tile_count):
    section = lax.axis_index("section")
    n = lax.axis_size("rows")
    h = n // 2
    sections = lax.axis_size("section")
    ticks = support.shape[1]
    layers = support.shape[2]
    rows, width = grad_last.shape
    tile = tile_vals.shape[-1]
    row_tiles = rows // tile
    chunk = width // h
    words = packed(tile_row, tile_col, tile_count, row_tiles)

    handed = []
    turned = None
    weight_acc = [None] * layers
    kept_chunks, pending = [], []
    initial = []
    base = dict(
        n=n, tile=tile, rows=rows, width=width, layers=layers, sections=sections, chunk=chunk,
        ticks=ticks,
    )
    layer_cost = cost(2 * rows * width * (width + (n + 1) * tile), (6 + 2 * n) * rows * width)
    small_cost = cost(rows * width, 2 * n * rows * width)
    relay_cost = cost(rows * width, 8 * n * rows * width)
    call = Call()
    call.give(VMEM, words)
    call.want(VMEM, (ticks, width), F32)
    call.want(VMEM, (2 * ticks, width), F32, h - 1)
    names, *asking = call.run(functools.partial(name_kernel, n, row_tiles), "name", small_cost)
    asked = shared(asking)

    adjs = [None] * ticks
    for tick in range(ticks):
        final = tick == ticks - 1
        if tick > 0:
            passed = lowered(handed[-1], 0)
        image = got = joined = None
        toward = 0.0
        for layer in reversed(range(layers)):
            entry = layer == layers - 1
            beta = jnp.log(BETA_SCALE / (layers * section + layer + 1).astype(F32) + 1.0)
            c = dict(
                base, layer=layer, tick=tick, entry=entry, final=final, joined=joined,
                first=tick == 0 and entry, pending=0 if layer else len(pending),
            )
            if c["first"]:
                masked = jnp.where(
                    preact[0, tick, layer] > 0, grad_in[0], jnp.zeros_like(grad_in[0])
                )
                product = jnp.dot(masked, weights[0, layer].T, preferred_element_type=F32)
                image = ((1.0 - beta) * masked.astype(F32) + beta * product).astype(BF16)
            else:
                call = Call()
                call.give(VMEM, preact, weights, names, *asked)
                if entry:
                    call.give(VMEM, grad_last, passed)
                else:
                    call.give(VMEM, adjs[tick], image, *got)
                if final:
                    call.give(VMEM, support, weight_acc[layer])
                    if layer == 0:
                        call.give(VMEM, *pending)
                call.want(VMEM, (rows, width), BF16)
                if not entry:
                    message = tile + (layers * chunk if final and layer == 0 else 0)
                    call.want(VMEM, (message, width), BF16, h - 1)
                if final and layer:
                    call.want(VMEM, (chunk, width), BF16, h - 1)
                if final:
                    call.want(VMEM, (chunk, width), F32)
                else:
                    call.want(VMEM, (rows, width), BF16)
                if final:
                    call.scratch = [pltpu.VMEM((width, width), F32)]
                results = Refs(
                    call.run(
                        functools.partial(layer_kernel, c),
                        "home" if entry else "middle",
                        layer_cost,
                    )
                )
                image = results.take()
                sends = [] if entry else results.take(h - 1)
                if final and layer:
                    pending = results.take(h - 1) + pending
                kept = masked = results.take()
            if turned is not None:
                far = lowered(turned[0], h)
                near = shared(turned[1:], lowered)
                far, *near = lax.optimization_barrier((far, *near))
                turned = None
                if final:
                    parts = shared(sends)
            else:
                far = swapped(image, h)
                near = [] if c["first"] else shared(sends)
            ready = image
            if c["first"]:
                adjs[0] = densify(0, words, tile_vals, row_tiles, n)
                ready, adjs[0] = lax.optimization_barrier((image, adjs[0]))
            call = Call()
            call.give(VMEM, far)
            if c["first"]:
                call.give(VMEM, ready)
            call.give(VMEM, *asked)
            call.want(VMEM, (tile * (1 + c["first"]), width), BF16, h - 1)
            relays = call.run(functools.partial(forward_kernel, c), "forward", small_cost)
            relayed = shared(relays)
            if entry and not final:
                later, _ = lax.optimization_barrier((words, relays))
                adjs[tick + 1] = densify(tick + 1, later, tile_vals, row_tiles, n)
                relayed, adjs[tick + 1] = lax.optimization_barrier((relayed, adjs[tick + 1]))
            if final:
                kept_chunks.insert(0, kept)
            if final and layer == 0:
                kept, _ = lax.optimization_barrier((kept_chunks, relays))
                call = Call()
                call.give(VMEM, *kept, *near)
                call.want(VMEM, (layers, chunk, width), BF16)
                (mine,) = call.run(
                    functools.partial(half_sum_kernel, layers, tile), "half_sum", small_cost
                )
            got = [far, *near, *relayed]
            joined = c["first"]
            toward = toward + ALPHA * image.astype(F32)
            if not final:
                term = beta * jnp.dot(
                    support[0, tick, layer].T, masked, preferred_element_type=F32
                )
                old = weight_acc[layer]
                weight_acc[layer] = term if old is None else old + term
        initial.append(toward)
        c = dict(base, tick=tick, final=final, joined=joined)
        call = Call()
        call.give(VMEM, names, adjs[tick], image, *got)
        if not final:
            up = Call()
            up.give(HBM, preact, weights)
            up.give(VMEM, *asked)
            length = rows + width + -(-2 * ticks * (h - 1) // 16) * 16
            up.want(VMEM, (length, width), BF16)
            up.scratch = [pltpu.SemaphoreType.DMA((2,))]
            (pack,) = up.run(
                functools.partial(pack_kernel, tick + 1, layers - 1), "pack", small_cost
            )
            call.give(VMEM, raised(pack), grad_last)
            call.want(VMEM, (rows, width), BF16, 2)
            call.want(VMEM, (tile, width), BF16, h - 1)
            grad, *turned = call.run(functools.partial(turn_kernel, c), "turn", layer_cost)
            handed.append(grad)
            continue
        call.give(VMEM, *handed)
        call.want(HBM, (ticks, 1, rows, width), BF16)
        call.scratch = [pltpu.VMEM((rows, width), BF16), pltpu.SemaphoreType.DMA((ticks,))]
        (handoff,) = call.run(functools.partial(exit_kernel, c), "exit", layer_cost)
    call = Call()
    call.give(VMEM, mine, swapped(mine, h))
    call.want(VMEM, (layers, chunk, width), BF16)
    (total,) = call.run(total_kernel, "total", small_cost)
    call = Call()
    call.give(VMEM, total, *shared([total] * (h - 1)))
    call.want(HBM, (1, layers, width, width), F32)
    call.scratch = [pltpu.VMEM((layers, width, width), F32), pltpu.SemaphoreType.DMA((layers,))]
    (weight_grad,) = call.run(functools.partial(finish_kernel, h), "finish", small_cost)
    return handoff, jnp.stack(initial)[None], weight_grad


def solution(mesh):
    return jax.shard_map(
        shards,
        mesh=mesh,
        in_specs=(
            P("section", "rows", None),
            P("rows", None),
            P("section", None, None, "rows", None),
            P("section", None, None, "rows", None),
            P("section", None, None, None),
            P("section", None, "rows", None, None),
            P("section", None, "rows"),
            P("section", None, "rows"),
            P("section", None, "rows"),
        ),
        out_specs=(
            P(None, "section", "rows", None),
            P("section", None, "rows", None),
            P("section", None, None, None),
        ),
        check_vma=False,
    )
```

```python
import functools

import jax
import jax.numpy as jnp
from jax import lax
from jax.experimental import pallas as pl
from jax.experimental.pallas import tpu as pltpu
from jax.sharding import PartitionSpec as P

ALPHA = 0.1
BETA_SCALE = 0.5
VMEM = pl.BlockSpec(memory_space=pltpu.VMEM)
SMEM = pl.BlockSpec(memory_space=pltpu.SMEM)
HBM = pl.BlockSpec(memory_space=pltpu.HBM)
PARAMS = pltpu.CompilerParams(vmem_limit_bytes=24 * 2**20)
F32 = jnp.float32
BF16 = jnp.bfloat16


def cost(flops, nbytes):
    return pl.CostEstimate(flops=flops, bytes_accessed=nbytes, transcendentals=0)


def swapped(block, k):
    n = lax.axis_size("rows")
    return lax.ppermute(block, "rows", [(i, i ^ k) for i in range(n)])


def lowered(block, k):
    n, sections = lax.axis_size("rows"), lax.axis_size("section")
    route = [
        (s * n + i, (s - 1) % sections * n + (i ^ k)) for s in range(sections) for i in range(n)
    ]
    return lax.ppermute(block, ("section", "rows"), route)


def raised(block):
    sections = lax.axis_size("section")
    return lax.ppermute(block, "section", [(s, (s + 1) % sections) for s in range(sections)])


def shared(blocks, move=swapped):
    moved = {k: move(block, k) for k, block in reversed(list(enumerate(blocks, 1)))}
    return [moved[k] for k in sorted(moved)]


class Refs:
    def __init__(self, refs):
        self.refs = list(refs)

    def take(self, count=None):
        many = 1 if count is None else count
        taken, self.refs = self.refs[:many], self.refs[many:]
        return taken[0] if count is None else taken


class Call:
    def __init__(self):
        self.operands, self.specs, self.outs, self.out_specs, self.scratch = [], [], [], [], []
        self.aliases = {}

    def give(self, spec, *arrays):
        self.operands += arrays
        self.specs += [spec] * len(arrays)

    def want(self, spec, shape, dtype, count=1):
        self.outs += [jax.ShapeDtypeStruct(shape, dtype)] * count
        self.out_specs += [spec] * count

    def run(self, kernel, name, estimate, params=PARAMS):
        return pl.pallas_call(
            kernel,
            out_shape=self.outs,
            in_specs=self.specs,
            out_specs=self.out_specs,
            scratch_shapes=self.scratch,
            input_output_aliases=self.aliases,
            compiler_params=params,
            cost_estimate=estimate,
            name=name,
        )(*self.operands)


COUNT_UNIT = 1 << 16


def packed(tile_row, tile_col, tile_count, row_tiles):
    owner = jnp.bitwise_xor(tile_col // row_tiles, lax.axis_index("rows"))
    words = (owner * row_tiles + tile_col % row_tiles) * row_tiles + tile_row
    words = words + tile_count * COUNT_UNIT
    live = lax.broadcasted_iota(jnp.int32, words.shape, 2) < tile_count
    return jnp.where(live, words, -1)[0]


def densify_kernel(tick, row_tiles, n, chunks, words_ref, vals_ref, out_ref, vals, acc, sems):
    entries, tile = vals.shape[:2]
    chunk = entries // chunks
    copies = []
    for c in range(chunks):
        part = pl.ds(c * chunk, chunk)
        copies.append(
            pltpu.make_async_copy(vals_ref.at[0, tick, part], vals.at[part], sems.at[c])
        )
        copies[c].start()
    acc[...] = jnp.zeros_like(acc)

    def add(e):
        word = lax.rem(words_ref[tick, e], COUNT_UNIT)
        row = lax.rem(word, row_tiles)
        block = lax.rem(lax.div(word, row_tiles), row_tiles)
        slot = lax.div(word, row_tiles * row_tiles)
        slot = jnp.where((slot == 0) & (block > 0), n - 1 + block, slot)
        rows = pl.ds(pl.multiple_of(row * tile, tile), tile)
        cols = pl.ds(pl.multiple_of(slot * tile, tile), tile)
        acc[rows, cols] += vals[e].astype(F32)

    count = lax.div(jnp.maximum(words_ref[tick, 0], 0), COUNT_UNIT)
    for c in range(chunks):
        copies[c].wait()
        live = jnp.clip(count - c * chunk, 0, chunk)

        @pl.loop(0, live // 2)
        def _(i):
            add(c * chunk + 2 * i)
            add(c * chunk + 2 * i + 1)

        @pl.when(live % 2 == 1)
        def _():
            add(c * chunk + live - 1)

    out_ref[...] = acc[...].astype(BF16)


def densify(tick, words, vals, row_tiles, n):
    entries, tile = vals.shape[2:4]
    chunks = 4 if entries % 4 == 0 else 1
    shape = (row_tiles * tile, (n + row_tiles - 1) * tile)
    call = Call()
    call.give(SMEM, words)
    call.give(HBM, vals)
    call.want(VMEM, shape, BF16)
    call.scratch = [
        pltpu.VMEM(vals.shape[2:], BF16),
        pltpu.VMEM(shape, F32),
        pltpu.SemaphoreType.DMA((chunks,)),
    ]
    (adj,) = call.run(
        functools.partial(densify_kernel, tick, row_tiles, n, chunks),
        "densify",
        cost(entries * tile * tile * 20, entries * tile * tile * 2),
        pltpu.CompilerParams(vmem_limit_bytes=50 * 2**20),
    )
    return adj


def tile_at(ref, index, tile):
    return ref[pl.ds(pl.multiple_of(index * tile, tile), tile), :]


def name_kernel(n, row_tiles, words_ref, *out_refs):
    ticks, width = out_refs[0].shape
    for t in range(ticks):
        words = words_ref[t : t + 1, :]
        index = jnp.where(words < 0, -1, words % COUNT_UNIT // row_tiles)

        def named(k):
            block = index - k * row_tiles
            block = jnp.where((block >= 0) & (block < row_tiles), block, 0)
            most = jnp.max(block.astype(F32), axis=1, keepdims=True)
            return jnp.broadcast_to(most, (1, width))

        for k in range(1, n // 2):
            out_refs[k][2 * t : 2 * t + 1, :] = named(k)
            out_refs[k][2 * t + 1 : 2 * t + 2, :] = named(n // 2 + k)
        out_refs[0][t : t + 1, :] = named(n // 2)


def pack_kernel(tick, layer, preact_all, weight_all, *refs):
    asked, (out_ref, sems) = refs[:-2], refs[-2:]
    rows, width = preact_all.shape[-2:]
    loads = [
        pltpu.make_async_copy(preact_all.at[0, tick, layer], out_ref.at[:rows], sems.at[0]),
        pltpu.make_async_copy(
            weight_all.at[0, layer], out_ref.at[rows : rows + width], sems.at[1]
        ),
    ]
    for load in loads:
        load.start()
    used = sum(ref.shape[0] for ref in asked)
    rest = out_ref.shape[0] - rows - width - used
    parts = [ref[...] for ref in asked] + ([jnp.zeros((rest, width), F32)] if rest else [])
    out_ref[rows + width :, :] = jnp.concatenate(parts, axis=0).astype(BF16)
    for load in loads:
        load.wait()


def chosen(image_ref, row, rows, tile):
    index = jnp.broadcast_to(row.astype(BF16), (tile, row.shape[1]))
    result = image_ref[:tile, :]
    for i in range(1, rows // tile):
        result = jnp.where(index > i - 0.5, image_ref[i * tile : (i + 1) * tile, :], result)
    return result


def take_got(refs, c):
    far, near = refs.take(), refs.take(c["n"] // 2 - 1)
    if c["joined"]:
        return far, near, [ref.at[c["tile"] :, :] for ref in near]
    return far, near, refs.take(c["n"] // 2 - 1)


def spread_of(adj_ref, own_ref, got, names_ref, c):
    tile, rows = c["tile"], c["rows"]
    far, near, relayed = got
    far = chosen(far, names_ref[c["tick"] : c["tick"] + 1, :], rows, tile)
    near = [ref[:tile, :] for ref in near]
    relayed = [ref[:tile, :] for ref in relayed]
    blocks = jnp.concatenate(
        [own_ref[:tile, :]] + near + [far] + relayed + [own_ref[tile:, :]], axis=0
    )
    total = jnp.dot(adj_ref[...], blocks, preferred_element_type=F32)
    return ((1.0 - ALPHA) * total).astype(BF16)


def image_of(c, section, layer, grad, preact, weight):
    step = (c["layers"] * section + layer + 1).astype(F32)
    beta = jnp.log(BETA_SCALE / jnp.full((1, c["width"]), step, F32) + 1.0)
    masked = jnp.where(preact > 0, grad, jnp.zeros_like(grad))
    product = lax.dot_general(
        masked, weight, (((1,), (1,)), ((), ())), preferred_element_type=F32
    )
    image = ((1.0 - beta) * masked.astype(F32) + beta * product).astype(BF16)
    return beta, masked, image


def layer_kernel(c, *refs):
    refs = Refs(refs)
    n, tile, width, chunk = c["n"], c["tile"], c["width"], c["chunk"]
    h = n // 2
    preact_all, weight_all, names_ref = refs.take(3)
    asked = refs.take(h - 1)
    if c["entry"]:
        last_ref, passed_ref = refs.take(2)
    else:
        adj_ref, own_ref = refs.take(2)
        got = take_got(refs, c)
    if c["final"]:
        support_all, acc_ref = refs.take(2)
        pending = refs.take(c["pending"])
    image_ref = refs.take()
    sends = [] if c["entry"] else refs.take(h - 1)
    parts = refs.take(h - 1) if c["final"] and c["layer"] else []
    out_ref = refs.take()
    if c["final"]:
        term_ref = refs.take()
    preact_ref = preact_all.at[0, c["tick"], c["layer"]]
    weight_ref = weight_all.at[0, c["layer"]]
    section = lax.axis_index("section")
    if not c["entry"]:
        grad = spread_of(adj_ref, own_ref, got, names_ref, c)
    if c["entry"]:
        grad = jnp.where(section == c["sections"] - 1, last_ref[...], passed_ref[...])

    beta, masked, image = image_of(
        c, section, c["layer"], grad, preact_ref[...], weight_ref[...]
    )
    image_ref[...] = image
    if not c["entry"]:
        for send, asked_ref in zip(sends, asked):
            row = asked_ref[2 * c["tick"] : 2 * c["tick"] + 1, :]
            send[:tile, :] = chosen(image_ref, row, c["rows"], tile)
    if c["final"]:
        term = lax.dot_general(
            support_all[0, c["tick"], c["layer"]],
            masked,
            (((0,), (0,)), ((), ())),
            preferred_element_type=F32,
        )
        term_ref[...] = acc_ref[...] + beta * term
        place = lax.rem(lax.axis_index("rows"), h)
        for k in range(1, h):
            part = tile_at(term_ref, jnp.bitwise_xor(place, k), chunk).astype(BF16)
            if c["layer"]:
                parts[k - 1][...] = part
            else:
                sends[k - 1][tile : tile + chunk, :] = part
                for i, ref in enumerate(pending[k - 1 :: h - 1], 1):
                    sends[k - 1][tile + i * chunk : tile + (i + 1) * chunk, :] = ref[...]
        out_ref[...] = tile_at(term_ref, place, chunk)
    else:
        out_ref[...] = masked


def forward_kernel(c, *refs):
    refs = Refs(refs)
    count, tile, rows = c["n"] // 2 - 1, c["tile"], c["rows"]
    far_ref = refs.take()
    own_ref = refs.take() if c["first"] else None
    asked = refs.take(count)
    for asked_ref, send in zip(asked, refs.take(count)):
        row = 2 * c["tick"]
        if c["first"]:
            send[:tile, :] = chosen(own_ref, asked_ref[row : row + 1, :], rows, tile)
            send[tile:, :] = chosen(far_ref, asked_ref[row + 1 : row + 2, :], rows, tile)
        else:
            send[...] = chosen(far_ref, asked_ref[row + 1 : row + 2, :], rows, tile)


def half_sum_kernel(layers, tile, *refs):
    out_ref = refs[-1]
    chunk = out_ref.shape[1]
    for layer in range(layers):
        total = refs[layer][...]
        at = tile + layer * chunk
        for ref in refs[layers:-1]:
            total = total + ref[at : at + chunk, :].astype(F32)
        out_ref[layer] = total.astype(BF16)


def total_kernel(mine_ref, far_ref, out_ref):
    out_ref[...] = (mine_ref[...].astype(F32) + far_ref[...].astype(F32)).astype(BF16)


def turn_kernel(c, *refs):
    refs = Refs(refs)
    names_ref, adj_ref, own_ref = refs.take(3)
    got = take_got(refs, c)
    below_ref, last_ref = refs.take(2)
    grad_ref, image_ref = refs.take(2)
    sends = refs.take(c["n"] // 2 - 1)
    tile, rows, width = c["tile"], c["rows"], c["width"]
    grad = spread_of(adj_ref, own_ref, got, names_ref, c)
    grad_ref[...] = grad
    section = lax.axis_index("section")
    grad = jnp.where(section == 0, last_ref[...], grad)
    below = jnp.where(section == 0, c["sections"], section) - 1
    _, _, image = image_of(
        c, below, c["layers"] - 1, grad, below_ref[:rows, :], below_ref[rows : rows + width, :]
    )
    image_ref[...] = image
    asked = below_ref[rows + width :, :].astype(F32)
    for k, send in enumerate(sends):
        row = 2 * (k * c["ticks"] + c["tick"] + 1)
        send[...] = chosen(image_ref, asked[row : row + 1, :], rows, tile)


def exit_kernel(c, *refs):
    refs = Refs(refs)
    names_ref, adj_ref, own_ref = refs.take(3)
    got = take_got(refs, c)
    handed = refs.take(c["tick"])
    out_ref, hold_ref, sems = refs.take(3)
    copies = [
        pltpu.make_async_copy(ref, out_ref.at[t, 0], sems.at[t])
        for t, ref in enumerate(handed + [hold_ref])
    ]
    for copy in copies[:-1]:
        copy.start()
    hold_ref[...] = spread_of(adj_ref, own_ref, got, names_ref, c)
    copies[-1].start()
    for copy in copies:
        copy.wait()


def finish_kernel(h, *refs):
    sums, (out_ref, hold_ref, sems) = refs[:h], refs[h:]
    layers, chunk, _ = sums[0].shape
    place = lax.rem(lax.axis_index("rows"), h)
    copies = []
    for layer in range(layers):
        for k in range(h):
            start = pl.multiple_of(jnp.bitwise_xor(place, k) * chunk, chunk)
            hold_ref[layer, pl.ds(start, chunk), :] = sums[k][layer].astype(F32)
        copy = pltpu.make_async_copy(hold_ref.at[layer], out_ref.at[0, layer], sems.at[layer])
        copy.start()
        copies.append(copy)
    for copy in copies:
        copy.wait()


def shards(grad_in, grad_last, support, preact, weights, tile_vals, tile_row, tile_col, tile_count):
    section = lax.axis_index("section")
    n = lax.axis_size("rows")
    h = n // 2
    sections = lax.axis_size("section")
    ticks = support.shape[1]
    layers = support.shape[2]
    rows, width = grad_last.shape
    tile = tile_vals.shape[-1]
    row_tiles = rows // tile
    chunk = width // h
    words = packed(tile_row, tile_col, tile_count, row_tiles)

    handed = []
    turned = None
    weight_acc = [None] * layers
    kept_chunks, pending = [], []
    initial = []
    base = dict(
        n=n, tile=tile, rows=rows, width=width, layers=layers, sections=sections, chunk=chunk,
        ticks=ticks,
    )
    layer_cost = cost(2 * rows * width * (width + (n + 1) * tile), (6 + 2 * n) * rows * width)
    small_cost = cost(rows * width, 2 * n * rows * width)
    relay_cost = cost(rows * width, 8 * n * rows * width)
    call = Call()
    call.give(VMEM, words)
    call.want(VMEM, (ticks, width), F32)
    call.want(VMEM, (2 * ticks, width), F32, h - 1)
    names, *asking = call.run(functools.partial(name_kernel, n, row_tiles), "name", small_cost)
    asked = shared(asking)

    adjs = [None] * ticks
    for tick in range(ticks):
        final = tick == ticks - 1
        if tick > 0:
            passed = lowered(handed[-1], 0)
        image = got = joined = None
        toward = 0.0
        for layer in reversed(range(layers)):
            entry = layer == layers - 1
            beta = jnp.log(BETA_SCALE / (layers * section + layer + 1).astype(F32) + 1.0)
            c = dict(
                base, layer=layer, tick=tick, entry=entry, final=final, joined=joined,
                first=tick == 0 and entry, pending=0 if layer else len(pending),
            )
            if c["first"]:
                masked = jnp.where(
                    preact[0, tick, layer] > 0, grad_in[0], jnp.zeros_like(grad_in[0])
                )
                product = jnp.dot(masked, weights[0, layer].T, preferred_element_type=F32)
                image = ((1.0 - beta) * masked.astype(F32) + beta * product).astype(BF16)
            else:
                call = Call()
                call.give(VMEM, preact, weights, names, *asked)
                if entry:
                    call.give(VMEM, grad_last, passed)
                else:
                    call.give(VMEM, adjs[tick], image, *got)
                if final:
                    call.give(VMEM, support, weight_acc[layer])
                    if layer == 0:
                        call.give(VMEM, *pending)
                call.want(VMEM, (rows, width), BF16)
                if not entry:
                    message = tile + (layers * chunk if final and layer == 0 else 0)
                    call.want(VMEM, (message, width), BF16, h - 1)
                if final and layer:
                    call.want(VMEM, (chunk, width), BF16, h - 1)
                if final:
                    call.want(VMEM, (chunk, width), F32)
                else:
                    call.want(VMEM, (rows, width), BF16)
                if final:
                    call.scratch = [pltpu.VMEM((width, width), F32)]
                results = Refs(
                    call.run(
                        functools.partial(layer_kernel, c),
                        "home" if entry else "middle",
                        layer_cost,
                    )
                )
                image = results.take()
                sends = [] if entry else results.take(h - 1)
                if final and layer:
                    pending = results.take(h - 1) + pending
                kept = masked = results.take()
            if turned is not None:
                far = lowered(turned[0], h)
                near = shared(turned[1:], lowered)
                far, *near = lax.optimization_barrier((far, *near))
                turned = None
                if final:
                    parts = shared(sends)
            else:
                far = swapped(image, h)
                near = [] if c["first"] else shared(sends)
            ready = image
            if c["first"]:
                adjs[0] = densify(0, words, tile_vals, row_tiles, n)
                ready, adjs[0] = lax.optimization_barrier((image, adjs[0]))
            call = Call()
            call.give(VMEM, far)
            if c["first"]:
                call.give(VMEM, ready)
            call.give(VMEM, *asked)
            call.want(VMEM, (tile * (1 + c["first"]), width), BF16, h - 1)
            relays = call.run(functools.partial(forward_kernel, c), "forward", small_cost)
            relayed = shared(relays)
            if entry and not final:
                later, _ = lax.optimization_barrier((words, relays))
                adjs[tick + 1] = densify(tick + 1, later, tile_vals, row_tiles, n)
                relayed, adjs[tick + 1] = lax.optimization_barrier((relayed, adjs[tick + 1]))
            if final:
                kept_chunks.insert(0, kept)
            if final and layer == 0:
                kept, _ = lax.optimization_barrier((kept_chunks, relays))
                call = Call()
                call.give(VMEM, *kept, *near)
                call.want(VMEM, (layers, chunk, width), BF16)
                (mine,) = call.run(
                    functools.partial(half_sum_kernel, layers, tile), "half_sum", small_cost
                )
            got = [far, *near, *relayed]
            joined = c["first"]
            toward = toward + ALPHA * image.astype(F32)
            if not final:
                term = beta * jnp.dot(
                    support[0, tick, layer].T, masked, preferred_element_type=F32
                )
                old = weight_acc[layer]
                weight_acc[layer] = term if old is None else old + term
        initial.append(toward)
        c = dict(base, tick=tick, final=final, joined=joined)
        call = Call()
        call.give(VMEM, names, adjs[tick], image, *got)
        if not final:
            up = Call()
            up.give(HBM, preact, weights)
            up.give(VMEM, *asked)
            length = rows + width + -(-2 * ticks * (h - 1) // 16) * 16
            up.want(VMEM, (length, width), BF16)
            up.scratch = [pltpu.SemaphoreType.DMA((2,))]
            (pack,) = up.run(
                functools.partial(pack_kernel, tick + 1, layers - 1), "pack", small_cost
            )
            call.give(VMEM, raised(pack), grad_last)
            call.want(VMEM, (rows, width), BF16, 2)
            call.want(VMEM, (tile, width), BF16, h - 1)
            grad, *turned = call.run(functools.partial(turn_kernel, c), "turn", layer_cost)
            handed.append(grad)
            continue
        call.give(VMEM, *handed)
        call.want(HBM, (ticks, 1, rows, width), BF16)
        call.scratch = [pltpu.VMEM((rows, width), BF16), pltpu.SemaphoreType.DMA((ticks,))]
        (handoff,) = call.run(functools.partial(exit_kernel, c), "exit", layer_cost)
    call = Call()
    call.give(VMEM, mine, swapped(mine, h))
    call.want(VMEM, (layers, chunk, width), BF16)
    (total,) = call.run(total_kernel, "total", small_cost)
    call = Call()
    call.give(VMEM, total, *shared([total] * (h - 1)))
    call.want(HBM, (1, layers, width, width), F32)
    call.scratch = [pltpu.VMEM((layers, width, width), F32), pltpu.SemaphoreType.DMA((layers,))]
    (weight_grad,) = call.run(functools.partial(finish_kernel, h), "finish", small_cost)
    return handoff, jnp.stack(initial)[None], weight_grad


def solution(mesh):
    return jax.shard_map(
        shards,
        mesh=mesh,
        in_specs=(
            P("section", "rows", None),
            P("rows", None),
            P("section", None, None, "rows", None),
            P("section", None, None, "rows", None),
            P("section", None, None, None),
            P("section", None, "rows", None, None),
            P("section", None, "rows"),
            P("section", None, "rows"),
            P("section", None, "rows"),
        ),
        out_specs=(
            P(None, "section", "rows", None),
            P("section", None, "rows", None),
            P("section", None, None, None),
        ),
        check_vma=False,
    )
```

```python
import functools

import jax
import jax.numpy as jnp
from jax import lax
from jax.experimental import pallas as pl
from jax.experimental.pallas import tpu as pltpu
from jax.sharding import PartitionSpec as P

ALPHA = 0.1
BETA_SCALE = 0.5
VMEM = pl.BlockSpec(memory_space=pltpu.VMEM)
SMEM = pl.BlockSpec(memory_space=pltpu.SMEM)
HBM = pl.BlockSpec(memory_space=pltpu.HBM)
PARAMS = pltpu.CompilerParams(vmem_limit_bytes=24 * 2**20)
F32 = jnp.float32
BF16 = jnp.bfloat16


def cost(flops, nbytes):
    return pl.CostEstimate(flops=flops, bytes_accessed=nbytes, transcendentals=0)


def swapped(block, k):
    n = lax.axis_size("rows")
    return lax.ppermute(block, "rows", [(i, i ^ k) for i in range(n)])


def lowered(block, k):
    n, sections = lax.axis_size("rows"), lax.axis_size("section")
    route = [
        (s * n + i, (s - 1) % sections * n + (i ^ k)) for s in range(sections) for i in range(n)
    ]
    return lax.ppermute(block, ("section", "rows"), route)


def raised(block):
    sections = lax.axis_size("section")
    return lax.ppermute(block, "section", [(s, (s + 1) % sections) for s in range(sections)])


def shared(blocks, move=swapped):
    moved = {k: move(block, k) for k, block in reversed(list(enumerate(blocks, 1)))}
    return [moved[k] for k in sorted(moved)]


class Refs:
    def __init__(self, refs):
        self.refs = list(refs)

    def take(self, count=None):
        many = 1 if count is None else count
        taken, self.refs = self.refs[:many], self.refs[many:]
        return taken[0] if count is None else taken


class Call:
    def __init__(self):
        self.operands, self.specs, self.outs, self.out_specs, self.scratch = [], [], [], [], []
        self.aliases = {}

    def give(self, spec, *arrays):
        self.operands += arrays
        self.specs += [spec] * len(arrays)

    def want(self, spec, shape, dtype, count=1):
        self.outs += [jax.ShapeDtypeStruct(shape, dtype)] * count
        self.out_specs += [spec] * count

    def run(self, kernel, name, estimate, params=PARAMS):
        return pl.pallas_call(
            kernel,
            out_shape=self.outs,
            in_specs=self.specs,
            out_specs=self.out_specs,
            scratch_shapes=self.scratch,
            input_output_aliases=self.aliases,
            compiler_params=params,
            cost_estimate=estimate,
            name=name,
        )(*self.operands)


def packed(tile_row, tile_col, tile_count, row_tiles):
    owner = jnp.bitwise_xor(tile_col // row_tiles, lax.axis_index("rows"))
    words = (owner * row_tiles + tile_col % row_tiles) * row_tiles + tile_row
    live = lax.broadcasted_iota(jnp.int32, words.shape, 2) < tile_count
    return jnp.where(live, words, -1)[0]


def densify_kernel(tick, row_tiles, n, chunks, words_ref, vals_ref, out_ref, vals, acc, sems):
    entries, tile = vals.shape[:2]
    chunk = entries // chunks
    copies = []
    for c in range(chunks):
        part = pl.ds(c * chunk, chunk)
        copies.append(
            pltpu.make_async_copy(vals_ref.at[0, tick, part], vals.at[part], sems.at[c])
        )
        copies[c].start()
    acc[...] = jnp.zeros_like(acc)

    def add(e):
        word = words_ref[tick, e]
        row = lax.rem(word, row_tiles)
        block = lax.rem(lax.div(word, row_tiles), row_tiles)
        slot = lax.div(word, row_tiles * row_tiles)
        slot = jnp.where((slot == 0) & (block > 0), n - 1 + block, slot)
        rows = pl.ds(pl.multiple_of(row * tile, tile), tile)
        cols = pl.ds(pl.multiple_of(slot * tile, tile), tile)
        acc[rows, cols] += vals[e].astype(F32)

    count, step = jnp.int32(0), 1 << (entries.bit_length() - 1)
    while step:
        probe = count + step
        live = (probe <= entries) & (words_ref[tick, jnp.minimum(probe, entries) - 1] >= 0)
        count = jnp.where(live, probe, count)
        step //= 2
    for c in range(chunks):
        copies[c].wait()
        live = jnp.clip(count - c * chunk, 0, chunk)

        @pl.loop(0, live // 2)
        def _(i):
            add(c * chunk + 2 * i)
            add(c * chunk + 2 * i + 1)

        @pl.when(live % 2 == 1)
        def _():
            add(c * chunk + live - 1)

    out_ref[...] = acc[...].astype(BF16)


def densify(tick, words, vals, row_tiles, n):
    entries, tile = vals.shape[2:4]
    chunks = 4 if entries % 4 == 0 else 1
    shape = (row_tiles * tile, (n + row_tiles - 1) * tile)
    call = Call()
    call.give(SMEM, words)
    call.give(HBM, vals)
    call.want(VMEM, shape, BF16)
    call.scratch = [
        pltpu.VMEM(vals.shape[2:], BF16),
        pltpu.VMEM(shape, F32),
        pltpu.SemaphoreType.DMA((chunks,)),
    ]
    (adj,) = call.run(
        functools.partial(densify_kernel, tick, row_tiles, n, chunks),
        "densify",
        cost(entries * tile * tile * 20, entries * tile * tile * 2),
        pltpu.CompilerParams(vmem_limit_bytes=50 * 2**20),
    )
    return adj


def tile_at(ref, index, tile):
    return ref[pl.ds(pl.multiple_of(index * tile, tile), tile), :]


def name_kernel(n, row_tiles, words_ref, *out_refs):
    ticks, width = out_refs[0].shape
    for t in range(ticks):
        words = words_ref[t : t + 1, :]
        index = jnp.where(words < 0, -1, words // row_tiles)

        def named(k):
            block = index - k * row_tiles
            block = jnp.where((block >= 0) & (block < row_tiles), block, 0)
            most = jnp.max(block.astype(F32), axis=1, keepdims=True)
            return jnp.broadcast_to(most, (1, width))

        for k in range(1, n // 2):
            out_refs[k][2 * t : 2 * t + 1, :] = named(k)
            out_refs[k][2 * t + 1 : 2 * t + 2, :] = named(n // 2 + k)
        out_refs[0][t : t + 1, :] = named(n // 2)


def pack_kernel(tick, layer, preact_all, weight_all, *refs):
    asked, (out_ref, sems) = refs[:-2], refs[-2:]
    rows, width = preact_all.shape[-2:]
    loads = [
        pltpu.make_async_copy(preact_all.at[0, tick, layer], out_ref.at[:rows], sems.at[0]),
        pltpu.make_async_copy(
            weight_all.at[0, layer], out_ref.at[rows : rows + width], sems.at[1]
        ),
    ]
    for load in loads:
        load.start()
    used = sum(ref.shape[0] for ref in asked)
    rest = out_ref.shape[0] - rows - width - used
    parts = [ref[...] for ref in asked] + ([jnp.zeros((rest, width), F32)] if rest else [])
    out_ref[rows + width :, :] = jnp.concatenate(parts, axis=0).astype(BF16)
    for load in loads:
        load.wait()


def chosen(image_ref, row, rows, tile):
    index = jnp.broadcast_to(row.astype(BF16), (tile, row.shape[1]))
    result = image_ref[:tile, :]
    for i in range(1, rows // tile):
        result = jnp.where(index > i - 0.5, image_ref[i * tile : (i + 1) * tile, :], result)
    return result


def take_got(refs, c):
    far, near = refs.take(), refs.take(c["n"] // 2 - 1)
    if c["joined"]:
        return far, near, [ref.at[c["tile"] :, :] for ref in near]
    return far, near, refs.take(c["n"] // 2 - 1)


def spread_of(adj_ref, own_ref, got, names_ref, c):
    tile, rows = c["tile"], c["rows"]
    far, near, relayed = got
    far = chosen(far, names_ref[c["tick"] : c["tick"] + 1, :], rows, tile)
    near = [ref[:tile, :] for ref in near]
    relayed = [ref[:tile, :] for ref in relayed]
    blocks = jnp.concatenate(
        [own_ref[:tile, :]] + near + [far] + relayed + [own_ref[tile:, :]], axis=0
    )
    total = jnp.dot(adj_ref[...], blocks, preferred_element_type=F32)
    return ((1.0 - ALPHA) * total).astype(BF16)


def image_of(c, section, layer, grad, preact, weight):
    step = (c["layers"] * section + layer + 1).astype(F32)
    beta = jnp.log(BETA_SCALE / jnp.full((1, c["width"]), step, F32) + 1.0)
    masked = jnp.where(preact > 0, grad, jnp.zeros_like(grad))
    product = lax.dot_general(
        masked, weight, (((1,), (1,)), ((), ())), preferred_element_type=F32
    )
    image = ((1.0 - beta) * masked.astype(F32) + beta * product).astype(BF16)
    return beta, masked, image


def layer_kernel(c, *refs):
    refs = Refs(refs)
    n, tile, width, chunk = c["n"], c["tile"], c["width"], c["chunk"]
    h = n // 2
    preact_all, weight_all, names_ref = refs.take(3)
    asked = refs.take(h - 1)
    if c["entry"]:
        last_ref, passed_ref = refs.take(2)
    else:
        adj_ref, own_ref = refs.take(2)
        got = take_got(refs, c)
    if c["final"]:
        support_all, acc_ref = refs.take(2)
        pending = refs.take(c["pending"])
    image_ref = refs.take()
    sends = [] if c["entry"] else refs.take(h - 1)
    parts = refs.take(h - 1) if c["final"] and c["layer"] else []
    out_ref = refs.take()
    if c["final"]:
        term_ref = refs.take()
    preact_ref = preact_all.at[0, c["tick"], c["layer"]]
    weight_ref = weight_all.at[0, c["layer"]]
    section = lax.axis_index("section")
    if not c["entry"]:
        grad = spread_of(adj_ref, own_ref, got, names_ref, c)
    if c["entry"]:
        grad = jnp.where(section == c["sections"] - 1, last_ref[...], passed_ref[...])

    beta, masked, image = image_of(
        c, section, c["layer"], grad, preact_ref[...], weight_ref[...]
    )
    image_ref[...] = image
    if not c["entry"]:
        for send, asked_ref in zip(sends, asked):
            row = asked_ref[2 * c["tick"] : 2 * c["tick"] + 1, :]
            send[:tile, :] = chosen(image_ref, row, c["rows"], tile)
    if c["final"]:
        term = lax.dot_general(
            support_all[0, c["tick"], c["layer"]],
            masked,
            (((0,), (0,)), ((), ())),
            preferred_element_type=F32,
        )
        term_ref[...] = acc_ref[...] + beta * term
        place = lax.rem(lax.axis_index("rows"), h)
        for k in range(1, h):
            part = tile_at(term_ref, jnp.bitwise_xor(place, k), chunk).astype(BF16)
            if c["layer"]:
                parts[k - 1][...] = part
            else:
                sends[k - 1][tile : tile + chunk, :] = part
                for i, ref in enumerate(pending[k - 1 :: h - 1], 1):
                    sends[k - 1][tile + i * chunk : tile + (i + 1) * chunk, :] = ref[...]
        out_ref[...] = tile_at(term_ref, place, chunk)
    else:
        out_ref[...] = masked


def forward_kernel(c, *refs):
    refs = Refs(refs)
    count, tile, rows = c["n"] // 2 - 1, c["tile"], c["rows"]
    far_ref = refs.take()
    own_ref = refs.take() if c["first"] else None
    asked = refs.take(count)
    for asked_ref, send in zip(asked, refs.take(count)):
        row = 2 * c["tick"]
        if c["first"]:
            send[:tile, :] = chosen(own_ref, asked_ref[row : row + 1, :], rows, tile)
            send[tile:, :] = chosen(far_ref, asked_ref[row + 1 : row + 2, :], rows, tile)
        else:
            send[...] = chosen(far_ref, asked_ref[row + 1 : row + 2, :], rows, tile)


def half_sum_kernel(layers, tile, *refs):
    out_ref = refs[-1]
    chunk = out_ref.shape[1]
    for layer in range(layers):
        total = refs[layer][...]
        at = tile + layer * chunk
        for ref in refs[layers:-1]:
            total = total + ref[at : at + chunk, :].astype(F32)
        out_ref[layer] = total.astype(BF16)


def total_kernel(mine_ref, far_ref, out_ref):
    out_ref[...] = (mine_ref[...].astype(F32) + far_ref[...].astype(F32)).astype(BF16)


def turn_kernel(c, *refs):
    refs = Refs(refs)
    names_ref, adj_ref, own_ref = refs.take(3)
    got = take_got(refs, c)
    below_ref, last_ref = refs.take(2)
    grad_ref, image_ref = refs.take(2)
    sends = refs.take(c["n"] // 2 - 1)
    tile, rows, width = c["tile"], c["rows"], c["width"]
    grad = spread_of(adj_ref, own_ref, got, names_ref, c)
    grad_ref[...] = grad
    section = lax.axis_index("section")
    grad = jnp.where(section == 0, last_ref[...], grad)
    below = jnp.where(section == 0, c["sections"], section) - 1
    _, _, image = image_of(
        c, below, c["layers"] - 1, grad, below_ref[:rows, :], below_ref[rows : rows + width, :]
    )
    image_ref[...] = image
    asked = below_ref[rows + width :, :].astype(F32)
    for k, send in enumerate(sends):
        row = 2 * (k * c["ticks"] + c["tick"] + 1)
        send[...] = chosen(image_ref, asked[row : row + 1, :], rows, tile)


def exit_kernel(c, *refs):
    refs = Refs(refs)
    names_ref, adj_ref, own_ref = refs.take(3)
    got = take_got(refs, c)
    handed = refs.take(c["tick"])
    out_ref, hold_ref, sems = refs.take(3)
    copies = [
        pltpu.make_async_copy(ref, out_ref.at[t, 0], sems.at[t])
        for t, ref in enumerate(handed + [hold_ref])
    ]
    for copy in copies[:-1]:
        copy.start()
    hold_ref[...] = spread_of(adj_ref, own_ref, got, names_ref, c)
    copies[-1].start()
    for copy in copies:
        copy.wait()


def finish_kernel(h, *refs):
    sums, (out_ref, hold_ref, sems) = refs[:h], refs[h:]
    layers, chunk, _ = sums[0].shape
    place = lax.rem(lax.axis_index("rows"), h)
    copies = []
    for layer in range(layers):
        for k in range(h):
            start = pl.multiple_of(jnp.bitwise_xor(place, k) * chunk, chunk)
            hold_ref[layer, pl.ds(start, chunk), :] = sums[k][layer].astype(F32)
        copy = pltpu.make_async_copy(hold_ref.at[layer], out_ref.at[0, layer], sems.at[layer])
        copy.start()
        copies.append(copy)
    for copy in copies:
        copy.wait()


def shards(grad_in, grad_last, support, preact, weights, tile_vals, tile_row, tile_col, tile_count):
    section = lax.axis_index("section")
    n = lax.axis_size("rows")
    h = n // 2
    sections = lax.axis_size("section")
    ticks = support.shape[1]
    layers = support.shape[2]
    rows, width = grad_last.shape
    tile = tile_vals.shape[-1]
    row_tiles = rows // tile
    chunk = width // h
    words = packed(tile_row, tile_col, tile_count, row_tiles)

    handed = []
    turned = None
    weight_acc = [None] * layers
    kept_chunks, pending = [], []
    initial = []
    base = dict(
        n=n, tile=tile, rows=rows, width=width, layers=layers, sections=sections, chunk=chunk,
        ticks=ticks,
    )
    layer_cost = cost(2 * rows * width * (width + (n + 1) * tile), (6 + 2 * n) * rows * width)
    small_cost = cost(rows * width, 2 * n * rows * width)
    relay_cost = cost(rows * width, 8 * n * rows * width)
    call = Call()
    call.give(VMEM, words)
    call.want(VMEM, (ticks, width), F32)
    call.want(VMEM, (2 * ticks, width), F32, h - 1)
    names, *asking = call.run(functools.partial(name_kernel, n, row_tiles), "name", small_cost)
    asked = shared(asking)

    adjs = [None] * ticks
    for tick in range(ticks):
        final = tick == ticks - 1
        if tick > 0:
            passed = lowered(handed[-1], 0)
        image = got = joined = None
        toward = 0.0
        for layer in reversed(range(layers)):
            entry = layer == layers - 1
            beta = jnp.log(BETA_SCALE / (layers * section + layer + 1).astype(F32) + 1.0)
            c = dict(
                base, layer=layer, tick=tick, entry=entry, final=final, joined=joined,
                first=tick == 0 and entry, pending=0 if layer else len(pending),
            )
            if c["first"]:
                masked = jnp.where(
                    preact[0, tick, layer] > 0, grad_in[0], jnp.zeros_like(grad_in[0])
                )
                product = jnp.dot(masked, weights[0, layer].T, preferred_element_type=F32)
                image = ((1.0 - beta) * masked.astype(F32) + beta * product).astype(BF16)
            else:
                call = Call()
                call.give(VMEM, preact, weights, names, *asked)
                if entry:
                    call.give(VMEM, grad_last, passed)
                else:
                    call.give(VMEM, adjs[tick], image, *got)
                if final:
                    call.give(VMEM, support, weight_acc[layer])
                    if layer == 0:
                        call.give(VMEM, *pending)
                call.want(VMEM, (rows, width), BF16)
                if not entry:
                    message = tile + (layers * chunk if final and layer == 0 else 0)
                    call.want(VMEM, (message, width), BF16, h - 1)
                if final and layer:
                    call.want(VMEM, (chunk, width), BF16, h - 1)
                if final:
                    call.want(VMEM, (chunk, width), F32)
                else:
                    call.want(VMEM, (rows, width), BF16)
                if final:
                    call.scratch = [pltpu.VMEM((width, width), F32)]
                results = Refs(
                    call.run(
                        functools.partial(layer_kernel, c),
                        "home" if entry else "middle",
                        layer_cost,
                    )
                )
                image = results.take()
                sends = [] if entry else results.take(h - 1)
                if final and layer:
                    pending = results.take(h - 1) + pending
                kept = masked = results.take()
            if turned is not None:
                far = lowered(turned[0], h)
                near = shared(turned[1:], lowered)
                far, *near = lax.optimization_barrier((far, *near))
                turned = None
                if final:
                    parts = shared(sends)
            else:
                far = swapped(image, h)
                near = [] if c["first"] else shared(sends)
            ready = image
            if c["first"]:
                adjs[0] = densify(0, words, tile_vals, row_tiles, n)
                ready, adjs[0] = lax.optimization_barrier((image, adjs[0]))
            call = Call()
            call.give(VMEM, far)
            if c["first"]:
                call.give(VMEM, ready)
            call.give(VMEM, *asked)
            call.want(VMEM, (tile * (1 + c["first"]), width), BF16, h - 1)
            relays = call.run(functools.partial(forward_kernel, c), "forward", small_cost)
            relayed = shared(relays)
            if layer == 0 and not final:
                later, *_ = lax.optimization_barrier((words, *near))
                adjs[tick + 1] = densify(tick + 1, later, tile_vals, row_tiles, n)
                relayed, adjs[tick + 1] = lax.optimization_barrier((relayed, adjs[tick + 1]))
            if final:
                kept_chunks.insert(0, kept)
            if final and layer == 0:
                kept, _ = lax.optimization_barrier((kept_chunks, relays))
                call = Call()
                call.give(VMEM, *kept, *near)
                call.want(VMEM, (layers, chunk, width), BF16)
                (mine,) = call.run(
                    functools.partial(half_sum_kernel, layers, tile), "half_sum", small_cost
                )
            got = [far, *near, *relayed]
            joined = c["first"]
            toward = toward + ALPHA * image.astype(F32)
            if not final:
                term = beta * jnp.dot(
                    support[0, tick, layer].T, masked, preferred_element_type=F32
                )
                old = weight_acc[layer]
                weight_acc[layer] = term if old is None else old + term
        initial.append(toward)
        c = dict(base, tick=tick, final=final, joined=joined)
        call = Call()
        call.give(VMEM, names, adjs[tick], image, *got)
        if not final:
            up = Call()
            up.give(HBM, preact, weights)
            up.give(VMEM, *asked)
            length = rows + width + -(-2 * ticks * (h - 1) // 16) * 16
            up.want(VMEM, (length, width), BF16)
            up.scratch = [pltpu.SemaphoreType.DMA((2,))]
            (pack,) = up.run(
                functools.partial(pack_kernel, tick + 1, layers - 1), "pack", small_cost
            )
            call.give(VMEM, raised(pack), grad_last)
            call.want(VMEM, (rows, width), BF16, 2)
            call.want(VMEM, (tile, width), BF16, h - 1)
            grad, *turned = call.run(functools.partial(turn_kernel, c), "turn", layer_cost)
            handed.append(grad)
            continue
        call.give(VMEM, *handed)
        call.want(HBM, (ticks, 1, rows, width), BF16)
        call.scratch = [pltpu.VMEM((rows, width), BF16), pltpu.SemaphoreType.DMA((ticks,))]
        (handoff,) = call.run(functools.partial(exit_kernel, c), "exit", layer_cost)
    call = Call()
    call.give(VMEM, mine, swapped(mine, h))
    call.want(VMEM, (layers, chunk, width), BF16)
    (total,) = call.run(total_kernel, "total", small_cost)
    call = Call()
    call.give(VMEM, total, *shared([total] * (h - 1)))
    call.want(HBM, (1, layers, width, width), F32)
    call.scratch = [pltpu.VMEM((layers, width, width), F32), pltpu.SemaphoreType.DMA((layers,))]
    (weight_grad,) = call.run(functools.partial(finish_kernel, h), "finish", small_cost)
    return handoff, jnp.stack(initial)[None], weight_grad


def solution(mesh):
    return jax.shard_map(
        shards,
        mesh=mesh,
        in_specs=(
            P("section", "rows", None),
            P("rows", None),
            P("section", None, None, "rows", None),
            P("section", None, None, "rows", None),
            P("section", None, None, None),
            P("section", None, "rows", None, None),
            P("section", None, "rows"),
            P("section", None, "rows"),
            P("section", None, "rows"),
        ),
        out_specs=(
            P(None, "section", "rows", None),
            P("section", None, "rows", None),
            P("section", None, None, None),
        ),
        check_vma=False,
    )
```

```python
import functools

import jax
import jax.numpy as jnp
from jax import lax
from jax.experimental import pallas as pl
from jax.experimental.pallas import tpu as pltpu
from jax.sharding import PartitionSpec as P

ALPHA = 0.1
BETA_SCALE = 0.5
VMEM = pl.BlockSpec(memory_space=pltpu.VMEM)
SMEM = pl.BlockSpec(memory_space=pltpu.SMEM)
HBM = pl.BlockSpec(memory_space=pltpu.HBM)
PARAMS = pltpu.CompilerParams(vmem_limit_bytes=24 * 2**20)
F32 = jnp.float32
BF16 = jnp.bfloat16


def cost(flops, nbytes):
    return pl.CostEstimate(flops=flops, bytes_accessed=nbytes, transcendentals=0)


def swapped(block, k):
    n = lax.axis_size("rows")
    return lax.ppermute(block, "rows", [(i, i ^ k) for i in range(n)])


def lowered(block, k):
    n, sections = lax.axis_size("rows"), lax.axis_size("section")
    route = [
        (s * n + i, (s - 1) % sections * n + (i ^ k)) for s in range(sections) for i in range(n)
    ]
    return lax.ppermute(block, ("section", "rows"), route)


def raised(block):
    sections = lax.axis_size("section")
    return lax.ppermute(block, "section", [(s, (s + 1) % sections) for s in range(sections)])


def shared(blocks):
    moved = {k: swapped(block, k) for k, block in reversed(list(enumerate(blocks, 1)))}
    return [moved[k] for k in sorted(moved)]


class Refs:
    def __init__(self, refs):
        self.refs = list(refs)

    def take(self, count=None):
        many = 1 if count is None else count
        taken, self.refs = self.refs[:many], self.refs[many:]
        return taken[0] if count is None else taken


class Call:
    def __init__(self):
        self.operands, self.specs, self.outs, self.out_specs, self.scratch = [], [], [], [], []
        self.aliases = {}

    def give(self, spec, *arrays):
        self.operands += arrays
        self.specs += [spec] * len(arrays)

    def want(self, spec, shape, dtype, count=1):
        self.outs += [jax.ShapeDtypeStruct(shape, dtype)] * count
        self.out_specs += [spec] * count

    def run(self, kernel, name, estimate, params=PARAMS):
        return pl.pallas_call(
            kernel,
            out_shape=self.outs,
            in_specs=self.specs,
            out_specs=self.out_specs,
            scratch_shapes=self.scratch,
            input_output_aliases=self.aliases,
            compiler_params=params,
            cost_estimate=estimate,
            name=name,
        )(*self.operands)


def packed(tile_row, tile_col, tile_count, row_tiles):
    owner = jnp.bitwise_xor(tile_col // row_tiles, lax.axis_index("rows"))
    words = (owner * row_tiles + tile_col % row_tiles) * row_tiles + tile_row
    live = lax.broadcasted_iota(jnp.int32, words.shape, 2) < tile_count
    return jnp.where(live, words, -1)[0]


def densify_kernel(tick, row_tiles, n, chunks, words_ref, vals_ref, out_ref, vals, acc, sems):
    entries, tile = vals.shape[:2]
    chunk = entries // chunks
    copies = []
    for c in range(chunks):
        part = pl.ds(c * chunk, chunk)
        copies.append(
            pltpu.make_async_copy(vals_ref.at[0, tick, part], vals.at[part], sems.at[c])
        )
        copies[c].start()
    acc[...] = jnp.zeros_like(acc)

    def add(e):
        word = words_ref[tick, e]
        row = lax.rem(word, row_tiles)
        block = lax.rem(lax.div(word, row_tiles), row_tiles)
        slot = lax.div(word, row_tiles * row_tiles)
        slot = jnp.where((slot == 0) & (block > 0), n - 1 + block, slot)
        rows = pl.ds(pl.multiple_of(row * tile, tile), tile)
        cols = pl.ds(pl.multiple_of(slot * tile, tile), tile)
        acc[rows, cols] += vals[e].astype(F32)

    count, step = jnp.int32(0), 1 << (entries.bit_length() - 1)
    while step:
        probe = count + step
        live = (probe <= entries) & (words_ref[tick, jnp.minimum(probe, entries) - 1] >= 0)
        count = jnp.where(live, probe, count)
        step //= 2
    for c in range(chunks):
        copies[c].wait()
        live = jnp.clip(count - c * chunk, 0, chunk)

        @pl.loop(0, live // 2)
        def _(i):
            add(c * chunk + 2 * i)
            add(c * chunk + 2 * i + 1)

        @pl.when(live % 2 == 1)
        def _():
            add(c * chunk + live - 1)

    out_ref[...] = acc[...].astype(BF16)


def densify(tick, words, vals, row_tiles, n):
    entries, tile = vals.shape[2:4]
    chunks = 4 if entries % 4 == 0 else 1
    shape = (row_tiles * tile, (n + row_tiles - 1) * tile)
    call = Call()
    call.give(SMEM, words)
    call.give(HBM, vals)
    call.want(VMEM, shape, BF16)
    call.scratch = [
        pltpu.VMEM(vals.shape[2:], BF16),
        pltpu.VMEM(shape, F32),
        pltpu.SemaphoreType.DMA((chunks,)),
    ]
    (adj,) = call.run(
        functools.partial(densify_kernel, tick, row_tiles, n, chunks),
        "densify",
        cost(entries * tile * tile * 20, entries * tile * tile * 2),
        pltpu.CompilerParams(vmem_limit_bytes=50 * 2**20),
    )
    return adj


def tile_at(ref, index, tile):
    return ref[pl.ds(pl.multiple_of(index * tile, tile), tile), :]


def name_kernel(n, row_tiles, words_ref, *out_refs):
    ticks, width = out_refs[0].shape
    for t in range(ticks):
        words = words_ref[t : t + 1, :]
        index = jnp.where(words < 0, -1, words // row_tiles)

        def named(k):
            block = index - k * row_tiles
            block = jnp.where((block >= 0) & (block < row_tiles), block, 0)
            most = jnp.max(block.astype(F32), axis=1, keepdims=True)
            return jnp.broadcast_to(most, (1, width))

        for k in range(1, n // 2):
            out_refs[k][2 * t : 2 * t + 1, :] = named(k)
            out_refs[k][2 * t + 1 : 2 * t + 2, :] = named(n // 2 + k)
        out_refs[0][t : t + 1, :] = named(n // 2)


def pack_kernel(tick, layer, preact_all, weight_all, out_ref, sems):
    rows = preact_all.shape[-2]
    loads = [
        pltpu.make_async_copy(preact_all.at[0, tick, layer], out_ref.at[:rows], sems.at[0]),
        pltpu.make_async_copy(weight_all.at[0, layer], out_ref.at[rows:], sems.at[1]),
    ]
    for load in loads:
        load.start()
    for load in loads:
        load.wait()


def chosen(image_ref, row, rows, tile):
    index = jnp.broadcast_to(row.astype(BF16), (tile, row.shape[1]))
    result = image_ref[:tile, :]
    for i in range(1, rows // tile):
        result = jnp.where(index > i - 0.5, image_ref[i * tile : (i + 1) * tile, :], result)
    return result


def take_got(refs, c):
    far, near = refs.take(), refs.take(c["n"] // 2 - 1)
    if c["joined"]:
        return far, near, [ref.at[c["tile"] :, :] for ref in near]
    return far, near, refs.take(c["n"] // 2 - 1)


def spread_of(adj_ref, own_ref, got, names_ref, c):
    tile, rows = c["tile"], c["rows"]
    far, near, relayed = got
    far = chosen(far, names_ref[c["tick"] : c["tick"] + 1, :], rows, tile)
    near = [ref[:tile, :] for ref in near]
    relayed = [ref[:tile, :] for ref in relayed]
    blocks = jnp.concatenate(
        [own_ref[:tile, :]] + near + [far] + relayed + [own_ref[tile:, :]], axis=0
    )
    total = jnp.dot(adj_ref[...], blocks, preferred_element_type=F32)
    return ((1.0 - ALPHA) * total).astype(BF16)


def image_of(c, section, layer, grad, preact, weight):
    step = (c["layers"] * section + layer + 1).astype(F32)
    beta = jnp.log(BETA_SCALE / jnp.full((1, c["width"]), step, F32) + 1.0)
    masked = jnp.where(preact > 0, grad, jnp.zeros_like(grad))
    product = lax.dot_general(
        masked, weight, (((1,), (1,)), ((), ())), preferred_element_type=F32
    )
    image = ((1.0 - beta) * masked.astype(F32) + beta * product).astype(BF16)
    return beta, masked, image


def layer_kernel(c, *refs):
    refs = Refs(refs)
    n, tile, width, chunk = c["n"], c["tile"], c["width"], c["chunk"]
    h = n // 2
    preact_all, weight_all, names_ref = refs.take(3)
    asked = refs.take(h - 1)
    if c["entry"]:
        last_ref, passed_ref = refs.take(2)
    else:
        adj_ref, own_ref = refs.take(2)
        got = take_got(refs, c)
    if c["final"]:
        support_all, acc_ref = refs.take(2)
        pending = refs.take(c["pending"])
    image_ref = refs.take()
    sends = [] if c["entry"] else refs.take(h - 1)
    parts = refs.take(h - 1) if c["final"] and c["layer"] else []
    out_ref = refs.take()
    if c["final"]:
        term_ref = refs.take()
    preact_ref = preact_all.at[0, c["tick"], c["layer"]]
    weight_ref = weight_all.at[0, c["layer"]]
    section = lax.axis_index("section")
    if not c["entry"]:
        grad = spread_of(adj_ref, own_ref, got, names_ref, c)
    if c["entry"]:
        grad = jnp.where(section == c["sections"] - 1, last_ref[...], passed_ref[...])

    beta, masked, image = image_of(
        c, section, c["layer"], grad, preact_ref[...], weight_ref[...]
    )
    image_ref[...] = image
    if not c["entry"]:
        for send, asked_ref in zip(sends, asked):
            row = asked_ref[2 * c["tick"] : 2 * c["tick"] + 1, :]
            send[:tile, :] = chosen(image_ref, row, c["rows"], tile)
    if c["final"]:
        term = lax.dot_general(
            support_all[0, c["tick"], c["layer"]],
            masked,
            (((0,), (0,)), ((), ())),
            preferred_element_type=F32,
        )
        term_ref[...] = acc_ref[...] + beta * term
        place = lax.rem(lax.axis_index("rows"), h)
        for k in range(1, h):
            part = tile_at(term_ref, jnp.bitwise_xor(place, k), chunk).astype(BF16)
            if c["layer"]:
                parts[k - 1][...] = part
            else:
                sends[k - 1][tile : tile + chunk, :] = part
                for i, ref in enumerate(pending[k - 1 :: h - 1], 1):
                    sends[k - 1][tile + i * chunk : tile + (i + 1) * chunk, :] = ref[...]
        out_ref[...] = tile_at(term_ref, place, chunk)
    else:
        out_ref[...] = masked


def forward_kernel(c, *refs):
    refs = Refs(refs)
    count, tile, rows = c["n"] // 2 - 1, c["tile"], c["rows"]
    far_ref = refs.take()
    own_ref = refs.take() if c["entry"] else None
    asked = refs.take(count)
    for asked_ref, send in zip(asked, refs.take(count)):
        row = 2 * c["tick"]
        if c["entry"]:
            send[:tile, :] = chosen(own_ref, asked_ref[row : row + 1, :], rows, tile)
            send[tile:, :] = chosen(far_ref, asked_ref[row + 1 : row + 2, :], rows, tile)
        else:
            send[...] = chosen(far_ref, asked_ref[row + 1 : row + 2, :], rows, tile)


def half_sum_kernel(layers, tile, *refs):
    out_ref = refs[-1]
    chunk = out_ref.shape[1]
    for layer in range(layers):
        total = refs[layer][...]
        at = tile + layer * chunk
        for ref in refs[layers:-1]:
            total = total + ref[at : at + chunk, :].astype(F32)
        out_ref[layer] = total.astype(BF16)


def total_kernel(mine_ref, far_ref, out_ref):
    out_ref[...] = (mine_ref[...].astype(F32) + far_ref[...].astype(F32)).astype(BF16)


def turn_kernel(c, *refs):
    refs = Refs(refs)
    names_ref, adj_ref, own_ref = refs.take(3)
    got = take_got(refs, c)
    below_ref, last_ref = refs.take(2)
    grad_ref, image_ref = refs.take(2)
    rows = c["rows"]
    grad = spread_of(adj_ref, own_ref, got, names_ref, c)
    grad_ref[...] = grad
    section = lax.axis_index("section")
    grad = jnp.where(section == 0, last_ref[...], grad)
    below = jnp.where(section == 0, c["sections"], section) - 1
    _, _, image = image_of(
        c, below, c["layers"] - 1, grad, below_ref[:rows, :], below_ref[rows:, :]
    )
    image_ref[...] = image


def exit_kernel(c, *refs):
    refs = Refs(refs)
    names_ref, adj_ref, own_ref = refs.take(3)
    got = take_got(refs, c)
    handed = refs.take(c["tick"])
    out_ref, hold_ref, sems = refs.take(3)
    copies = [
        pltpu.make_async_copy(ref, out_ref.at[t, 0], sems.at[t])
        for t, ref in enumerate(handed + [hold_ref])
    ]
    for copy in copies[:-1]:
        copy.start()
    hold_ref[...] = spread_of(adj_ref, own_ref, got, names_ref, c)
    copies[-1].start()
    for copy in copies:
        copy.wait()


def finish_kernel(h, *refs):
    sums, (out_ref, hold_ref, sems) = refs[:h], refs[h:]
    layers, chunk, _ = sums[0].shape
    place = lax.rem(lax.axis_index("rows"), h)
    copies = []
    for layer in range(layers):
        for k in range(h):
            start = pl.multiple_of(jnp.bitwise_xor(place, k) * chunk, chunk)
            hold_ref[layer, pl.ds(start, chunk), :] = sums[k][layer].astype(F32)
        copy = pltpu.make_async_copy(hold_ref.at[layer], out_ref.at[0, layer], sems.at[layer])
        copy.start()
        copies.append(copy)
    for copy in copies:
        copy.wait()


def shards(grad_in, grad_last, support, preact, weights, tile_vals, tile_row, tile_col, tile_count):
    section = lax.axis_index("section")
    n = lax.axis_size("rows")
    h = n // 2
    sections = lax.axis_size("section")
    ticks = support.shape[1]
    layers = support.shape[2]
    rows, width = grad_last.shape
    tile = tile_vals.shape[-1]
    row_tiles = rows // tile
    chunk = width // h
    words = packed(tile_row, tile_col, tile_count, row_tiles)

    handed = []
    turned = None
    weight_acc = [None] * layers
    kept_chunks, pending = [], []
    initial = []
    base = dict(
        n=n, tile=tile, rows=rows, width=width, layers=layers, sections=sections, chunk=chunk,
        ticks=ticks,
    )
    layer_cost = cost(2 * rows * width * (width + (n + 1) * tile), (6 + 2 * n) * rows * width)
    small_cost = cost(rows * width, 2 * n * rows * width)
    relay_cost = cost(rows * width, 8 * n * rows * width)
    call = Call()
    call.give(VMEM, words)
    call.want(VMEM, (ticks, width), F32)
    call.want(VMEM, (2 * ticks, width), F32, h - 1)
    names, *asking = call.run(functools.partial(name_kernel, n, row_tiles), "name", small_cost)
    asked = shared(asking)

    adjs = [None] * ticks
    for tick in range(ticks):
        final = tick == ticks - 1
        if tick > 0:
            passed = lowered(handed[-1], 0)
        image = got = joined = None
        toward = 0.0
        for layer in reversed(range(layers)):
            entry = layer == layers - 1
            beta = jnp.log(BETA_SCALE / (layers * section + layer + 1).astype(F32) + 1.0)
            c = dict(
                base, layer=layer, tick=tick, entry=entry, final=final, joined=joined,
                first=tick == 0 and entry, pending=0 if layer else len(pending),
            )
            if c["first"]:
                masked = jnp.where(
                    preact[0, tick, layer] > 0, grad_in[0], jnp.zeros_like(grad_in[0])
                )
                product = jnp.dot(masked, weights[0, layer].T, preferred_element_type=F32)
                image = ((1.0 - beta) * masked.astype(F32) + beta * product).astype(BF16)
            else:
                call = Call()
                call.give(VMEM, preact, weights, names, *asked)
                if entry:
                    call.give(VMEM, grad_last, passed)
                else:
                    call.give(VMEM, adjs[tick], image, *got)
                if final:
                    call.give(VMEM, support, weight_acc[layer])
                    if layer == 0:
                        call.give(VMEM, *pending)
                call.want(VMEM, (rows, width), BF16)
                if not entry:
                    message = tile + (layers * chunk if final and layer == 0 else 0)
                    call.want(VMEM, (message, width), BF16, h - 1)
                if final and layer:
                    call.want(VMEM, (chunk, width), BF16, h - 1)
                if final:
                    call.want(VMEM, (chunk, width), F32)
                else:
                    call.want(VMEM, (rows, width), BF16)
                if final:
                    call.scratch = [pltpu.VMEM((width, width), F32)]
                results = Refs(
                    call.run(
                        functools.partial(layer_kernel, c),
                        "home" if entry else "middle",
                        layer_cost,
                    )
                )
                image = results.take()
                sends = [] if entry else results.take(h - 1)
                if final and layer:
                    pending = results.take(h - 1) + pending
                kept = masked = results.take()
            if turned is not None:
                far = lowered(turned, h)
                turned = None
            else:
                far = swapped(image, h)
            near = [] if entry else shared(sends)
            ready = image
            if c["first"]:
                adjs[0] = densify(0, words, tile_vals, row_tiles, n)
                ready, adjs[0] = lax.optimization_barrier((image, adjs[0]))
            call = Call()
            call.give(VMEM, far)
            if entry:
                call.give(VMEM, ready)
            call.give(VMEM, *asked)
            call.want(VMEM, (tile * (1 + entry), width), BF16, h - 1)
            relays = call.run(functools.partial(forward_kernel, c), "forward", small_cost)
            relayed = shared(relays)
            if layer == 0 and not final:
                later, *_ = lax.optimization_barrier((words, *near))
                adjs[tick + 1] = densify(tick + 1, later, tile_vals, row_tiles, n)
                relayed, adjs[tick + 1] = lax.optimization_barrier((relayed, adjs[tick + 1]))
            if final:
                kept_chunks.insert(0, kept)
            if final and layer == 0:
                kept, _ = lax.optimization_barrier((kept_chunks, relays))
                call = Call()
                call.give(VMEM, *kept, *near)
                call.want(VMEM, (layers, chunk, width), BF16)
                (mine,) = call.run(
                    functools.partial(half_sum_kernel, layers, tile), "half_sum", small_cost
                )
            got = [far, *near, *relayed]
            joined = entry
            toward = toward + ALPHA * image.astype(F32)
            if not final:
                term = beta * jnp.dot(
                    support[0, tick, layer].T, masked, preferred_element_type=F32
                )
                old = weight_acc[layer]
                weight_acc[layer] = term if old is None else old + term
        initial.append(toward)
        c = dict(base, tick=tick, final=final, joined=joined)
        call = Call()
        call.give(VMEM, names, adjs[tick], image, *got)
        if not final:
            up = Call()
            up.give(HBM, preact, weights)
            up.want(VMEM, (rows + width, width), BF16)
            up.scratch = [pltpu.SemaphoreType.DMA((2,))]
            (pack,) = up.run(
                functools.partial(pack_kernel, tick + 1, layers - 1), "pack", small_cost
            )
            call.give(VMEM, raised(pack), grad_last)
            call.want(VMEM, (rows, width), BF16, 2)
            grad, turned = call.run(functools.partial(turn_kernel, c), "turn", layer_cost)
            handed.append(grad)
            continue
        call.give(VMEM, *handed)
        call.want(HBM, (ticks, 1, rows, width), BF16)
        call.scratch = [pltpu.VMEM((rows, width), BF16), pltpu.SemaphoreType.DMA((ticks,))]
        (handoff,) = call.run(functools.partial(exit_kernel, c), "exit", layer_cost)
    call = Call()
    call.give(VMEM, mine, swapped(mine, h))
    call.want(VMEM, (layers, chunk, width), BF16)
    (total,) = call.run(total_kernel, "total", small_cost)
    call = Call()
    call.give(VMEM, total, *shared([total] * (h - 1)))
    call.want(HBM, (1, layers, width, width), F32)
    call.scratch = [pltpu.VMEM((layers, width, width), F32), pltpu.SemaphoreType.DMA((layers,))]
    (weight_grad,) = call.run(functools.partial(finish_kernel, h), "finish", small_cost)
    return handoff, jnp.stack(initial)[None], weight_grad


def solution(mesh):
    return jax.shard_map(
        shards,
        mesh=mesh,
        in_specs=(
            P("section", "rows", None),
            P("rows", None),
            P("section", None, None, "rows", None),
            P("section", None, None, "rows", None),
            P("section", None, None, None),
            P("section", None, "rows", None, None),
            P("section", None, "rows"),
            P("section", None, "rows"),
            P("section", None, "rows"),
        ),
        out_specs=(
            P(None, "section", "rows", None),
            P("section", None, "rows", None),
            P("section", None, None, None),
        ),
        check_vma=False,
    )
```

```python
import functools

import jax
import jax.numpy as jnp
from jax import lax
from jax.experimental import pallas as pl
from jax.experimental.pallas import tpu as pltpu
from jax.sharding import PartitionSpec as P

ALPHA = 0.1
BETA_SCALE = 0.5
VMEM = pl.BlockSpec(memory_space=pltpu.VMEM)
SMEM = pl.BlockSpec(memory_space=pltpu.SMEM)
HBM = pl.BlockSpec(memory_space=pltpu.HBM)
PARAMS = pltpu.CompilerParams(vmem_limit_bytes=24 * 2**20)
F32 = jnp.float32
BF16 = jnp.bfloat16


def cost(flops, nbytes):
    return pl.CostEstimate(flops=flops, bytes_accessed=nbytes, transcendentals=0)


def swapped(block, k):
    n = lax.axis_size("rows")
    return lax.ppermute(block, "rows", [(i, i ^ k) for i in range(n)])


def lowered(block, k):
    n, sections = lax.axis_size("rows"), lax.axis_size("section")
    route = [
        (s * n + i, (s - 1) % sections * n + (i ^ k)) for s in range(sections) for i in range(n)
    ]
    return lax.ppermute(block, ("section", "rows"), route)


def raised(block):
    sections = lax.axis_size("section")
    return lax.ppermute(block, "section", [(s, (s + 1) % sections) for s in range(sections)])


def shared(blocks, move=swapped):
    moved = {k: move(block, k) for k, block in reversed(list(enumerate(blocks, 1)))}
    return [moved[k] for k in sorted(moved)]


class Refs:
    def __init__(self, refs):
        self.refs = list(refs)

    def take(self, count=None):
        many = 1 if count is None else count
        taken, self.refs = self.refs[:many], self.refs[many:]
        return taken[0] if count is None else taken


class Call:
    def __init__(self):
        self.operands, self.specs, self.outs, self.out_specs, self.scratch = [], [], [], [], []
        self.aliases = {}

    def give(self, spec, *arrays):
        self.operands += arrays
        self.specs += [spec] * len(arrays)

    def want(self, spec, shape, dtype, count=1):
        self.outs += [jax.ShapeDtypeStruct(shape, dtype)] * count
        self.out_specs += [spec] * count

    def run(self, kernel, name, estimate, params=PARAMS):
        return pl.pallas_call(
            kernel,
            out_shape=self.outs,
            in_specs=self.specs,
            out_specs=self.out_specs,
            scratch_shapes=self.scratch,
            input_output_aliases=self.aliases,
            compiler_params=params,
            cost_estimate=estimate,
            name=name,
        )(*self.operands)


def packed(tile_row, tile_col, tile_count, row_tiles):
    owner = jnp.bitwise_xor(tile_col // row_tiles, lax.axis_index("rows"))
    words = (owner * row_tiles + tile_col % row_tiles) * row_tiles + tile_row
    live = lax.broadcasted_iota(jnp.int32, words.shape, 2) < tile_count
    return jnp.where(live, words, -1)[0]


def densify_kernel(tick, row_tiles, n, chunks, words_ref, vals_ref, out_ref, vals, acc, sems):
    entries, tile = vals.shape[:2]
    chunk = entries // chunks
    copies = []
    for c in range(chunks):
        part = pl.ds(c * chunk, chunk)
        copies.append(
            pltpu.make_async_copy(vals_ref.at[0, tick, part], vals.at[part], sems.at[c])
        )
        copies[c].start()
    acc[...] = jnp.zeros_like(acc)

    def add(e):
        word = words_ref[tick, e]
        row = lax.rem(word, row_tiles)
        block = lax.rem(lax.div(word, row_tiles), row_tiles)
        slot = lax.div(word, row_tiles * row_tiles)
        slot = jnp.where((slot == 0) & (block > 0), n - 1 + block, slot)
        rows = pl.ds(pl.multiple_of(row * tile, tile), tile)
        cols = pl.ds(pl.multiple_of(slot * tile, tile), tile)
        acc[rows, cols] += vals[e].astype(F32)

    count, step = jnp.int32(0), 1 << (entries.bit_length() - 1)
    while step:
        probe = count + step
        live = (probe <= entries) & (words_ref[tick, jnp.minimum(probe, entries) - 1] >= 0)
        count = jnp.where(live, probe, count)
        step //= 2
    for c in range(chunks):
        copies[c].wait()
        live = jnp.clip(count - c * chunk, 0, chunk)

        @pl.loop(0, live // 2)
        def _(i):
            add(c * chunk + 2 * i)
            add(c * chunk + 2 * i + 1)

        @pl.when(live % 2 == 1)
        def _():
            add(c * chunk + live - 1)

    out_ref[...] = acc[...].astype(BF16)


def densify(tick, words, vals, row_tiles, n):
    entries, tile = vals.shape[2:4]
    chunks = 4 if entries % 4 == 0 else 1
    shape = (row_tiles * tile, (n + row_tiles - 1) * tile)
    call = Call()
    call.give(SMEM, words)
    call.give(HBM, vals)
    call.want(VMEM, shape, BF16)
    call.scratch = [
        pltpu.VMEM(vals.shape[2:], BF16),
        pltpu.VMEM(shape, F32),
        pltpu.SemaphoreType.DMA((chunks,)),
    ]
    (adj,) = call.run(
        functools.partial(densify_kernel, tick, row_tiles, n, chunks),
        "densify",
        cost(entries * tile * tile * 20, entries * tile * tile * 2),
        pltpu.CompilerParams(vmem_limit_bytes=50 * 2**20),
    )
    return adj


def tile_at(ref, index, tile):
    return ref[pl.ds(pl.multiple_of(index * tile, tile), tile), :]


def name_kernel(n, row_tiles, words_ref, *out_refs):
    ticks, width = out_refs[0].shape
    for t in range(ticks):
        words = words_ref[t : t + 1, :]
        index = jnp.where(words < 0, -1, words // row_tiles)

        def named(k):
            block = index - k * row_tiles
            block = jnp.where((block >= 0) & (block < row_tiles), block, 0)
            most = jnp.max(block.astype(F32), axis=1, keepdims=True)
            return jnp.broadcast_to(most, (1, width))

        for k in range(1, n // 2):
            out_refs[k][2 * t : 2 * t + 1, :] = named(k)
            out_refs[k][2 * t + 1 : 2 * t + 2, :] = named(n // 2 + k)
        out_refs[0][t : t + 1, :] = named(n // 2)


def pack_kernel(tick, layer, preact_all, weight_all, *refs):
    asked, (out_ref, sems) = refs[:-2], refs[-2:]
    rows, width = preact_all.shape[-2:]
    loads = [
        pltpu.make_async_copy(preact_all.at[0, tick, layer], out_ref.at[:rows], sems.at[0]),
        pltpu.make_async_copy(
            weight_all.at[0, layer], out_ref.at[rows : rows + width], sems.at[1]
        ),
    ]
    for load in loads:
        load.start()
    used = sum(ref.shape[0] for ref in asked)
    rest = out_ref.shape[0] - rows - width - used
    parts = [ref[...] for ref in asked] + ([jnp.zeros((rest, width), F32)] if rest else [])
    out_ref[rows + width :, :] = jnp.concatenate(parts, axis=0).astype(BF16)
    for load in loads:
        load.wait()


def chosen(image_ref, row, rows, tile):
    index = jnp.broadcast_to(row.astype(BF16), (tile, row.shape[1]))
    result = image_ref[:tile, :]
    for i in range(1, rows // tile):
        result = jnp.where(index > i - 0.5, image_ref[i * tile : (i + 1) * tile, :], result)
    return result


def take_got(refs, c):
    far, near = refs.take(), refs.take(c["n"] // 2 - 1)
    if c["joined"]:
        return far, near, [ref.at[c["tile"] :, :] for ref in near]
    return far, near, refs.take(c["n"] // 2 - 1)


def spread_of(adj_ref, own_ref, got, names_ref, c):
    tile, rows = c["tile"], c["rows"]
    far, near, relayed = got
    far = chosen(far, names_ref[c["tick"] : c["tick"] + 1, :], rows, tile)
    near = [ref[:tile, :] for ref in near]
    relayed = [ref[:tile, :] for ref in relayed]
    blocks = jnp.concatenate(
        [own_ref[:tile, :]] + near + [far] + relayed + [own_ref[tile:, :]], axis=0
    )
    total = jnp.dot(adj_ref[...], blocks, preferred_element_type=F32)
    return ((1.0 - ALPHA) * total).astype(BF16)


def image_of(c, section, layer, grad, preact, weight):
    step = (c["layers"] * section + layer + 1).astype(F32)
    beta = jnp.log(BETA_SCALE / jnp.full((1, c["width"]), step, F32) + 1.0)
    masked = jnp.where(preact > 0, grad, jnp.zeros_like(grad))
    product = lax.dot_general(
        masked, weight, (((1,), (1,)), ((), ())), preferred_element_type=F32
    )
    image = ((1.0 - beta) * masked.astype(F32) + beta * product).astype(BF16)
    return beta, masked, image


def layer_kernel(c, *refs):
    refs = Refs(refs)
    n, tile, width, chunk = c["n"], c["tile"], c["width"], c["chunk"]
    h = n // 2
    preact_all, weight_all, names_ref = refs.take(3)
    asked = refs.take(h - 1)
    if c["entry"]:
        last_ref, passed_ref = refs.take(2)
    else:
        adj_ref, own_ref = refs.take(2)
        got = take_got(refs, c)
    if c["final"]:
        support_all, acc_ref = refs.take(2)
        pending = refs.take(c["pending"])
    image_ref = refs.take()
    sends = [] if c["entry"] else refs.take(h - 1)
    parts = refs.take(h - 1) if c["final"] and c["layer"] else []
    out_ref = refs.take()
    if c["final"]:
        term_ref = refs.take()
    preact_ref = preact_all.at[0, c["tick"], c["layer"]]
    weight_ref = weight_all.at[0, c["layer"]]
    section = lax.axis_index("section")
    if not c["entry"]:
        grad = spread_of(adj_ref, own_ref, got, names_ref, c)
    if c["entry"]:
        grad = jnp.where(section == c["sections"] - 1, last_ref[...], passed_ref[...])

    beta, masked, image = image_of(
        c, section, c["layer"], grad, preact_ref[...], weight_ref[...]
    )
    image_ref[...] = image
    if not c["entry"]:
        for send, asked_ref in zip(sends, asked):
            row = asked_ref[2 * c["tick"] : 2 * c["tick"] + 1, :]
            send[:tile, :] = chosen(image_ref, row, c["rows"], tile)
    if c["final"]:
        term = lax.dot_general(
            support_all[0, c["tick"], c["layer"]],
            masked,
            (((0,), (0,)), ((), ())),
            preferred_element_type=F32,
        )
        term_ref[...] = acc_ref[...] + beta * term
        place = lax.rem(lax.axis_index("rows"), h)
        for k in range(1, h):
            part = tile_at(term_ref, jnp.bitwise_xor(place, k), chunk).astype(BF16)
            if c["layer"]:
                parts[k - 1][...] = part
            else:
                sends[k - 1][tile : tile + chunk, :] = part
                for i, ref in enumerate(pending[k - 1 :: h - 1], 1):
                    sends[k - 1][tile + i * chunk : tile + (i + 1) * chunk, :] = ref[...]
        out_ref[...] = tile_at(term_ref, place, chunk)
    else:
        out_ref[...] = masked


def forward_kernel(c, *refs):
    refs = Refs(refs)
    count, tile, rows = c["n"] // 2 - 1, c["tile"], c["rows"]
    far_ref = refs.take()
    own_ref = refs.take() if c["first"] else None
    asked = refs.take(count)
    for asked_ref, send in zip(asked, refs.take(count)):
        row = 2 * c["tick"]
        if c["first"]:
            send[:tile, :] = chosen(own_ref, asked_ref[row : row + 1, :], rows, tile)
            send[tile:, :] = chosen(far_ref, asked_ref[row + 1 : row + 2, :], rows, tile)
        else:
            send[...] = chosen(far_ref, asked_ref[row + 1 : row + 2, :], rows, tile)


def half_sum_kernel(layers, tile, *refs):
    out_ref = refs[-1]
    chunk = out_ref.shape[1]
    for layer in range(layers):
        total = refs[layer][...]
        at = tile + layer * chunk
        for ref in refs[layers:-1]:
            total = total + ref[at : at + chunk, :].astype(F32)
        out_ref[layer] = total.astype(BF16)


def total_kernel(mine_ref, far_ref, out_ref):
    out_ref[...] = (mine_ref[...].astype(F32) + far_ref[...].astype(F32)).astype(BF16)


def turn_kernel(c, *refs):
    refs = Refs(refs)
    names_ref, adj_ref, own_ref = refs.take(3)
    got = take_got(refs, c)
    below_ref, last_ref = refs.take(2)
    grad_ref, image_ref = refs.take(2)
    sends = refs.take(c["n"] // 2 - 1)
    tile, rows, width = c["tile"], c["rows"], c["width"]
    grad = spread_of(adj_ref, own_ref, got, names_ref, c)
    grad_ref[...] = grad
    section = lax.axis_index("section")
    grad = jnp.where(section == 0, last_ref[...], grad)
    below = jnp.where(section == 0, c["sections"], section) - 1
    _, _, image = image_of(
        c, below, c["layers"] - 1, grad, below_ref[:rows, :], below_ref[rows : rows + width, :]
    )
    image_ref[...] = image
    asked = below_ref[rows + width :, :].astype(F32)
    for k, send in enumerate(sends):
        row = 2 * (k * c["ticks"] + c["tick"] + 1)
        send[...] = chosen(image_ref, asked[row : row + 1, :], rows, tile)


def exit_kernel(c, *refs):
    refs = Refs(refs)
    names_ref, adj_ref, own_ref = refs.take(3)
    got = take_got(refs, c)
    handed = refs.take(c["tick"])
    out_ref, hold_ref, sems = refs.take(3)
    copies = [
        pltpu.make_async_copy(ref, out_ref.at[t, 0], sems.at[t])
        for t, ref in enumerate(handed + [hold_ref])
    ]
    for copy in copies[:-1]:
        copy.start()
    hold_ref[...] = spread_of(adj_ref, own_ref, got, names_ref, c)
    copies[-1].start()
    for copy in copies:
        copy.wait()


def finish_kernel(h, *refs):
    sums, (out_ref, hold_ref, sems) = refs[:h], refs[h:]
    layers, chunk, _ = sums[0].shape
    place = lax.rem(lax.axis_index("rows"), h)
    copies = []
    for layer in range(layers):
        for k in range(h):
            start = pl.multiple_of(jnp.bitwise_xor(place, k) * chunk, chunk)
            hold_ref[layer, pl.ds(start, chunk), :] = sums[k][layer].astype(F32)
        copy = pltpu.make_async_copy(hold_ref.at[layer], out_ref.at[0, layer], sems.at[layer])
        copy.start()
        copies.append(copy)
    for copy in copies:
        copy.wait()


def shards(grad_in, grad_last, support, preact, weights, tile_vals, tile_row, tile_col, tile_count):
    section = lax.axis_index("section")
    n = lax.axis_size("rows")
    h = n // 2
    sections = lax.axis_size("section")
    ticks = support.shape[1]
    layers = support.shape[2]
    rows, width = grad_last.shape
    tile = tile_vals.shape[-1]
    row_tiles = rows // tile
    chunk = width // h
    words = packed(tile_row, tile_col, tile_count, row_tiles)

    handed = []
    turned = None
    weight_acc = [None] * layers
    kept_chunks, pending = [], []
    initial = []
    base = dict(
        n=n, tile=tile, rows=rows, width=width, layers=layers, sections=sections, chunk=chunk,
        ticks=ticks,
    )
    layer_cost = cost(2 * rows * width * (width + (n + 1) * tile), (6 + 2 * n) * rows * width)
    small_cost = cost(rows * width, 2 * n * rows * width)
    relay_cost = cost(rows * width, 8 * n * rows * width)
    call = Call()
    call.give(VMEM, words)
    call.want(VMEM, (ticks, width), F32)
    call.want(VMEM, (2 * ticks, width), F32, h - 1)
    names, *asking = call.run(functools.partial(name_kernel, n, row_tiles), "name", small_cost)
    asked = shared(asking)

    adjs = [None] * ticks
    for tick in range(ticks):
        final = tick == ticks - 1
        if tick > 0:
            passed = lowered(handed[-1], 0)
        image = got = joined = None
        toward = 0.0
        for layer in reversed(range(layers)):
            entry = layer == layers - 1
            beta = jnp.log(BETA_SCALE / (layers * section + layer + 1).astype(F32) + 1.0)
            c = dict(
                base, layer=layer, tick=tick, entry=entry, final=final, joined=joined,
                first=tick == 0 and entry, pending=0 if layer else len(pending),
            )
            if c["first"]:
                masked = jnp.where(
                    preact[0, tick, layer] > 0, grad_in[0], jnp.zeros_like(grad_in[0])
                )
                product = jnp.dot(masked, weights[0, layer].T, preferred_element_type=F32)
                image = ((1.0 - beta) * masked.astype(F32) + beta * product).astype(BF16)
            else:
                if turned is not None:
                    lowered_far = lowered(turned[0], h)
                    nearest, *others = shared(turned[1:], lowered)
                    lowered_far, *others = lax.optimization_barrier((lowered_far, *others))
                    passed, nearest = lax.optimization_barrier((passed, nearest))
                    lowered_near = [nearest, *others]
                call = Call()
                call.give(VMEM, preact, weights, names, *asked)
                if entry:
                    call.give(VMEM, grad_last, passed)
                else:
                    call.give(VMEM, adjs[tick], image, *got)
                if final:
                    call.give(VMEM, support, weight_acc[layer])
                    if layer == 0:
                        call.give(VMEM, *pending)
                call.want(VMEM, (rows, width), BF16)
                if not entry:
                    message = tile + (layers * chunk if final and layer == 0 else 0)
                    call.want(VMEM, (message, width), BF16, h - 1)
                if final and layer:
                    call.want(VMEM, (chunk, width), BF16, h - 1)
                if final:
                    call.want(VMEM, (chunk, width), F32)
                else:
                    call.want(VMEM, (rows, width), BF16)
                if final:
                    call.scratch = [pltpu.VMEM((width, width), F32)]
                results = Refs(
                    call.run(
                        functools.partial(layer_kernel, c),
                        "home" if entry else "middle",
                        layer_cost,
                    )
                )
                image = results.take()
                sends = [] if entry else results.take(h - 1)
                if final and layer:
                    pending = results.take(h - 1) + pending
                kept = masked = results.take()
            if turned is not None:
                far, near = lowered_far, lowered_near
                turned = None
            else:
                far = swapped(image, h)
                near = [] if c["first"] else shared(sends)
            ready = image
            if c["first"]:
                adjs[0] = densify(0, words, tile_vals, row_tiles, n)
                ready, adjs[0] = lax.optimization_barrier((image, adjs[0]))
            call = Call()
            call.give(VMEM, far)
            if c["first"]:
                call.give(VMEM, ready)
            call.give(VMEM, *asked)
            call.want(VMEM, (tile * (1 + c["first"]), width), BF16, h - 1)
            relays = call.run(functools.partial(forward_kernel, c), "forward", small_cost)
            relayed = shared(relays)
            if layer == 0 and not final:
                later, *_ = lax.optimization_barrier((words, *near))
                adjs[tick + 1] = densify(tick + 1, later, tile_vals, row_tiles, n)
                relayed, adjs[tick + 1] = lax.optimization_barrier((relayed, adjs[tick + 1]))
            if final:
                kept_chunks.insert(0, kept)
            if final and layer == 0:
                kept, _ = lax.optimization_barrier((kept_chunks, relays))
                call = Call()
                call.give(VMEM, *kept, *near)
                call.want(VMEM, (layers, chunk, width), BF16)
                (mine,) = call.run(
                    functools.partial(half_sum_kernel, layers, tile), "half_sum", small_cost
                )
            got = [far, *near, *relayed]
            joined = c["first"]
            toward = toward + ALPHA * image.astype(F32)
            if not final:
                term = beta * jnp.dot(
                    support[0, tick, layer].T, masked, preferred_element_type=F32
                )
                old = weight_acc[layer]
                weight_acc[layer] = term if old is None else old + term
        initial.append(toward)
        c = dict(base, tick=tick, final=final, joined=joined)
        call = Call()
        call.give(VMEM, names, adjs[tick], image, *got)
        if not final:
            up = Call()
            up.give(HBM, preact, weights)
            up.give(VMEM, *asked)
            length = rows + width + -(-2 * ticks * (h - 1) // 16) * 16
            up.want(VMEM, (length, width), BF16)
            up.scratch = [pltpu.SemaphoreType.DMA((2,))]
            (pack,) = up.run(
                functools.partial(pack_kernel, tick + 1, layers - 1), "pack", small_cost
            )
            call.give(VMEM, raised(pack), grad_last)
            call.want(VMEM, (rows, width), BF16, 2)
            call.want(VMEM, (tile, width), BF16, h - 1)
            grad, *turned = call.run(functools.partial(turn_kernel, c), "turn", layer_cost)
            handed.append(grad)
            continue
        call.give(VMEM, *handed)
        call.want(HBM, (ticks, 1, rows, width), BF16)
        call.scratch = [pltpu.VMEM((rows, width), BF16), pltpu.SemaphoreType.DMA((ticks,))]
        (handoff,) = call.run(functools.partial(exit_kernel, c), "exit", layer_cost)
    call = Call()
    call.give(VMEM, mine, swapped(mine, h))
    call.want(VMEM, (layers, chunk, width), BF16)
    (total,) = call.run(total_kernel, "total", small_cost)
    call = Call()
    call.give(VMEM, total, *shared([total] * (h - 1)))
    call.want(HBM, (1, layers, width, width), F32)
    call.scratch = [pltpu.VMEM((layers, width, width), F32), pltpu.SemaphoreType.DMA((layers,))]
    (weight_grad,) = call.run(functools.partial(finish_kernel, h), "finish", small_cost)
    return handoff, jnp.stack(initial)[None], weight_grad


def solution(mesh):
    return jax.shard_map(
        shards,
        mesh=mesh,
        in_specs=(
            P("section", "rows", None),
            P("rows", None),
            P("section", None, None, "rows", None),
            P("section", None, None, "rows", None),
            P("section", None, None, None),
            P("section", None, "rows", None, None),
            P("section", None, "rows"),
            P("section", None, "rows"),
            P("section", None, "rows"),
        ),
        out_specs=(
            P(None, "section", "rows", None),
            P("section", None, "rows", None),
            P("section", None, None, None),
        ),
        check_vma=False,
    )
```

```python
import functools

import jax
import jax.numpy as jnp
from jax import lax
from jax.experimental import pallas as pl
from jax.experimental.pallas import tpu as pltpu
from jax.sharding import PartitionSpec as P

ALPHA = 0.1
BETA_SCALE = 0.5
VMEM = pl.BlockSpec(memory_space=pltpu.VMEM)
SMEM = pl.BlockSpec(memory_space=pltpu.SMEM)
HBM = pl.BlockSpec(memory_space=pltpu.HBM)
PARAMS = pltpu.CompilerParams(vmem_limit_bytes=24 * 2**20)
F32 = jnp.float32
BF16 = jnp.bfloat16


def cost(flops, nbytes):
    return pl.CostEstimate(flops=flops, bytes_accessed=nbytes, transcendentals=0)


def swapped(block, k):
    n = lax.axis_size("rows")
    return lax.ppermute(block, "rows", [(i, i ^ k) for i in range(n)])


def lowered(block, k):
    n, sections = lax.axis_size("rows"), lax.axis_size("section")
    route = [
        (s * n + i, (s - 1) % sections * n + (i ^ k)) for s in range(sections) for i in range(n)
    ]
    return lax.ppermute(block, ("section", "rows"), route)


def raised(block):
    sections = lax.axis_size("section")
    return lax.ppermute(block, "section", [(s, (s + 1) % sections) for s in range(sections)])


def shared(blocks, move=swapped):
    moved = {k: move(block, k) for k, block in reversed(list(enumerate(blocks, 1)))}
    return [moved[k] for k in sorted(moved)]


class Refs:
    def __init__(self, refs):
        self.refs = list(refs)

    def take(self, count=None):
        many = 1 if count is None else count
        taken, self.refs = self.refs[:many], self.refs[many:]
        return taken[0] if count is None else taken


class Call:
    def __init__(self):
        self.operands, self.specs, self.outs, self.out_specs, self.scratch = [], [], [], [], []
        self.aliases = {}

    def give(self, spec, *arrays):
        self.operands += arrays
        self.specs += [spec] * len(arrays)

    def want(self, spec, shape, dtype, count=1):
        self.outs += [jax.ShapeDtypeStruct(shape, dtype)] * count
        self.out_specs += [spec] * count

    def run(self, kernel, name, estimate, params=PARAMS):
        return pl.pallas_call(
            kernel,
            out_shape=self.outs,
            in_specs=self.specs,
            out_specs=self.out_specs,
            scratch_shapes=self.scratch,
            input_output_aliases=self.aliases,
            compiler_params=params,
            cost_estimate=estimate,
            name=name,
        )(*self.operands)


def packed(tile_row, tile_col, tile_count, row_tiles):
    owner = jnp.bitwise_xor(tile_col // row_tiles, lax.axis_index("rows"))
    words = (owner * row_tiles + tile_col % row_tiles) * row_tiles + tile_row
    live = lax.broadcasted_iota(jnp.int32, words.shape, 2) < tile_count
    return jnp.where(live, words, -1)[0]


def densify_kernel(tick, row_tiles, n, chunks, words_ref, vals_ref, out_ref, vals, acc, sems):
    entries, tile = vals.shape[:2]
    chunk = entries // chunks
    copies = []
    for c in range(chunks):
        part = pl.ds(c * chunk, chunk)
        copies.append(
            pltpu.make_async_copy(vals_ref.at[0, tick, part], vals.at[part], sems.at[c])
        )
        copies[c].start()
    acc[...] = jnp.zeros_like(acc)

    def add(e):
        word = words_ref[tick, e]
        row = lax.rem(word, row_tiles)
        block = lax.rem(lax.div(word, row_tiles), row_tiles)
        slot = lax.div(word, row_tiles * row_tiles)
        slot = jnp.where((slot == 0) & (block > 0), n - 1 + block, slot)
        rows = pl.ds(pl.multiple_of(row * tile, tile), tile)
        cols = pl.ds(pl.multiple_of(slot * tile, tile), tile)
        acc[rows, cols] += vals[e].astype(F32)

    count, step = jnp.int32(0), 1 << (entries.bit_length() - 1)
    while step:
        probe = count + step
        live = (probe <= entries) & (words_ref[tick, jnp.minimum(probe, entries) - 1] >= 0)
        count = jnp.where(live, probe, count)
        step //= 2
    for c in range(chunks):
        copies[c].wait()
        live = jnp.clip(count - c * chunk, 0, chunk)

        @pl.loop(0, live // 2)
        def _(i):
            add(c * chunk + 2 * i)
            add(c * chunk + 2 * i + 1)

        @pl.when(live % 2 == 1)
        def _():
            add(c * chunk + live - 1)

    out_ref[...] = acc[...].astype(BF16)


def densify(tick, words, vals, row_tiles, n):
    entries, tile = vals.shape[2:4]
    chunks = 4 if entries % 4 == 0 else 1
    shape = (row_tiles * tile, (n + row_tiles - 1) * tile)
    call = Call()
    call.give(SMEM, words)
    call.give(HBM, vals)
    call.want(VMEM, shape, BF16)
    call.scratch = [
        pltpu.VMEM(vals.shape[2:], BF16),
        pltpu.VMEM(shape, F32),
        pltpu.SemaphoreType.DMA((chunks,)),
    ]
    (adj,) = call.run(
        functools.partial(densify_kernel, tick, row_tiles, n, chunks),
        "densify",
        cost(entries * tile * tile * 20, entries * tile * tile * 2),
        pltpu.CompilerParams(vmem_limit_bytes=50 * 2**20),
    )
    return adj


def tile_at(ref, index, tile):
    return ref[pl.ds(pl.multiple_of(index * tile, tile), tile), :]


def name_kernel(n, row_tiles, words_ref, *out_refs):
    ticks, width = out_refs[0].shape
    for t in range(ticks):
        words = words_ref[t : t + 1, :]
        index = jnp.where(words < 0, -1, words // row_tiles)

        def named(k):
            block = index - k * row_tiles
            block = jnp.where((block >= 0) & (block < row_tiles), block, 0)
            most = jnp.max(block.astype(F32), axis=1, keepdims=True)
            return jnp.broadcast_to(most, (1, width))

        for k in range(1, n // 2):
            out_refs[k][2 * t : 2 * t + 1, :] = named(k)
            out_refs[k][2 * t + 1 : 2 * t + 2, :] = named(n // 2 + k)
        out_refs[0][t : t + 1, :] = named(n // 2)


def pack_kernel(tick, layer, preact_all, weight_all, *refs):
    asked, (out_ref, sems) = refs[:-2], refs[-2:]
    rows, width = preact_all.shape[-2:]
    loads = [
        pltpu.make_async_copy(preact_all.at[0, tick, layer], out_ref.at[:rows], sems.at[0]),
        pltpu.make_async_copy(
            weight_all.at[0, layer], out_ref.at[rows : rows + width], sems.at[1]
        ),
    ]
    for load in loads:
        load.start()
    used = sum(ref.shape[0] for ref in asked)
    rest = out_ref.shape[0] - rows - width - used
    parts = [ref[...] for ref in asked] + ([jnp.zeros((rest, width), F32)] if rest else [])
    out_ref[rows + width :, :] = jnp.concatenate(parts, axis=0).astype(BF16)
    for load in loads:
        load.wait()


def chosen(image_ref, row, rows, tile):
    index = jnp.broadcast_to(row.astype(BF16), (tile, row.shape[1]))
    result = image_ref[:tile, :]
    for i in range(1, rows // tile):
        result = jnp.where(index > i - 0.5, image_ref[i * tile : (i + 1) * tile, :], result)
    return result


def take_got(refs, c):
    far, near = refs.take(), refs.take(c["n"] // 2 - 1)
    if c["joined"]:
        return far, near, [ref.at[c["tile"] :, :] for ref in near]
    return far, near, refs.take(c["n"] // 2 - 1)


def spread_of(adj_ref, own_ref, got, names_ref, c):
    tile, rows = c["tile"], c["rows"]
    far, near, relayed = got
    far = chosen(far, names_ref[c["tick"] : c["tick"] + 1, :], rows, tile)
    near = [ref[:tile, :] for ref in near]
    relayed = [ref[:tile, :] for ref in relayed]
    blocks = jnp.concatenate(
        [own_ref[:tile, :]] + near + [far] + relayed + [own_ref[tile:, :]], axis=0
    )
    total = jnp.dot(adj_ref[...], blocks, preferred_element_type=F32)
    return ((1.0 - ALPHA) * total).astype(BF16)


def image_of(c, section, layer, grad, preact, weight):
    step = (c["layers"] * section + layer + 1).astype(F32)
    beta = jnp.log(BETA_SCALE / jnp.full((1, c["width"]), step, F32) + 1.0)
    masked = jnp.where(preact > 0, grad, jnp.zeros_like(grad))
    product = lax.dot_general(
        masked, weight, (((1,), (1,)), ((), ())), preferred_element_type=F32
    )
    image = ((1.0 - beta) * masked.astype(F32) + beta * product).astype(BF16)
    return beta, masked, image


def layer_kernel(c, *refs):
    refs = Refs(refs)
    n, tile, width, chunk = c["n"], c["tile"], c["width"], c["chunk"]
    h = n // 2
    preact_all, weight_all, names_ref = refs.take(3)
    asked = refs.take(h - 1)
    if c["entry"]:
        last_ref, passed_ref = refs.take(2)
    else:
        adj_ref, own_ref = refs.take(2)
        got = take_got(refs, c)
    if c["final"]:
        support_all, acc_ref = refs.take(2)
        pending = refs.take(c["pending"])
    image_ref = refs.take()
    sends = [] if c["entry"] else refs.take(h - 1)
    parts = refs.take(h - 1) if c["final"] and c["layer"] else []
    out_ref = refs.take()
    if c["final"]:
        term_ref = refs.take()
    preact_ref = preact_all.at[0, c["tick"], c["layer"]]
    weight_ref = weight_all.at[0, c["layer"]]
    section = lax.axis_index("section")
    if not c["entry"]:
        grad = spread_of(adj_ref, own_ref, got, names_ref, c)
    if c["entry"]:
        grad = jnp.where(section == c["sections"] - 1, last_ref[...], passed_ref[...])

    beta, masked, image = image_of(
        c, section, c["layer"], grad, preact_ref[...], weight_ref[...]
    )
    image_ref[...] = image
    if not c["entry"]:
        for send, asked_ref in zip(sends, asked):
            row = asked_ref[2 * c["tick"] : 2 * c["tick"] + 1, :]
            send[:tile, :] = chosen(image_ref, row, c["rows"], tile)
    if c["final"]:
        term = lax.dot_general(
            support_all[0, c["tick"], c["layer"]],
            masked,
            (((0,), (0,)), ((), ())),
            preferred_element_type=F32,
        )
        term_ref[...] = acc_ref[...] + beta * term
        place = lax.rem(lax.axis_index("rows"), h)
        for k in range(1, h):
            part = tile_at(term_ref, jnp.bitwise_xor(place, k), chunk).astype(BF16)
            if c["layer"]:
                parts[k - 1][...] = part
            else:
                sends[k - 1][tile : tile + chunk, :] = part
                for i, ref in enumerate(pending[k - 1 :: h - 1], 1):
                    sends[k - 1][tile + i * chunk : tile + (i + 1) * chunk, :] = ref[...]
        out_ref[...] = tile_at(term_ref, place, chunk)
    else:
        out_ref[...] = masked


def forward_kernel(c, *refs):
    refs = Refs(refs)
    count, tile, rows = c["n"] // 2 - 1, c["tile"], c["rows"]
    far_ref = refs.take()
    own_ref = refs.take() if c["first"] else None
    asked = refs.take(count)
    for asked_ref, send in zip(asked, refs.take(count)):
        row = 2 * c["tick"]
        if c["first"]:
            send[:tile, :] = chosen(own_ref, asked_ref[row : row + 1, :], rows, tile)
            send[tile:, :] = chosen(far_ref, asked_ref[row + 1 : row + 2, :], rows, tile)
        else:
            send[...] = chosen(far_ref, asked_ref[row + 1 : row + 2, :], rows, tile)


def half_sum_kernel(layers, tile, *refs):
    out_ref = refs[-1]
    chunk = out_ref.shape[1]
    for layer in range(layers):
        total = refs[layer][...]
        at = tile + layer * chunk
        for ref in refs[layers:-1]:
            total = total + ref[at : at + chunk, :].astype(F32)
        out_ref[layer] = total.astype(BF16)


def total_kernel(mine_ref, far_ref, out_ref):
    out_ref[...] = (mine_ref[...].astype(F32) + far_ref[...].astype(F32)).astype(BF16)


def turn_kernel(c, *refs):
    refs = Refs(refs)
    names_ref, adj_ref, own_ref = refs.take(3)
    got = take_got(refs, c)
    below_ref, last_ref = refs.take(2)
    grad_ref, image_ref = refs.take(2)
    sends = refs.take(c["n"] // 2 - 1)
    tile, rows, width = c["tile"], c["rows"], c["width"]
    grad = spread_of(adj_ref, own_ref, got, names_ref, c)
    grad_ref[...] = grad
    section = lax.axis_index("section")
    grad = jnp.where(section == 0, last_ref[...], grad)
    below = jnp.where(section == 0, c["sections"], section) - 1
    _, _, image = image_of(
        c, below, c["layers"] - 1, grad, below_ref[:rows, :], below_ref[rows : rows + width, :]
    )
    image_ref[...] = image
    asked = below_ref[rows + width :, :].astype(F32)
    for k, send in enumerate(sends):
        row = 2 * (k * c["ticks"] + c["tick"] + 1)
        send[...] = chosen(image_ref, asked[row : row + 1, :], rows, tile)


def exit_kernel(c, *refs):
    refs = Refs(refs)
    names_ref, adj_ref, own_ref = refs.take(3)
    got = take_got(refs, c)
    handed = refs.take(c["tick"])
    out_ref, hold_ref, sems = refs.take(3)
    copies = [
        pltpu.make_async_copy(ref, out_ref.at[t, 0], sems.at[t])
        for t, ref in enumerate(handed + [hold_ref])
    ]
    for copy in copies[:-1]:
        copy.start()
    hold_ref[...] = spread_of(adj_ref, own_ref, got, names_ref, c)
    copies[-1].start()
    for copy in copies:
        copy.wait()


def finish_kernel(h, *refs):
    sums, (out_ref, hold_ref, sems) = refs[:h], refs[h:]
    layers, chunk, _ = sums[0].shape
    place = lax.rem(lax.axis_index("rows"), h)
    copies = []
    for layer in range(layers):
        for k in range(h):
            start = pl.multiple_of(jnp.bitwise_xor(place, k) * chunk, chunk)
            hold_ref[layer, pl.ds(start, chunk), :] = sums[k][layer].astype(F32)
        copy = pltpu.make_async_copy(hold_ref.at[layer], out_ref.at[0, layer], sems.at[layer])
        copy.start()
        copies.append(copy)
    for copy in copies:
        copy.wait()


def shards(grad_in, grad_last, support, preact, weights, tile_vals, tile_row, tile_col, tile_count):
    section = lax.axis_index("section")
    n = lax.axis_size("rows")
    h = n // 2
    sections = lax.axis_size("section")
    ticks = support.shape[1]
    layers = support.shape[2]
    rows, width = grad_last.shape
    tile = tile_vals.shape[-1]
    row_tiles = rows // tile
    chunk = width // h
    words = packed(tile_row, tile_col, tile_count, row_tiles)

    handed = []
    turned = None
    weight_acc = [None] * layers
    kept_chunks, pending = [], []
    initial = []
    base = dict(
        n=n, tile=tile, rows=rows, width=width, layers=layers, sections=sections, chunk=chunk,
        ticks=ticks,
    )
    layer_cost = cost(2 * rows * width * (width + (n + 1) * tile), (6 + 2 * n) * rows * width)
    small_cost = cost(rows * width, 2 * n * rows * width)
    relay_cost = cost(rows * width, 8 * n * rows * width)
    call = Call()
    call.give(VMEM, words)
    call.want(VMEM, (ticks, width), F32)
    call.want(VMEM, (2 * ticks, width), F32, h - 1)
    names, *asking = call.run(functools.partial(name_kernel, n, row_tiles), "name", small_cost)
    asked = shared(asking)

    adjs = [None] * ticks
    for tick in range(ticks):
        final = tick == ticks - 1
        if tick > 0:
            passed = lowered(handed[-1], 0)
        image = got = joined = None
        toward = 0.0
        for layer in reversed(range(layers)):
            entry = layer == layers - 1
            beta = jnp.log(BETA_SCALE / (layers * section + layer + 1).astype(F32) + 1.0)
            c = dict(
                base, layer=layer, tick=tick, entry=entry, final=final, joined=joined,
                first=tick == 0 and entry, pending=0 if layer else len(pending),
            )
            if c["first"]:
                masked = jnp.where(
                    preact[0, tick, layer] > 0, grad_in[0], jnp.zeros_like(grad_in[0])
                )
                product = jnp.dot(masked, weights[0, layer].T, preferred_element_type=F32)
                image = ((1.0 - beta) * masked.astype(F32) + beta * product).astype(BF16)
            else:
                if turned is not None:
                    lowered_far = lowered(turned[0], h)
                    *others, farthest = shared(turned[1:], lowered)
                    lowered_far, farthest = lax.optimization_barrier((lowered_far, farthest))
                    passed, others = lax.optimization_barrier((passed, others))
                    lowered_near = [*others, farthest]
                call = Call()
                call.give(VMEM, preact, weights, names, *asked)
                if entry:
                    call.give(VMEM, grad_last, passed)
                else:
                    call.give(VMEM, adjs[tick], image, *got)
                if final:
                    call.give(VMEM, support, weight_acc[layer])
                    if layer == 0:
                        call.give(VMEM, *pending)
                call.want(VMEM, (rows, width), BF16)
                if not entry:
                    message = tile + (layers * chunk if final and layer == 0 else 0)
                    call.want(VMEM, (message, width), BF16, h - 1)
                if final and layer:
                    call.want(VMEM, (chunk, width), BF16, h - 1)
                if final:
                    call.want(VMEM, (chunk, width), F32)
                else:
                    call.want(VMEM, (rows, width), BF16)
                if final:
                    call.scratch = [pltpu.VMEM((width, width), F32)]
                results = Refs(
                    call.run(
                        functools.partial(layer_kernel, c),
                        "home" if entry else "middle",
                        layer_cost,
                    )
                )
                image = results.take()
                sends = [] if entry else results.take(h - 1)
                if final and layer:
                    pending = results.take(h - 1) + pending
                kept = masked = results.take()
            if turned is not None:
                far, near = lowered_far, lowered_near
                turned = None
            else:
                far = swapped(image, h)
                near = [] if c["first"] else shared(sends)
            ready = image
            if c["first"]:
                adjs[0] = densify(0, words, tile_vals, row_tiles, n)
                ready, adjs[0] = lax.optimization_barrier((image, adjs[0]))
            call = Call()
            call.give(VMEM, far)
            if c["first"]:
                call.give(VMEM, ready)
            call.give(VMEM, *asked)
            call.want(VMEM, (tile * (1 + c["first"]), width), BF16, h - 1)
            relays = call.run(functools.partial(forward_kernel, c), "forward", small_cost)
            relayed = shared(relays)
            if c["first"]:
                asked_later, _ = lax.optimization_barrier((asked, relays))
            if layer == 0 and not final:
                later, *_ = lax.optimization_barrier((words, *near))
                adjs[tick + 1] = densify(tick + 1, later, tile_vals, row_tiles, n)
                relayed, adjs[tick + 1] = lax.optimization_barrier((relayed, adjs[tick + 1]))
            if final:
                kept_chunks.insert(0, kept)
            if final and layer == 0:
                kept, _ = lax.optimization_barrier((kept_chunks, relays))
                call = Call()
                call.give(VMEM, *kept, *near)
                call.want(VMEM, (layers, chunk, width), BF16)
                (mine,) = call.run(
                    functools.partial(half_sum_kernel, layers, tile), "half_sum", small_cost
                )
            got = [far, *near, *relayed]
            joined = c["first"]
            toward = toward + ALPHA * image.astype(F32)
            if not final:
                term = beta * jnp.dot(
                    support[0, tick, layer].T, masked, preferred_element_type=F32
                )
                old = weight_acc[layer]
                weight_acc[layer] = term if old is None else old + term
                if c["first"]:
                    got, weight_acc[layer] = lax.optimization_barrier((got, weight_acc[layer]))
        initial.append(toward)
        c = dict(base, tick=tick, final=final, joined=joined)
        call = Call()
        call.give(VMEM, names, adjs[tick], image, *got)
        if not final:
            up = Call()
            up.give(HBM, preact, weights)
            up.give(VMEM, *asked_later)
            length = rows + width + -(-2 * ticks * (h - 1) // 16) * 16
            up.want(VMEM, (length, width), BF16)
            up.scratch = [pltpu.SemaphoreType.DMA((2,))]
            (pack,) = up.run(
                functools.partial(pack_kernel, tick + 1, layers - 1), "pack", small_cost
            )
            call.give(VMEM, raised(pack), grad_last)
            call.want(VMEM, (rows, width), BF16, 2)
            call.want(VMEM, (tile, width), BF16, h - 1)
            grad, *turned = call.run(functools.partial(turn_kernel, c), "turn", layer_cost)
            handed.append(grad)
            continue
        call.give(VMEM, *handed)
        call.want(HBM, (ticks, 1, rows, width), BF16)
        call.scratch = [pltpu.VMEM((rows, width), BF16), pltpu.SemaphoreType.DMA((ticks,))]
        (handoff,) = call.run(functools.partial(exit_kernel, c), "exit", layer_cost)
    call = Call()
    call.give(VMEM, mine, swapped(mine, h))
    call.want(VMEM, (layers, chunk, width), BF16)
    (total,) = call.run(total_kernel, "total", small_cost)
    call = Call()
    call.give(VMEM, total, *shared([total] * (h - 1)))
    call.want(HBM, (1, layers, width, width), F32)
    call.scratch = [pltpu.VMEM((layers, width, width), F32), pltpu.SemaphoreType.DMA((layers,))]
    (weight_grad,) = call.run(functools.partial(finish_kernel, h), "finish", small_cost)
    return handoff, jnp.stack(initial)[None], weight_grad


def solution(mesh):
    return jax.shard_map(
        shards,
        mesh=mesh,
        in_specs=(
            P("section", "rows", None),
            P("rows", None),
            P("section", None, None, "rows", None),
            P("section", None, None, "rows", None),
            P("section", None, None, None),
            P("section", None, "rows", None, None),
            P("section", None, "rows"),
            P("section", None, "rows"),
            P("section", None, "rows"),
        ),
        out_specs=(
            P(None, "section", "rows", None),
            P("section", None, "rows", None),
            P("section", None, None, None),
        ),
        check_vma=False,
    )
```

```python
import functools

import jax
import jax.numpy as jnp
from jax import lax
from jax.experimental import pallas as pl
from jax.experimental.pallas import tpu as pltpu
from jax.sharding import PartitionSpec as P

ALPHA = 0.1
BETA_SCALE = 0.5
VMEM = pl.BlockSpec(memory_space=pltpu.VMEM)
SMEM = pl.BlockSpec(memory_space=pltpu.SMEM)
HBM = pl.BlockSpec(memory_space=pltpu.HBM)
PARAMS = pltpu.CompilerParams(vmem_limit_bytes=24 * 2**20)
F32 = jnp.float32
BF16 = jnp.bfloat16


def cost(flops, nbytes):
    return pl.CostEstimate(flops=flops, bytes_accessed=nbytes, transcendentals=0)


def swapped(block, k):
    n = lax.axis_size("rows")
    return lax.ppermute(block, "rows", [(i, i ^ k) for i in range(n)])


def lowered(block, k):
    n, sections = lax.axis_size("rows"), lax.axis_size("section")
    route = [
        (s * n + i, (s - 1) % sections * n + (i ^ k)) for s in range(sections) for i in range(n)
    ]
    return lax.ppermute(block, ("section", "rows"), route)


def raised(block):
    sections = lax.axis_size("section")
    return lax.ppermute(block, "section", [(s, (s + 1) % sections) for s in range(sections)])


def shared(blocks, move=swapped):
    moved = {k: move(block, k) for k, block in reversed(list(enumerate(blocks, 1)))}
    return [moved[k] for k in sorted(moved)]


class Refs:
    def __init__(self, refs):
        self.refs = list(refs)

    def take(self, count=None):
        many = 1 if count is None else count
        taken, self.refs = self.refs[:many], self.refs[many:]
        return taken[0] if count is None else taken


class Call:
    def __init__(self):
        self.operands, self.specs, self.outs, self.out_specs, self.scratch = [], [], [], [], []
        self.aliases = {}

    def give(self, spec, *arrays):
        self.operands += arrays
        self.specs += [spec] * len(arrays)

    def want(self, spec, shape, dtype, count=1):
        self.outs += [jax.ShapeDtypeStruct(shape, dtype)] * count
        self.out_specs += [spec] * count

    def run(self, kernel, name, estimate, params=PARAMS):
        return pl.pallas_call(
            kernel,
            out_shape=self.outs,
            in_specs=self.specs,
            out_specs=self.out_specs,
            scratch_shapes=self.scratch,
            input_output_aliases=self.aliases,
            compiler_params=params,
            cost_estimate=estimate,
            name=name,
        )(*self.operands)


def packed(tile_row, tile_col, tile_count, row_tiles):
    owner = jnp.bitwise_xor(tile_col // row_tiles, lax.axis_index("rows"))
    words = (owner * row_tiles + tile_col % row_tiles) * row_tiles + tile_row
    live = lax.broadcasted_iota(jnp.int32, words.shape, 2) < tile_count
    return jnp.where(live, words, -1)[0]


def densify_kernel(tick, row_tiles, n, chunks, words_ref, vals_ref, out_ref, vals, acc, sems):
    entries, tile = vals.shape[:2]
    chunk = entries // chunks
    copies = []
    for c in range(chunks):
        part = pl.ds(c * chunk, chunk)
        copies.append(
            pltpu.make_async_copy(vals_ref.at[0, tick, part], vals.at[part], sems.at[c])
        )
        copies[c].start()
    acc[...] = jnp.zeros_like(acc)

    def add(e):
        word = words_ref[tick, e]
        row = lax.rem(word, row_tiles)
        block = lax.rem(lax.div(word, row_tiles), row_tiles)
        slot = lax.div(word, row_tiles * row_tiles)
        slot = jnp.where((slot == 0) & (block > 0), n - 1 + block, slot)
        rows = pl.ds(pl.multiple_of(row * tile, tile), tile)
        cols = pl.ds(pl.multiple_of(slot * tile, tile), tile)
        acc[rows, cols] += vals[e].astype(F32)

    count, step = jnp.int32(0), 1 << (entries.bit_length() - 1)
    while step:
        probe = count + step
        live = (probe <= entries) & (words_ref[tick, jnp.minimum(probe, entries) - 1] >= 0)
        count = jnp.where(live, probe, count)
        step //= 2
    for c in range(chunks):
        copies[c].wait()
        live = jnp.clip(count - c * chunk, 0, chunk)

        @pl.loop(0, live // 2)
        def _(i):
            add(c * chunk + 2 * i)
            add(c * chunk + 2 * i + 1)

        @pl.when(live % 2 == 1)
        def _():
            add(c * chunk + live - 1)

    out_ref[...] = acc[...].astype(BF16)


def densify(tick, words, vals, row_tiles, n):
    entries, tile = vals.shape[2:4]
    chunks = 4 if entries % 4 == 0 else 1
    shape = (row_tiles * tile, (n + row_tiles - 1) * tile)
    call = Call()
    call.give(SMEM, words)
    call.give(HBM, vals)
    call.want(VMEM, shape, BF16)
    call.scratch = [
        pltpu.VMEM(vals.shape[2:], BF16),
        pltpu.VMEM(shape, F32),
        pltpu.SemaphoreType.DMA((chunks,)),
    ]
    (adj,) = call.run(
        functools.partial(densify_kernel, tick, row_tiles, n, chunks),
        "densify",
        cost(entries * tile * tile * 20, entries * tile * tile * 2),
        pltpu.CompilerParams(vmem_limit_bytes=48 * 2**20),
    )
    return adj


def tile_at(ref, index, tile):
    return ref[pl.ds(pl.multiple_of(index * tile, tile), tile), :]


def name_kernel(n, row_tiles, words_ref, *out_refs):
    ticks, width = out_refs[0].shape
    for t in range(ticks):
        words = words_ref[t : t + 1, :]
        index = jnp.where(words < 0, -1, words // row_tiles)

        def named(k):
            block = index - k * row_tiles
            block = jnp.where((block >= 0) & (block < row_tiles), block, 0)
            most = jnp.max(block.astype(F32), axis=1, keepdims=True)
            return jnp.broadcast_to(most, (1, width))

        for k in range(1, n // 2):
            out_refs[k][2 * t : 2 * t + 1, :] = named(k)
            out_refs[k][2 * t + 1 : 2 * t + 2, :] = named(n // 2 + k)
        out_refs[0][t : t + 1, :] = named(n // 2)


def pack_kernel(tick, layer, preact_all, weight_all, *refs):
    asked, (out_ref, sems) = refs[:-2], refs[-2:]
    rows, width = preact_all.shape[-2:]
    loads = [
        pltpu.make_async_copy(preact_all.at[0, tick, layer], out_ref.at[:rows], sems.at[0]),
        pltpu.make_async_copy(
            weight_all.at[0, layer], out_ref.at[rows : rows + width], sems.at[1]
        ),
    ]
    for load in loads:
        load.start()
    used = sum(ref.shape[0] for ref in asked)
    rest = out_ref.shape[0] - rows - width - used
    parts = [ref[...] for ref in asked] + ([jnp.zeros((rest, width), F32)] if rest else [])
    out_ref[rows + width :, :] = jnp.concatenate(parts, axis=0).astype(BF16)
    for load in loads:
        load.wait()


def chosen(image_ref, row, rows, tile):
    index = jnp.broadcast_to(row.astype(BF16), (tile, row.shape[1]))
    result = image_ref[:tile, :]
    for i in range(1, rows // tile):
        result = jnp.where(index > i - 0.5, image_ref[i * tile : (i + 1) * tile, :], result)
    return result


def take_got(refs, c):
    far, near = refs.take(), refs.take(c["n"] // 2 - 1)
    if c["joined"]:
        return far, near, [ref.at[c["tile"] :, :] for ref in near]
    return far, near, refs.take(c["n"] // 2 - 1)


def spread_of(adj_ref, own_ref, got, names_ref, c):
    tile, rows = c["tile"], c["rows"]
    far, near, relayed = got
    far = chosen(far, names_ref[c["tick"] : c["tick"] + 1, :], rows, tile)
    near = [ref[:tile, :] for ref in near]
    relayed = [ref[:tile, :] for ref in relayed]
    blocks = jnp.concatenate(
        [own_ref[:tile, :]] + near + [far] + relayed + [own_ref[tile:, :]], axis=0
    )
    total = jnp.dot(adj_ref[...], blocks, preferred_element_type=F32)
    return ((1.0 - ALPHA) * total).astype(BF16)


def image_of(c, section, layer, grad, preact, weight):
    step = (c["layers"] * section + layer + 1).astype(F32)
    beta = jnp.log(BETA_SCALE / jnp.full((1, c["width"]), step, F32) + 1.0)
    masked = jnp.where(preact > 0, grad, jnp.zeros_like(grad))
    product = lax.dot_general(
        masked, weight, (((1,), (1,)), ((), ())), preferred_element_type=F32
    )
    image = ((1.0 - beta) * masked.astype(F32) + beta * product).astype(BF16)
    return beta, masked, image


def layer_kernel(c, *refs):
    refs = Refs(refs)
    n, tile, width, chunk = c["n"], c["tile"], c["width"], c["chunk"]
    h = n // 2
    preact_all, weight_all, names_ref = refs.take(3)
    asked = refs.take(h - 1)
    if c["entry"]:
        last_ref, passed_ref = refs.take(2)
    else:
        adj_ref, own_ref = refs.take(2)
        got = take_got(refs, c)
    if c["final"]:
        support_all, acc_ref = refs.take(2)
        pending = refs.take(c["pending"])
    image_ref = refs.take()
    sends = [] if c["entry"] else refs.take(h - 1)
    parts = refs.take(h - 1) if c["final"] and c["layer"] else []
    out_ref = refs.take()
    if c["final"]:
        term_ref = refs.take()
    preact_ref = preact_all.at[0, c["tick"], c["layer"]]
    weight_ref = weight_all.at[0, c["layer"]]
    section = lax.axis_index("section")
    if not c["entry"]:
        grad = spread_of(adj_ref, own_ref, got, names_ref, c)
    if c["entry"]:
        grad = jnp.where(section == c["sections"] - 1, last_ref[...], passed_ref[...])

    beta, masked, image = image_of(
        c, section, c["layer"], grad, preact_ref[...], weight_ref[...]
    )
    image_ref[...] = image
    if not c["entry"]:
        for send, asked_ref in zip(sends, asked):
            row = asked_ref[2 * c["tick"] : 2 * c["tick"] + 1, :]
            send[:tile, :] = chosen(image_ref, row, c["rows"], tile)
    if c["final"]:
        term = lax.dot_general(
            support_all[0, c["tick"], c["layer"]],
            masked,
            (((0,), (0,)), ((), ())),
            preferred_element_type=F32,
        )
        term_ref[...] = acc_ref[...] + beta * term
        place = lax.rem(lax.axis_index("rows"), h)
        for k in range(1, h):
            part = tile_at(term_ref, jnp.bitwise_xor(place, k), chunk).astype(BF16)
            if c["layer"]:
                parts[k - 1][...] = part
            else:
                sends[k - 1][tile : tile + chunk, :] = part
                for i, ref in enumerate(pending[k - 1 :: h - 1], 1):
                    sends[k - 1][tile + i * chunk : tile + (i + 1) * chunk, :] = ref[...]
        out_ref[...] = tile_at(term_ref, place, chunk)
    else:
        out_ref[...] = masked


def forward_kernel(c, *refs):
    refs = Refs(refs)
    count, tile, rows = c["n"] // 2 - 1, c["tile"], c["rows"]
    far_ref = refs.take()
    own_ref = refs.take() if c["first"] else None
    asked = refs.take(count)
    for asked_ref, send in zip(asked, refs.take(count)):
        row = 2 * c["tick"]
        if c["first"]:
            send[:tile, :] = chosen(own_ref, asked_ref[row : row + 1, :], rows, tile)
            send[tile:, :] = chosen(far_ref, asked_ref[row + 1 : row + 2, :], rows, tile)
        else:
            send[...] = chosen(far_ref, asked_ref[row + 1 : row + 2, :], rows, tile)


def half_sum_kernel(layers, tile, *refs):
    out_ref = refs[-1]
    chunk = out_ref.shape[1]
    for layer in range(layers):
        total = refs[layer][...]
        at = tile + layer * chunk
        for ref in refs[layers:-1]:
            total = total + ref[at : at + chunk, :].astype(F32)
        out_ref[layer] = total.astype(BF16)


def total_kernel(mine_ref, far_ref, out_ref):
    out_ref[...] = (mine_ref[...].astype(F32) + far_ref[...].astype(F32)).astype(BF16)


def turn_kernel(c, *refs):
    refs = Refs(refs)
    names_ref, adj_ref, own_ref = refs.take(3)
    got = take_got(refs, c)
    below_ref, last_ref = refs.take(2)
    grad_ref, image_ref = refs.take(2)
    sends = refs.take(c["n"] // 2 - 1)
    tile, rows, width = c["tile"], c["rows"], c["width"]
    grad = spread_of(adj_ref, own_ref, got, names_ref, c)
    grad_ref[...] = grad
    section = lax.axis_index("section")
    grad = jnp.where(section == 0, last_ref[...], grad)
    below = jnp.where(section == 0, c["sections"], section) - 1
    _, _, image = image_of(
        c, below, c["layers"] - 1, grad, below_ref[:rows, :], below_ref[rows : rows + width, :]
    )
    image_ref[...] = image
    asked = below_ref[rows + width :, :].astype(F32)
    for k, send in enumerate(sends):
        row = 2 * (k * c["ticks"] + c["tick"] + 1)
        send[...] = chosen(image_ref, asked[row : row + 1, :], rows, tile)


def exit_kernel(c, *refs):
    refs = Refs(refs)
    names_ref, adj_ref, own_ref = refs.take(3)
    got = take_got(refs, c)
    handed = refs.take(c["tick"])
    out_ref, hold_ref, sems = refs.take(3)
    copies = [
        pltpu.make_async_copy(ref, out_ref.at[t, 0], sems.at[t])
        for t, ref in enumerate(handed + [hold_ref])
    ]
    for copy in copies[:-1]:
        copy.start()
    hold_ref[...] = spread_of(adj_ref, own_ref, got, names_ref, c)
    copies[-1].start()
    for copy in copies:
        copy.wait()


def finish_kernel(h, *refs):
    sums, (out_ref, hold_ref, sems) = refs[:h], refs[h:]
    layers, chunk, _ = sums[0].shape
    place = lax.rem(lax.axis_index("rows"), h)
    copies = []
    for layer in range(layers):
        for k in range(h):
            start = pl.multiple_of(jnp.bitwise_xor(place, k) * chunk, chunk)
            hold_ref[layer, pl.ds(start, chunk), :] = sums[k][layer].astype(F32)
        copy = pltpu.make_async_copy(hold_ref.at[layer], out_ref.at[0, layer], sems.at[layer])
        copy.start()
        copies.append(copy)
    for copy in copies:
        copy.wait()


def shards(grad_in, grad_last, support, preact, weights, tile_vals, tile_row, tile_col, tile_count):
    section = lax.axis_index("section")
    n = lax.axis_size("rows")
    h = n // 2
    sections = lax.axis_size("section")
    ticks = support.shape[1]
    layers = support.shape[2]
    rows, width = grad_last.shape
    tile = tile_vals.shape[-1]
    row_tiles = rows // tile
    chunk = width // h
    words = packed(tile_row, tile_col, tile_count, row_tiles)

    handed = []
    turned = None
    weight_acc = [None] * layers
    kept_chunks, pending = [], []
    initial = []
    base = dict(
        n=n, tile=tile, rows=rows, width=width, layers=layers, sections=sections, chunk=chunk,
        ticks=ticks,
    )
    layer_cost = cost(2 * rows * width * (width + (n + 1) * tile), (6 + 2 * n) * rows * width)
    small_cost = cost(rows * width, 2 * n * rows * width)
    relay_cost = cost(rows * width, 8 * n * rows * width)
    call = Call()
    call.give(VMEM, words)
    call.want(VMEM, (ticks, width), F32)
    call.want(VMEM, (2 * ticks, width), F32, h - 1)
    names, *asking = call.run(functools.partial(name_kernel, n, row_tiles), "name", small_cost)
    asked = shared(asking)

    adjs = [None] * ticks
    for tick in range(ticks):
        final = tick == ticks - 1
        if tick > 0:
            passed = lowered(handed[-1], 0)
        image = got = joined = None
        toward = 0.0
        for layer in reversed(range(layers)):
            entry = layer == layers - 1
            beta = jnp.log(BETA_SCALE / (layers * section + layer + 1).astype(F32) + 1.0)
            c = dict(
                base, layer=layer, tick=tick, entry=entry, final=final, joined=joined,
                first=tick == 0 and entry, pending=0 if layer else len(pending),
            )
            if c["first"]:
                masked = jnp.where(
                    preact[0, tick, layer] > 0, grad_in[0], jnp.zeros_like(grad_in[0])
                )
                product = jnp.dot(masked, weights[0, layer].T, preferred_element_type=F32)
                image = ((1.0 - beta) * masked.astype(F32) + beta * product).astype(BF16)
            else:
                if turned is not None:
                    lowered_far = lowered(turned[0], h)
                    *others, farthest = shared(turned[1:], lowered)
                    lowered_far, farthest = lax.optimization_barrier((lowered_far, farthest))
                    passed, others = lax.optimization_barrier((passed, others))
                    lowered_near = [*others, farthest]
                call = Call()
                call.give(VMEM, preact, weights, names, *asked)
                if entry:
                    call.give(VMEM, grad_last, passed)
                else:
                    call.give(VMEM, adjs[tick], image, *got)
                if final:
                    call.give(VMEM, support, weight_acc[layer])
                    if layer == 0:
                        call.give(VMEM, *pending)
                call.want(VMEM, (rows, width), BF16)
                if not entry:
                    message = tile + (layers * chunk if final and layer == 0 else 0)
                    call.want(VMEM, (message, width), BF16, h - 1)
                if final and layer:
                    call.want(VMEM, (chunk, width), BF16, h - 1)
                if final:
                    call.want(VMEM, (chunk, width), F32)
                else:
                    call.want(VMEM, (rows, width), BF16)
                if final:
                    call.scratch = [pltpu.VMEM((width, width), F32)]
                results = Refs(
                    call.run(
                        functools.partial(layer_kernel, c),
                        "home" if entry else "middle",
                        layer_cost,
                    )
                )
                image = results.take()
                sends = [] if entry else results.take(h - 1)
                if final and layer:
                    pending = results.take(h - 1) + pending
                kept = masked = results.take()
            if turned is not None:
                far, near = lowered_far, lowered_near
                turned = None
            else:
                far = swapped(image, h)
                near = [] if c["first"] else shared(sends)
            ready = image
            if c["first"]:
                adjs[0] = densify(0, words, tile_vals, row_tiles, n)
                ready, adjs[0] = lax.optimization_barrier((image, adjs[0]))
            call = Call()
            call.give(VMEM, far)
            if c["first"]:
                call.give(VMEM, ready)
            call.give(VMEM, *asked)
            call.want(VMEM, (tile * (1 + c["first"]), width), BF16, h - 1)
            relays = call.run(functools.partial(forward_kernel, c), "forward", small_cost)
            relayed = shared(relays)
            if c["first"]:
                asked_later, _ = lax.optimization_barrier((asked, relays))
            if layer == 0 and not final:
                later, *_ = lax.optimization_barrier((words, *near))
                adjs[tick + 1] = densify(tick + 1, later, tile_vals, row_tiles, n)
                relayed, adjs[tick + 1] = lax.optimization_barrier((relayed, adjs[tick + 1]))
            if final:
                kept_chunks.insert(0, kept)
            if final and layer == 0:
                kept, _ = lax.optimization_barrier((kept_chunks, relays))
                call = Call()
                call.give(VMEM, *kept, *near)
                call.want(VMEM, (layers, chunk, width), BF16)
                (mine,) = call.run(
                    functools.partial(half_sum_kernel, layers, tile), "half_sum", small_cost
                )
            got = [far, *near, *relayed]
            joined = c["first"]
            toward = toward + ALPHA * image.astype(F32)
            if not final:
                term = beta * jnp.dot(
                    support[0, tick, layer].T, masked, preferred_element_type=F32
                )
                old = weight_acc[layer]
                weight_acc[layer] = term if old is None else old + term
                if c["first"]:
                    got, weight_acc[layer] = lax.optimization_barrier((got, weight_acc[layer]))
        initial.append(toward)
        c = dict(base, tick=tick, final=final, joined=joined)
        call = Call()
        call.give(VMEM, names, adjs[tick], image, *got)
        if not final:
            up = Call()
            up.give(HBM, preact, weights)
            up.give(VMEM, *asked_later)
            length = rows + width + -(-2 * ticks * (h - 1) // 16) * 16
            up.want(VMEM, (length, width), BF16)
            up.scratch = [pltpu.SemaphoreType.DMA((2,))]
            (pack,) = up.run(
                functools.partial(pack_kernel, tick + 1, layers - 1), "pack", small_cost
            )
            call.give(VMEM, raised(pack), grad_last)
            call.want(VMEM, (rows, width), BF16, 2)
            call.want(VMEM, (tile, width), BF16, h - 1)
            grad, *turned = call.run(functools.partial(turn_kernel, c), "turn", layer_cost)
            handed.append(grad)
            continue
        call.give(VMEM, *handed)
        call.want(HBM, (ticks, 1, rows, width), BF16)
        call.scratch = [pltpu.VMEM((rows, width), BF16), pltpu.SemaphoreType.DMA((ticks,))]
        (handoff,) = call.run(functools.partial(exit_kernel, c), "exit", layer_cost)
    call = Call()
    call.give(VMEM, mine, swapped(mine, h))
    call.want(VMEM, (layers, chunk, width), BF16)
    (total,) = call.run(total_kernel, "total", small_cost)
    call = Call()
    call.give(VMEM, total, *shared([total] * (h - 1)))
    call.want(HBM, (1, layers, width, width), F32)
    call.scratch = [pltpu.VMEM((layers, width, width), F32), pltpu.SemaphoreType.DMA((layers,))]
    (weight_grad,) = call.run(functools.partial(finish_kernel, h), "finish", small_cost)
    return handoff, jnp.stack(initial)[None], weight_grad


def solution(mesh):
    return jax.shard_map(
        shards,
        mesh=mesh,
        in_specs=(
            P("section", "rows", None),
            P("rows", None),
            P("section", None, None, "rows", None),
            P("section", None, None, "rows", None),
            P("section", None, None, None),
            P("section", None, "rows", None, None),
            P("section", None, "rows"),
            P("section", None, "rows"),
            P("section", None, "rows"),
        ),
        out_specs=(
            P(None, "section", "rows", None),
            P("section", None, "rows", None),
            P("section", None, None, None),
        ),
        check_vma=False,
    )
```

```python
import functools

import jax
import jax.numpy as jnp
from jax import lax
from jax.experimental import pallas as pl
from jax.experimental.pallas import tpu as pltpu
from jax.sharding import PartitionSpec as P

ALPHA = 0.1
BETA_SCALE = 0.5
VMEM = pl.BlockSpec(memory_space=pltpu.VMEM)
SMEM = pl.BlockSpec(memory_space=pltpu.SMEM)
HBM = pl.BlockSpec(memory_space=pltpu.HBM)
PARAMS = pltpu.CompilerParams(vmem_limit_bytes=24 * 2**20)
F32 = jnp.float32
BF16 = jnp.bfloat16


def cost(flops, nbytes):
    return pl.CostEstimate(flops=flops, bytes_accessed=nbytes, transcendentals=0)


def swapped(block, k):
    n = lax.axis_size("rows")
    return lax.ppermute(block, "rows", [(i, i ^ k) for i in range(n)])


def lowered(block, k):
    n, sections = lax.axis_size("rows"), lax.axis_size("section")
    route = [
        (s * n + i, (s - 1) % sections * n + (i ^ k)) for s in range(sections) for i in range(n)
    ]
    return lax.ppermute(block, ("section", "rows"), route)


def raised(block):
    sections = lax.axis_size("section")
    return lax.ppermute(block, "section", [(s, (s + 1) % sections) for s in range(sections)])


def shared(blocks, move=swapped):
    moved = {k: move(block, k) for k, block in reversed(list(enumerate(blocks, 1)))}
    return [moved[k] for k in sorted(moved)]


class Refs:
    def __init__(self, refs):
        self.refs = list(refs)

    def take(self, count=None):
        many = 1 if count is None else count
        taken, self.refs = self.refs[:many], self.refs[many:]
        return taken[0] if count is None else taken


class Call:
    def __init__(self):
        self.operands, self.specs, self.outs, self.out_specs, self.scratch = [], [], [], [], []
        self.aliases = {}

    def give(self, spec, *arrays):
        self.operands += arrays
        self.specs += [spec] * len(arrays)

    def want(self, spec, shape, dtype, count=1):
        self.outs += [jax.ShapeDtypeStruct(shape, dtype)] * count
        self.out_specs += [spec] * count

    def run(self, kernel, name, estimate, params=PARAMS):
        return pl.pallas_call(
            kernel,
            out_shape=self.outs,
            in_specs=self.specs,
            out_specs=self.out_specs,
            scratch_shapes=self.scratch,
            input_output_aliases=self.aliases,
            compiler_params=params,
            cost_estimate=estimate,
            name=name,
        )(*self.operands)


def packed(tile_row, tile_col, tile_count, row_tiles):
    owner = jnp.bitwise_xor(tile_col // row_tiles, lax.axis_index("rows"))
    words = (owner * row_tiles + tile_col % row_tiles) * row_tiles + tile_row
    live = lax.broadcasted_iota(jnp.int32, words.shape, 2) < tile_count
    return jnp.where(live, words, -1)[0]


def densify_kernel(tick, row_tiles, n, chunks, words_ref, vals_ref, out_ref, vals, acc, sems):
    entries, tile = vals.shape[:2]
    chunk = entries // chunks
    copies = []
    for c in range(chunks):
        part = pl.ds(c * chunk, chunk)
        copies.append(
            pltpu.make_async_copy(vals_ref.at[0, tick, part], vals.at[part], sems.at[c])
        )
        copies[c].start()
    acc[...] = jnp.zeros_like(acc)

    def add(e):
        word = words_ref[tick, e]
        row = lax.rem(word, row_tiles)
        block = lax.rem(lax.div(word, row_tiles), row_tiles)
        slot = lax.div(word, row_tiles * row_tiles)
        slot = jnp.where((slot == 0) & (block > 0), n - 1 + block, slot)
        rows = pl.ds(pl.multiple_of(row * tile, tile), tile)
        cols = pl.ds(pl.multiple_of(slot * tile, tile), tile)
        acc[rows, cols] += vals[e].astype(F32)

    count, step = jnp.int32(0), 1 << (entries.bit_length() - 1)
    while step:
        probe = count + step
        live = (probe <= entries) & (words_ref[tick, jnp.minimum(probe, entries) - 1] >= 0)
        count = jnp.where(live, probe, count)
        step //= 2
    for c in range(chunks):
        copies[c].wait()
        live = jnp.clip(count - c * chunk, 0, chunk)

        @pl.loop(0, live // 2)
        def _(i):
            add(c * chunk + 2 * i)
            add(c * chunk + 2 * i + 1)

        @pl.when(live % 2 == 1)
        def _():
            add(c * chunk + live - 1)

    out_ref[...] = acc[...].astype(BF16)


def densify(tick, words, vals, row_tiles, n):
    entries, tile = vals.shape[2:4]
    chunks = 4 if entries % 4 == 0 else 1
    shape = (row_tiles * tile, (n + row_tiles - 1) * tile)
    call = Call()
    call.give(SMEM, words)
    call.give(HBM, vals)
    call.want(VMEM, shape, BF16)
    call.scratch = [
        pltpu.VMEM(vals.shape[2:], BF16),
        pltpu.VMEM(shape, F32),
        pltpu.SemaphoreType.DMA((chunks,)),
    ]
    (adj,) = call.run(
        functools.partial(densify_kernel, tick, row_tiles, n, chunks),
        "densify",
        cost(entries * tile * tile * 20, entries * tile * tile * 2),
        pltpu.CompilerParams(vmem_limit_bytes=50 * 2**20),
    )
    return adj


def tile_at(ref, index, tile):
    return ref[pl.ds(pl.multiple_of(index * tile, tile), tile), :]


def name_kernel(n, row_tiles, words_ref, *out_refs):
    ticks, width = out_refs[0].shape
    for t in range(ticks):
        words = words_ref[t : t + 1, :]
        index = jnp.where(words < 0, -1, words // row_tiles)

        def named(k):
            block = index - k * row_tiles
            block = jnp.where((block >= 0) & (block < row_tiles), block, 0)
            most = jnp.max(block.astype(F32), axis=1, keepdims=True)
            return jnp.broadcast_to(most, (1, width))

        for k in range(1, n // 2):
            out_refs[k][2 * t : 2 * t + 1, :] = named(k)
            out_refs[k][2 * t + 1 : 2 * t + 2, :] = named(n // 2 + k)
        out_refs[0][t : t + 1, :] = named(n // 2)


def pack_kernel(tick, layer, preact_all, weight_all, *refs):
    asked, (out_ref, sems) = refs[:-2], refs[-2:]
    rows, width = preact_all.shape[-2:]
    loads = [
        pltpu.make_async_copy(preact_all.at[0, tick, layer], out_ref.at[:rows], sems.at[0]),
        pltpu.make_async_copy(
            weight_all.at[0, layer], out_ref.at[rows : rows + width], sems.at[1]
        ),
    ]
    for load in loads:
        load.start()
    used = sum(ref.shape[0] for ref in asked)
    rest = out_ref.shape[0] - rows - width - used
    parts = [ref[...] for ref in asked] + ([jnp.zeros((rest, width), F32)] if rest else [])
    out_ref[rows + width :, :] = jnp.concatenate(parts, axis=0).astype(BF16)
    for load in loads:
        load.wait()


def chosen(image_ref, row, rows, tile):
    index = jnp.broadcast_to(row.astype(BF16), (tile, row.shape[1]))
    result = image_ref[:tile, :]
    for i in range(1, rows // tile):
        result = jnp.where(index > i - 0.5, image_ref[i * tile : (i + 1) * tile, :], result)
    return result


def take_got(refs, c):
    far, near = refs.take(), refs.take(c["n"] // 2 - 1)
    if c["joined"]:
        return far, near, [ref.at[c["tile"] :, :] for ref in near]
    return far, near, refs.take(c["n"] // 2 - 1)


def spread_of(adj_ref, own_ref, got, names_ref, c):
    tile, rows = c["tile"], c["rows"]
    far, near, relayed = got
    far = chosen(far, names_ref[c["tick"] : c["tick"] + 1, :], rows, tile)
    near = [ref[:tile, :] for ref in near]
    relayed = [ref[:tile, :] for ref in relayed]
    blocks = jnp.concatenate(
        [own_ref[:tile, :]] + near + [far] + relayed + [own_ref[tile:, :]], axis=0
    )
    total = jnp.dot(adj_ref[...], blocks, preferred_element_type=F32)
    return ((1.0 - ALPHA) * total).astype(BF16)


def image_of(c, section, layer, grad, preact, weight):
    step = (c["layers"] * section + layer + 1).astype(F32)
    beta = jnp.log(BETA_SCALE / jnp.full((1, c["width"]), step, F32) + 1.0)
    masked = jnp.where(preact > 0, grad, jnp.zeros_like(grad))
    product = lax.dot_general(
        masked, weight, (((1,), (1,)), ((), ())), preferred_element_type=F32
    )
    image = ((1.0 - beta) * masked.astype(F32) + beta * product).astype(BF16)
    return beta, masked, image


def layer_kernel(c, *refs):
    refs = Refs(refs)
    n, tile, width, chunk = c["n"], c["tile"], c["width"], c["chunk"]
    h = n // 2
    preact_all, weight_all, names_ref = refs.take(3)
    asked = refs.take(h - 1)
    if c["entry"]:
        last_ref, passed_ref = refs.take(2)
    else:
        adj_ref, own_ref = refs.take(2)
        got = take_got(refs, c)
    if c["final"]:
        support_all, acc_ref = refs.take(2)
        pending = refs.take(c["pending"])
    image_ref = refs.take()
    sends = [] if c["entry"] else refs.take(h - 1)
    parts = refs.take(h - 1) if c["final"] and c["layer"] else []
    out_ref = refs.take()
    if c["final"]:
        term_ref = refs.take()
    preact_ref = preact_all.at[0, c["tick"], c["layer"]]
    weight_ref = weight_all.at[0, c["layer"]]
    section = lax.axis_index("section")
    if not c["entry"]:
        grad = spread_of(adj_ref, own_ref, got, names_ref, c)
    if c["entry"]:
        grad = jnp.where(section == c["sections"] - 1, last_ref[...], passed_ref[...])

    beta, masked, image = image_of(
        c, section, c["layer"], grad, preact_ref[...], weight_ref[...]
    )
    image_ref[...] = image
    if not c["entry"]:
        for send, asked_ref in zip(sends, asked):
            row = asked_ref[2 * c["tick"] : 2 * c["tick"] + 1, :]
            send[:tile, :] = chosen(image_ref, row, c["rows"], tile)
    if c["final"]:
        term = lax.dot_general(
            support_all[0, c["tick"], c["layer"]],
            masked,
            (((0,), (0,)), ((), ())),
            preferred_element_type=F32,
        )
        term_ref[...] = acc_ref[...] + beta * term
        place = lax.rem(lax.axis_index("rows"), h)
        for k in range(1, h):
            part = tile_at(term_ref, jnp.bitwise_xor(place, k), chunk).astype(BF16)
            if c["layer"]:
                parts[k - 1][...] = part
            else:
                sends[k - 1][tile : tile + chunk, :] = part
                for i, ref in enumerate(pending[k - 1 :: h - 1], 1):
                    sends[k - 1][tile + i * chunk : tile + (i + 1) * chunk, :] = ref[...]
        out_ref[...] = tile_at(term_ref, place, chunk)
    else:
        out_ref[...] = masked


def forward_kernel(c, *refs):
    refs = Refs(refs)
    count, tile, rows = c["n"] // 2 - 1, c["tile"], c["rows"]
    far_ref = refs.take()
    own_ref = refs.take() if c["first"] else None
    asked = refs.take(count)
    for asked_ref, send in zip(asked, refs.take(count)):
        row = 2 * c["tick"]
        if c["first"]:
            send[:tile, :] = chosen(own_ref, asked_ref[row : row + 1, :], rows, tile)
            send[tile:, :] = chosen(far_ref, asked_ref[row + 1 : row + 2, :], rows, tile)
        else:
            send[...] = chosen(far_ref, asked_ref[row + 1 : row + 2, :], rows, tile)


def half_sum_kernel(layers, tile, *refs):
    out_ref = refs[-1]
    chunk = out_ref.shape[1]
    for layer in range(layers):
        total = refs[layer][...]
        at = tile + layer * chunk
        for ref in refs[layers:-1]:
            total = total + ref[at : at + chunk, :].astype(F32)
        out_ref[layer] = total.astype(BF16)


def total_kernel(mine_ref, far_ref, out_ref):
    out_ref[...] = (mine_ref[...].astype(F32) + far_ref[...].astype(F32)).astype(BF16)


def turn_kernel(c, *refs):
    refs = Refs(refs)
    names_ref, adj_ref, own_ref = refs.take(3)
    got = take_got(refs, c)
    below_ref, last_ref = refs.take(2)
    grad_ref, image_ref = refs.take(2)
    sends = refs.take(c["n"] // 2 - 1)
    tile, rows, width = c["tile"], c["rows"], c["width"]
    grad = spread_of(adj_ref, own_ref, got, names_ref, c)
    grad_ref[...] = grad
    section = lax.axis_index("section")
    grad = jnp.where(section == 0, last_ref[...], grad)
    below = jnp.where(section == 0, c["sections"], section) - 1
    _, _, image = image_of(
        c, below, c["layers"] - 1, grad, below_ref[:rows, :], below_ref[rows : rows + width, :]
    )
    image_ref[...] = image
    asked = below_ref[rows + width :, :].astype(F32)
    for k, send in enumerate(sends):
        row = 2 * (k * c["ticks"] + c["tick"] + 1)
        send[...] = chosen(image_ref, asked[row : row + 1, :], rows, tile)


def exit_kernel(c, *refs):
    refs = Refs(refs)
    names_ref, adj_ref, own_ref = refs.take(3)
    got = take_got(refs, c)
    handed = refs.take(c["tick"])
    out_ref, hold_ref, sems = refs.take(3)
    copies = [
        pltpu.make_async_copy(ref, out_ref.at[t, 0], sems.at[t])
        for t, ref in enumerate(handed + [hold_ref])
    ]
    for copy in copies[:-1]:
        copy.start()
    hold_ref[...] = spread_of(adj_ref, own_ref, got, names_ref, c)
    copies[-1].start()
    for copy in copies:
        copy.wait()


def finish_kernel(h, *refs):
    sums, (out_ref, hold_ref, sems) = refs[:h], refs[h:]
    layers, chunk, _ = sums[0].shape
    place = lax.rem(lax.axis_index("rows"), h)
    copies = []
    for layer in range(layers):
        for k in range(h):
            start = pl.multiple_of(jnp.bitwise_xor(place, k) * chunk, chunk)
            hold_ref[layer, pl.ds(start, chunk), :] = sums[k][layer].astype(F32)
        copy = pltpu.make_async_copy(hold_ref.at[layer], out_ref.at[0, layer], sems.at[layer])
        copy.start()
        copies.append(copy)
    for copy in copies:
        copy.wait()


def shards(grad_in, grad_last, support, preact, weights, tile_vals, tile_row, tile_col, tile_count):
    section = lax.axis_index("section")
    n = lax.axis_size("rows")
    h = n // 2
    sections = lax.axis_size("section")
    ticks = support.shape[1]
    layers = support.shape[2]
    rows, width = grad_last.shape
    tile = tile_vals.shape[-1]
    row_tiles = rows // tile
    chunk = width // h
    words = packed(tile_row, tile_col, tile_count, row_tiles)

    handed = []
    turned = None
    weight_acc = [None] * layers
    kept_chunks, pending = [], []
    initial = []
    base = dict(
        n=n, tile=tile, rows=rows, width=width, layers=layers, sections=sections, chunk=chunk,
        ticks=ticks,
    )
    layer_cost = cost(2 * rows * width * (width + (n + 1) * tile), (6 + 2 * n) * rows * width)
    small_cost = cost(rows * width, 2 * n * rows * width)
    relay_cost = cost(rows * width, 8 * n * rows * width)
    call = Call()
    call.give(VMEM, words)
    call.want(VMEM, (ticks, width), F32)
    call.want(VMEM, (2 * ticks, width), F32, h - 1)
    names, *asking = call.run(functools.partial(name_kernel, n, row_tiles), "name", small_cost)
    asked = shared(asking)

    adjs = [None] * ticks
    for tick in range(ticks):
        final = tick == ticks - 1
        if tick > 0:
            passed = lowered(handed[-1], 0)
        image = got = joined = None
        toward = 0.0
        for layer in reversed(range(layers)):
            entry = layer == layers - 1
            beta = jnp.log(BETA_SCALE / (layers * section + layer + 1).astype(F32) + 1.0)
            c = dict(
                base, layer=layer, tick=tick, entry=entry, final=final, joined=joined,
                first=tick == 0 and entry, pending=0 if layer else len(pending),
            )
            if c["first"]:
                masked = jnp.where(
                    preact[0, tick, layer] > 0, grad_in[0], jnp.zeros_like(grad_in[0])
                )
                product = jnp.dot(masked, weights[0, layer].T, preferred_element_type=F32)
                image = ((1.0 - beta) * masked.astype(F32) + beta * product).astype(BF16)
            else:
                if turned is not None:
                    lowered_far = lowered(turned[0], h)
                    *others, farthest = shared(turned[1:], lowered)
                    lowered_far, farthest = lax.optimization_barrier((lowered_far, farthest))
                    passed, others = lax.optimization_barrier((passed, others))
                    lowered_near = [*others, farthest]
                call = Call()
                call.give(VMEM, preact, weights, names, *asked)
                if entry:
                    call.give(VMEM, grad_last, passed)
                else:
                    call.give(VMEM, adjs[tick], image, *got)
                if final:
                    call.give(VMEM, support, weight_acc[layer])
                    if layer == 0:
                        call.give(VMEM, *pending)
                call.want(VMEM, (rows, width), BF16)
                if not entry:
                    message = tile + (layers * chunk if final and layer == 0 else 0)
                    call.want(VMEM, (message, width), BF16, h - 1)
                if final and layer:
                    call.want(VMEM, (chunk, width), BF16, h - 1)
                if final:
                    call.want(VMEM, (chunk, width), F32)
                else:
                    call.want(VMEM, (rows, width), BF16)
                if final:
                    call.scratch = [pltpu.VMEM((width, width), F32)]
                results = Refs(
                    call.run(
                        functools.partial(layer_kernel, c),
                        "home" if entry else "middle",
                        layer_cost,
                    )
                )
                image = results.take()
                sends = [] if entry else results.take(h - 1)
                if final and layer:
                    pending = results.take(h - 1) + pending
                kept = masked = results.take()
            if turned is not None:
                far, near = lowered_far, lowered_near
                turned = None
            else:
                far = swapped(image, h)
                near = [] if c["first"] else shared(sends)
            ready = image
            if c["first"]:
                adjs[0] = densify(0, words, tile_vals, row_tiles, n)
                ready, adjs[0] = lax.optimization_barrier((image, adjs[0]))
            call = Call()
            call.give(VMEM, far)
            if c["first"]:
                call.give(VMEM, ready)
            call.give(VMEM, *asked)
            call.want(VMEM, (tile * (1 + c["first"]), width), BF16, h - 1)
            relays = call.run(functools.partial(forward_kernel, c), "forward", small_cost)
            relayed = shared(relays)
            if layer == 0 and not final:
                later, *_ = lax.optimization_barrier((words, *near))
                adjs[tick + 1] = densify(tick + 1, later, tile_vals, row_tiles, n)
                relayed, adjs[tick + 1] = lax.optimization_barrier((relayed, adjs[tick + 1]))
            if final:
                kept_chunks.insert(0, kept)
            if final and layer == 0:
                kept, _ = lax.optimization_barrier((kept_chunks, relays))
                call = Call()
                call.give(VMEM, *kept, *near)
                call.want(VMEM, (layers, chunk, width), BF16)
                (mine,) = call.run(
                    functools.partial(half_sum_kernel, layers, tile), "half_sum", small_cost
                )
            got = [far, *near, *relayed]
            joined = c["first"]
            toward = toward + ALPHA * image.astype(F32)
            if not final:
                term = beta * jnp.dot(
                    support[0, tick, layer].T, masked, preferred_element_type=F32
                )
                old = weight_acc[layer]
                weight_acc[layer] = term if old is None else old + term
        initial.append(toward)
        c = dict(base, tick=tick, final=final, joined=joined)
        call = Call()
        call.give(VMEM, names, adjs[tick], image, *got)
        if not final:
            up = Call()
            up.give(HBM, preact, weights)
            up.give(VMEM, *asked)
            length = rows + width + -(-2 * ticks * (h - 1) // 16) * 16
            up.want(VMEM, (length, width), BF16)
            up.scratch = [pltpu.SemaphoreType.DMA((2,))]
            (pack,) = up.run(
                functools.partial(pack_kernel, tick + 1, layers - 1), "pack", small_cost
            )
            call.give(VMEM, raised(pack), grad_last)
            call.want(VMEM, (rows, width), BF16, 2)
            call.want(VMEM, (tile, width), BF16, h - 1)
            grad, *turned = call.run(functools.partial(turn_kernel, c), "turn", layer_cost)
            handed.append(grad)
            continue
        call.give(VMEM, *handed)
        call.want(HBM, (ticks, 1, rows, width), BF16)
        call.scratch = [pltpu.VMEM((rows, width), BF16), pltpu.SemaphoreType.DMA((ticks,))]
        (handoff,) = call.run(functools.partial(exit_kernel, c), "exit", layer_cost)
    call = Call()
    call.give(VMEM, mine, swapped(mine, h))
    call.want(VMEM, (layers, chunk, width), BF16)
    (total,) = call.run(total_kernel, "total", small_cost)
    call = Call()
    call.give(VMEM, total, *shared([total] * (h - 1)))
    call.want(HBM, (1, layers, width, width), F32)
    call.scratch = [pltpu.VMEM((layers, width, width), F32), pltpu.SemaphoreType.DMA((layers,))]
    (weight_grad,) = call.run(functools.partial(finish_kernel, h), "finish", small_cost)
    return handoff, jnp.stack(initial)[None], weight_grad


def solution(mesh):
    return jax.shard_map(
        shards,
        mesh=mesh,
        in_specs=(
            P("section", "rows", None),
            P("rows", None),
            P("section", None, None, "rows", None),
            P("section", None, None, "rows", None),
            P("section", None, None, None),
            P("section", None, "rows", None, None),
            P("section", None, "rows"),
            P("section", None, "rows"),
            P("section", None, "rows"),
        ),
        out_specs=(
            P(None, "section", "rows", None),
            P("section", None, "rows", None),
            P("section", None, None, None),
        ),
        check_vma=False,
    )
```

```python
import functools

import jax
import jax.numpy as jnp
from jax import lax
from jax.experimental import pallas as pl
from jax.experimental.pallas import tpu as pltpu
from jax.sharding import PartitionSpec as P

ALPHA = 0.1
BETA_SCALE = 0.5
VMEM = pl.BlockSpec(memory_space=pltpu.VMEM)
SMEM = pl.BlockSpec(memory_space=pltpu.SMEM)
HBM = pl.BlockSpec(memory_space=pltpu.HBM)
PARAMS = pltpu.CompilerParams(vmem_limit_bytes=24 * 2**20)
F32 = jnp.float32
BF16 = jnp.bfloat16


def cost(flops, nbytes):
    return pl.CostEstimate(flops=flops, bytes_accessed=nbytes, transcendentals=0)


def swapped(block, k):
    n = lax.axis_size("rows")
    return lax.ppermute(block, "rows", [(i, i ^ k) for i in range(n)])


def lowered(block, k):
    n, sections = lax.axis_size("rows"), lax.axis_size("section")
    route = [
        (s * n + i, (s - 1) % sections * n + (i ^ k)) for s in range(sections) for i in range(n)
    ]
    return lax.ppermute(block, ("section", "rows"), route)


def raised(block):
    sections = lax.axis_size("section")
    return lax.ppermute(block, "section", [(s, (s + 1) % sections) for s in range(sections)])


def shared(blocks, move=swapped):
    moved = {k: move(block, k) for k, block in reversed(list(enumerate(blocks, 1)))}
    return [moved[k] for k in sorted(moved)]


class Refs:
    def __init__(self, refs):
        self.refs = list(refs)

    def take(self, count=None):
        many = 1 if count is None else count
        taken, self.refs = self.refs[:many], self.refs[many:]
        return taken[0] if count is None else taken


class Call:
    def __init__(self):
        self.operands, self.specs, self.outs, self.out_specs, self.scratch = [], [], [], [], []
        self.aliases = {}

    def give(self, spec, *arrays):
        self.operands += arrays
        self.specs += [spec] * len(arrays)

    def want(self, spec, shape, dtype, count=1):
        self.outs += [jax.ShapeDtypeStruct(shape, dtype)] * count
        self.out_specs += [spec] * count

    def run(self, kernel, name, estimate, params=PARAMS):
        return pl.pallas_call(
            kernel,
            out_shape=self.outs,
            in_specs=self.specs,
            out_specs=self.out_specs,
            scratch_shapes=self.scratch,
            input_output_aliases=self.aliases,
            compiler_params=params,
            cost_estimate=estimate,
            name=name,
        )(*self.operands)


def packed(tile_row, tile_col, tile_count, row_tiles):
    owner = jnp.bitwise_xor(tile_col // row_tiles, lax.axis_index("rows"))
    words = (owner * row_tiles + tile_col % row_tiles) * row_tiles + tile_row
    live = lax.broadcasted_iota(jnp.int32, words.shape, 2) < tile_count
    return jnp.where(live, words, -1)[0]


def densify_kernel(tick, row_tiles, n, chunks, words_ref, vals_ref, out_ref, vals, acc, sems):
    entries, tile = vals.shape[:2]
    chunk = entries // chunks
    copies = []
    for c in range(chunks):
        part = pl.ds(c * chunk, chunk)
        copies.append(
            pltpu.make_async_copy(vals_ref.at[0, tick, part], vals.at[part], sems.at[c])
        )
        copies[c].start()
    acc[...] = jnp.zeros_like(acc)

    def add(e):
        word = words_ref[tick, e]
        row = lax.rem(word, row_tiles)
        block = lax.rem(lax.div(word, row_tiles), row_tiles)
        slot = lax.div(word, row_tiles * row_tiles)
        slot = jnp.where((slot == 0) & (block > 0), n - 1 + block, slot)
        rows = pl.ds(pl.multiple_of(row * tile, tile), tile)
        cols = pl.ds(pl.multiple_of(slot * tile, tile), tile)
        acc[rows, cols] += vals[e].astype(F32)

    count, step = jnp.int32(0), 1 << (entries.bit_length() - 1)
    while step:
        probe = count + step
        live = (probe <= entries) & (words_ref[tick, jnp.minimum(probe, entries) - 1] >= 0)
        count = jnp.where(live, probe, count)
        step //= 2
    for c in range(chunks):
        copies[c].wait()
        live = jnp.clip(count - c * chunk, 0, chunk)

        @pl.loop(0, live // 2)
        def _(i):
            add(c * chunk + 2 * i)
            add(c * chunk + 2 * i + 1)

        @pl.when(live % 2 == 1)
        def _():
            add(c * chunk + live - 1)

    out_ref[...] = acc[...].astype(BF16)


def densify(tick, words, vals, row_tiles, n):
    entries, tile = vals.shape[2:4]
    chunks = 4 if entries % 4 == 0 else 1
    shape = (row_tiles * tile, (n + row_tiles - 1) * tile)
    call = Call()
    call.give(SMEM, words)
    call.give(HBM, vals)
    call.want(VMEM, shape, BF16)
    call.scratch = [
        pltpu.VMEM(vals.shape[2:], BF16),
        pltpu.VMEM(shape, F32),
        pltpu.SemaphoreType.DMA((chunks,)),
    ]
    (adj,) = call.run(
        functools.partial(densify_kernel, tick, row_tiles, n, chunks),
        "densify",
        cost(entries * tile * tile * 20, entries * tile * tile * 2),
        pltpu.CompilerParams(vmem_limit_bytes=50 * 2**20),
    )
    return adj


def tile_at(ref, index, tile):
    return ref[pl.ds(pl.multiple_of(index * tile, tile), tile), :]


def name_kernel(n, row_tiles, words_ref, *out_refs):
    ticks, width = out_refs[0].shape
    for t in range(ticks):
        words = words_ref[t : t + 1, :]
        index = jnp.where(words < 0, -1, words // row_tiles)

        def named(k):
            block = index - k * row_tiles
            block = jnp.where((block >= 0) & (block < row_tiles), block, 0)
            most = jnp.max(block.astype(F32), axis=1, keepdims=True)
            return jnp.broadcast_to(most, (1, width))

        for k in range(1, n // 2):
            out_refs[k][2 * t : 2 * t + 1, :] = named(k)
            out_refs[k][2 * t + 1 : 2 * t + 2, :] = named(n // 2 + k)
        out_refs[0][t : t + 1, :] = named(n // 2)


def pack_kernel(tick, layer, preact_all, weight_all, *refs):
    asked, (out_ref, sems) = refs[:-2], refs[-2:]
    rows, width = preact_all.shape[-2:]
    loads = [
        pltpu.make_async_copy(preact_all.at[0, tick, layer], out_ref.at[:rows], sems.at[0]),
        pltpu.make_async_copy(
            weight_all.at[0, layer], out_ref.at[rows : rows + width], sems.at[1]
        ),
    ]
    for load in loads:
        load.start()
    used = sum(ref.shape[0] for ref in asked)
    rest = out_ref.shape[0] - rows - width - used
    parts = [ref[...] for ref in asked] + ([jnp.zeros((rest, width), F32)] if rest else [])
    out_ref[rows + width :, :] = jnp.concatenate(parts, axis=0).astype(BF16)
    for load in loads:
        load.wait()


def chosen(image_ref, row, rows, tile):
    index = jnp.broadcast_to(row.astype(BF16), (tile, row.shape[1]))
    result = image_ref[:tile, :]
    for i in range(1, rows // tile):
        result = jnp.where(index > i - 0.5, image_ref[i * tile : (i + 1) * tile, :], result)
    return result


def take_got(refs, c):
    far, near = refs.take(), refs.take(c["n"] // 2 - 1)
    if c["joined"]:
        return far, near, [ref.at[c["tile"] :, :] for ref in near]
    return far, near, refs.take(c["n"] // 2 - 1)


def spread_of(adj_ref, own_ref, got, names_ref, c):
    tile, rows = c["tile"], c["rows"]
    far, near, relayed = got
    far = chosen(far, names_ref[c["tick"] : c["tick"] + 1, :], rows, tile)
    near = [ref[:tile, :] for ref in near]
    relayed = [ref[:tile, :] for ref in relayed]
    blocks = jnp.concatenate(
        [own_ref[:tile, :]] + near + [far] + relayed + [own_ref[tile:, :]], axis=0
    )
    total = jnp.dot(adj_ref[...], blocks, preferred_element_type=F32)
    return ((1.0 - ALPHA) * total).astype(BF16)


def image_of(c, section, layer, grad, preact, weight):
    step = (c["layers"] * section + layer + 1).astype(F32)
    beta = jnp.log(BETA_SCALE / jnp.full((1, c["width"]), step, F32) + 1.0)
    masked = jnp.where(preact > 0, grad, jnp.zeros_like(grad))
    product = lax.dot_general(
        masked, weight, (((1,), (1,)), ((), ())), preferred_element_type=F32
    )
    image = ((1.0 - beta) * masked.astype(F32) + beta * product).astype(BF16)
    return beta, masked, image


def layer_kernel(c, *refs):
    refs = Refs(refs)
    n, tile, width, chunk = c["n"], c["tile"], c["width"], c["chunk"]
    h = n // 2
    preact_all, weight_all, names_ref = refs.take(3)
    asked = refs.take(h - 1)
    if c["entry"]:
        last_ref, passed_ref = refs.take(2)
    else:
        adj_ref, own_ref = refs.take(2)
        got = take_got(refs, c)
    if c["final"]:
        support_all, acc_ref = refs.take(2)
        pending = refs.take(c["pending"])
    image_ref = refs.take()
    sends = [] if c["entry"] else refs.take(h - 1)
    parts = refs.take(h - 1) if c["final"] and c["layer"] else []
    out_ref = refs.take()
    if c["final"]:
        term_ref = refs.take()
    preact_ref = preact_all.at[0, c["tick"], c["layer"]]
    weight_ref = weight_all.at[0, c["layer"]]
    section = lax.axis_index("section")
    if not c["entry"]:
        grad = spread_of(adj_ref, own_ref, got, names_ref, c)
    if c["entry"]:
        grad = jnp.where(section == c["sections"] - 1, last_ref[...], passed_ref[...])

    beta, masked, image = image_of(
        c, section, c["layer"], grad, preact_ref[...], weight_ref[...]
    )
    image_ref[...] = image
    if not c["entry"]:
        for send, asked_ref in zip(sends, asked):
            row = asked_ref[2 * c["tick"] : 2 * c["tick"] + 1, :]
            send[:tile, :] = chosen(image_ref, row, c["rows"], tile)
    if c["final"]:
        term = lax.dot_general(
            support_all[0, c["tick"], c["layer"]],
            masked,
            (((0,), (0,)), ((), ())),
            preferred_element_type=F32,
        )
        term_ref[...] = acc_ref[...] + beta * term
        place = lax.rem(lax.axis_index("rows"), h)
        for k in range(1, h):
            part = tile_at(term_ref, jnp.bitwise_xor(place, k), chunk).astype(BF16)
            if c["layer"]:
                parts[k - 1][...] = part
            else:
                sends[k - 1][tile : tile + chunk, :] = part
                for i, ref in enumerate(pending[k - 1 :: h - 1], 1):
                    sends[k - 1][tile + i * chunk : tile + (i + 1) * chunk, :] = ref[...]
        out_ref[...] = tile_at(term_ref, place, chunk)
    else:
        out_ref[...] = masked


def forward_kernel(c, *refs):
    refs = Refs(refs)
    count, tile, rows = c["n"] // 2 - 1, c["tile"], c["rows"]
    far_ref = refs.take()
    own_ref = refs.take() if c["first"] else None
    asked = refs.take(count)
    for asked_ref, send in zip(asked, refs.take(count)):
        row = 2 * c["tick"]
        if c["first"]:
            send[:tile, :] = chosen(own_ref, asked_ref[row : row + 1, :], rows, tile)
            send[tile:, :] = chosen(far_ref, asked_ref[row + 1 : row + 2, :], rows, tile)
        else:
            send[...] = chosen(far_ref, asked_ref[row + 1 : row + 2, :], rows, tile)


def half_sum_kernel(layers, tile, *refs):
    out_ref = refs[-1]
    chunk = out_ref.shape[1]
    for layer in range(layers):
        total = refs[layer][...]
        at = tile + layer * chunk
        for ref in refs[layers:-1]:
            total = total + ref[at : at + chunk, :].astype(F32)
        out_ref[layer] = total.astype(BF16)


def total_kernel(mine_ref, far_ref, out_ref):
    out_ref[...] = (mine_ref[...].astype(F32) + far_ref[...].astype(F32)).astype(BF16)


def turn_kernel(c, *refs):
    refs = Refs(refs)
    names_ref, adj_ref, own_ref = refs.take(3)
    got = take_got(refs, c)
    below_ref, last_ref = refs.take(2)
    grad_ref, image_ref = refs.take(2)
    sends = refs.take(c["n"] // 2 - 1)
    tile, rows, width = c["tile"], c["rows"], c["width"]
    grad = spread_of(adj_ref, own_ref, got, names_ref, c)
    grad_ref[...] = grad
    section = lax.axis_index("section")
    grad = jnp.where(section == 0, last_ref[...], grad)
    below = jnp.where(section == 0, c["sections"], section) - 1
    _, _, image = image_of(
        c, below, c["layers"] - 1, grad, below_ref[:rows, :], below_ref[rows : rows + width, :]
    )
    image_ref[...] = image
    asked = below_ref[rows + width :, :].astype(F32)
    for k, send in enumerate(sends):
        row = 2 * (k * c["ticks"] + c["tick"] + 1)
        send[...] = chosen(image_ref, asked[row : row + 1, :], rows, tile)


def exit_kernel(c, *refs):
    refs = Refs(refs)
    names_ref, adj_ref, own_ref = refs.take(3)
    got = take_got(refs, c)
    handed = refs.take(c["tick"])
    out_ref, hold_ref, sems = refs.take(3)
    copies = [
        pltpu.make_async_copy(ref, out_ref.at[t, 0], sems.at[t])
        for t, ref in enumerate(handed + [hold_ref])
    ]
    for copy in copies[:-1]:
        copy.start()
    hold_ref[...] = spread_of(adj_ref, own_ref, got, names_ref, c)
    copies[-1].start()
    for copy in copies:
        copy.wait()


def finish_kernel(h, *refs):
    sums, (out_ref, hold_ref, sems) = refs[:h], refs[h:]
    layers, chunk, _ = sums[0].shape
    place = lax.rem(lax.axis_index("rows"), h)
    copies = []
    for layer in range(layers):
        for k in range(h):
            start = pl.multiple_of(jnp.bitwise_xor(place, k) * chunk, chunk)
            hold_ref[layer, pl.ds(start, chunk), :] = sums[k][layer].astype(F32)
        copy = pltpu.make_async_copy(hold_ref.at[layer], out_ref.at[0, layer], sems.at[layer])
        copy.start()
        copies.append(copy)
    for copy in copies:
        copy.wait()


def shards(grad_in, grad_last, support, preact, weights, tile_vals, tile_row, tile_col, tile_count):
    section = lax.axis_index("section")
    n = lax.axis_size("rows")
    h = n // 2
    sections = lax.axis_size("section")
    ticks = support.shape[1]
    layers = support.shape[2]
    rows, width = grad_last.shape
    tile = tile_vals.shape[-1]
    row_tiles = rows // tile
    chunk = width // h
    words = packed(tile_row, tile_col, tile_count, row_tiles)

    handed = []
    turned = None
    weight_acc = [None] * layers
    kept_chunks, pending = [], []
    initial = []
    base = dict(
        n=n, tile=tile, rows=rows, width=width, layers=layers, sections=sections, chunk=chunk,
        ticks=ticks,
    )
    layer_cost = cost(2 * rows * width * (width + (n + 1) * tile), (6 + 2 * n) * rows * width)
    small_cost = cost(rows * width, 2 * n * rows * width)
    relay_cost = cost(rows * width, 8 * n * rows * width)
    call = Call()
    call.give(VMEM, words)
    call.want(VMEM, (ticks, width), F32)
    call.want(VMEM, (2 * ticks, width), F32, h - 1)
    names, *asking = call.run(functools.partial(name_kernel, n, row_tiles), "name", small_cost)
    asked = shared(asking)

    adjs = [None] * ticks
    for tick in range(ticks):
        final = tick == ticks - 1
        if tick > 0:
            passed = lowered(handed[-1], 0)
        image = got = joined = None
        toward = 0.0
        for layer in reversed(range(layers)):
            entry = layer == layers - 1
            beta = jnp.log(BETA_SCALE / (layers * section + layer + 1).astype(F32) + 1.0)
            c = dict(
                base, layer=layer, tick=tick, entry=entry, final=final, joined=joined,
                first=tick == 0 and entry, pending=0 if layer else len(pending),
            )
            if c["first"]:
                masked = jnp.where(
                    preact[0, tick, layer] > 0, grad_in[0], jnp.zeros_like(grad_in[0])
                )
                product = jnp.dot(masked, weights[0, layer].T, preferred_element_type=F32)
                image = ((1.0 - beta) * masked.astype(F32) + beta * product).astype(BF16)
            else:
                if turned is not None:
                    lowered_far = lowered(turned[0], h)
                    nearest, *others = shared(turned[1:], lowered)
                    lowered_far, *others = lax.optimization_barrier((lowered_far, *others))
                    passed, nearest = lax.optimization_barrier((passed, nearest))
                    lowered_near = [nearest, *others]
                call = Call()
                call.give(VMEM, preact, weights, names, *asked)
                if entry:
                    call.give(VMEM, grad_last, passed)
                else:
                    call.give(VMEM, adjs[tick], image, *got)
                if final:
                    call.give(VMEM, support, weight_acc[layer])
                    if layer == 0:
                        call.give(VMEM, *pending)
                call.want(VMEM, (rows, width), BF16)
                if not entry:
                    message = tile + (layers * chunk if final and layer == 0 else 0)
                    call.want(VMEM, (message, width), BF16, h - 1)
                if final and layer:
                    call.want(VMEM, (chunk, width), BF16, h - 1)
                if final:
                    call.want(VMEM, (chunk, width), F32)
                else:
                    call.want(VMEM, (rows, width), BF16)
                if final:
                    call.scratch = [pltpu.VMEM((width, width), F32)]
                results = Refs(
                    call.run(
                        functools.partial(layer_kernel, c),
                        "home" if entry else "middle",
                        layer_cost,
                    )
                )
                image = results.take()
                sends = [] if entry else results.take(h - 1)
                if final and layer:
                    pending = results.take(h - 1) + pending
                kept = masked = results.take()
            if turned is not None:
                far, near = lowered_far, lowered_near
                turned = None
            else:
                far = swapped(image, h)
                near = [] if c["first"] else shared(sends)
            ready = image
            if c["first"]:
                adjs[0] = densify(0, words, tile_vals, row_tiles, n)
                ready, adjs[0] = lax.optimization_barrier((image, adjs[0]))
            call = Call()
            call.give(VMEM, far)
            if c["first"]:
                call.give(VMEM, ready)
            call.give(VMEM, *asked)
            call.want(VMEM, (tile * (1 + c["first"]), width), BF16, h - 1)
            relays = call.run(functools.partial(forward_kernel, c), "forward", small_cost)
            relayed = shared(relays)
            if layer == 0 and not final:
                later, *_ = lax.optimization_barrier((words, *near))
                adjs[tick + 1] = densify(tick + 1, later, tile_vals, row_tiles, n)
                relayed, adjs[tick + 1] = lax.optimization_barrier((relayed, adjs[tick + 1]))
            if final:
                kept_chunks.insert(0, kept)
            if final and layer == 0:
                kept, _ = lax.optimization_barrier((kept_chunks, relays))
                call = Call()
                call.give(VMEM, *kept, *near)
                call.want(VMEM, (layers, chunk, width), BF16)
                (mine,) = call.run(
                    functools.partial(half_sum_kernel, layers, tile), "half_sum", small_cost
                )
            got = [far, *near, *relayed]
            joined = c["first"]
            toward = toward + ALPHA * image.astype(F32)
            if not final:
                term = beta * jnp.dot(
                    support[0, tick, layer].T, masked, preferred_element_type=F32
                )
                old = weight_acc[layer]
                weight_acc[layer] = term if old is None else old + term
        initial.append(toward)
        c = dict(base, tick=tick, final=final, joined=joined)
        call = Call()
        call.give(VMEM, names, adjs[tick], image, *got)
        if not final:
            up = Call()
            up.give(HBM, preact, weights)
            up.give(VMEM, *asked)
            length = rows + width + -(-2 * ticks * (h - 1) // 16) * 16
            up.want(VMEM, (length, width), BF16)
            up.scratch = [pltpu.SemaphoreType.DMA((2,))]
            (pack,) = up.run(
                functools.partial(pack_kernel, tick + 1, layers - 1), "pack", small_cost
            )
            call.give(VMEM, raised(pack), grad_last)
            call.want(VMEM, (rows, width), BF16, 2)
            call.want(VMEM, (tile, width), BF16, h - 1)
            grad, *turned = call.run(functools.partial(turn_kernel, c), "turn", layer_cost)
            handed.append(grad)
            continue
        call.give(VMEM, *handed)
        call.want(HBM, (ticks, 1, rows, width), BF16)
        call.scratch = [pltpu.VMEM((rows, width), BF16), pltpu.SemaphoreType.DMA((ticks,))]
        exit_cost = cost(16 * 2 * rows * width * (n + 1) * tile, 16 * 2 * n * rows * width)
        (handoff,) = call.run(functools.partial(exit_kernel, c), "exit", exit_cost)
    call = Call()
    call.give(VMEM, mine, swapped(mine, h))
    call.want(VMEM, (layers, chunk, width), BF16)
    (total,) = call.run(total_kernel, "total", small_cost)
    call = Call()
    call.give(VMEM, total, *shared([total] * (h - 1)))
    call.want(HBM, (1, layers, width, width), F32)
    call.scratch = [pltpu.VMEM((layers, width, width), F32), pltpu.SemaphoreType.DMA((layers,))]
    (weight_grad,) = call.run(functools.partial(finish_kernel, h), "finish", small_cost)
    return handoff, jnp.stack(initial)[None], weight_grad


def solution(mesh):
    return jax.shard_map(
        shards,
        mesh=mesh,
        in_specs=(
            P("section", "rows", None),
            P("rows", None),
            P("section", None, None, "rows", None),
            P("section", None, None, "rows", None),
            P("section", None, None, None),
            P("section", None, "rows", None, None),
            P("section", None, "rows"),
            P("section", None, "rows"),
            P("section", None, "rows"),
        ),
        out_specs=(
            P(None, "section", "rows", None),
            P("section", None, "rows", None),
            P("section", None, None, None),
        ),
        check_vma=False,
    )
```

```python
import functools

import jax
import jax.numpy as jnp
from jax import lax
from jax.experimental import pallas as pl
from jax.experimental.pallas import tpu as pltpu
from jax.sharding import PartitionSpec as P

ALPHA = 0.1
BETA_SCALE = 0.5
VMEM = pl.BlockSpec(memory_space=pltpu.VMEM)
SMEM = pl.BlockSpec(memory_space=pltpu.SMEM)
HBM = pl.BlockSpec(memory_space=pltpu.HBM)
PARAMS = pltpu.CompilerParams(vmem_limit_bytes=24 * 2**20)
F32 = jnp.float32
BF16 = jnp.bfloat16


def cost(flops, nbytes):
    return pl.CostEstimate(flops=flops, bytes_accessed=nbytes, transcendentals=0)


def swapped(block, k):
    n = lax.axis_size("rows")
    return lax.ppermute(block, "rows", [(i, i ^ k) for i in range(n)])


def lowered(block, k):
    n, sections = lax.axis_size("rows"), lax.axis_size("section")
    route = [
        (s * n + i, (s - 1) % sections * n + (i ^ k)) for s in range(sections) for i in range(n)
    ]
    return lax.ppermute(block, ("section", "rows"), route)


def raised(block):
    sections = lax.axis_size("section")
    return lax.ppermute(block, "section", [(s, (s + 1) % sections) for s in range(sections)])


def shared(blocks, move=swapped):
    moved = {k: move(block, k) for k, block in reversed(list(enumerate(blocks, 1)))}
    return [moved[k] for k in sorted(moved)]


class Refs:
    def __init__(self, refs):
        self.refs = list(refs)

    def take(self, count=None):
        many = 1 if count is None else count
        taken, self.refs = self.refs[:many], self.refs[many:]
        return taken[0] if count is None else taken


class Call:
    def __init__(self):
        self.operands, self.specs, self.outs, self.out_specs, self.scratch = [], [], [], [], []
        self.aliases = {}

    def give(self, spec, *arrays):
        self.operands += arrays
        self.specs += [spec] * len(arrays)

    def want(self, spec, shape, dtype, count=1):
        self.outs += [jax.ShapeDtypeStruct(shape, dtype)] * count
        self.out_specs += [spec] * count

    def run(self, kernel, name, estimate, params=PARAMS):
        return pl.pallas_call(
            kernel,
            out_shape=self.outs,
            in_specs=self.specs,
            out_specs=self.out_specs,
            scratch_shapes=self.scratch,
            input_output_aliases=self.aliases,
            compiler_params=params,
            cost_estimate=estimate,
            name=name,
        )(*self.operands)


def packed(tile_row, tile_col, tile_count, row_tiles):
    owner = jnp.bitwise_xor(tile_col // row_tiles, lax.axis_index("rows"))
    words = (owner * row_tiles + tile_col % row_tiles) * row_tiles + tile_row
    live = lax.broadcasted_iota(jnp.int32, words.shape, 2) < tile_count
    return jnp.where(live, words, -1)[0]


def densify_kernel(tick, row_tiles, n, chunks, words_ref, vals_ref, out_ref, vals, acc, sems):
    entries, tile = vals.shape[:2]
    chunk = entries // chunks
    copies = []
    for c in range(chunks):
        part = pl.ds(c * chunk, chunk)
        copies.append(
            pltpu.make_async_copy(vals_ref.at[0, tick, part], vals.at[part], sems.at[c])
        )
        copies[c].start()
    acc[...] = jnp.zeros_like(acc)

    def add(e):
        word = words_ref[tick, e]
        row = lax.rem(word, row_tiles)
        block = lax.rem(lax.div(word, row_tiles), row_tiles)
        slot = lax.div(word, row_tiles * row_tiles)
        slot = jnp.where((slot == 0) & (block > 0), n - 1 + block, slot)
        rows = pl.ds(pl.multiple_of(row * tile, tile), tile)
        cols = pl.ds(pl.multiple_of(slot * tile, tile), tile)
        acc[rows, cols] += vals[e].astype(F32)

    count, step = jnp.int32(0), 1 << (entries.bit_length() - 1)
    while step:
        probe = count + step
        live = (probe <= entries) & (words_ref[tick, jnp.minimum(probe, entries) - 1] >= 0)
        count = jnp.where(live, probe, count)
        step //= 2
    for c in range(chunks):
        copies[c].wait()
        live = jnp.clip(count - c * chunk, 0, chunk)

        @pl.loop(0, live // 2)
        def _(i):
            add(c * chunk + 2 * i)
            add(c * chunk + 2 * i + 1)

        @pl.when(live % 2 == 1)
        def _():
            add(c * chunk + live - 1)

    out_ref[...] = acc[...].astype(BF16)


def densify(tick, words, vals, row_tiles, n):
    entries, tile = vals.shape[2:4]
    chunks = 4 if entries % 4 == 0 else 1
    shape = (row_tiles * tile, (n + row_tiles - 1) * tile)
    call = Call()
    call.give(SMEM, words)
    call.give(HBM, vals)
    call.want(VMEM, shape, BF16)
    call.scratch = [
        pltpu.VMEM(vals.shape[2:], BF16),
        pltpu.VMEM(shape, F32),
        pltpu.SemaphoreType.DMA((chunks,)),
    ]
    (adj,) = call.run(
        functools.partial(densify_kernel, tick, row_tiles, n, chunks),
        "densify",
        cost(entries * tile * tile * 20, entries * tile * tile * 2),
        pltpu.CompilerParams(vmem_limit_bytes=50 * 2**20),
    )
    return adj


def tile_at(ref, index, tile):
    return ref[pl.ds(pl.multiple_of(index * tile, tile), tile), :]


def name_kernel(n, row_tiles, words_ref, *out_refs):
    ticks, width = out_refs[0].shape
    for t in range(ticks):
        words = words_ref[t : t + 1, :]
        index = jnp.where(words < 0, -1, words // row_tiles)

        def named(k):
            block = index - k * row_tiles
            block = jnp.where((block >= 0) & (block < row_tiles), block, 0)
            most = jnp.max(block.astype(F32), axis=1, keepdims=True)
            return jnp.broadcast_to(most, (1, width))

        for k in range(1, n // 2):
            out_refs[k][2 * t : 2 * t + 1, :] = named(k)
            out_refs[k][2 * t + 1 : 2 * t + 2, :] = named(n // 2 + k)
        out_refs[0][t : t + 1, :] = named(n // 2)


def pack_kernel(tick, layer, preact_all, weight_all, *refs):
    asked, (out_ref, sems) = refs[:-2], refs[-2:]
    rows, width = preact_all.shape[-2:]
    loads = [
        pltpu.make_async_copy(preact_all.at[0, tick, layer], out_ref.at[:rows], sems.at[0]),
        pltpu.make_async_copy(
            weight_all.at[0, layer], out_ref.at[rows : rows + width], sems.at[1]
        ),
    ]
    for load in loads:
        load.start()
    used = sum(ref.shape[0] for ref in asked)
    rest = out_ref.shape[0] - rows - width - used
    parts = [ref[...] for ref in asked] + ([jnp.zeros((rest, width), F32)] if rest else [])
    out_ref[rows + width :, :] = jnp.concatenate(parts, axis=0).astype(BF16)
    for load in loads:
        load.wait()


def chosen(image_ref, row, rows, tile):
    index = jnp.broadcast_to(row.astype(BF16), (tile, row.shape[1]))
    result = image_ref[:tile, :]
    for i in range(1, rows // tile):
        result = jnp.where(index > i - 0.5, image_ref[i * tile : (i + 1) * tile, :], result)
    return result


def take_got(refs, c):
    far, near = refs.take(), refs.take(c["n"] // 2 - 1)
    if c["joined"]:
        return far, near, [ref.at[c["tile"] :, :] for ref in near]
    return far, near, refs.take(c["n"] // 2 - 1)


def spread_of(adj_ref, own_ref, got, names_ref, c):
    tile, rows = c["tile"], c["rows"]
    far, near, relayed = got
    far = chosen(far, names_ref[c["tick"] : c["tick"] + 1, :], rows, tile)
    near = [ref[:tile, :] for ref in near]
    relayed = [ref[:tile, :] for ref in relayed]
    blocks = jnp.concatenate(
        [own_ref[:tile, :]] + near + [far] + relayed + [own_ref[tile:, :]], axis=0
    )
    total = jnp.dot(adj_ref[...], blocks, preferred_element_type=F32)
    return ((1.0 - ALPHA) * total).astype(BF16)


def image_of(c, section, layer, grad, preact, weight):
    step = (c["layers"] * section + layer + 1).astype(F32)
    beta = jnp.log(BETA_SCALE / jnp.full((1, c["width"]), step, F32) + 1.0)
    masked = jnp.where(preact > 0, grad, jnp.zeros_like(grad))
    product = lax.dot_general(
        masked, weight, (((1,), (1,)), ((), ())), preferred_element_type=F32
    )
    image = ((1.0 - beta) * masked.astype(F32) + beta * product).astype(BF16)
    return beta, masked, image


def layer_kernel(c, *refs):
    refs = Refs(refs)
    n, tile, width, chunk = c["n"], c["tile"], c["width"], c["chunk"]
    h = n // 2
    preact_all, weight_all, names_ref = refs.take(3)
    asked = refs.take(h - 1)
    if c["entry"]:
        last_ref, passed_ref = refs.take(2)
    else:
        adj_ref, own_ref = refs.take(2)
        got = take_got(refs, c)
    if c["final"]:
        support_all, acc_ref = refs.take(2)
        pending = refs.take(c["pending"])
    image_ref = refs.take()
    sends = [] if c["entry"] else refs.take(h - 1)
    parts = refs.take(h - 1) if c["final"] and c["layer"] else []
    out_ref = refs.take()
    if c["final"]:
        term_ref = refs.take()
    preact_ref = preact_all.at[0, c["tick"], c["layer"]]
    weight_ref = weight_all.at[0, c["layer"]]
    section = lax.axis_index("section")
    if not c["entry"]:
        grad = spread_of(adj_ref, own_ref, got, names_ref, c)
    if c["entry"]:
        grad = jnp.where(section == c["sections"] - 1, last_ref[...], passed_ref[...])

    beta, masked, image = image_of(
        c, section, c["layer"], grad, preact_ref[...], weight_ref[...]
    )
    image_ref[...] = image
    if not c["entry"]:
        for send, asked_ref in zip(sends, asked):
            row = asked_ref[2 * c["tick"] : 2 * c["tick"] + 1, :]
            send[:tile, :] = chosen(image_ref, row, c["rows"], tile)
    if c["final"]:
        term = lax.dot_general(
            support_all[0, c["tick"], c["layer"]],
            masked,
            (((0,), (0,)), ((), ())),
            preferred_element_type=F32,
        )
        term_ref[...] = acc_ref[...] + beta * term
        place = lax.rem(lax.axis_index("rows"), h)
        for k in range(1, h):
            part = tile_at(term_ref, jnp.bitwise_xor(place, k), chunk).astype(BF16)
            if c["layer"]:
                parts[k - 1][...] = part
            else:
                sends[k - 1][tile : tile + chunk, :] = part
                for i, ref in enumerate(pending[k - 1 :: h - 1], 1):
                    sends[k - 1][tile + i * chunk : tile + (i + 1) * chunk, :] = ref[...]
        out_ref[...] = tile_at(term_ref, place, chunk)
    else:
        out_ref[...] = masked


def forward_kernel(c, *refs):
    refs = Refs(refs)
    count, tile, rows = c["n"] // 2 - 1, c["tile"], c["rows"]
    far_ref = refs.take()
    own_ref = refs.take() if c["first"] else None
    asked = refs.take(count)
    for asked_ref, send in zip(asked, refs.take(count)):
        row = 2 * c["tick"]
        if c["first"]:
            send[:tile, :] = chosen(own_ref, asked_ref[row : row + 1, :], rows, tile)
            send[tile:, :] = chosen(far_ref, asked_ref[row + 1 : row + 2, :], rows, tile)
        else:
            send[...] = chosen(far_ref, asked_ref[row + 1 : row + 2, :], rows, tile)


def half_sum_kernel(layers, tile, *refs):
    out_ref = refs[-1]
    chunk = out_ref.shape[1]
    for layer in range(layers):
        total = refs[layer][...]
        at = tile + layer * chunk
        for ref in refs[layers:-1]:
            total = total + ref[at : at + chunk, :].astype(F32)
        out_ref[layer] = total.astype(BF16)


def total_kernel(mine_ref, far_ref, out_ref):
    out_ref[...] = (mine_ref[...].astype(F32) + far_ref[...].astype(F32)).astype(BF16)


def turn_kernel(c, *refs):
    refs = Refs(refs)
    names_ref, adj_ref, own_ref = refs.take(3)
    got = take_got(refs, c)
    below_ref, last_ref = refs.take(2)
    grad_ref, image_ref = refs.take(2)
    sends = refs.take(c["n"] // 2 - 1)
    tile, rows, width = c["tile"], c["rows"], c["width"]
    grad = spread_of(adj_ref, own_ref, got, names_ref, c)
    grad_ref[...] = grad
    section = lax.axis_index("section")
    grad = jnp.where(section == 0, last_ref[...], grad)
    below = jnp.where(section == 0, c["sections"], section) - 1
    _, _, image = image_of(
        c, below, c["layers"] - 1, grad, below_ref[:rows, :], below_ref[rows : rows + width, :]
    )
    image_ref[...] = image
    asked = below_ref[rows + width :, :].astype(F32)
    for k, send in enumerate(sends):
        row = 2 * (k * c["ticks"] + c["tick"] + 1)
        send[...] = chosen(image_ref, asked[row : row + 1, :], rows, tile)


def exit_kernel(c, *refs):
    refs = Refs(refs)
    names_ref, adj_ref, own_ref = refs.take(3)
    got = take_got(refs, c)
    handed = refs.take(c["tick"])
    out_ref, hold_ref, sems = refs.take(3)
    copies = [
        pltpu.make_async_copy(ref, out_ref.at[t, 0], sems.at[t])
        for t, ref in enumerate(handed + [hold_ref])
    ]
    for copy in copies[:-1]:
        copy.start()
    hold_ref[...] = spread_of(adj_ref, own_ref, got, names_ref, c)
    copies[-1].start()
    for copy in copies:
        copy.wait()


def finish_kernel(h, *refs):
    sums, (out_ref, hold_ref, sems) = refs[:h], refs[h:]
    layers, chunk, _ = sums[0].shape
    place = lax.rem(lax.axis_index("rows"), h)
    copies = []
    for layer in range(layers):
        for k in range(h):
            start = pl.multiple_of(jnp.bitwise_xor(place, k) * chunk, chunk)
            hold_ref[layer, pl.ds(start, chunk), :] = sums[k][layer].astype(F32)
        copy = pltpu.make_async_copy(hold_ref.at[layer], out_ref.at[0, layer], sems.at[layer])
        copy.start()
        copies.append(copy)
    for copy in copies:
        copy.wait()


def shards(grad_in, grad_last, support, preact, weights, tile_vals, tile_row, tile_col, tile_count):
    section = lax.axis_index("section")
    n = lax.axis_size("rows")
    h = n // 2
    sections = lax.axis_size("section")
    ticks = support.shape[1]
    layers = support.shape[2]
    rows, width = grad_last.shape
    tile = tile_vals.shape[-1]
    row_tiles = rows // tile
    chunk = width // h
    words = packed(tile_row, tile_col, tile_count, row_tiles)

    handed = []
    turned = None
    weight_acc = [None] * layers
    kept_chunks, pending = [], []
    initial = []
    base = dict(
        n=n, tile=tile, rows=rows, width=width, layers=layers, sections=sections, chunk=chunk,
        ticks=ticks,
    )
    layer_cost = cost(2 * rows * width * (width + (n + 1) * tile), (6 + 2 * n) * rows * width)
    small_cost = cost(rows * width, 2 * n * rows * width)
    relay_cost = cost(rows * width, 8 * n * rows * width)
    call = Call()
    call.give(VMEM, words)
    call.want(VMEM, (ticks, width), F32)
    call.want(VMEM, (2 * ticks, width), F32, h - 1)
    names, *asking = call.run(functools.partial(name_kernel, n, row_tiles), "name", small_cost)
    asked = shared(asking)

    adjs = [None] * ticks
    for tick in range(ticks):
        final = tick == ticks - 1
        if tick > 0:
            passed = lowered(handed[-1], 0)
        image = got = joined = None
        toward = 0.0
        for layer in reversed(range(layers)):
            entry = layer == layers - 1
            beta = jnp.log(BETA_SCALE / (layers * section + layer + 1).astype(F32) + 1.0)
            c = dict(
                base, layer=layer, tick=tick, entry=entry, final=final, joined=joined,
                first=tick == 0 and entry, pending=0 if layer else len(pending),
            )
            if c["first"]:
                masked = jnp.where(
                    preact[0, tick, layer] > 0, grad_in[0], jnp.zeros_like(grad_in[0])
                )
                product = jnp.dot(masked, weights[0, layer].T, preferred_element_type=F32)
                image = ((1.0 - beta) * masked.astype(F32) + beta * product).astype(BF16)
            else:
                if turned is not None:
                    lowered_far = lowered(turned[0], h)
                    nearest, *others = shared(turned[1:], lowered)
                    lowered_far, *others = lax.optimization_barrier((lowered_far, *others))
                    passed, nearest = lax.optimization_barrier((passed, nearest))
                    lowered_near = [nearest, *others]
                call = Call()
                call.give(VMEM, preact, weights, names, *asked)
                if entry:
                    call.give(VMEM, grad_last, passed)
                else:
                    call.give(VMEM, adjs[tick], image, *got)
                if final:
                    call.give(VMEM, support, weight_acc[layer])
                    if layer == 0:
                        call.give(VMEM, *pending)
                call.want(VMEM, (rows, width), BF16)
                if not entry:
                    message = tile + (layers * chunk if final and layer == 0 else 0)
                    call.want(VMEM, (message, width), BF16, h - 1)
                if final and layer:
                    call.want(VMEM, (chunk, width), BF16, h - 1)
                if final:
                    call.want(VMEM, (chunk, width), F32)
                else:
                    call.want(VMEM, (rows, width), BF16)
                if final:
                    call.scratch = [pltpu.VMEM((width, width), F32)]
                results = Refs(
                    call.run(
                        functools.partial(layer_kernel, c),
                        "home" if entry else "middle",
                        layer_cost,
                    )
                )
                image = results.take()
                sends = [] if entry else results.take(h - 1)
                if final and layer:
                    pending = results.take(h - 1) + pending
                kept = masked = results.take()
            if turned is not None:
                far, near = lowered_far, lowered_near
                turned = None
            else:
                far = swapped(image, h)
                near = [] if c["first"] else shared(sends)
            ready = image
            if c["first"]:
                adjs[0] = densify(0, words, tile_vals, row_tiles, n)
                ready, adjs[0] = lax.optimization_barrier((image, adjs[0]))
            call = Call()
            call.give(VMEM, far)
            if c["first"]:
                call.give(VMEM, ready)
            call.give(VMEM, *asked)
            call.want(VMEM, (tile * (1 + c["first"]), width), BF16, h - 1)
            relays = call.run(functools.partial(forward_kernel, c), "forward", small_cost)
            relayed = shared(relays)
            if layer == 0 and not final:
                later, *_ = lax.optimization_barrier((words, *near))
                adjs[tick + 1] = densify(tick + 1, later, tile_vals, row_tiles, n)
                relayed, adjs[tick + 1] = lax.optimization_barrier((relayed, adjs[tick + 1]))
            if final:
                kept_chunks.insert(0, kept)
            if final and layer == 0:
                kept, _ = lax.optimization_barrier((kept_chunks, relays))
                call = Call()
                call.give(VMEM, *kept, *near)
                call.want(VMEM, (layers, chunk, width), BF16)
                (mine,) = call.run(
                    functools.partial(half_sum_kernel, layers, tile), "half_sum", small_cost
                )
            got = [far, *near, *relayed]
            joined = c["first"]
            toward = toward + ALPHA * image.astype(F32)
            if not final:
                term = beta * jnp.dot(
                    support[0, tick, layer].T, masked, preferred_element_type=F32
                )
                old = weight_acc[layer]
                weight_acc[layer] = term if old is None else old + term
        initial.append(toward)
        c = dict(base, tick=tick, final=final, joined=joined)
        call = Call()
        call.give(VMEM, names, adjs[tick], image, *got)
        if not final:
            up = Call()
            up.give(HBM, preact, weights)
            up.give(VMEM, *asked)
            length = rows + width + -(-2 * ticks * (h - 1) // 16) * 16
            up.want(VMEM, (length, width), BF16)
            up.scratch = [pltpu.SemaphoreType.DMA((2,))]
            (pack,) = up.run(
                functools.partial(pack_kernel, tick + 1, layers - 1), "pack", small_cost
            )
            call.give(VMEM, raised(pack), grad_last)
            call.want(VMEM, (rows, width), BF16, 2)
            call.want(VMEM, (tile, width), BF16, h - 1)
            grad, *turned = call.run(functools.partial(turn_kernel, c), "turn", layer_cost)
            handed.append(grad)
            continue
        call.give(VMEM, *handed)
        call.want(HBM, (ticks, 1, rows, width), BF16)
        call.scratch = [pltpu.VMEM((rows, width), BF16), pltpu.SemaphoreType.DMA((ticks,))]
        (handoff,) = call.run(functools.partial(exit_kernel, c), "exit", layer_cost)
    call = Call()
    call.give(VMEM, mine, swapped(mine, h))
    call.want(VMEM, (layers, chunk, width), BF16)
    (total,) = call.run(total_kernel, "total", small_cost)
    call = Call()
    call.give(VMEM, total, *(swapped(total, k) for k in range(1, h)))
    call.want(HBM, (1, layers, width, width), F32)
    call.scratch = [pltpu.VMEM((layers, width, width), F32), pltpu.SemaphoreType.DMA((layers,))]
    (weight_grad,) = call.run(functools.partial(finish_kernel, h), "finish", small_cost)
    return handoff, jnp.stack(initial)[None], weight_grad


def solution(mesh):
    return jax.shard_map(
        shards,
        mesh=mesh,
        in_specs=(
            P("section", "rows", None),
            P("rows", None),
            P("section", None, None, "rows", None),
            P("section", None, None, "rows", None),
            P("section", None, None, None),
            P("section", None, "rows", None, None),
            P("section", None, "rows"),
            P("section", None, "rows"),
            P("section", None, "rows"),
        ),
        out_specs=(
            P(None, "section", "rows", None),
            P("section", None, "rows", None),
            P("section", None, None, None),
        ),
        check_vma=False,
    )
```
